32 devices in a mesh: blk: 8 (over z, x), tm: 4 (over y, core).
Axes of the slice: x: 2, y: 2, z: 4, core: 2. Of those that a mesh axis runs over, the one named last changes fastest.
Arguments:
- intensity: bfloat16 [768, 16384], P('tm', 'blk'), may hold values from 0.04 to 330, as said below
- block_cycle: int32 [128], P('blk'), may hold values from 0 to 7, as said below
- cycle_order: int32 [8], replicated, may hold values from 0 to 7, as said below
Outputs:
- twotime: float32 [8, 768, 768], P('blk', 'tm')
The draws below stay inside these ranges and needn't reach their ends.
Inputs may be any that keep to these rules, and one draw needn't show every extreme that they name: `intensity`: positive corrected intensities. `block_cycle`: every cycle holds 1 to 31 blocks of the whole detector, and some cycle exactly 31; the 16 blocks of one index of blk hold at most 4 blocks of one cycle, and exactly 4 for some cycle. `cycle_order`: each cycle once.
All inputs are finite; a program needn't handle non-finite values.
Results may differ from the reference program's by a relative error of at most 0.0003.
Values may be sent and summed in bfloat16 or wider, within the bound.
No kernel may reach another device: no remote copies, remote signals or barrier semaphores. Data moves between devices by JAX's collectives and lax.ppermute only.
A program may use at most 64 MiB of HBM per device.

```python
import math
import jax
import jax.numpy as jnp
from jax import lax

BLOCK = 128
BLK_DEV = 16
PANEL = 192
CAP = 4
CYCLES = 8
RCAP = 31
NBLK = 128
PIXELS = 16384
FRAMES = 768


def draw_intensity(key, part):
    keys = jax.random.split(jax.random.fold_in(key, 7), 3)
    base = jnp.exp(jax.random.uniform(keys[0], (FRAMES, PIXELS), jnp.float32, math.log(0.05), math.log(2.0)))
    frame_scale = jnp.exp(jax.random.uniform(keys[1], (FRAMES, 1), jnp.float32, 0.0, math.log(10.0)))
    pixel_scale = jnp.exp(jax.random.uniform(keys[2], (1, PIXELS), jnp.float32, 0.0, math.log(10.0)))
    return (base * frame_scale * pixel_scale).astype(jnp.bfloat16)


def cycle_plan(key):
    half = CYCLES // 2
    keys = jax.random.split(jax.random.fold_in(key, 3), 5)
    spread = jax.random.randint(keys[0], (half,), 0, BLK_DEV).astype(jnp.int32)
    spread = spread.at[0].set(BLK_DEV - 1)
    sizes = jnp.concatenate([BLK_DEV + spread, BLK_DEV - spread]).astype(jnp.int32)
    labels = jax.random.permutation(keys[1], CYCLES).astype(jnp.int32)
    order = jax.random.permutation(keys[2], CYCLES).astype(jnp.int32)
    run_sizes = sizes[order]
    run_labels = labels[order]
    ends = jnp.cumsum(run_sizes).astype(jnp.int32)
    offset = jax.random.randint(keys[3], (), 0, NBLK).astype(jnp.int32)
    position = jnp.arange(NBLK, dtype=jnp.int32)
    shifted = (position + offset) % NBLK
    run = jnp.sum((shifted[:, None] >= ends[None, :]).astype(jnp.int32), axis=1)
    cycle_here = run_labels[run]
    device = position // CAP % CYCLES
    local = position // (CAP * CYCLES) * CAP + position % CAP
    block = device * BLK_DEV + local
    block_cycle = jnp.zeros((NBLK,), jnp.int32).at[block].set(cycle_here)
    biggest = labels[0]
    first_block = jnp.min(jnp.where(block_cycle == biggest, position, NBLK)).astype(jnp.int32)
    target = (first_block // BLK_DEV + half) % CYCLES
    perm = jax.random.permutation(keys[4], CYCLES).astype(jnp.int32)
    cycle_ids = jnp.arange(CYCLES, dtype=jnp.int32)
    where_big = jnp.sum(jnp.where(perm == biggest, cycle_ids, 0)).astype(jnp.int32)
    displaced = perm[target]
    perm = perm.at[where_big].set(displaced)
    perm = perm.at[target].set(biggest)
    return (block_cycle, perm)


def draw_block_cycle(key, part):
    return cycle_plan(key)[0]


def draw_cycle_order(key, part):
    return cycle_plan(key)[1]


def setup_inputs(seed: int = 0) -> dict:
    key_of = jax.random.split(jax.random.key(seed), 4)
    intensity = draw_intensity(jax.random.fold_in(key_of[3], 71), 0)
    block_cycle = draw_block_cycle(jax.random.fold_in(key_of[3], 71), 0)
    cycle_order = draw_cycle_order(jax.random.fold_in(key_of[3], 71), 0)
    return dict(intensity=intensity, block_cycle=block_cycle, cycle_order=cycle_order)


def reference(intensity, block_cycle, cycle_order):
    blocks = intensity.reshape(FRAMES, NBLK, BLOCK)
    tile_of = jnp.arange(FRAMES, dtype=jnp.int32) // PANEL
    upper = tile_of[:, None] <= tile_of[None, :]

    def one_cycle(cycle):
        member = block_cycle == cycle
        keyed = jnp.where(member, 0, 1).astype(jnp.int32)
        picked = jnp.argsort(keyed, stable=True)[:RCAP].astype(jnp.int32)
        valid = member[picked].astype(jnp.float32)
        rows = jnp.take(blocks, picked, axis=1).astype(jnp.float32) * valid[None, :, None]
        rows = rows.reshape(FRAMES, RCAP * BLOCK)
        gram = jnp.dot(rows, rows.T, precision=lax.Precision.HIGHEST)
        sums = jnp.sum(rows, axis=1)
        count = jnp.sum(member.astype(jnp.float32)) * BLOCK
        scaled = gram * count / (sums[:, None] * sums[None, :])
        return jnp.where(upper, scaled, jnp.float32(0.0))

    return lax.map(one_cycle, cycle_order)
```

```python
import functools
import math

import jax
import jax.numpy as jnp
from jax import lax
from jax.experimental import pallas as pl
from jax.experimental.pallas import tpu as pltpu
from jax.sharding import PartitionSpec as P

BLOCK = 128
EXTRA = 16
NONE = -32768
LEAST, MOST = -3.0, 28.0
PER_OCTAVE = 65534 / (MOST - LEAST)
MIDDLE = (MOST + LEAST) / 2
PART_UNIT, HALF_UNIT = 4096.0, 1024.0
LOW_BITS = 15
VMEM = pl.BlockSpec(memory_space=pltpu.VMEM)
SMEM = pl.BlockSpec(memory_space=pltpu.SMEM)


def times(left, right):
    return lax.dot_general(
        left, right, (((1,), (1,)), ((), ())), preferred_element_type=jnp.float32
    )


def encode(x):
    level = (jnp.log2(jnp.maximum(x, 2.0**LEAST)) - MIDDLE) * PER_OCTAVE
    code = jnp.floor(level + 0.5).astype(jnp.int32)
    return jnp.where(x > 0, code, NONE).astype(jnp.int16)


def decode(code):
    code = code.astype(jnp.int32)
    x = jnp.exp2(code.astype(jnp.float32) * (1 / PER_OCTAVE) + MIDDLE)
    return jnp.where(code == NONE, 0.0, x)


def rows_of(sums, count, like):
    row = lax.broadcasted_iota(jnp.int32, like, 0)
    return jnp.where(row == 0, sums, jnp.where(row == 1, count, 0.0))


def encode_rows(rows, unit):
    whole = (rows[0:1] * unit).astype(jnp.int32)
    row = lax.broadcasted_iota(jnp.int32, rows.shape, 0)
    high = lax.shift_right_logical(whole, LOW_BITS)
    low = lax.bitwise_and(whole, (1 << LOW_BITS) - 1)
    count = rows[1:2].astype(jnp.int32)
    zero = jnp.zeros(rows.shape, jnp.int32)
    return jnp.where(
        row == 0, high, jnp.where(row == 1, low, jnp.where(row == 2, count, zero))
    ).astype(jnp.int16)


def decode_rows(code, unit):
    code = code.astype(jnp.int32).astype(jnp.float32)
    sums = (code[0:1] * float(1 << LOW_BITS) + code[1:2]) * (1 / unit)
    return rows_of(sums, code[2:3], code.shape)


def find_slots(cap, cycle_ref, order_ref, where_ref, fill_ref, slot_ref):
    cycles = order_ref.shape[0]
    for s in range(cycles):
        where_ref[order_ref[s]] = s
        fill_ref[s] = 0
    for j in range(cycle_ref.shape[0]):
        p = where_ref[cycle_ref[j]]
        r = fill_ref[p]
        slot_ref[p * cap + r] = j
        fill_ref[p] = r + 1


def gathered(ref, s, cap, fill_ref, slot_ref, masked):
    parts = []
    for r in range(cap):
        here = r < fill_ref[s]
        j = jnp.where(here, slot_ref[s * cap + r], 0)
        x = ref[:, pl.ds(pl.multiple_of(j * BLOCK, BLOCK), BLOCK)]
        parts.append(jnp.where(here, x, jnp.zeros_like(x)) if masked else x)
    return jnp.concatenate(parts, axis=1)


def early_kernel(cap, cycle_ref, order_ref, own_ref, other_ref, *refs):
    *outs, where_ref, fill_ref, slot_ref = refs
    find_slots(cap, cycle_ref, order_ref, where_ref, fill_ref, slot_ref)
    inner = len(outs)
    panel = own_ref.shape[0]
    half = panel // 2
    mine = lax.rem(lax.axis_index("blk"), inner)
    first = lax.rem(lax.axis_index("tm"), 2) == 0
    ones = jnp.ones((EXTRA, cap * BLOCK), jnp.bfloat16)
    for k in range(inner):
        for h in range(2):
            s = h * inner + lax.bitwise_xor(mine, k)
            own = gathered(own_ref, s, cap, fill_ref, slot_ref, True)
            other = gathered(other_ref, s, cap, fill_ref, slot_ref, True)
            left = jnp.where(first, own[:half], other[half:])
            right = jnp.where(first, other, own)
            count = fill_ref[s].astype(jnp.float32)
            rows = rows_of(times(ones, own)[0:1], count, (EXTRA, panel))
            tile, part = times(own, own), times(left, right)
            if k:
                outs[k][h, :panel] = encode(tile)
                outs[k][h, panel:panel + half] = encode(part)
                outs[k][h, panel + half:] = encode_rows(rows, PART_UNIT)
            else:
                outs[k][h, :panel] = tile
                outs[k][h, panel:panel + half] = part
                outs[k][h, panel + half:] = rows


def late_kernel(cap, cycle_ref, order_ref, own_ref, other_ref, *refs):
    *refs, where_ref, fill_ref, slot_ref = refs
    find_slots(cap, cycle_ref, order_ref, where_ref, fill_ref, slot_ref)
    inner = lax.axis_size("blk") // 2
    panel = own_ref.shape[0]
    came, outs = refs[:-inner], refs[-inner:]
    mine = lax.rem(lax.axis_index("blk"), inner)
    chip = lax.div(lax.axis_index("tm"), 2)
    ones = jnp.ones((EXTRA, cap * BLOCK), jnp.bfloat16)
    for k in range(inner):
        for h in range(2):
            s = h * inner + lax.bitwise_xor(mine, k)
            own = gathered(own_ref, s, cap, fill_ref, slot_ref, True)
            other = gathered(other_ref, s, cap, fill_ref, slot_ref, True)
            count = fill_ref[s].astype(jnp.float32)
            for d, ref in enumerate(came):
                lower = chip < lax.bitwise_xor(chip, d + 1)
                far = gathered(ref, s, cap, fill_ref, slot_ref, True)
                tile = times(far, jnp.where(lower, own, other))
                sums = times(ones, jnp.where(lower, far, other))[0:1]
                rows = rows_of(sums, count, (EXTRA, panel))
                if k:
                    outs[k][h, d, :panel] = encode(tile)
                    outs[k][h, d, panel:] = encode_rows(rows, PART_UNIT)
                else:
                    outs[k][h, d, :panel] = tile
                    outs[k][h, d, panel:] = rows


def total_of(parts, h, body):
    tiles, rows = parts[0][h, ..., :body, :], parts[0][h, ..., body:, :]
    for part in parts[1:]:
        tiles = tiles + decode(part[h, ..., :body, :])
        rows = rows + decode_rows(part[h, ..., body:, :], HALF_UNIT * 4)
    return tiles, rows


def early_sum_kernel(*refs):
    *parts, home_ref, away_ref = refs
    body = home_ref.shape[0] - EXTRA
    side = lax.div(lax.axis_index("blk"), lax.axis_size("blk") // 2)
    tiles, rows = total_of(parts, side, body)
    home_ref[:body], home_ref[body:] = tiles, rows
    tiles, rows = total_of(parts, 1 - side, body)
    away_ref[:body], away_ref[body:] = encode(tiles), encode_rows(rows, HALF_UNIT)


def late_sum_kernel(*refs):
    *parts, home_ref, near_ref, away_ref = refs
    pairs, body = home_ref.shape[0], home_ref.shape[1] - EXTRA
    side = lax.div(lax.axis_index("blk"), lax.axis_size("blk") // 2)
    for d in range(pairs):
        here = [part.at[:, d] for part in parts]
        tiles, rows = total_of(here, side, body)
        home_ref[d, :body], home_ref[d, body:] = tiles, rows
        near_ref[d, :body], near_ref[d, body:] = encode(tiles), encode_rows(rows, HALF_UNIT)
        tiles, rows = total_of(here, 1 - side, body)
        away_ref[d, :body], away_ref[d, body:] = encode(tiles), encode_rows(rows, HALF_UNIT)


def early_end_kernel(home_ref, came_ref, tile_ref, part_ref):
    panel = tile_ref.shape[1]
    half = panel // 2
    body = panel + half
    tile_ref[:panel] = home_ref[:panel] + decode(came_ref[:panel])
    rows = home_ref[body:] + decode_rows(came_ref[body:], HALF_UNIT)
    tile_ref[panel:] = rows
    part_ref[:half] = home_ref[panel:body] + decode(came_ref[panel:body])
    part_ref[half:] = rows


def last_kernel(pairs, tile_ref, part_ref, other_ref, home_ref, across_ref, *refs):
    near, away = refs[:pairs], refs[pairs:2 * pairs]
    out_ref, tiles, scales = refs[2 * pairs:]
    panel = tile_ref.shape[1]
    half = panel // 2
    steps = tiles.shape[0]
    me = lax.axis_index("tm")
    chip, core = lax.div(me, 2), lax.rem(me, 2)
    mate = lax.bitwise_xor(me, 1)
    tiles[me] = tile_ref[:panel]
    tiles[mate, :half] = part_ref[:half]
    tiles[mate, half:] = other_ref[:half]
    own_sums = tile_ref[panel:panel + 1]
    scales[me] = jnp.broadcast_to(1.0 / own_sums, scales.shape[1:])
    scales[mate] = jnp.broadcast_to(1.0 / other_ref[half:half + 1], scales.shape[1:])
    for d in range(pairs):
        far_chip = lax.bitwise_xor(chip, d + 1)

        @pl.when(chip < far_chip)
        def _():
            straight, crossed = 2 * far_chip + core, 2 * far_chip + 1 - core
            tiles[straight] = (home_ref[d, :panel] + decode(across_ref[d, :panel])).T
            rows = home_ref[d, panel:] + decode_rows(across_ref[d, panel:], HALF_UNIT)
            scales[straight] = jnp.broadcast_to(1.0 / rows[0:1], scales.shape[1:])
            tiles[crossed] = decode(near[d][0, :panel]) + decode(away[d][0, :panel])
            rows = decode_rows(near[d][0, panel:], HALF_UNIT) + decode_rows(
                away[d][0, panel:], HALF_UNIT
            )
            scales[crossed] = jnp.broadcast_to(1.0 / rows[0:1], scales.shape[1:])

    count = tile_ref[panel + 1:panel + 2] * float(BLOCK)
    down = jnp.broadcast_to(count / own_sums, (panel, panel)).T
    for u in range(steps):

        @pl.when(u >= me)
        def _():
            out_ref[0, :, u * panel:(u + 1) * panel] = tiles[u] * down * scales[u, 0:1]

        @pl.when(u < me)
        def _():
            out_ref[0, :, u * panel:(u + 1) * panel] = jnp.zeros((panel, panel), jnp.float32)


def call(kernel, outs, ins, scratch=(), flops=0):
    moved = sum(math.prod(x.shape) * x.dtype.itemsize for x in (*outs, *ins))
    many = isinstance(outs, list)
    return pl.pallas_call(
        kernel,
        out_shape=outs if many else outs[0],
        in_specs=[SMEM if x.ndim == 1 else VMEM for x in ins],
        out_specs=[VMEM] * len(outs) if many else VMEM,
        scratch_shapes=scratch,
        compiler_params=pltpu.CompilerParams(vmem_limit_bytes=48 * 2**20),
        cost_estimate=pl.CostEstimate(flops=flops, bytes_accessed=moved, transcendentals=0),
    )(*ins)


def on_device(intensity, block_cycle, cycle_order):
    panel = intensity.shape[0]
    blk_dev = block_cycle.shape[0]
    cycles = cycle_order.shape[0]
    groups = lax.axis_size("blk")
    steps = lax.axis_size("tm")
    inner = groups // 2
    pairs = steps // 2 - 1
    cap = 2 * max(1, blk_dev // cycles)
    early = panel + panel // 2 + EXTRA
    late = panel + EXTRA

    def hop(x, by_blk, by_tm, sends=lambda b, t: True):
        perm = [
            (b * steps + t, (b ^ by_blk) * steps + (t ^ by_tm))
            for b in range(groups)
            for t in range(steps)
            if sends(b, t)
        ]
        return lax.ppermute(x, ("blk", "tm"), perm)

    far = [hop(intensity, 0, 2 * d) for d in range(1, pairs + 1)]
    other = hop(intensity, 0, 1)
    f32, i16 = jnp.float32, jnp.int16
    shape = jax.ShapeDtypeStruct
    scratch = [
        pltpu.SMEM((cycles,), jnp.int32),
        pltpu.SMEM((cycles,), jnp.int32),
        pltpu.SMEM((cycles * cap,), jnp.int32),
    ]
    depth = cap * BLOCK
    work = 2 * cycles * panel * panel * depth
    parts = call(
        functools.partial(early_kernel, cap),
        [shape((2, early, panel), i16 if k else f32) for k in range(inner)],
        (block_cycle, cycle_order, intensity, other),
        scratch,
        2 * work,
    )
    parts = [hop(x, k, 0) if k else x for k, x in enumerate(parts)]
    home, away = call(
        early_sum_kernel, [shape((early, panel), f32), shape((early, panel), i16)], parts
    )
    tile, part = call(
        early_end_kernel,
        [shape((panel + EXTRA, panel), f32), shape((panel // 2 + EXTRA, panel), f32)],
        (home, hop(away, inner, 0)),
    )
    other_part = hop(part, 0, 1)

    parts = call(
        functools.partial(late_kernel, cap),
        [shape((2, pairs, late, panel), i16 if k else f32) for k in range(inner)],
        (block_cycle, cycle_order, intensity, other, *far),
        scratch,
        2 * pairs * work,
    )
    parts = [hop(x, k, 0) if k else x for k, x in enumerate(parts)]
    home, near, away = call(
        late_sum_kernel,
        [shape((pairs, late, panel), t) for t in (f32, i16, i16)],
        parts,
    )

    def is_lower(t, d):
        return t // 2 < (t // 2 ^ d)

    offsets = range(1, pairs + 1)
    across = hop(away, inner, 0, lambda b, t: any(is_lower(t, d) for d in offsets))
    from_away = [
        hop(away[d - 1:d], inner, 2 * d, lambda b, t, d=d: not is_lower(t, d)) for d in offsets
    ]
    from_near = [
        hop(near[d - 1:d], 0, 2 * d, lambda b, t, d=d: not is_lower(t, d)) for d in offsets
    ]
    return call(
        functools.partial(last_kernel, pairs),
        (shape((1, panel, steps * panel), f32),),
        (tile, part, other_part, home, across, *from_near, *from_away),
        [pltpu.VMEM((steps, panel, panel), f32), pltpu.VMEM((steps, 8, panel), f32)],
    )


def solution(mesh):
    placed = (P("tm", "blk"), P("blk"), P())
    return jax.shard_map(
        on_device, mesh=mesh, in_specs=placed, out_specs=P("blk", "tm", None), check_vma=False
    )
```

```python
import functools
import math

import jax
import jax.numpy as jnp
from jax import lax
from jax.experimental import pallas as pl
from jax.experimental.pallas import tpu as pltpu
from jax.sharding import PartitionSpec as P

BLOCK = 128
EXTRA = 16
NONE = -32768
LEAST, MOST = -3.0, 28.0
PER_OCTAVE = 65534 / (MOST - LEAST)
MIDDLE = (MOST + LEAST) / 2
PART_UNIT, HALF_UNIT = 4096.0, 1024.0
LOW_BITS = 15
VMEM = pl.BlockSpec(memory_space=pltpu.VMEM)
SMEM = pl.BlockSpec(memory_space=pltpu.SMEM)


def times(left, right):
    return lax.dot_general(
        left, right, (((1,), (1,)), ((), ())), preferred_element_type=jnp.float32
    )


def encode(x):
    level = (jnp.log2(jnp.maximum(x, 2.0**LEAST)) - MIDDLE) * PER_OCTAVE
    code = jnp.floor(level + 0.5).astype(jnp.int32)
    return jnp.where(x > 0, code, NONE).astype(jnp.int16)


def decode(code):
    code = code.astype(jnp.int32)
    x = jnp.exp2(code.astype(jnp.float32) * (1 / PER_OCTAVE) + MIDDLE)
    return jnp.where(code == NONE, 0.0, x)


def rows_of(sums, count, like):
    row = lax.broadcasted_iota(jnp.int32, like, 0)
    return jnp.where(row == 0, sums, jnp.where(row == 1, count, 0.0))


def encode_rows(rows, unit):
    whole = (rows[0:1] * unit).astype(jnp.int32)
    row = lax.broadcasted_iota(jnp.int32, rows.shape, 0)
    high = lax.shift_right_logical(whole, LOW_BITS)
    low = lax.bitwise_and(whole, (1 << LOW_BITS) - 1)
    count = rows[1:2].astype(jnp.int32)
    zero = jnp.zeros(rows.shape, jnp.int32)
    return jnp.where(
        row == 0, high, jnp.where(row == 1, low, jnp.where(row == 2, count, zero))
    ).astype(jnp.int16)


def decode_rows(code, unit):
    code = code.astype(jnp.int32).astype(jnp.float32)
    sums = (code[0:1] * float(1 << LOW_BITS) + code[1:2]) * (1 / unit)
    return rows_of(sums, code[2:3], code.shape)


def find_slots(cap, plan_ref, where_ref, fill_ref, slot_ref):
    cycles = where_ref.shape[0]
    for s in range(cycles):
        where_ref[plan_ref[s]] = s
        fill_ref[s] = 0
    for j in range(plan_ref.shape[0] - cycles):
        p = where_ref[plan_ref[cycles + j]]
        r = fill_ref[p]
        slot_ref[p * cap + r] = j
        fill_ref[p] = r + 1


def gathered(ref, s, cap, fill_ref, slot_ref, masked):
    parts = []
    for r in range(cap):
        here = r < fill_ref[s]
        j = jnp.where(here, slot_ref[s * cap + r], 0)
        x = ref[:, pl.ds(pl.multiple_of(j * BLOCK, BLOCK), BLOCK)]
        parts.append(jnp.where(here, x, jnp.zeros_like(x)) if masked else x)
    return jnp.concatenate(parts, axis=1)


def early_kernel(cap, plan_ref, own_ref, other_ref, *refs):
    *outs, where_ref, fill_ref, slot_ref = refs
    find_slots(cap, plan_ref, where_ref, fill_ref, slot_ref)
    inner = len(outs)
    panel = own_ref.shape[0]
    half = panel // 2
    mine = lax.rem(lax.axis_index("blk"), inner)
    first = lax.rem(lax.axis_index("tm"), 2) == 0
    ones = jnp.ones((EXTRA, cap * BLOCK), jnp.bfloat16)
    for k in range(inner):
        for h in range(2):
            s = h * inner + lax.bitwise_xor(mine, k)
            own = gathered(own_ref, s, cap, fill_ref, slot_ref, True)
            other = gathered(other_ref, s, cap, fill_ref, slot_ref, True)
            left = jnp.where(first, own[:half], other[half:])
            right = jnp.where(first, other, own)
            count = fill_ref[s].astype(jnp.float32)
            rows = rows_of(times(ones, own)[0:1], count, (EXTRA, panel))
            tile, part = times(own, own), times(left, right)
            if k:
                outs[k][h, :panel] = encode(tile)
                outs[k][h, panel:panel + half] = encode(part)
                outs[k][h, panel + half:] = encode_rows(rows, PART_UNIT)
            else:
                outs[k][h, :panel] = tile
                outs[k][h, panel:panel + half] = part
                outs[k][h, panel + half:] = rows


def late_kernel(cap, plan_ref, own_ref, other_ref, first_ref, *refs):
    *refs, where_ref, fill_ref, slot_ref = refs
    find_slots(cap, plan_ref, where_ref, fill_ref, slot_ref)
    inner = lax.axis_size("blk") // 2
    panel = own_ref.shape[0]
    came, outs = refs[:-inner], refs[-inner:]
    mine = lax.rem(lax.axis_index("blk"), inner)
    chip = lax.div(lax.axis_index("tm"), 2)
    ones = jnp.ones((EXTRA, cap * BLOCK), jnp.bfloat16)
    for k in range(inner):
        for h in range(2):
            s = h * inner + lax.bitwise_xor(mine, k)
            own = gathered(own_ref, s, cap, fill_ref, slot_ref, True)
            other = gathered(other_ref, s, cap, fill_ref, slot_ref, True)
            count = fill_ref[s].astype(jnp.float32)
            for d, ref in enumerate(came):
                lower = chip < lax.bitwise_xor(chip, d + 1)
                far = gathered(ref, s, cap, fill_ref, slot_ref, True)
                tile = times(far, jnp.where(lower, own, other))
                sums = times(ones, jnp.where(lower, far, other))[0:1]
                rows = rows_of(sums, count, (EXTRA, panel))
                if k:
                    outs[k][h, d, :panel] = encode(tile)
                    outs[k][h, d, panel:] = encode_rows(rows, PART_UNIT)
                else:
                    outs[k][h, d, :panel] = tile
                    outs[k][h, d, panel:] = rows


def total_of(parts, h, body):
    tiles, rows = parts[0][h, ..., :body, :], parts[0][h, ..., body:, :]
    for part in parts[1:]:
        tiles = tiles + decode(part[h, ..., :body, :])
        rows = rows + decode_rows(part[h, ..., body:, :], PART_UNIT)
    return tiles, rows


def early_sum_kernel(*refs):
    *parts, home_ref, home_part_ref, away_ref, away_part_ref = refs
    panel = home_ref.shape[1]
    body = home_ref.shape[0] - EXTRA
    side = lax.div(lax.axis_index("blk"), lax.axis_size("blk") // 2)
    tiles, rows = total_of(parts, side, body)
    home_ref[:body], home_ref[body:] = tiles, rows
    home_part_ref[:-EXTRA], home_part_ref[-EXTRA:] = tiles[panel:], rows
    tiles, rows = total_of(parts, 1 - side, body)
    tiles, rows = encode(tiles), encode_rows(rows, HALF_UNIT)
    away_ref[:body], away_ref[body:] = tiles, rows
    away_part_ref[:-EXTRA], away_part_ref[-EXTRA:] = tiles[panel:], rows


def late_sum_kernel(*refs):
    *parts, home_ref, near_ref, away_ref = refs
    pairs, body = home_ref.shape[0], home_ref.shape[1] - EXTRA
    side = lax.div(lax.axis_index("blk"), lax.axis_size("blk") // 2)
    for d in range(pairs):
        here = [part.at[:, d] for part in parts]
        tiles, rows = total_of(here, side, body)
        home_ref[d, :body], home_ref[d, body:] = tiles, rows
        near_ref[d, :body], near_ref[d, body:] = encode(tiles), encode_rows(rows, HALF_UNIT)
        tiles, rows = total_of(here, 1 - side, body)
        away_ref[d, :body], away_ref[d, body:] = encode(tiles), encode_rows(rows, HALF_UNIT)


def last_kernel(pairs, home_ref, came_ref, mate_home_ref, mate_came_ref, late_ref, across_ref, *refs):
    near, away = refs[:pairs], refs[pairs:2 * pairs]
    out_ref, tiles, scales = refs[2 * pairs:]
    panel = home_ref.shape[1]
    half = panel // 2
    body = panel + half
    steps = tiles.shape[0]
    me = lax.axis_index("tm")
    chip, core = lax.div(me, 2), lax.rem(me, 2)
    rows = home_ref[body:] + decode_rows(came_ref[body:], HALF_UNIT)
    own_sums, count = rows[0:1], rows[1:2] * float(BLOCK)
    tiles[me] = home_ref[:panel] + decode(came_ref[:panel])
    scales[me] = jnp.broadcast_to(1.0 / own_sums, scales.shape[1:])

    @pl.when(core == 0)
    def _():
        tiles[me + 1, :half] = home_ref[panel:body] + decode(came_ref[panel:body])
        tiles[me + 1, half:] = mate_home_ref[:half] + decode(mate_came_ref[:half])
        rows = mate_home_ref[half:] + decode_rows(mate_came_ref[half:], HALF_UNIT)
        scales[me + 1] = jnp.broadcast_to(1.0 / rows[0:1], scales.shape[1:])

    for d in range(pairs):
        far_chip = lax.bitwise_xor(chip, d + 1)

        @pl.when(chip < far_chip)
        def _():
            straight, crossed = 2 * far_chip + core, 2 * far_chip + 1 - core
            tiles[straight] = (late_ref[d, :panel] + decode(across_ref[d, :panel])).T
            rows = late_ref[d, panel:] + decode_rows(across_ref[d, panel:], HALF_UNIT)
            scales[straight] = jnp.broadcast_to(1.0 / rows[0:1], scales.shape[1:])
            tiles[crossed] = decode(near[d][0, :panel]) + decode(away[d][0, :panel])
            rows = decode_rows(near[d][0, panel:], HALF_UNIT) + decode_rows(
                away[d][0, panel:], HALF_UNIT
            )
            scales[crossed] = jnp.broadcast_to(1.0 / rows[0:1], scales.shape[1:])

    down = jnp.broadcast_to(count / own_sums, (panel, panel)).T
    for u in range(steps):

        @pl.when(u >= me)
        def _():
            out_ref[0, :, u * panel:(u + 1) * panel] = tiles[u] * down * scales[u, 0:1]

        @pl.when(u < me)
        def _():
            out_ref[0, :, u * panel:(u + 1) * panel] = jnp.zeros((panel, panel), jnp.float32)


def call(kernel, outs, ins, scratch=(), flops=0):
    moved = sum(math.prod(x.shape) * x.dtype.itemsize for x in (*outs, *ins))
    many = isinstance(outs, list)
    return pl.pallas_call(
        kernel,
        out_shape=outs if many else outs[0],
        in_specs=[SMEM if x.ndim == 1 else VMEM for x in ins],
        out_specs=[VMEM] * len(outs) if many else VMEM,
        scratch_shapes=scratch,
        compiler_params=pltpu.CompilerParams(vmem_limit_bytes=48 * 2**20),
        cost_estimate=pl.CostEstimate(flops=flops, bytes_accessed=moved, transcendentals=0),
    )(*ins)


def on_device(intensity, block_cycle, cycle_order):
    panel = intensity.shape[0]
    blk_dev = block_cycle.shape[0]
    cycles = cycle_order.shape[0]
    groups = lax.axis_size("blk")
    steps = lax.axis_size("tm")
    inner = groups // 2
    pairs = steps // 2 - 1
    cap = 2 * max(1, blk_dev // cycles)
    early = panel + panel // 2 + EXTRA
    late = panel + EXTRA

    def hop(x, by_blk, by_tm, sends=lambda b, t: True):
        perm = [
            (b * steps + t, (b ^ by_blk) * steps + (t ^ by_tm))
            for b in range(groups)
            for t in range(steps)
            if sends(b, t)
        ]
        return lax.ppermute(x, ("blk", "tm"), perm)

    far = [hop(intensity, 0, 2 * d) for d in range(1, pairs + 1)]
    other = hop(intensity, 0, 1)
    f32, i16 = jnp.float32, jnp.int16
    shape = jax.ShapeDtypeStruct
    scratch = [
        pltpu.SMEM((cycles,), jnp.int32),
        pltpu.SMEM((cycles,), jnp.int32),
        pltpu.SMEM((cycles * cap,), jnp.int32),
    ]
    plan = jnp.concatenate([cycle_order, block_cycle])
    depth = cap * BLOCK
    work = 2 * cycles * panel * panel * depth
    parts = call(
        functools.partial(early_kernel, cap),
        [shape((2, early, panel), i16 if k else f32) for k in range(inner)],
        (plan, intensity, other),
        scratch,
        2 * work,
    )
    parts = [hop(x, k, 0) if k else x for k, x in enumerate(parts)]
    shared = panel // 2 + EXTRA
    home, home_part, away, away_part = call(
        early_sum_kernel, [shape((n, panel), t) for t in (f32, i16) for n in (early, shared)], parts
    )
    came = hop(away, inner, 0)
    mate_home = hop(home_part, 0, 1, lambda b, t: t % 2 == 1)
    mate_came = hop(away_part, inner, 1, lambda b, t: t % 2 == 1)

    parts = call(
        functools.partial(late_kernel, cap),
        [shape((2, pairs, late, panel), i16 if k else f32) for k in range(inner)],
        (plan, intensity, other, away, *far),
        scratch,
        2 * pairs * work,
    )
    parts = [hop(x, k, 0) if k else x for k, x in enumerate(parts)]
    late_home, near, late_away = call(
        late_sum_kernel,
        [shape((pairs, late, panel), t) for t in (f32, i16, i16)],
        parts,
    )

    def is_lower(t, d):
        return t // 2 < (t // 2 ^ d)

    offsets = range(1, pairs + 1)
    across = hop(late_away, inner, 0, lambda b, t: any(is_lower(t, d) for d in offsets))
    from_away = [
        hop(late_away[d - 1:d], inner, 2 * d, lambda b, t, d=d: not is_lower(t, d)) for d in offsets
    ]
    from_near = [
        hop(near[d - 1:d], 0, 2 * d, lambda b, t, d=d: not is_lower(t, d)) for d in offsets
    ]
    return call(
        functools.partial(last_kernel, pairs),
        (shape((1, panel, steps * panel), f32),),
        (home, came, mate_home, mate_came, late_home, across, *from_near, *from_away),
        [pltpu.VMEM((steps, panel, panel), f32), pltpu.VMEM((steps, 8, panel), f32)],
    )


def solution(mesh):
    placed = (P("tm", "blk"), P("blk"), P())
    return jax.shard_map(
        on_device, mesh=mesh, in_specs=placed, out_specs=P("blk", "tm", None), check_vma=False
    )
```

```python
import functools
import math

import jax
import jax.numpy as jnp
from jax import lax
from jax.experimental import pallas as pl
from jax.experimental.pallas import tpu as pltpu
from jax.sharding import PartitionSpec as P

BLOCK = 128
LANES = 128
ROWS = 8
NONE = -32768
LEAST, MOST = -3.0, 28.0
PER_OCTAVE = 65534 / (MOST - LEAST)
MIDDLE = (MOST + LEAST) / 2
PART_UNIT, HALF_UNIT = 4096.0, 1024.0
LOW_BITS = 15
VMEM = pl.BlockSpec(memory_space=pltpu.VMEM)
SMEM = pl.BlockSpec(memory_space=pltpu.SMEM)


def times(left, right):
    return lax.dot_general(
        left, right, (((1,), (1,)), ((), ())), preferred_element_type=jnp.float32
    )


def encode(x):
    level = (jnp.log2(jnp.maximum(x, 2.0**LEAST)) - MIDDLE) * PER_OCTAVE
    code = jnp.floor(level + 0.5).astype(jnp.int32)
    return jnp.where(x > 0, code, NONE).astype(jnp.int16)


def decode(code):
    code = code.astype(jnp.int32)
    x = jnp.exp2(code.astype(jnp.float32) * (1 / PER_OCTAVE) + MIDDLE)
    return jnp.where(code == NONE, 0.0, x)


def split(panel):
    whole, rest = divmod(panel, LANES)
    return whole, LANES // rest if rest else 0


def packed_rows(rows, panel, symmetric=False):
    whole, fold = split(panel)
    body = sum((i + 1) * LANES if symmetric else rows for i in range(whole))
    return body + (rows // fold if fold else 0)


def pack(tile, symmetric=False):
    rows, panel = tile.shape
    whole, fold = split(panel)
    parts = [
        tile[: (i + 1) * LANES if symmetric else rows, i * LANES:(i + 1) * LANES]
        for i in range(whole)
    ]
    if fold:
        n = rows // fold
        left = [tile[i * n:(i + 1) * n, whole * LANES:] for i in range(fold)]
        parts.append(jnp.concatenate(left, axis=1))
    return jnp.concatenate(parts, axis=0)


def unpack(x, out, symmetric=False):
    rows, panel = out.shape
    whole, fold = split(panel)
    at = 0
    for i in range(whole):
        n = (i + 1) * LANES if symmetric else rows
        out[:n, i * LANES:(i + 1) * LANES] = x[at:at + n]
        at += n
    if fold:
        n, width = rows // fold, LANES // fold
        for i in range(fold):
            out[i * n:(i + 1) * n, whole * LANES:] = x[at:, i * width:(i + 1) * width]
    if symmetric:
        for i in range(whole):
            n = (i + 1) * LANES
            if n < panel:
                out[n:, i * LANES:n] = out[i * LANES:n, n:].T


def rows_of(sums, count):
    panel = sums[0].shape[1]
    row = lax.broadcasted_iota(jnp.int32, (ROWS, LANES), 0)
    out, at = jnp.zeros((ROWS, LANES), jnp.float32), 0
    for x in sums:
        for start in range(0, panel, LANES):
            piece = x[:, start:start + LANES]
            if piece.shape[1] < LANES:
                piece = jnp.concatenate([piece] * (LANES // piece.shape[1]), axis=1)
            out = jnp.where(row == at, piece, out)
            at += 1
    return jnp.where(row == at, count, out)


def sums_of(rows, panel, which):
    per = -(-panel // LANES)
    starts = range(0, panel, LANES)
    return [
        (start, rows[which * per + i:which * per + i + 1, :min(LANES, panel - start)])
        for i, start in enumerate(starts)
    ]


def encode_rows(rows, unit):
    whole = (rows * unit).astype(jnp.int32)
    high = lax.shift_right_logical(whole, LOW_BITS)
    low = lax.bitwise_and(whole, (1 << LOW_BITS) - 1)
    return jnp.concatenate([high, low], axis=0).astype(jnp.int16)


def decode_rows(code, unit):
    x = code.astype(jnp.int32).astype(jnp.float32)
    return (x[:ROWS] * float(1 << LOW_BITS) + x[ROWS:]) * (1 / unit)


def find_slots(cap, plan_ref, where_ref, fill_ref, slot_ref):
    cycles = where_ref.shape[0]
    for s in range(cycles):
        where_ref[plan_ref[s]] = s
        fill_ref[s] = 0
    for j in range(plan_ref.shape[0] - cycles):
        p = where_ref[plan_ref[cycles + j]]
        r = fill_ref[p]
        slot_ref[p * cap + r] = j
        fill_ref[p] = r + 1


def gathered(ref, s, cap, fill_ref, slot_ref, masked):
    parts = []
    for r in range(cap):
        here = r < fill_ref[s]
        j = jnp.where(here, slot_ref[s * cap + r], 0)
        x = ref[:, pl.ds(pl.multiple_of(j * BLOCK, BLOCK), BLOCK)]
        parts.append(jnp.where(here, x, jnp.zeros_like(x)) if masked else x)
    return jnp.concatenate(parts, axis=1)


def early_kernel(cap, plan_ref, own_ref, other_ref, *refs):
    *outs, where_ref, fill_ref, slot_ref = refs
    rows, *outs = outs
    find_slots(cap, plan_ref, where_ref, fill_ref, slot_ref)
    inner = len(outs)
    panel = own_ref.shape[0]
    half = panel // 2
    mine = lax.rem(lax.axis_index("blk"), inner)
    first = lax.rem(lax.axis_index("tm"), 2) == 0
    ones = jnp.ones((16, cap * BLOCK), jnp.bfloat16)
    body = outs[0].shape[1]
    for k in range(inner):
        for h in range(2):
            s = h * inner + lax.bitwise_xor(mine, k)
            own = gathered(own_ref, s, cap, fill_ref, slot_ref, True)
            other = gathered(other_ref, s, cap, fill_ref, slot_ref, True)
            left = jnp.where(first, own[:half], other[half:])
            right = jnp.where(first, other, own)
            count = fill_ref[s].astype(jnp.float32)
            tile, part = times(own, own), times(left, right)
            sums = [times(ones, x)[0:1] for x in (own, other)]
            found = jnp.concatenate([pack(tile, True), pack(part)], axis=0)
            if k:
                outs[k][h, :body] = encode(found)
                outs[k][h, body:] = encode_rows(rows_of(sums, count), PART_UNIT)
            else:
                outs[k][h] = found
                rows[h] = rows_of(sums, count)


def late_kernel(cap, plan_ref, own_ref, other_ref, first_ref, *refs):
    *refs, where_ref, fill_ref, slot_ref = refs
    find_slots(cap, plan_ref, where_ref, fill_ref, slot_ref)
    inner = lax.axis_size("blk") // 2
    came, outs = refs[:-inner], refs[-inner:]
    mine = lax.rem(lax.axis_index("blk"), inner)
    chip = lax.div(lax.axis_index("tm"), 2)
    for k in range(inner):
        for h in range(2):
            s = h * inner + lax.bitwise_xor(mine, k)
            own = gathered(own_ref, s, cap, fill_ref, slot_ref, True)
            other = gathered(other_ref, s, cap, fill_ref, slot_ref, True)
            for d, ref in enumerate(came):
                lower = chip < lax.bitwise_xor(chip, d + 1)
                far = gathered(ref, s, cap, fill_ref, slot_ref, False)
                tile = pack(times(far, jnp.where(lower, own, other)))
                outs[k][h, d] = encode(tile) if k else tile


def early_sum_kernel(own_ref, own_rows_ref, *refs):
    *parts, home_ref, home_part_ref, home_rows_ref, away_ref, away_part_ref = refs
    body = home_ref.shape[0]
    shared = home_part_ref.shape[0]
    side = lax.div(lax.axis_index("blk"), lax.axis_size("blk") // 2)

    def total(h):
        tiles, rows = own_ref[h], own_rows_ref[h]
        for part in parts:
            tiles = tiles + decode(part[h, :body])
            rows = rows + decode_rows(part[h, body:], PART_UNIT)
        return tiles, rows

    home_ref[...], home_rows_ref[...] = total(side)
    home_part_ref[...] = home_ref[body - shared:]
    tiles, rows = total(1 - side)
    away_ref[:body], away_ref[body:] = encode(tiles), encode_rows(rows, HALF_UNIT)
    away_part_ref[...] = away_ref[body - shared:body]


def late_sum_kernel(home_rows_ref, early_away_ref, own_ref, *refs):
    *parts, home_ref, near_ref, away_ref = refs
    pairs, body = home_ref.shape[:2]
    side = lax.div(lax.axis_index("blk"), lax.axis_size("blk") // 2)

    def total(h, d):
        tiles = own_ref[h, d]
        for part in parts:
            tiles = tiles + decode(part[h, d])
        return tiles

    near_rows = encode_rows(home_rows_ref[...], HALF_UNIT)
    away_rows = early_away_ref[-2 * ROWS:]
    for d in range(pairs):
        tiles = total(side, d)
        home_ref[d] = tiles
        near_ref[d, :body], near_ref[d, body:] = encode(tiles), near_rows
        away_ref[d, :body], away_ref[d, body:] = encode(total(1 - side, d)), away_rows


def last_kernel(
    pairs, home_ref, rows_ref, came_ref, mate_home_ref, mate_came_ref, late_ref, across_ref, *refs
):
    near, away = refs[:pairs], refs[pairs:2 * pairs]
    out_ref, tiles, scales, turned = refs[2 * pairs:]
    steps, panel = tiles.shape[:2]
    half = panel // 2
    body, shared = home_ref.shape[0], mate_home_ref.shape[0]
    diagonal = body - shared
    me = lax.axis_index("tm")
    chip, core = lax.div(me, 2), lax.rem(me, 2)

    def set_scale(u, rows, which):
        for start, x in sums_of(rows, panel, which):
            scales[u, 0:1, start:start + x.shape[1]] = 1.0 / x

    rows = rows_ref[...] + decode_rows(came_ref[body:], HALF_UNIT)
    at = 2 * -(-panel // LANES)
    count = rows[at:at + 1, 0:1] * float(BLOCK)
    set_scale(me, rows, 0)
    unpack(home_ref[:diagonal] + decode(came_ref[:diagonal]), tiles.at[me], True)

    @pl.when(core == 0)
    def _():
        set_scale(me + 1, rows, 1)
        unpack(
            home_ref[diagonal:] + decode(came_ref[diagonal:body]), tiles.at[me + 1, pl.ds(0, half)]
        )
        unpack(
            mate_home_ref[...] + decode(mate_came_ref[...]),
            tiles.at[me + 1, pl.ds(half, panel - half)],
        )

    for d in range(pairs):
        far_chip = lax.bitwise_xor(chip, d + 1)
        late = late_ref.shape[1]

        @pl.when(chip < far_chip)
        def _():
            straight, crossed = 2 * far_chip + core, 2 * far_chip + 1 - core
            unpack(late_ref[d] + decode(across_ref[d, :late]), turned)
            tiles[straight] = turned[...].T
            unpack(decode(near[d][0, :late]) + decode(away[d][0, :late]), tiles.at[crossed])
            rows = decode_rows(near[d][0, late:], HALF_UNIT) + decode_rows(
                away[d][0, late:], HALF_UNIT
            )
            set_scale(straight, rows, 0)
            set_scale(crossed, rows, 1)

    down = jnp.broadcast_to(scales[me, 0:1] * count, (panel, panel)).T
    for u in range(steps):

        @pl.when(u >= me)
        def _():
            out_ref[0, :, u * panel:(u + 1) * panel] = tiles[u] * down * scales[u, 0:1]

        @pl.when(u < me)
        def _():
            out_ref[0, :, u * panel:(u + 1) * panel] = jnp.zeros((panel, panel), jnp.float32)


def call(kernel, outs, ins, scratch=(), flops=0):
    moved = sum(math.prod(x.shape) * x.dtype.itemsize for x in (*outs, *ins))
    many = isinstance(outs, list)
    return pl.pallas_call(
        kernel,
        out_shape=outs if many else outs[0],
        in_specs=[SMEM if x.ndim == 1 else VMEM for x in ins],
        out_specs=[VMEM] * len(outs) if many else VMEM,
        scratch_shapes=scratch,
        compiler_params=pltpu.CompilerParams(vmem_limit_bytes=48 * 2**20),
        cost_estimate=pl.CostEstimate(flops=flops, bytes_accessed=moved, transcendentals=0),
    )(*ins)


def on_device(intensity, block_cycle, cycle_order):
    panel = intensity.shape[0]
    blk_dev = block_cycle.shape[0]
    cycles = cycle_order.shape[0]
    groups = lax.axis_size("blk")
    steps = lax.axis_size("tm")
    inner = groups // 2
    pairs = steps // 2 - 1
    cap = 2 * max(1, blk_dev // cycles)
    shared = packed_rows(panel // 2, panel)
    early = packed_rows(panel, panel, True) + shared
    late = packed_rows(panel, panel)

    def hop(x, by_blk, by_tm, sends=lambda b, t: True):
        perm = [
            (b * steps + t, (b ^ by_blk) * steps + (t ^ by_tm))
            for b in range(groups)
            for t in range(steps)
            if sends(b, t)
        ]
        return lax.ppermute(x, ("blk", "tm"), perm)

    far = [hop(intensity, 0, 2 * d) for d in range(1, pairs + 1)]
    other = hop(intensity, 0, 1)
    f32, i16 = jnp.float32, jnp.int16
    shape = jax.ShapeDtypeStruct
    scratch = [
        pltpu.SMEM((cycles,), jnp.int32),
        pltpu.SMEM((cycles,), jnp.int32),
        pltpu.SMEM((cycles * cap,), jnp.int32),
    ]
    plan = jnp.concatenate([cycle_order, block_cycle])
    depth = cap * BLOCK
    work = 2 * cycles * panel * panel * depth
    own_rows, *parts = call(
        functools.partial(early_kernel, cap),
        [
            shape((2, ROWS, LANES), f32),
            shape((2, early, LANES), f32),
            *[shape((2, early + 2 * ROWS, LANES), i16)] * (inner - 1),
        ],
        (plan, intensity, other),
        scratch,
        2 * work,
    )
    parts = [hop(x, k, 0) if k else x for k, x in enumerate(parts)]
    home, home_part, home_rows, away, away_part = call(
        early_sum_kernel,
        [
            shape((early, LANES), f32),
            shape((shared, LANES), f32),
            shape((ROWS, LANES), f32),
            shape((early + 2 * ROWS, LANES), i16),
            shape((shared, LANES), i16),
        ],
        (parts[0], own_rows, *parts[1:]),
    )
    came = hop(away, inner, 0)
    mate_home = hop(home_part, 0, 1, lambda b, t: t % 2 == 1)
    mate_came = hop(away_part, inner, 1, lambda b, t: t % 2 == 1)

    parts = call(
        functools.partial(late_kernel, cap),
        [shape((2, pairs, late, LANES), i16 if k else f32) for k in range(inner)],
        (plan, intensity, other, away, *far),
        scratch,
        2 * pairs * work,
    )
    parts = [hop(x, k, 0) if k else x for k, x in enumerate(parts)]
    late_home, near, late_away = call(
        late_sum_kernel,
        [
            shape((pairs, late, LANES), f32),
            shape((pairs, late + 2 * ROWS, LANES), i16),
            shape((pairs, late + 2 * ROWS, LANES), i16),
        ],
        (home_rows, away, *parts),
    )

    def is_lower(t, d):
        return t // 2 < (t // 2 ^ d)

    offsets = range(1, pairs + 1)
    across = hop(late_away, inner, 0, lambda b, t: any(is_lower(t, d) for d in offsets))
    from_away = [
        hop(late_away[d - 1:d], inner, 2 * d, lambda b, t, d=d: not is_lower(t, d)) for d in offsets
    ]
    from_near = [
        hop(near[d - 1:d], 0, 2 * d, lambda b, t, d=d: not is_lower(t, d)) for d in offsets
    ]
    return call(
        functools.partial(last_kernel, pairs),
        (shape((1, panel, steps * panel), f32),),
        (home, home_rows, came, mate_home, mate_came, late_home, across, *from_near, *from_away),
        [
            pltpu.VMEM((steps, panel, panel), f32),
            pltpu.VMEM((steps, 8, panel), f32),
            pltpu.VMEM((panel, panel), f32),
        ],
    )


def solution(mesh):
    placed = (P("tm", "blk"), P("blk"), P())
    return jax.shard_map(
        on_device, mesh=mesh, in_specs=placed, out_specs=P("blk", "tm", None), check_vma=False
    )
```

```python
import functools
import math

import jax
import jax.numpy as jnp
from jax import lax
from jax.experimental import pallas as pl
from jax.experimental.pallas import tpu as pltpu
from jax.sharding import PartitionSpec as P

BLOCK = 128
LANES = 128
ROWS = 8
NONE = -32768
LEAST, MOST = -3.0, 28.0
PER_OCTAVE = 65534 / (MOST - LEAST)
MIDDLE = (MOST + LEAST) / 2
PART_UNIT, HALF_UNIT = 4096.0, 1024.0
LOW_BITS = 15
VMEM = pl.BlockSpec(memory_space=pltpu.VMEM)
SMEM = pl.BlockSpec(memory_space=pltpu.SMEM)


def times(left, right):
    return lax.dot_general(
        left, right, (((1,), (1,)), ((), ())), preferred_element_type=jnp.float32
    )


def encode(x):
    level = jnp.log(jnp.maximum(x, 2.0**LEAST)) * (PER_OCTAVE / math.log(2))
    code = (level + (0.5 - LEAST * PER_OCTAVE)).astype(jnp.int32) + (NONE + 1)
    return jnp.where(x[0:1] > 0, code, NONE).astype(jnp.int16)


def decode(code):
    code = code.astype(jnp.int32)
    level = code.astype(jnp.float32) * (math.log(2) / PER_OCTAVE) + MIDDLE * math.log(2)
    return jnp.where(code[0:1] > NONE, jnp.exp(level), 0.0)


def split(panel):
    whole, rest = divmod(panel, LANES)
    return whole, LANES // rest if rest else 0


def packed_rows(rows, panel, symmetric=False):
    whole, fold = split(panel)
    body = sum((i + 1) * LANES if symmetric else rows for i in range(whole))
    return body + (rows // fold if fold else 0)


def pack(tile, symmetric=False):
    rows, panel = tile.shape
    whole, fold = split(panel)
    parts = [
        tile[: (i + 1) * LANES if symmetric else rows, i * LANES:(i + 1) * LANES]
        for i in range(whole)
    ]
    if fold:
        n = rows // fold
        left = [tile[i * n:(i + 1) * n, whole * LANES:] for i in range(fold)]
        parts.append(jnp.concatenate(left, axis=1))
    return jnp.concatenate(parts, axis=0)


def unpack(x, out, symmetric=False):
    rows, panel = out.shape
    whole, fold = split(panel)
    at = 0
    for i in range(whole):
        n = (i + 1) * LANES if symmetric else rows
        out[:n, i * LANES:(i + 1) * LANES] = x[at:at + n]
        at += n
    if fold:
        n, width = rows // fold, LANES // fold
        for i in range(fold):
            out[i * n:(i + 1) * n, whole * LANES:] = x[at:, i * width:(i + 1) * width]
    if symmetric:
        for i in range(whole):
            n = (i + 1) * LANES
            if n < panel:
                out[n:, i * LANES:n] = out[i * LANES:n, n:].T


def rows_of(sums, count):
    panel = sums[0].shape[1]
    row = lax.broadcasted_iota(jnp.int32, (ROWS, LANES), 0)
    out, at = jnp.zeros((ROWS, LANES), jnp.float32), 0
    for x in sums:
        for start in range(0, panel, LANES):
            piece = x[:, start:start + LANES]
            if piece.shape[1] < LANES:
                piece = jnp.concatenate([piece] * (LANES // piece.shape[1]), axis=1)
            out = jnp.where(row == at, piece, out)
            at += 1
    return jnp.where(row == at, count, out)


def sums_of(rows, panel, which):
    per = -(-panel // LANES)
    starts = range(0, panel, LANES)
    return [
        (start, rows[which * per + i:which * per + i + 1, :min(LANES, panel - start)])
        for i, start in enumerate(starts)
    ]


def encode_rows(rows, unit):
    whole = (rows * unit).astype(jnp.int32)
    high = lax.shift_right_logical(whole, LOW_BITS)
    low = lax.bitwise_and(whole, (1 << LOW_BITS) - 1)
    return jnp.concatenate([high, low], axis=0).astype(jnp.int16)


def decode_rows(code, unit):
    x = code.astype(jnp.int32).astype(jnp.float32)
    return (x[:ROWS] * float(1 << LOW_BITS) + x[ROWS:]) * (1 / unit)


def find_slots(cap, plan_ref, where_ref, fill_ref, slot_ref):
    cycles = where_ref.shape[0]
    for s in range(cycles):
        where_ref[plan_ref[s]] = s
        fill_ref[s] = 0
    for j in range(plan_ref.shape[0] - cycles):
        p = where_ref[plan_ref[cycles + j]]
        r = fill_ref[p]
        slot_ref[p * cap + r] = j
        fill_ref[p] = r + 1


def gathered(ref, s, cap, fill_ref, slot_ref, masked):
    parts = []
    for r in range(cap):
        here = r < fill_ref[s]
        j = jnp.where(here, slot_ref[s * cap + r], 0)
        x = ref[:, pl.ds(pl.multiple_of(j * BLOCK, BLOCK), BLOCK)]
        parts.append(jnp.where(here, x, jnp.zeros_like(x)) if masked else x)
    return jnp.concatenate(parts, axis=1)


def early_kernel(cap, plan_ref, own_ref, other_ref, *refs):
    *outs, where_ref, fill_ref, slot_ref = refs
    rows, *outs = outs
    find_slots(cap, plan_ref, where_ref, fill_ref, slot_ref)
    inner = len(outs)
    panel = own_ref.shape[0]
    half = panel // 2
    mine = lax.rem(lax.axis_index("blk"), inner)
    first = lax.rem(lax.axis_index("tm"), 2) == 0
    ones = jnp.ones((16, cap * BLOCK), jnp.bfloat16)
    body = outs[0].shape[1]
    for k in range(inner):
        for h in range(2):
            s = h * inner + lax.bitwise_xor(mine, k)
            own = gathered(own_ref, s, cap, fill_ref, slot_ref, True)
            other = gathered(other_ref, s, cap, fill_ref, slot_ref, True)
            left = jnp.where(first, own[:half], other[half:])
            right = jnp.where(first, other, own)
            count = fill_ref[s].astype(jnp.float32)
            tile, part = times(own, own), times(left, right)
            sums = [times(ones, x)[0:1] for x in (own, other)]
            found = jnp.concatenate([pack(tile, True), pack(part)], axis=0)
            if k:
                outs[k][h, :body] = encode(found)
                outs[k][h, body:] = encode_rows(rows_of(sums, count), PART_UNIT)
            else:
                outs[k][h] = found
                rows[h] = rows_of(sums, count)


def late_kernel(cap, plan_ref, own_ref, other_ref, first_ref, *refs):
    *refs, where_ref, fill_ref, slot_ref = refs
    find_slots(cap, plan_ref, where_ref, fill_ref, slot_ref)
    inner = lax.axis_size("blk") // 2
    came, outs = refs[:-inner], refs[-inner:]
    mine = lax.rem(lax.axis_index("blk"), inner)
    chip = lax.div(lax.axis_index("tm"), 2)
    for k in range(inner):
        for h in range(2):
            s = h * inner + lax.bitwise_xor(mine, k)
            own = gathered(own_ref, s, cap, fill_ref, slot_ref, True)
            other = gathered(other_ref, s, cap, fill_ref, slot_ref, True)
            for d, ref in enumerate(came):
                lower = chip < lax.bitwise_xor(chip, d + 1)
                far = gathered(ref, s, cap, fill_ref, slot_ref, False)
                tile = pack(times(far, jnp.where(lower, own, other)))
                outs[k][h, d] = encode(tile) if k else tile


def early_sum_kernel(own_ref, own_rows_ref, *refs):
    *parts, home_ref, home_part_ref, home_rows_ref, away_ref, away_part_ref = refs
    body = home_ref.shape[0]
    shared = home_part_ref.shape[0]
    side = lax.div(lax.axis_index("blk"), lax.axis_size("blk") // 2)

    def total(h):
        tiles, rows = own_ref[h], own_rows_ref[h]
        for part in parts:
            tiles = tiles + decode(part[h, :body])
            rows = rows + decode_rows(part[h, body:], PART_UNIT)
        return tiles, rows

    home_ref[...], home_rows_ref[...] = total(side)
    home_part_ref[...] = home_ref[body - shared:]
    tiles, rows = total(1 - side)
    away_ref[:body], away_ref[body:] = encode(tiles), encode_rows(rows, HALF_UNIT)
    away_part_ref[...] = away_ref[body - shared:body]


def late_sum_kernel(home_rows_ref, early_away_ref, own_ref, *refs):
    *parts, home_ref, near_ref, away_ref = refs
    pairs, body = home_ref.shape[:2]
    side = lax.div(lax.axis_index("blk"), lax.axis_size("blk") // 2)

    def total(h, d):
        tiles = own_ref[h, d]
        for part in parts:
            tiles = tiles + decode(part[h, d])
        return tiles

    near_rows = encode_rows(home_rows_ref[...], HALF_UNIT)
    away_rows = early_away_ref[-2 * ROWS:]
    for d in range(pairs):
        tiles = total(side, d)
        home_ref[d] = tiles
        near_ref[d, :body], near_ref[d, body:] = encode(tiles), near_rows
        away_ref[d, :body], away_ref[d, body:] = encode(total(1 - side, d)), away_rows


def last_kernel(
    pairs, home_ref, rows_ref, came_ref, mate_home_ref, mate_came_ref, late_ref, *refs
):
    away, near = refs[:pairs], refs[pairs:2 * pairs]
    across_ref, out_ref, tiles, scales, turned = refs[2 * pairs:]
    steps, panel = tiles.shape[:2]
    half = panel // 2
    body, shared = home_ref.shape[0], mate_home_ref.shape[0]
    diagonal = body - shared
    me = lax.axis_index("tm")
    chip, core = lax.div(me, 2), lax.rem(me, 2)

    def set_scale(u, rows, which):
        for start, x in sums_of(rows, panel, which):
            scales[u, 0:1, start:start + x.shape[1]] = 1.0 / x

    rows = rows_ref[...] + decode_rows(came_ref[body:], HALF_UNIT)
    at = 2 * -(-panel // LANES)
    count = rows[at:at + 1, 0:1] * float(BLOCK)
    set_scale(me, rows, 0)
    unpack(home_ref[:diagonal] + decode(came_ref[:diagonal]), tiles.at[me], True)

    @pl.when(core == 0)
    def _():
        set_scale(me + 1, rows, 1)
        unpack(
            home_ref[diagonal:] + decode(came_ref[diagonal:body]), tiles.at[me + 1, pl.ds(0, half)]
        )
        unpack(
            mate_home_ref[...] + decode(mate_came_ref[...]),
            tiles.at[me + 1, pl.ds(half, panel - half)],
        )

    for d in range(pairs):
        far_chip = lax.bitwise_xor(chip, d + 1)
        late = late_ref.shape[1]

        @pl.when(chip < far_chip)
        def _():
            straight, crossed = 2 * far_chip + core, 2 * far_chip + 1 - core
            unpack(late_ref[d] + decode(across_ref[d, :late]), turned)
            tiles[straight] = turned[...].T
            unpack(decode(near[d][0, :late]) + decode(away[d][0, :late]), tiles.at[crossed])
            rows = decode_rows(near[d][0, late:], HALF_UNIT) + decode_rows(
                away[d][0, late:], HALF_UNIT
            )
            set_scale(straight, rows, 0)
            set_scale(crossed, rows, 1)

    down = jnp.broadcast_to(scales[me, 0:1] * count, (panel, panel)).T
    for u in range(steps):

        @pl.when(u >= me)
        def _():
            out_ref[0, :, u * panel:(u + 1) * panel] = tiles[u] * down * scales[u, 0:1]

        @pl.when(u < me)
        def _():
            out_ref[0, :, u * panel:(u + 1) * panel] = jnp.zeros((panel, panel), jnp.float32)


def call(kernel, outs, ins, scratch=(), flops=0):
    moved = sum(math.prod(x.shape) * x.dtype.itemsize for x in (*outs, *ins))
    many = isinstance(outs, list)
    return pl.pallas_call(
        kernel,
        out_shape=outs if many else outs[0],
        in_specs=[SMEM if x.ndim == 1 else VMEM for x in ins],
        out_specs=[VMEM] * len(outs) if many else VMEM,
        scratch_shapes=scratch,
        compiler_params=pltpu.CompilerParams(vmem_limit_bytes=48 * 2**20),
        cost_estimate=pl.CostEstimate(flops=flops, bytes_accessed=moved, transcendentals=0),
    )(*ins)


def on_device(intensity, block_cycle, cycle_order):
    panel = intensity.shape[0]
    blk_dev = block_cycle.shape[0]
    cycles = cycle_order.shape[0]
    groups = lax.axis_size("blk")
    steps = lax.axis_size("tm")
    inner = groups // 2
    pairs = steps // 2 - 1
    cap = 2 * max(1, blk_dev // cycles)
    shared = packed_rows(panel // 2, panel)
    early = packed_rows(panel, panel, True) + shared
    late = packed_rows(panel, panel)

    def hop(x, by_blk, by_tm, sends=lambda b, t: True):
        perm = [
            (b * steps + t, (b ^ by_blk) * steps + (t ^ by_tm))
            for b in range(groups)
            for t in range(steps)
            if sends(b, t)
        ]
        return lax.ppermute(x, ("blk", "tm"), perm)

    far = [hop(intensity, 0, 2 * d) for d in range(1, pairs + 1)]
    other = hop(intensity, 0, 1)
    f32, i16 = jnp.float32, jnp.int16
    shape = jax.ShapeDtypeStruct
    scratch = [
        pltpu.SMEM((cycles,), jnp.int32),
        pltpu.SMEM((cycles,), jnp.int32),
        pltpu.SMEM((cycles * cap,), jnp.int32),
    ]
    plan = jnp.concatenate([cycle_order, block_cycle])
    depth = cap * BLOCK
    work = 2 * cycles * panel * panel * depth
    own_rows, *parts = call(
        functools.partial(early_kernel, cap),
        [
            shape((2, ROWS, LANES), f32),
            shape((2, early, LANES), f32),
            *[shape((2, early + 2 * ROWS, LANES), i16)] * (inner - 1),
        ],
        (plan, intensity, other),
        scratch,
        2 * work,
    )
    parts = [hop(x, k, 0) if k else x for k, x in enumerate(parts)]
    home, home_part, home_rows, away, away_part = call(
        early_sum_kernel,
        [
            shape((early, LANES), f32),
            shape((shared, LANES), f32),
            shape((ROWS, LANES), f32),
            shape((early + 2 * ROWS, LANES), i16),
            shape((shared, LANES), i16),
        ],
        (parts[0], own_rows, *parts[1:]),
    )
    came = hop(away, inner, 0)
    mate_home = hop(home_part, 0, 1, lambda b, t: t % 2 == 1)
    mate_came = hop(away_part, inner, 1, lambda b, t: t % 2 == 1)

    parts = call(
        functools.partial(late_kernel, cap),
        [shape((2, pairs, late, LANES), i16 if k else f32) for k in range(inner)],
        (plan, intensity, other, away, *far),
        scratch,
        2 * pairs * work,
    )
    parts = [hop(x, k, 0) if k else x for k, x in enumerate(parts)]
    late_home, near, late_away = call(
        late_sum_kernel,
        [
            shape((pairs, late, LANES), f32),
            shape((pairs, late + 2 * ROWS, LANES), i16),
            shape((pairs, late + 2 * ROWS, LANES), i16),
        ],
        (home_rows, away, *parts),
    )

    def is_lower(t, d):
        return t // 2 < (t // 2 ^ d)

    offsets = range(1, pairs + 1)
    across = hop(late_away, inner, 0, lambda b, t: any(is_lower(t, d) for d in offsets))
    from_away = [
        hop(late_away[d - 1:d], inner, 2 * d, lambda b, t, d=d: not is_lower(t, d)) for d in offsets
    ]
    from_near = [
        hop(near[d - 1:d], 0, 2 * d, lambda b, t, d=d: not is_lower(t, d)) for d in offsets
    ]
    return call(
        functools.partial(last_kernel, pairs),
        (shape((1, panel, steps * panel), f32),),
        (home, home_rows, came, mate_home, mate_came, late_home, *from_away, *from_near, across),
        [
            pltpu.VMEM((steps, panel, panel), f32),
            pltpu.VMEM((steps, 8, panel), f32),
            pltpu.VMEM((panel, panel), f32),
        ],
    )


def solution(mesh):
    placed = (P("tm", "blk"), P("blk"), P())
    return jax.shard_map(
        on_device, mesh=mesh, in_specs=placed, out_specs=P("blk", "tm", None), check_vma=False
    )
```

```python
import functools
import math

import jax
import jax.numpy as jnp
from jax import lax
from jax.experimental import pallas as pl
from jax.experimental.pallas import tpu as pltpu
from jax.sharding import PartitionSpec as P

BLOCK = 128
LANES = 128
ROWS = 8
NONE = -32768
LEAST, MOST = -3.0, 28.0
PER_OCTAVE = 65534 / (MOST - LEAST)
MIDDLE = (MOST + LEAST) / 2
PART_UNIT, HALF_UNIT = 4096.0, 1024.0
LOW_BITS = 15
VMEM = pl.BlockSpec(memory_space=pltpu.VMEM)
SMEM = pl.BlockSpec(memory_space=pltpu.SMEM)


def times(left, right):
    return lax.dot_general(
        left, right, (((1,), (1,)), ((), ())), preferred_element_type=jnp.float32
    )


def encode(x):
    level = jnp.log(jnp.maximum(x, 2.0**LEAST)) * (PER_OCTAVE / math.log(2))
    code = (level + (0.5 - LEAST * PER_OCTAVE)).astype(jnp.int32) + (NONE + 1)
    return jnp.where(x[0:1] > 0, code, NONE).astype(jnp.int16)


def decode(code):
    code = code.astype(jnp.int32)
    level = code.astype(jnp.float32) * (math.log(2) / PER_OCTAVE) + MIDDLE * math.log(2)
    return jnp.where(code[0:1] > NONE, jnp.exp(level), 0.0)


def split(panel):
    whole, rest = divmod(panel, LANES)
    return whole, LANES // rest if rest else 0


def packed_rows(rows, panel, symmetric=False):
    whole, fold = split(panel)
    body = sum((i + 1) * LANES if symmetric else rows for i in range(whole))
    return body + (rows // fold if fold else 0)


def pack(tile, symmetric=False):
    rows, panel = tile.shape
    whole, fold = split(panel)
    parts = [
        tile[: (i + 1) * LANES if symmetric else rows, i * LANES:(i + 1) * LANES]
        for i in range(whole)
    ]
    if fold:
        n = rows // fold
        left = [tile[i * n:(i + 1) * n, whole * LANES:] for i in range(fold)]
        parts.append(jnp.concatenate(left, axis=1))
    return jnp.concatenate(parts, axis=0)


def unpack(x, out, symmetric=False):
    rows, panel = out.shape
    whole, fold = split(panel)
    at = 0
    for i in range(whole):
        n = (i + 1) * LANES if symmetric else rows
        out[:n, i * LANES:(i + 1) * LANES] = x[at:at + n]
        at += n
    if fold:
        n, width = rows // fold, LANES // fold
        for i in range(fold):
            out[i * n:(i + 1) * n, whole * LANES:] = x[at:, i * width:(i + 1) * width]
    if symmetric:
        for i in range(whole):
            n = (i + 1) * LANES
            if n < panel:
                out[n:, i * LANES:n] = out[i * LANES:n, n:].T


def rows_of(sums, count):
    panel = sums[0].shape[1]
    row = lax.broadcasted_iota(jnp.int32, (ROWS, LANES), 0)
    out, at = jnp.zeros((ROWS, LANES), jnp.float32), 0
    for x in sums:
        for start in range(0, panel, LANES):
            piece = x[:, start:start + LANES]
            if piece.shape[1] < LANES:
                piece = jnp.concatenate([piece] * (LANES // piece.shape[1]), axis=1)
            out = jnp.where(row == at, piece, out)
            at += 1
    return jnp.where(row == at, count, out)


def sums_of(rows, panel, which):
    per = -(-panel // LANES)
    starts = range(0, panel, LANES)
    return [
        (start, rows[which * per + i:which * per + i + 1, :min(LANES, panel - start)])
        for i, start in enumerate(starts)
    ]


def encode_rows(rows, unit):
    whole = (rows * unit).astype(jnp.int32)
    high = lax.shift_right_logical(whole, LOW_BITS)
    low = lax.bitwise_and(whole, (1 << LOW_BITS) - 1)
    return jnp.concatenate([high, low], axis=0).astype(jnp.int16)


def decode_rows(code, unit):
    x = code.astype(jnp.int32).astype(jnp.float32)
    return (x[:ROWS] * float(1 << LOW_BITS) + x[ROWS:]) * (1 / unit)


def find_slots(cap, plan_ref, where_ref, fill_ref, slot_ref):
    cycles = where_ref.shape[0]
    for s in range(cycles):
        where_ref[plan_ref[s]] = s
        fill_ref[s] = 0
    for j in range(plan_ref.shape[0] - cycles):
        p = where_ref[plan_ref[cycles + j]]
        r = fill_ref[p]
        slot_ref[p * cap + r] = j
        fill_ref[p] = r + 1


def gathered(ref, s, cap, fill_ref, slot_ref, masked):
    parts = []
    for r in range(cap):
        here = r < fill_ref[s]
        j = jnp.where(here, slot_ref[s * cap + r], 0)
        x = ref[:, pl.ds(pl.multiple_of(j * BLOCK, BLOCK), BLOCK)]
        parts.append(jnp.where(here, x, jnp.zeros_like(x)) if masked else x)
    return jnp.concatenate(parts, axis=1)


def early_kernel(cap, plan_ref, own_ref, other_ref, *refs):
    *outs, where_ref, fill_ref, slot_ref = refs
    rows, *outs = outs
    find_slots(cap, plan_ref, where_ref, fill_ref, slot_ref)
    inner = len(outs)
    panel = own_ref.shape[0]
    half = panel // 2
    mine = lax.rem(lax.axis_index("blk"), inner)
    first = lax.rem(lax.axis_index("tm"), 2) == 0
    ones = jnp.ones((16, cap * BLOCK), jnp.bfloat16)
    body = outs[0].shape[1]
    for k in range(inner):
        for h in range(2):
            s = h * inner + lax.bitwise_xor(mine, k)
            own = gathered(own_ref, s, cap, fill_ref, slot_ref, True)
            other = gathered(other_ref, s, cap, fill_ref, slot_ref, True)
            left = jnp.where(first, own[:half], other[half:])
            right = jnp.where(first, other, own)
            count = fill_ref[s].astype(jnp.float32)
            tile, part = times(own, own), times(left, right)
            sums = [times(ones, x)[0:1] for x in (own, other)]
            found = jnp.concatenate([pack(tile, True), pack(part)], axis=0)
            if k:
                outs[k][h, :body] = encode(found)
                outs[k][h, body:] = encode_rows(rows_of(sums, count), PART_UNIT)
            else:
                outs[k][h] = found
                rows[h] = rows_of(sums, count)


def late_kernel(cap, after, plan_ref, own_ref, other_ref, *refs):
    *refs, where_ref, fill_ref, slot_ref = refs[after:]
    find_slots(cap, plan_ref, where_ref, fill_ref, slot_ref)
    inner = lax.axis_size("blk") // 2
    came, outs = refs[:-inner], refs[-inner:]
    mine = lax.rem(lax.axis_index("blk"), inner)
    chip = lax.div(lax.axis_index("tm"), 2)
    for k in range(inner):
        for h in range(2):
            s = h * inner + lax.bitwise_xor(mine, k)
            own = gathered(own_ref, s, cap, fill_ref, slot_ref, True)
            other = gathered(other_ref, s, cap, fill_ref, slot_ref, True)
            for d, ref in enumerate(came):
                lower = chip < lax.bitwise_xor(chip, d + 1)
                far = gathered(ref, s, cap, fill_ref, slot_ref, False)
                tile = pack(times(far, jnp.where(lower, own, other)))
                outs[k][h, d] = encode(tile) if k else tile


def early_sum_kernel(own_ref, own_rows_ref, *refs):
    *parts, home_ref, home_part_ref, home_rows_ref, away_ref, away_part_ref = refs
    body = home_ref.shape[0]
    shared = home_part_ref.shape[0]
    side = lax.div(lax.axis_index("blk"), lax.axis_size("blk") // 2)

    def total(h):
        tiles, rows = own_ref[h], own_rows_ref[h]
        for part in parts:
            tiles = tiles + decode(part[h, :body])
            rows = rows + decode_rows(part[h, body:], PART_UNIT)
        return tiles, rows

    home_ref[...], home_rows_ref[...] = total(side)
    home_part_ref[...] = home_ref[body - shared:]
    tiles, rows = total(1 - side)
    away_ref[:body], away_ref[body:] = encode(tiles), encode_rows(rows, HALF_UNIT)
    away_part_ref[...] = away_ref[body - shared:body]


def late_sum_kernel(pieces, home_rows_ref, early_away_ref, first_ref, *refs):
    *parts, home_ref, near_ref, away_ref = refs
    pairs, body = home_ref.shape[:2]
    inner = len(parts) // pieces
    side = lax.div(lax.axis_index("blk"), lax.axis_size("blk") // 2)

    def total(h, d, piece):
        own, *came = parts[piece * inner:(piece + 1) * inner]
        tiles = own[h, d]
        for part in came:
            tiles = tiles + decode(part[h, d])
        return tiles

    near_rows = encode_rows(home_rows_ref[...], HALF_UNIT)
    away_rows = early_away_ref[-2 * ROWS:]
    for d in range(pairs):
        at = 0
        for piece in range(pieces):
            here = pl.ds(at, parts[piece * inner].shape[2])
            tiles = total(side, d, piece)
            home_ref[d, here] = tiles
            near_ref[d, here] = encode(tiles)
            away_ref[d, here] = encode(total(1 - side, d, piece))
            at += here.size
        near_ref[d, body:], away_ref[d, body:] = near_rows, away_rows


def early_end_kernel(
    home_ref, rows_ref, came_ref, mate_home_ref, mate_came_ref, own_ref, mate_ref, down_ref, scale_ref
):
    panel = own_ref.shape[0]
    half = panel // 2
    body, shared = home_ref.shape[0], mate_home_ref.shape[0]
    diagonal = body - shared
    rows = rows_ref[...] + decode_rows(came_ref[body:], HALF_UNIT)
    at = 2 * -(-panel // LANES)
    count = rows[at:at + 1, 0:1] * float(BLOCK)
    for which in range(2):
        set_scale(scale_ref.at[which], rows, which)
    down = jnp.broadcast_to(scale_ref[0, 0:1] * count, (panel, panel)).T
    down_ref[...] = down
    unpack(home_ref[:diagonal] + decode(came_ref[:diagonal]), own_ref, True)
    unpack(
        home_ref[diagonal:] + decode(came_ref[diagonal:body]), mate_ref.at[pl.ds(0, half)]
    )
    unpack(
        mate_home_ref[...] + decode(mate_came_ref[...]), mate_ref.at[pl.ds(half, panel - half)]
    )
    own_ref[...] = own_ref[...] * down * scale_ref[0, 0:1]
    mate_ref[...] = mate_ref[...] * down * scale_ref[1, 0:1]


def set_scale(ref, rows, which):
    for start, x in sums_of(rows, ref.shape[1], which):
        ref[0:1, start:start + x.shape[1]] = 1.0 / x


def last_kernel(pairs, pieces, own_ref, mate_ref, down_ref, late_ref, *refs):
    away, near = refs[:pairs], refs[pairs:2 * pairs]
    across_ref, out_ref, tiles, scale, turned = refs[2 * pairs:]
    steps, panel = tiles.shape[:2]
    me = lax.axis_index("tm")
    chip, core = lax.div(me, 2), lax.rem(me, 2)
    tiles[me] = own_ref[...]

    @pl.when(core == 0)
    def _():
        tiles[me + 1] = mate_ref[...]

    def unpack_pieces(x, out):
        at = row = 0
        for n in pieces:
            packed = packed_rows(n, panel)
            unpack(x[at:at + packed], out.at[pl.ds(row, n)])
            at, row = at + packed, row + n

    for d in range(pairs):
        far_chip = lax.bitwise_xor(chip, d + 1)
        late = late_ref.shape[1]

        @pl.when(chip < far_chip)
        def _():
            straight, crossed = 2 * far_chip + core, 2 * far_chip + 1 - core
            rows = decode_rows(near[d][0, late:], HALF_UNIT) + decode_rows(
                away[d][0, late:], HALF_UNIT
            )
            unpack_pieces(late_ref[d] + decode(across_ref[d, :late]), turned)
            set_scale(scale, rows, 0)
            tiles[straight] = turned[...].T * down_ref[...] * scale[0:1]
            unpack_pieces(decode(near[d][0, :late]) + decode(away[d][0, :late]), turned)
            set_scale(scale, rows, 1)
            tiles[crossed] = turned[...] * down_ref[...] * scale[0:1]

    for u in range(steps):

        @pl.when(u >= me)
        def _():
            out_ref[0, :, u * panel:(u + 1) * panel] = tiles[u]

        @pl.when(u < me)
        def _():
            out_ref[0, :, u * panel:(u + 1) * panel] = jnp.zeros((panel, panel), jnp.float32)


def call(kernel, outs, ins, scratch=(), flops=0):
    moved = sum(math.prod(x.shape) * x.dtype.itemsize for x in (*outs, *ins))
    many = isinstance(outs, list)
    return pl.pallas_call(
        kernel,
        out_shape=outs if many else outs[0],
        in_specs=[SMEM if x.ndim == 1 else VMEM for x in ins],
        out_specs=[VMEM] * len(outs) if many else VMEM,
        scratch_shapes=scratch,
        compiler_params=pltpu.CompilerParams(vmem_limit_bytes=48 * 2**20),
        cost_estimate=pl.CostEstimate(flops=flops, bytes_accessed=moved, transcendentals=0),
    )(*ins)


def on_device(intensity, block_cycle, cycle_order):
    panel = intensity.shape[0]
    blk_dev = block_cycle.shape[0]
    cycles = cycle_order.shape[0]
    groups = lax.axis_size("blk")
    steps = lax.axis_size("tm")
    inner = groups // 2
    pairs = steps // 2 - 1
    cap = 2 * max(1, blk_dev // cycles)
    shared = packed_rows(panel // 2, panel)
    early = packed_rows(panel, panel, True) + shared
    first = panel * 2 // 3 // 32 * 32
    pieces = (first, panel - first)
    late = [packed_rows(n, panel) for n in pieces]

    def hop(x, by_blk, by_tm, sends=lambda b, t: True):
        perm = [
            (b * steps + t, (b ^ by_blk) * steps + (t ^ by_tm))
            for b in range(groups)
            for t in range(steps)
            if sends(b, t)
        ]
        return lax.ppermute(x, ("blk", "tm"), perm)

    offsets = range(1, pairs + 1)
    other = hop(intensity, 0, 1)
    far = [[hop(intensity[:first], 0, 2 * d) for d in offsets]]
    far.append([hop(intensity[first:], 0, 2 * d) for d in offsets])
    f32, i16 = jnp.float32, jnp.int16
    shape = jax.ShapeDtypeStruct
    scratch = [
        pltpu.SMEM((cycles,), jnp.int32),
        pltpu.SMEM((cycles,), jnp.int32),
        pltpu.SMEM((cycles * cap,), jnp.int32),
    ]
    plan = jnp.concatenate([cycle_order, block_cycle])
    depth = cap * BLOCK
    work = 2 * cycles * panel * panel * depth
    own_rows, *parts = call(
        functools.partial(early_kernel, cap),
        [
            shape((2, ROWS, LANES), f32),
            shape((2, early, LANES), f32),
            *[shape((2, early + 2 * ROWS, LANES), i16)] * (inner - 1),
        ],
        (plan, intensity, other),
        scratch,
        2 * work,
    )
    parts = [hop(x, k, 0) if k else x for k, x in enumerate(parts)]
    home, home_part, home_rows, away, away_part = call(
        early_sum_kernel,
        [
            shape((early, LANES), f32),
            shape((shared, LANES), f32),
            shape((ROWS, LANES), f32),
            shape((early + 2 * ROWS, LANES), i16),
            shape((shared, LANES), i16),
        ],
        (parts[0], own_rows, *parts[1:]),
    )
    came = hop(away, inner, 0)
    mate_home = hop(home_part, 0, 1, lambda b, t: t % 2 == 1)
    mate_came = hop(away_part, inner, 1, lambda b, t: t % 2 == 1)

    parts, after = [], ()
    for rows, came_rows in zip(late, far):
        made = call(
            functools.partial(late_kernel, cap, len(after)),
            [shape((2, pairs, rows, LANES), i16 if k else f32) for k in range(inner)],
            (plan, intensity, other, *after, *came_rows),
            scratch,
            pairs * work,
        )
        parts += [hop(x, k, 0) if k else x for k, x in enumerate(made)]
        after = (away, made[1])
    late_home, near, late_away = call(
        functools.partial(late_sum_kernel, len(pieces)),
        [
            shape((pairs, sum(late), LANES), f32),
            shape((pairs, sum(late) + 2 * ROWS, LANES), i16),
            shape((pairs, sum(late) + 2 * ROWS, LANES), i16),
        ],
        (home_rows, away, mate_home, *parts),
    )
    own_tile, mate_tile, down, _ = call(
        early_end_kernel,
        [shape((panel, panel), f32)] * 3 + [shape((2, 8, panel), f32)],
        (home, home_rows, came, mate_home, mate_came),
    )

    def is_lower(t, d):
        return t // 2 < (t // 2 ^ d)

    across = hop(late_away, inner, 0, lambda b, t: any(is_lower(t, d) for d in offsets))
    from_away = [
        hop(late_away[d - 1:d], inner, 2 * d, lambda b, t, d=d: not is_lower(t, d)) for d in offsets
    ]
    from_near = [
        hop(near[d - 1:d], 0, 2 * d, lambda b, t, d=d: not is_lower(t, d)) for d in offsets
    ]
    return call(
        functools.partial(last_kernel, pairs, pieces),
        (shape((1, panel, steps * panel), f32),),
        (own_tile, mate_tile, down, late_home, *from_away, *from_near, across),
        [
            pltpu.VMEM((steps, panel, panel), f32),
            pltpu.VMEM((8, panel), f32),
            pltpu.VMEM((panel, panel), f32),
        ],
    )


def solution(mesh):
    placed = (P("tm", "blk"), P("blk"), P())
    return jax.shard_map(
        on_device, mesh=mesh, in_specs=placed, out_specs=P("blk", "tm", None), check_vma=False
    )
```

```python
import functools
import math

import jax
import jax.numpy as jnp
from jax import lax
from jax.experimental import pallas as pl
from jax.experimental.pallas import tpu as pltpu
from jax.sharding import PartitionSpec as P

BLOCK = 128
LANES = 128
ROWS = 8
NONE = -32768
LEAST, MOST = -3.0, 28.0
PER_OCTAVE = 65534 / (MOST - LEAST)
MIDDLE = (MOST + LEAST) / 2
PART_UNIT, HALF_UNIT, WHOLE_UNIT = 8192.0, 2048.0, 1024.0
LOW = 1 << 16
VMEM = pl.BlockSpec(memory_space=pltpu.VMEM)
SMEM = pl.BlockSpec(memory_space=pltpu.SMEM)


def times(left, right):
    return lax.dot_general(
        left, right, (((1,), (1,)), ((), ())), preferred_element_type=jnp.float32
    )


def encode(x):
    level = jnp.log(jnp.maximum(x, 2.0**LEAST)) * (PER_OCTAVE / math.log(2))
    code = (level + (0.5 - LEAST * PER_OCTAVE)).astype(jnp.int32) + (NONE + 1)
    return jnp.where(x[0:1] > 0, code, NONE).astype(jnp.int16)


def decode(code):
    code = code.astype(jnp.int32)
    level = code.astype(jnp.float32) * (math.log(2) / PER_OCTAVE) + MIDDLE * math.log(2)
    return jnp.where(code[0:1] > NONE, jnp.exp(level), 0.0)


def split(panel):
    whole, rest = divmod(panel, LANES)
    return whole, LANES // rest if rest else 0


def packed_rows(rows, panel, symmetric=False):
    whole, fold = split(panel)
    body = sum((i + 1) * LANES if symmetric else rows for i in range(whole))
    return body + (rows // fold if fold else 0)


def pack(tile, symmetric=False):
    rows, panel = tile.shape
    whole, fold = split(panel)
    parts = [
        tile[: (i + 1) * LANES if symmetric else rows, i * LANES:(i + 1) * LANES]
        for i in range(whole)
    ]
    if fold:
        n = rows // fold
        left = [tile[i * n:(i + 1) * n, whole * LANES:] for i in range(fold)]
        parts.append(jnp.concatenate(left, axis=1))
    return jnp.concatenate(parts, axis=0)


def unpack(x, out, symmetric=False):
    rows, panel = out.shape
    whole, fold = split(panel)
    at = 0
    for i in range(whole):
        n = (i + 1) * LANES if symmetric else rows
        out[:n, i * LANES:(i + 1) * LANES] = x[at:at + n]
        at += n
    if fold:
        n, width = rows // fold, LANES // fold
        for i in range(fold):
            out[i * n:(i + 1) * n, whole * LANES:] = x[at:, i * width:(i + 1) * width]
    if symmetric:
        for i in range(whole):
            n = (i + 1) * LANES
            if n < panel:
                out[n:, i * LANES:n] = out[i * LANES:n, n:].T


def rows_of(sums, count):
    panel = sums[0].shape[1]
    row = lax.broadcasted_iota(jnp.int32, (ROWS, LANES), 0)
    out, at = jnp.zeros((ROWS, LANES), jnp.float32), 0
    for x in sums:
        for start in range(0, panel, LANES):
            piece = x[:, start:start + LANES]
            if piece.shape[1] < LANES:
                piece = jnp.concatenate([piece] * (LANES // piece.shape[1]), axis=1)
            out = jnp.where(row == at, piece, out)
            at += 1
    return jnp.where(row == at, count, out)


def sums_of(rows, panel, which):
    per = -(-panel // LANES)
    starts = range(0, panel, LANES)
    return [
        (start, rows[which * per + i:which * per + i + 1, :min(LANES, panel - start)])
        for i, start in enumerate(starts)
    ]


def encode_rows(rows, unit):
    whole = (rows * unit + 0.5).astype(jnp.int32)
    high = lax.shift_right_logical(whole, 16)
    low = lax.bitwise_and(whole, LOW - 1) - LOW // 2
    return jnp.concatenate([high, low], axis=0).astype(jnp.int16)


def decode_rows(code, unit):
    x = code.astype(jnp.int32).astype(jnp.float32)
    return (x[:ROWS] * float(LOW) + (x[ROWS:] + LOW / 2)) * (1 / unit)


def find_slots(cap, plan_ref, where_ref, fill_ref, slot_ref):
    cycles = where_ref.shape[0]
    for s in range(cycles):
        where_ref[plan_ref[s]] = s
        fill_ref[s] = 0
    for j in range(plan_ref.shape[0] - cycles):
        p = where_ref[plan_ref[cycles + j]]
        r = fill_ref[p]
        slot_ref[p * cap + r] = j
        fill_ref[p] = r + 1


def gathered(ref, s, cap, fill_ref, slot_ref, masked):
    parts = []
    for r in range(cap):
        here = r < fill_ref[s]
        j = jnp.where(here, slot_ref[s * cap + r], 0)
        x = ref[:, pl.ds(pl.multiple_of(j * BLOCK, BLOCK), BLOCK)]
        parts.append(jnp.where(here, x, jnp.zeros_like(x)) if masked else x)
    return jnp.concatenate(parts, axis=1)


def early_kernel(cap, plan_ref, own_ref, other_ref, *refs):
    sorted_ref, rows_ref, *outs, where_ref, fill_ref, slot_ref = refs
    find_slots(cap, plan_ref, where_ref, fill_ref, slot_ref)
    inner = len(outs)
    panel = own_ref.shape[0]
    half = panel // 2
    mine = lax.rem(lax.axis_index("blk"), inner)
    first = lax.rem(lax.axis_index("tm"), 2) == 0
    ones = jnp.ones((16, cap * BLOCK), jnp.bfloat16)
    body = outs[0].shape[1]
    for k in range(inner):
        for h in range(2):
            s = h * inner + lax.bitwise_xor(mine, k)
            own = gathered(own_ref, s, cap, fill_ref, slot_ref, True)
            other = gathered(other_ref, s, cap, fill_ref, slot_ref, True)
            sorted_ref[0, k, h] = own
            sorted_ref[1, k, h] = other
            left = jnp.where(first, own[:half], other[half:])
            right = jnp.where(first, other, own)
            count = fill_ref[s].astype(jnp.float32)
            tile, part = times(own, own), times(left, right)
            sums = [times(ones, x)[0:1] for x in (own, other)]
            found = jnp.concatenate([pack(tile, True), pack(part)], axis=0)
            if k:
                outs[k][h, :body] = encode(found)
                outs[k][h, body:] = encode_rows(rows_of(sums, count), PART_UNIT)
            else:
                outs[k][h] = found
                rows_ref[h] = rows_of(sums, count)


def late_kernel(cap, after, plan_ref, sorted_ref, *refs):
    *refs, where_ref, fill_ref, slot_ref = refs[after:]
    find_slots(cap, plan_ref, where_ref, fill_ref, slot_ref)
    inner = lax.axis_size("blk") // 2
    came, outs = refs[:-inner], refs[-inner:]
    mine = lax.rem(lax.axis_index("blk"), inner)
    chip = lax.div(lax.axis_index("tm"), 2)
    for k in range(inner):
        for h in range(2):
            s = h * inner + lax.bitwise_xor(mine, k)
            for d, ref in enumerate(came):
                upper = (chip > lax.bitwise_xor(chip, d + 1)).astype(jnp.int32)
                far = gathered(ref, s, cap, fill_ref, slot_ref, False)
                tile = pack(times(sorted_ref[upper, k, h], far))
                outs[k][h, d] = encode(tile) if k else tile


def early_sum_kernel(own_ref, own_rows_ref, *refs):
    *parts, home_ref, rows_ref, away_ref = refs
    body = home_ref.shape[0]
    side = lax.div(lax.axis_index("blk"), lax.axis_size("blk") // 2)

    def total(h):
        tiles, rows = own_ref[h], own_rows_ref[h]
        for part in parts:
            tiles = tiles + decode(part[h, :body])
            rows = rows + decode_rows(part[h, body:], PART_UNIT)
        return tiles, rows

    home_ref[...], rows_ref[...] = total(side)
    tiles, rows = total(1 - side)
    away_ref[:body], away_ref[body:] = encode(tiles), encode_rows(rows, HALF_UNIT)


def late_sum_kernel(pieces, *refs):
    *parts, home_ref, away_ref = refs
    inner = len(parts) // pieces
    side = lax.div(lax.axis_index("blk"), lax.axis_size("blk") // 2)
    for d in range(home_ref.shape[0]):
        at = 0
        for piece in range(pieces):
            own, *came = parts[piece * inner:(piece + 1) * inner]
            here = pl.ds(at, own.shape[2])
            for h, out in ((side, home_ref), (1 - side, away_ref)):
                tiles = own[h, d]
                for part in came:
                    tiles = tiles + decode(part[h, d])
                out[d, here] = tiles if out is home_ref else encode(tiles)
            at += own.shape[2]


def late_end_kernel(home_ref, across_ref, rows_ref, came_ref, near_ref):
    pairs, body = home_ref.shape[:2]
    rows = rows_ref[...] + decode_rows(came_ref[-2 * ROWS:], HALF_UNIT)
    rows = encode_rows(rows, WHOLE_UNIT)
    for d in range(pairs):
        near_ref[d, :body] = encode(home_ref[d] + decode(across_ref[d]))
        near_ref[d, body:] = rows


def set_scale(ref, rows, which):
    for start, x in sums_of(rows, ref.shape[1], which):
        ref[0:1, start:start + x.shape[1]] = 1.0 / x


def early_end_kernel(
    home_ref, rows_ref, came_ref, late_ref, across_ref, after_ref,
    own_ref, part_ref, straight_ref, down_ref, scale_ref,
):
    half, panel = part_ref.shape
    body, diagonal = home_ref.shape[0], packed_rows(panel, panel, True)
    rows = rows_ref[...] + decode_rows(came_ref[body:], HALF_UNIT)
    unpack(home_ref[diagonal:] + decode(came_ref[diagonal:body]), part_ref)
    unpack(home_ref[:diagonal] + decode(came_ref[:diagonal]), own_ref, True)
    at = 2 * -(-panel // LANES)
    count = rows[at:at + 1, 0:1] * float(BLOCK)
    for which in range(2):
        set_scale(scale_ref.at[which], rows, which)
    down = jnp.broadcast_to(scale_ref[0, 0:1] * count, (panel, panel)).T
    down_ref[...] = down
    own_ref[...] = own_ref[...] * down * scale_ref[0, 0:1]
    for d in range(late_ref.shape[0]):
        unpack(late_ref[d] + decode(across_ref[d]), straight_ref.at[d])


def last_kernel(own_ref, part_ref, mate_part_ref, straight_ref, down_ref, scale_ref, *refs):
    *near, out_ref, tiles, scale, turned = refs
    steps, panel = tiles.shape[:2]
    half = panel // 2
    me = lax.axis_index("tm")
    chip, core = lax.div(me, 2), lax.rem(me, 2)
    tiles[me] = own_ref[...]

    @pl.when(core == 0)
    def _():
        tiles[me + 1, :half] = part_ref[...] * down_ref[:half] * scale_ref[1, 0:1]
        tiles[me + 1, half:] = mate_part_ref[...] * down_ref[half:] * scale_ref[1, 0:1]

    for d, ref in enumerate(near):
        far_chip = lax.bitwise_xor(chip, d + 1)
        body = ref.shape[1] - 2 * ROWS

        @pl.when(chip < far_chip)
        def _():
            rows = decode_rows(ref[0, body:], WHOLE_UNIT)
            set_scale(scale, rows, 0)
            tiles[2 * far_chip + core] = straight_ref[d] * down_ref[...] * scale[0:1]
            unpack(decode(ref[0, :body]), turned)
            set_scale(scale, rows, 1)
            tiles[2 * far_chip + 1 - core] = turned[...].T * down_ref[...] * scale[0:1]

    for u in range(steps):

        @pl.when(u >= me)
        def _():
            out_ref[0, :, u * panel:(u + 1) * panel] = tiles[u]

        @pl.when(u < me)
        def _():
            out_ref[0, :, u * panel:(u + 1) * panel] = jnp.zeros((panel, panel), jnp.float32)


def call(kernel, outs, ins, scratch=(), flops=0):
    moved = sum(math.prod(x.shape) * x.dtype.itemsize for x in (*outs, *ins))
    many = isinstance(outs, list)
    return pl.pallas_call(
        kernel,
        out_shape=outs if many else outs[0],
        in_specs=[SMEM if x.ndim == 1 else VMEM for x in ins],
        out_specs=[VMEM] * len(outs) if many else VMEM,
        scratch_shapes=scratch,
        compiler_params=pltpu.CompilerParams(vmem_limit_bytes=48 * 2**20),
        cost_estimate=pl.CostEstimate(flops=flops, bytes_accessed=moved, transcendentals=0),
    )(*ins)


def on_device(intensity, block_cycle, cycle_order):
    panel = intensity.shape[0]
    blk_dev = block_cycle.shape[0]
    cycles = cycle_order.shape[0]
    groups = lax.axis_size("blk")
    steps = lax.axis_size("tm")
    inner = groups // 2
    pairs = steps // 2 - 1
    cap = 2 * max(1, blk_dev // cycles)
    early = packed_rows(panel, panel, True) + packed_rows(panel // 2, panel)
    first = panel // LANES * LANES
    pieces = [n for n in (first, panel - first) if n]
    late = [panel * n // LANES for n in pieces]

    def hop(x, by_blk, by_tm, sends=lambda b, t: True):
        perm = [
            (b * steps + t, (b ^ by_blk) * steps + (t ^ by_tm))
            for b in range(groups)
            for t in range(steps)
            if sends(b, t)
        ]
        return lax.ppermute(x, ("blk", "tm"), perm)

    offsets = range(1, pairs + 1)
    other = hop(intensity, 0, 1)
    starts = [sum(pieces[:i]) for i in range(len(pieces))]
    far = [[hop(intensity[at:at + n], 0, 2 * d) for d in offsets] for at, n in zip(starts, pieces)]
    f32, i16 = jnp.float32, jnp.int16
    shape = jax.ShapeDtypeStruct
    scratch = [
        pltpu.SMEM((cycles,), jnp.int32),
        pltpu.SMEM((cycles,), jnp.int32),
        pltpu.SMEM((cycles * cap,), jnp.int32),
    ]
    plan = jnp.concatenate([cycle_order, block_cycle])
    depth = cap * BLOCK
    work = 2 * cycles * panel * panel * depth
    gathers, own_rows, *parts = call(
        functools.partial(early_kernel, cap),
        [
            shape((2, inner, 2, panel, depth), jnp.bfloat16),
            shape((2, ROWS, LANES), f32),
            shape((2, early, LANES), f32),
            *[shape((2, early + 2 * ROWS, LANES), i16)] * (inner - 1),
        ],
        (plan, intensity, other),
        scratch,
        2 * work,
    )
    parts = [hop(x, k, 0) if k else x for k, x in enumerate(parts)]
    home, home_rows, away = call(
        early_sum_kernel,
        [
            shape((early, LANES), f32),
            shape((ROWS, LANES), f32),
            shape((early + 2 * ROWS, LANES), i16),
        ],
        (parts[0], own_rows, *parts[1:]),
    )
    came = hop(away, inner, 0)

    parts, after = [], ()
    for rows, came_rows in zip(late, far):
        made = call(
            functools.partial(late_kernel, cap, len(after)),
            [shape((2, pairs, rows, LANES), i16 if k else f32) for k in range(inner)],
            (plan, gathers, *after, *came_rows),
            scratch,
            pairs * work,
        )
        parts += [hop(x, k, 0) if k else x for k, x in enumerate(made)]
        after = (away, made[1])
    late_home, late_away = call(
        functools.partial(late_sum_kernel, len(pieces)),
        [shape((pairs, sum(late), LANES), t) for t in (f32, i16)],
        parts,
    )
    across = hop(late_away, inner, 0)
    near = call(
        late_end_kernel,
        (shape((pairs, sum(late) + 2 * ROWS, LANES), i16),),
        (late_home, across, home_rows, came),
    )
    own_tile, part, straight, down, scale = call(
        early_end_kernel,
        [
            shape((panel, panel), f32),
            shape((panel // 2, panel), f32),
            shape((pairs, panel, panel), f32),
            shape((panel, panel), f32),
            shape((2, 8, panel), f32),
        ],
        (home, home_rows, came, late_home, across, near),
    )
    mate_part = hop(part, 0, 1, lambda b, t: t % 2 == 1)
    from_near = [
        hop(near[d - 1:d], 0, 2 * d, lambda b, t, d=d: t // 2 > (t // 2 ^ d)) for d in offsets
    ]
    return call(
        last_kernel,
        (shape((1, panel, steps * panel), f32),),
        (own_tile, part, mate_part, straight, down, scale, *from_near),
        [
            pltpu.VMEM((steps, panel, panel), f32),
            pltpu.VMEM((8, panel), f32),
            pltpu.VMEM((panel, panel), f32),
        ],
    )


def solution(mesh):
    placed = (P("tm", "blk"), P("blk"), P())
    return jax.shard_map(
        on_device, mesh=mesh, in_specs=placed, out_specs=P("blk", "tm", None), check_vma=False
    )
```

```python
import functools
import math

import jax
import jax.numpy as jnp
from jax import lax
from jax.experimental import pallas as pl
from jax.experimental.pallas import tpu as pltpu
from jax.sharding import PartitionSpec as P

BLOCK = 128
LANES = 128
ROWS = 8
NONE = -32768
LEAST, MOST = -3.0, 28.0
PER_OCTAVE = 65534 / (MOST - LEAST)
MIDDLE = (MOST + LEAST) / 2
PART_UNIT, HALF_UNIT, WHOLE_UNIT = 8192.0, 2048.0, 1024.0
LOW = 1 << 16
VMEM = pl.BlockSpec(memory_space=pltpu.VMEM)
SMEM = pl.BlockSpec(memory_space=pltpu.SMEM)


def times(left, right):
    return lax.dot_general(
        left, right, (((1,), (1,)), ((), ())), preferred_element_type=jnp.float32
    )


def encode(x):
    level = jnp.log(jnp.maximum(x, 2.0**LEAST)) * (PER_OCTAVE / math.log(2))
    code = (level + (0.5 - LEAST * PER_OCTAVE)).astype(jnp.int32) + (NONE + 1)
    return jnp.where(x[0:1] > 0, code, NONE).astype(jnp.int16)


def decode(code):
    code = code.astype(jnp.int32)
    level = code.astype(jnp.float32) * (math.log(2) / PER_OCTAVE) + MIDDLE * math.log(2)
    return jnp.where(code[0:1] > NONE, jnp.exp(level), 0.0)


def split(panel):
    whole, rest = divmod(panel, LANES)
    return whole, LANES // rest if rest else 0


def packed_rows(rows, panel, symmetric=False):
    whole, fold = split(panel)
    body = sum((i + 1) * LANES if symmetric else rows for i in range(whole))
    return body + (rows // fold if fold else 0)


def pack(tile, symmetric=False):
    rows, panel = tile.shape
    whole, fold = split(panel)
    parts = [
        tile[: (i + 1) * LANES if symmetric else rows, i * LANES:(i + 1) * LANES]
        for i in range(whole)
    ]
    if fold:
        n = rows // fold
        left = [tile[i * n:(i + 1) * n, whole * LANES:] for i in range(fold)]
        parts.append(jnp.concatenate(left, axis=1))
    return jnp.concatenate(parts, axis=0)


def unpack(x, out, symmetric=False):
    rows, panel = out.shape
    whole, fold = split(panel)
    at = 0
    for i in range(whole):
        n = (i + 1) * LANES if symmetric else rows
        out[:n, i * LANES:(i + 1) * LANES] = x[at:at + n]
        at += n
    if fold:
        n, width = rows // fold, LANES // fold
        for i in range(fold):
            out[i * n:(i + 1) * n, whole * LANES:] = x[at:, i * width:(i + 1) * width]
    if symmetric:
        for i in range(whole):
            n = (i + 1) * LANES
            if n < panel:
                out[n:, i * LANES:n] = out[i * LANES:n, n:].T


def rows_of(sums, count):
    panel = sums[0].shape[1]
    row = lax.broadcasted_iota(jnp.int32, (ROWS, LANES), 0)
    out, at = jnp.zeros((ROWS, LANES), jnp.float32), 0
    for x in sums:
        for start in range(0, panel, LANES):
            piece = x[:, start:start + LANES]
            if piece.shape[1] < LANES:
                piece = jnp.concatenate([piece] * (LANES // piece.shape[1]), axis=1)
            out = jnp.where(row == at, piece, out)
            at += 1
    return jnp.where(row == at, count, out)


def sums_of(rows, panel, which):
    per = -(-panel // LANES)
    starts = range(0, panel, LANES)
    return [
        (start, rows[which * per + i:which * per + i + 1, :min(LANES, panel - start)])
        for i, start in enumerate(starts)
    ]


def encode_rows(rows, unit):
    whole = (rows * unit + 0.5).astype(jnp.int32)
    high = lax.shift_right_logical(whole, 16)
    low = lax.bitwise_and(whole, LOW - 1) - LOW // 2
    return jnp.concatenate([high, low], axis=0).astype(jnp.int16)


def decode_rows(code, unit):
    x = code.astype(jnp.int32).astype(jnp.float32)
    return (x[:ROWS] * float(LOW) + (x[ROWS:] + LOW / 2)) * (1 / unit)


def find_slots(cap, plan_ref, where_ref, fill_ref, slot_ref):
    cycles = where_ref.shape[0]
    for s in range(cycles):
        where_ref[plan_ref[s]] = s
        fill_ref[s] = 0
    for j in range(plan_ref.shape[0] - cycles):
        p = where_ref[plan_ref[cycles + j]]
        r = fill_ref[p]
        slot_ref[p * cap + r] = j
        fill_ref[p] = r + 1


def gathered(ref, s, cap, fill_ref, slot_ref, masked):
    parts = []
    for r in range(cap):
        here = r < fill_ref[s]
        j = jnp.where(here, slot_ref[s * cap + r], 0)
        x = ref[:, pl.ds(pl.multiple_of(j * BLOCK, BLOCK), BLOCK)]
        parts.append(jnp.where(here, x, jnp.zeros_like(x)) if masked else x)
    return jnp.concatenate(parts, axis=1)


def early_kernel(cap, plan_ref, own_ref, other_ref, *refs):
    sorted_ref, rows_ref, *outs, where_ref, fill_ref, slot_ref = refs
    find_slots(cap, plan_ref, where_ref, fill_ref, slot_ref)
    inner = lax.axis_size("blk") // 2
    pieces, outs = outs[:-inner], outs[-inner:]
    at = own_ref.shape[0] - sum(piece.shape[0] for piece in pieces)
    for piece in pieces:
        piece[...] = own_ref[at:at + piece.shape[0]]
        at += piece.shape[0]
    panel = own_ref.shape[0]
    half = panel // 2
    mine = lax.rem(lax.axis_index("blk"), inner)
    first = lax.rem(lax.axis_index("tm"), 2) == 0
    ones = jnp.ones((16, cap * BLOCK), jnp.bfloat16)
    body = outs[0].shape[1]
    for k in range(inner):
        for h in range(2):
            s = h * inner + lax.bitwise_xor(mine, k)
            own = gathered(own_ref, s, cap, fill_ref, slot_ref, True)
            other = gathered(other_ref, s, cap, fill_ref, slot_ref, True)
            sorted_ref[0, k, h] = own
            sorted_ref[1, k, h] = other
            left = jnp.where(first, own[:half], other[half:])
            right = jnp.where(first, other, own)
            count = fill_ref[s].astype(jnp.float32)
            tile, part = times(own, own), times(left, right)
            sums = [times(ones, x)[0:1] for x in (own, other)]
            found = jnp.concatenate([pack(tile, True), pack(part)], axis=0)
            if k:
                outs[k][h, :body] = encode(found)
                outs[k][h, body:] = encode_rows(rows_of(sums, count), PART_UNIT)
            else:
                outs[k][h] = found
                rows_ref[h] = rows_of(sums, count)


def late_kernel(cap, after, plan_ref, sorted_ref, *refs):
    *refs, where_ref, fill_ref, slot_ref = refs[after:]
    find_slots(cap, plan_ref, where_ref, fill_ref, slot_ref)
    inner = lax.axis_size("blk") // 2
    came, outs = refs[:-inner], refs[-inner:]
    mine = lax.rem(lax.axis_index("blk"), inner)
    chip = lax.div(lax.axis_index("tm"), 2)
    for k in range(inner):
        for h in range(2):
            s = h * inner + lax.bitwise_xor(mine, k)
            for d, ref in enumerate(came):
                upper = (chip > lax.bitwise_xor(chip, d + 1)).astype(jnp.int32)
                far = gathered(ref, s, cap, fill_ref, slot_ref, False)
                tile = pack(times(sorted_ref[upper, k, h], far))
                outs[k][h, d] = encode(tile) if k else tile


def early_sum_kernel(own_ref, own_rows_ref, *refs):
    *parts, home_ref, rows_ref, away_ref = refs
    body = home_ref.shape[0]
    side = lax.div(lax.axis_index("blk"), lax.axis_size("blk") // 2)

    def total(h):
        tiles, rows = own_ref[h], own_rows_ref[h]
        for part in parts:
            tiles = tiles + decode(part[h, :body])
            rows = rows + decode_rows(part[h, body:], PART_UNIT)
        return tiles, rows

    home_ref[...], rows_ref[...] = total(side)
    tiles, rows = total(1 - side)
    away_ref[:body], away_ref[body:] = encode(tiles), encode_rows(rows, HALF_UNIT)


def late_sum_kernel(pieces, *refs):
    *parts, home_ref, away_ref = refs
    inner = len(parts) // pieces
    side = lax.div(lax.axis_index("blk"), lax.axis_size("blk") // 2)
    for d in range(home_ref.shape[0]):
        at = 0
        for piece in range(pieces):
            own, *came = parts[piece * inner:(piece + 1) * inner]
            here = pl.ds(at, own.shape[2])
            for h, out in ((side, home_ref), (1 - side, away_ref)):
                tiles = own[h, d]
                for part in came:
                    tiles = tiles + decode(part[h, d])
                out[d, here] = tiles if out is home_ref else encode(tiles)
            at += own.shape[2]


def late_end_kernel(home_ref, across_ref, rows_ref, came_ref, near_ref):
    pairs, body = home_ref.shape[:2]
    rows = rows_ref[...] + decode_rows(came_ref[-2 * ROWS:], HALF_UNIT)
    rows = encode_rows(rows, WHOLE_UNIT)
    for d in range(pairs):
        near_ref[d, :body] = encode(home_ref[d] + decode(across_ref[d]))
        near_ref[d, body:] = rows


def set_scale(ref, rows, which):
    for start, x in sums_of(rows, ref.shape[1], which):
        ref[0:1, start:start + x.shape[1]] = 1.0 / x


def early_end_kernel(
    home_ref, rows_ref, came_ref, late_ref, across_ref, after_ref,
    own_ref, part_ref, straight_ref, down_ref, scale_ref,
):
    half, panel = part_ref.shape
    body, diagonal = home_ref.shape[0], packed_rows(panel, panel, True)
    rows = rows_ref[...] + decode_rows(came_ref[body:], HALF_UNIT)
    unpack(home_ref[diagonal:] + decode(came_ref[diagonal:body]), part_ref)
    unpack(home_ref[:diagonal] + decode(came_ref[:diagonal]), own_ref, True)
    at = 2 * -(-panel // LANES)
    count = rows[at:at + 1, 0:1] * float(BLOCK)
    for which in range(2):
        set_scale(scale_ref.at[which], rows, which)
    down = jnp.broadcast_to(scale_ref[0, 0:1] * count, (panel, panel)).T
    down_ref[...] = down
    own_ref[...] = own_ref[...] * down * scale_ref[0, 0:1]
    for d in range(late_ref.shape[0]):
        unpack(late_ref[d] + decode(across_ref[d]), straight_ref.at[d])


def last_kernel(own_ref, part_ref, mate_part_ref, straight_ref, down_ref, scale_ref, *refs):
    *near, out_ref, tiles, scale, turned = refs
    steps, panel = tiles.shape[:2]
    half = panel // 2
    me = lax.axis_index("tm")
    chip, core = lax.div(me, 2), lax.rem(me, 2)
    tiles[me] = own_ref[...]

    @pl.when(core == 0)
    def _():
        tiles[me + 1, :half] = part_ref[...] * down_ref[:half] * scale_ref[1, 0:1]
        tiles[me + 1, half:] = mate_part_ref[...] * down_ref[half:] * scale_ref[1, 0:1]

    for d, ref in enumerate(near):
        far_chip = lax.bitwise_xor(chip, d + 1)
        body = ref.shape[1] - 2 * ROWS

        @pl.when(chip < far_chip)
        def _():
            rows = decode_rows(ref[0, body:], WHOLE_UNIT)
            set_scale(scale, rows, 0)
            tiles[2 * far_chip + core] = straight_ref[d] * down_ref[...] * scale[0:1]
            unpack(decode(ref[0, :body]), turned)
            set_scale(scale, rows, 1)
            tiles[2 * far_chip + 1 - core] = turned[...].T * down_ref[...] * scale[0:1]

    for u in range(steps):

        @pl.when(u >= me)
        def _():
            out_ref[0, :, u * panel:(u + 1) * panel] = tiles[u]

        @pl.when(u < me)
        def _():
            out_ref[0, :, u * panel:(u + 1) * panel] = jnp.zeros((panel, panel), jnp.float32)


def call(kernel, outs, ins, scratch=(), flops=0):
    moved = sum(math.prod(x.shape) * x.dtype.itemsize for x in (*outs, *ins))
    many = isinstance(outs, list)
    return pl.pallas_call(
        kernel,
        out_shape=outs if many else outs[0],
        in_specs=[SMEM if x.ndim == 1 else VMEM for x in ins],
        out_specs=[VMEM] * len(outs) if many else VMEM,
        scratch_shapes=scratch,
        compiler_params=pltpu.CompilerParams(vmem_limit_bytes=48 * 2**20),
        cost_estimate=pl.CostEstimate(flops=flops, bytes_accessed=moved, transcendentals=0),
    )(*ins)


def on_device(intensity, block_cycle, cycle_order):
    panel = intensity.shape[0]
    blk_dev = block_cycle.shape[0]
    cycles = cycle_order.shape[0]
    groups = lax.axis_size("blk")
    steps = lax.axis_size("tm")
    inner = groups // 2
    pairs = steps // 2 - 1
    cap = 2 * max(1, blk_dev // cycles)
    early = packed_rows(panel, panel, True) + packed_rows(panel // 2, panel)
    first = panel // LANES * LANES
    pieces = [n for n in (first, panel - first) if n]
    late = [panel * n // LANES for n in pieces]

    def hop(x, by_blk, by_tm):
        perm = [
            (b * steps + t, (b ^ by_blk) * steps + (t ^ by_tm))
            for b in range(groups)
            for t in range(steps)
        ]
        return lax.ppermute(x, ("blk", "tm"), perm)

    offsets = range(1, pairs + 1)
    other = hop(intensity, 0, 1)
    far = [[hop(intensity[:pieces[0]], 0, 2 * d) for d in offsets]]
    f32, i16 = jnp.float32, jnp.int16
    shape = jax.ShapeDtypeStruct
    scratch = [
        pltpu.SMEM((cycles,), jnp.int32),
        pltpu.SMEM((cycles,), jnp.int32),
        pltpu.SMEM((cycles * cap,), jnp.int32),
    ]
    plan = jnp.concatenate([cycle_order, block_cycle])
    depth = cap * BLOCK
    work = 2 * cycles * panel * panel * depth
    gathers, own_rows, *made = call(
        functools.partial(early_kernel, cap),
        [
            shape((2, inner, 2, panel, depth), jnp.bfloat16),
            shape((2, ROWS, LANES), f32),
            *[shape((n, intensity.shape[1]), jnp.bfloat16) for n in pieces[1:]],
            shape((2, early, LANES), f32),
            *[shape((2, early + 2 * ROWS, LANES), i16)] * (inner - 1),
        ],
        (plan, intensity, other),
        scratch,
        2 * work,
    )
    far += [[hop(x, 0, 2 * d) for d in offsets] for x in made[:-inner]]
    parts = [hop(x, k, 0) if k else x for k, x in enumerate(made[-inner:])]
    home, home_rows, away = call(
        early_sum_kernel,
        [
            shape((early, LANES), f32),
            shape((ROWS, LANES), f32),
            shape((early + 2 * ROWS, LANES), i16),
        ],
        (parts[0], own_rows, *parts[1:]),
    )
    came = hop(away, inner, 0)

    parts, after = [], ()
    for rows, came_rows in zip(late, far):
        made = call(
            functools.partial(late_kernel, cap, len(after)),
            [shape((2, pairs, rows, LANES), i16 if k else f32) for k in range(inner)],
            (plan, gathers, *after, *came_rows),
            scratch,
            pairs * work,
        )
        parts += [hop(x, k, 0) if k else x for k, x in enumerate(made)]
        after = (away, made[1])
    late_home, late_away = call(
        functools.partial(late_sum_kernel, len(pieces)),
        [shape((pairs, sum(late), LANES), t) for t in (f32, i16)],
        parts,
    )
    across = hop(late_away, inner, 0)
    near = call(
        late_end_kernel,
        (shape((pairs, sum(late) + 2 * ROWS, LANES), i16),),
        (late_home, across, home_rows, came),
    )
    own_tile, part, straight, down, scale = call(
        early_end_kernel,
        [
            shape((panel, panel), f32),
            shape((panel // 2, panel), f32),
            shape((pairs, panel, panel), f32),
            shape((panel, panel), f32),
            shape((2, 8, panel), f32),
        ],
        (home, home_rows, came, late_home, across, near),
    )
    mate_part = hop(part, 0, 1)
    from_near = [hop(near[d - 1:d], 0, 2 * d) for d in offsets]
    return call(
        last_kernel,
        (shape((1, panel, steps * panel), f32),),
        (own_tile, part, mate_part, straight, down, scale, *from_near),
        [
            pltpu.VMEM((steps, panel, panel), f32),
            pltpu.VMEM((8, panel), f32),
            pltpu.VMEM((panel, panel), f32),
        ],
    )


def solution(mesh):
    placed = (P("tm", "blk"), P("blk"), P())
    return jax.shard_map(
        on_device, mesh=mesh, in_specs=placed, out_specs=P("blk", "tm", None), check_vma=False
    )
```

```python
import functools
import math

import jax
import jax.numpy as jnp
from jax import lax
from jax.experimental import pallas as pl
from jax.experimental.pallas import tpu as pltpu
from jax.sharding import PartitionSpec as P

BLOCK = 128
LANES = 128
ROWS = 8
NONE = -32768
LEAST, MOST = -3.0, 28.0
PER_OCTAVE = 65534 / (MOST - LEAST)
MIDDLE = (MOST + LEAST) / 2
PART_UNIT, HALF_UNIT, WHOLE_UNIT = 8192.0, 2048.0, 1024.0
LOW = 1 << 16
VMEM = pl.BlockSpec(memory_space=pltpu.VMEM)
SMEM = pl.BlockSpec(memory_space=pltpu.SMEM)
HBM = pl.BlockSpec(memory_space=pltpu.HBM)


def times(left, right):
    return lax.dot_general(
        left, right, (((1,), (1,)), ((), ())), preferred_element_type=jnp.float32
    )


def encode(x):
    level = jnp.log(jnp.maximum(x, 2.0**LEAST)) * (PER_OCTAVE / math.log(2))
    code = (level + (0.5 - LEAST * PER_OCTAVE)).astype(jnp.int32) + (NONE + 1)
    return jnp.where(x[0:1] > 0, code, NONE).astype(jnp.int16)


def decode(code):
    code = code.astype(jnp.int32)
    level = code.astype(jnp.float32) * (math.log(2) / PER_OCTAVE) + MIDDLE * math.log(2)
    return jnp.where(code[0:1] > NONE, jnp.exp(level), 0.0)


def split(panel):
    whole, rest = divmod(panel, LANES)
    return whole, LANES // rest if rest else 0


def packed_rows(rows, panel, symmetric=False):
    whole, fold = split(panel)
    body = sum((i + 1) * LANES if symmetric else rows for i in range(whole))
    return body + (rows // fold if fold else 0)


def pack(tile, symmetric=False):
    rows, panel = tile.shape
    whole, fold = split(panel)
    parts = [
        tile[: (i + 1) * LANES if symmetric else rows, i * LANES:(i + 1) * LANES]
        for i in range(whole)
    ]
    if fold:
        n = rows // fold
        left = [tile[i * n:(i + 1) * n, whole * LANES:] for i in range(fold)]
        parts.append(jnp.concatenate(left, axis=1))
    return jnp.concatenate(parts, axis=0)


def unpack(x, out, symmetric=False):
    rows, panel = out.shape
    whole, fold = split(panel)
    at = 0
    for i in range(whole):
        n = (i + 1) * LANES if symmetric else rows
        out[:n, i * LANES:(i + 1) * LANES] = x[at:at + n]
        at += n
    if fold:
        n, width = rows // fold, LANES // fold
        for i in range(fold):
            out[i * n:(i + 1) * n, whole * LANES:] = x[at:, i * width:(i + 1) * width]
    if symmetric:
        for i in range(whole):
            n = (i + 1) * LANES
            if n < panel:
                out[n:, i * LANES:n] = out[i * LANES:n, n:].T


def rows_of(sums, count):
    panel = sums[0].shape[1]
    row = lax.broadcasted_iota(jnp.int32, (ROWS, LANES), 0)
    out, at = jnp.zeros((ROWS, LANES), jnp.float32), 0
    for x in sums:
        for start in range(0, panel, LANES):
            piece = x[:, start:start + LANES]
            if piece.shape[1] < LANES:
                piece = jnp.concatenate([piece] * (LANES // piece.shape[1]), axis=1)
            out = jnp.where(row == at, piece, out)
            at += 1
    return jnp.where(row == at, count, out)


def sums_of(rows, panel, which):
    per = -(-panel // LANES)
    starts = range(0, panel, LANES)
    return [
        (start, rows[which * per + i:which * per + i + 1, :min(LANES, panel - start)])
        for i, start in enumerate(starts)
    ]


def encode_rows(rows, unit):
    whole = (rows * unit + 0.5).astype(jnp.int32)
    high = lax.shift_right_logical(whole, 16)
    low = lax.bitwise_and(whole, LOW - 1) - LOW // 2
    return jnp.concatenate([high, low], axis=0).astype(jnp.int16)


def decode_rows(code, unit):
    x = code.astype(jnp.int32).astype(jnp.float32)
    return (x[:ROWS] * float(LOW) + (x[ROWS:] + LOW / 2)) * (1 / unit)


def find_slots(cap, cycle_ref, order_ref, where_ref, table_ref):
    cycles = order_ref.shape[0]
    for s in range(cycles):
        where_ref[order_ref[s]] = s
        table_ref[s] = 0
    for s in range(cycles * cap):
        table_ref[cycles + s] = 0
    for j in range(cycle_ref.shape[0]):
        p = where_ref[cycle_ref[j]]
        r = table_ref[p]
        table_ref[cycles + p * cap + r] = j
        table_ref[p] = r + 1


def gathered(ref, s, cap, table_ref, masked):
    cycles = table_ref.shape[0] // (cap + 1)
    parts = []
    for r in range(cap):
        j = table_ref[cycles + s * cap + r]
        x = ref[:, pl.ds(pl.multiple_of(j * BLOCK, BLOCK), BLOCK)]
        parts.append(jnp.where(r < table_ref[s], x, jnp.zeros_like(x)) if masked else x)
    return jnp.concatenate(parts, axis=1)


def early_kernel(cap, cycle_hbm, order_hbm, own_hbm, other_ref, *refs):
    table_ref, sorted_ref, rows_ref, *outs = refs[:-5]
    where_ref, cycle_ref, order_ref, own_ref, sems = refs[-5:]
    pairs = ((cycle_hbm, cycle_ref), (order_hbm, order_ref), (own_hbm, own_ref))
    copies = [pltpu.make_async_copy(*pair, sems.at[i]) for i, pair in enumerate(pairs)]
    for copy in copies:
        copy.start()
    copies[0].wait()
    copies[1].wait()
    find_slots(cap, cycle_ref, order_ref, where_ref, table_ref)
    copies[2].wait()
    inner = lax.axis_size("blk") // 2
    pieces, outs = outs[:-inner], outs[-inner:]
    for piece in pieces:
        piece[...] = own_ref[own_ref.shape[0] - piece.shape[0]:]
    panel = own_ref.shape[0]
    half = panel // 2
    mine = lax.rem(lax.axis_index("blk"), inner)
    first = lax.rem(lax.axis_index("tm"), 2) == 0
    ones = jnp.ones((16, cap * BLOCK), jnp.bfloat16)
    body = outs[0].shape[1]
    for k in range(inner):
        for h in range(2):
            s = h * inner + lax.bitwise_xor(mine, k)
            own = gathered(own_ref, s, cap, table_ref, True)
            other = gathered(other_ref, s, cap, table_ref, True)
            sorted_ref[0, k, h] = own
            sorted_ref[1, k, h] = other
            left = jnp.where(first, own[:half], other[half:])
            right = jnp.where(first, other, own)
            count = table_ref[s].astype(jnp.float32)
            tile, part = times(own, own), times(left, right)
            sums = [times(ones, x)[0:1] for x in (own, other)]
            found = jnp.concatenate([pack(tile, True), pack(part)], axis=0)
            if k:
                outs[k][h, :body] = encode(found)
                outs[k][h, body:] = encode_rows(rows_of(sums, count), PART_UNIT)
            else:
                outs[k][h] = found
                rows_ref[h] = rows_of(sums, count)


def late_kernel(cap, after, table_ref, sorted_ref, *refs):
    refs = refs[after:]
    inner = lax.axis_size("blk") // 2
    came, outs = refs[:-inner], refs[-inner:]
    mine = lax.rem(lax.axis_index("blk"), inner)
    chip = lax.div(lax.axis_index("tm"), 2)
    for k in range(inner):
        for h in range(2):
            s = h * inner + lax.bitwise_xor(mine, k)
            for d, ref in enumerate(came):
                upper = (chip > lax.bitwise_xor(chip, d + 1)).astype(jnp.int32)
                far = gathered(ref, s, cap, table_ref, False)
                tile = pack(times(sorted_ref[upper, k, h], far))
                outs[k][h, d] = encode(tile) if k else tile


def early_sum_kernel(own_ref, own_rows_ref, *refs):
    *parts, home_ref, rows_ref, away_ref = refs
    body = home_ref.shape[0]
    side = lax.div(lax.axis_index("blk"), lax.axis_size("blk") // 2)

    def total(h):
        tiles, rows = own_ref[h], own_rows_ref[h]
        for part in parts:
            tiles = tiles + decode(part[h, :body])
            rows = rows + decode_rows(part[h, body:], PART_UNIT)
        return tiles, rows

    home_ref[...], rows_ref[...] = total(side)
    tiles, rows = total(1 - side)
    away_ref[:body], away_ref[body:] = encode(tiles), encode_rows(rows, HALF_UNIT)


def late_sum_kernel(pieces, *refs):
    *parts, home_ref, away_ref = refs
    inner = len(parts) // pieces
    side = lax.div(lax.axis_index("blk"), lax.axis_size("blk") // 2)
    for d in range(home_ref.shape[0]):
        at = 0
        for piece in range(pieces):
            own, *came = parts[piece * inner:(piece + 1) * inner]
            here = pl.ds(at, own.shape[2])
            for h, out in ((side, home_ref), (1 - side, away_ref)):
                tiles = own[h, d]
                for part in came:
                    tiles = tiles + decode(part[h, d])
                out[d, here] = tiles if out is home_ref else encode(tiles)
            at += own.shape[2]


def late_end_kernel(home_ref, across_ref, rows_ref, came_ref, near_ref):
    pairs, body = home_ref.shape[:2]
    rows = rows_ref[...] + decode_rows(came_ref[-2 * ROWS:], HALF_UNIT)
    rows = encode_rows(rows, WHOLE_UNIT)
    for d in range(pairs):
        near_ref[d, :body] = encode(home_ref[d] + decode(across_ref[d]))
        near_ref[d, body:] = rows


def set_scale(ref, rows, which):
    for start, x in sums_of(rows, ref.shape[1], which):
        ref[0:1, start:start + x.shape[1]] = 1.0 / x


def early_end_kernel(
    home_ref, rows_ref, came_ref, late_ref, across_ref, after_ref,
    own_ref, part_ref, straight_ref, down_ref, scale_ref,
):
    half, panel = part_ref.shape
    body, diagonal = home_ref.shape[0], packed_rows(panel, panel, True)
    rows = rows_ref[...] + decode_rows(came_ref[body:], HALF_UNIT)
    unpack(home_ref[diagonal:] + decode(came_ref[diagonal:body]), part_ref)
    unpack(home_ref[:diagonal] + decode(came_ref[:diagonal]), own_ref, True)
    at = 2 * -(-panel // LANES)
    count = rows[at:at + 1, 0:1] * float(BLOCK)
    for which in range(2):
        set_scale(scale_ref.at[which], rows, which)
    down = jnp.broadcast_to(scale_ref[0, 0:1] * count, (panel, panel)).T
    down_ref[...] = down
    own_ref[...] = own_ref[...] * down * scale_ref[0, 0:1]
    for d in range(late_ref.shape[0]):
        unpack(late_ref[d] + decode(across_ref[d]), straight_ref.at[d])


def last_kernel(own_ref, part_ref, mate_part_ref, straight_ref, down_ref, scale_ref, *refs):
    *near, out_ref, tiles, scale, turned = refs
    steps, panel = tiles.shape[:2]
    half = panel // 2
    me = lax.axis_index("tm")
    chip, core = lax.div(me, 2), lax.rem(me, 2)
    tiles[me] = own_ref[...]

    @pl.when(core == 0)
    def _():
        tiles[me + 1, :half] = part_ref[...] * down_ref[:half] * scale_ref[1, 0:1]
        tiles[me + 1, half:] = mate_part_ref[...] * down_ref[half:] * scale_ref[1, 0:1]

    for d, ref in enumerate(near):
        far_chip = lax.bitwise_xor(chip, d + 1)
        body = ref.shape[1] - 2 * ROWS

        @pl.when(chip < far_chip)
        def _():
            rows = decode_rows(ref[0, body:], WHOLE_UNIT)
            set_scale(scale, rows, 0)
            tiles[2 * far_chip + core] = straight_ref[d] * down_ref[...] * scale[0:1]
            unpack(decode(ref[0, :body]), turned)
            set_scale(scale, rows, 1)
            tiles[2 * far_chip + 1 - core] = turned[...].T * down_ref[...] * scale[0:1]

    for u in range(steps):

        @pl.when(u >= me)
        def _():
            out_ref[0, :, u * panel:(u + 1) * panel] = tiles[u]

        @pl.when(u < me)
        def _():
            out_ref[0, :, u * panel:(u + 1) * panel] = jnp.zeros((panel, panel), jnp.float32)


def call(kernel, outs, ins, scratch=(), flops=0, in_hbm=0):
    moved = sum(math.prod(x.shape) * x.dtype.itemsize for x in (*outs, *ins))
    many = isinstance(outs, list)
    specs = [SMEM if x.ndim == 1 else VMEM for x in (*ins, *outs)]
    specs[:in_hbm] = [HBM] * in_hbm
    ins = [
        pltpu.with_memory_space_constraint(x, pltpu.HBM) if i < in_hbm else x
        for i, x in enumerate(ins)
    ]
    return pl.pallas_call(
        kernel,
        out_shape=outs if many else outs[0],
        in_specs=specs[:len(ins)],
        out_specs=specs[len(ins):] if many else specs[-1],
        scratch_shapes=scratch,
        compiler_params=pltpu.CompilerParams(vmem_limit_bytes=48 * 2**20),
        cost_estimate=pl.CostEstimate(flops=flops, bytes_accessed=moved, transcendentals=0),
    )(*ins)


def on_device(intensity, block_cycle, cycle_order):
    panel = intensity.shape[0]
    blk_dev = block_cycle.shape[0]
    cycles = cycle_order.shape[0]
    groups = lax.axis_size("blk")
    steps = lax.axis_size("tm")
    inner = groups // 2
    pairs = steps // 2 - 1
    cap = 2 * max(1, blk_dev // cycles)
    early = packed_rows(panel, panel, True) + packed_rows(panel // 2, panel)
    first = panel // LANES * LANES
    pieces = [n for n in (first, panel - first) if n]
    late = [panel * n // LANES for n in pieces]

    def hop(x, by_blk, by_tm):
        perm = [
            (b * steps + t, (b ^ by_blk) * steps + (t ^ by_tm))
            for b in range(groups)
            for t in range(steps)
        ]
        return lax.ppermute(x, ("blk", "tm"), perm)

    offsets = range(1, pairs + 1)
    other = hop(intensity, 0, 1)
    sent = intensity[:first] if len(pieces) > 1 else intensity
    far = [[hop(sent, 0, 2 * d) for d in offsets]]
    f32, i16 = jnp.float32, jnp.int16
    shape = jax.ShapeDtypeStruct
    depth = cap * BLOCK
    work = 2 * cycles * panel * panel * depth
    table, gathers, own_rows, *made = call(
        functools.partial(early_kernel, cap),
        [
            shape((cycles * (cap + 1),), jnp.int32),
            shape((2, inner, 2, panel, depth), jnp.bfloat16),
            shape((2, ROWS, LANES), f32),
            *[shape((n, intensity.shape[1]), jnp.bfloat16) for n in pieces[1:]],
            shape((2, early, LANES), f32),
            *[shape((2, early + 2 * ROWS, LANES), i16)] * (inner - 1),
        ],
        (block_cycle, cycle_order, intensity, other),
        [
            pltpu.SMEM(cycle_order.shape, jnp.int32),
            pltpu.SMEM(block_cycle.shape, jnp.int32),
            pltpu.SMEM(cycle_order.shape, jnp.int32),
            pltpu.VMEM(intensity.shape, jnp.bfloat16),
            pltpu.SemaphoreType.DMA((3,)),
        ],
        2 * work,
        3,
    )
    far += [[hop(x, 0, 2 * d) for d in offsets] for x in made[:-inner]]

    def exchange(made):
        order = sorted(range(inner), key=lambda k: (k > 0, -k.bit_count()))
        return [hop(made[k], k, 0) if k else made[k] for k in order]

    parts = exchange(made[-inner:])
    home, home_rows, away = call(
        early_sum_kernel,
        [
            shape((early, LANES), f32),
            shape((ROWS, LANES), f32),
            shape((early + 2 * ROWS, LANES), i16),
        ],
        (parts[0], own_rows, *parts[1:]),
    )
    came = hop(away, inner, 0)

    parts, after = [], ()
    for rows, came_rows in zip(late, far):
        made = call(
            functools.partial(late_kernel, cap, len(after)),
            [shape((2, pairs, rows, LANES), i16 if k else f32) for k in range(inner)],
            (table, gathers, *after, *came_rows),
            flops=pairs * work,
        )
        parts += exchange(made)
        after = (away, made[1])
    late_home, late_away = call(
        functools.partial(late_sum_kernel, len(pieces)),
        [shape((pairs, sum(late), LANES), t) for t in (f32, i16)],
        parts,
    )
    across = hop(late_away, inner, 0)
    near = call(
        late_end_kernel,
        (shape((pairs, sum(late) + 2 * ROWS, LANES), i16),),
        (late_home, across, home_rows, came),
    )
    own_tile, part, straight, down, scale = call(
        early_end_kernel,
        [
            shape((panel, panel), f32),
            shape((panel // 2, panel), f32),
            shape((pairs, panel, panel), f32),
            shape((panel, panel), f32),
            shape((2, 8, panel), f32),
        ],
        (home, home_rows, came, late_home, across, near),
    )
    mate_part = hop(part, 0, 1)
    from_near = [hop(near[d - 1:d], 0, 2 * d) for d in offsets]
    return call(
        last_kernel,
        (shape((1, panel, steps * panel), f32),),
        (own_tile, part, mate_part, straight, down, scale, *from_near),
        [
            pltpu.VMEM((steps, panel, panel), f32),
            pltpu.VMEM((8, panel), f32),
            pltpu.VMEM((panel, panel), f32),
        ],
    )


def solution(mesh):
    placed = (P("tm", "blk"), P("blk"), P())
    return jax.shard_map(
        on_device, mesh=mesh, in_specs=placed, out_specs=P("blk", "tm", None), check_vma=False
    )
```

```python
import functools
import math

import jax
import jax.numpy as jnp
from jax import lax
from jax.experimental import pallas as pl
from jax.experimental.pallas import tpu as pltpu
from jax.sharding import PartitionSpec as P

BLOCK = 128
LANES = 128
ROWS = 8
NONE = -32768
LEAST, MOST = -3.0, 28.0
PER_OCTAVE = 65534 / (MOST - LEAST)
MIDDLE = (MOST + LEAST) / 2
PART_UNIT, HALF_UNIT, WHOLE_UNIT = 8192.0, 2048.0, 1024.0
LOW = 1 << 16
VMEM = pl.BlockSpec(memory_space=pltpu.VMEM)
SMEM = pl.BlockSpec(memory_space=pltpu.SMEM)
HBM = pl.BlockSpec(memory_space=pltpu.HBM)


def times(left, right):
    return lax.dot_general(
        left, right, (((1,), (1,)), ((), ())), preferred_element_type=jnp.float32
    )


def encode(x):
    level = jnp.log(jnp.maximum(x, 2.0**LEAST)) * (PER_OCTAVE / math.log(2))
    code = (level + (0.5 - LEAST * PER_OCTAVE)).astype(jnp.int32) + (NONE + 1)
    return jnp.where(x[0:1] > 0, code, NONE).astype(jnp.int16)


def decode(code):
    code = code.astype(jnp.int32)
    level = code.astype(jnp.float32) * (math.log(2) / PER_OCTAVE) + MIDDLE * math.log(2)
    return jnp.where(code[0:1] > NONE, jnp.exp(level), 0.0)


def split(panel):
    whole, rest = divmod(panel, LANES)
    return whole, LANES // rest if rest else 0


def packed_rows(rows, panel, symmetric=False):
    whole, fold = split(panel)
    body = sum((i + 1) * LANES if symmetric else rows for i in range(whole))
    return body + (rows // fold if fold else 0)


def pack(tile, symmetric=False):
    rows, panel = tile.shape
    whole, fold = split(panel)
    parts = [
        tile[: (i + 1) * LANES if symmetric else rows, i * LANES:(i + 1) * LANES]
        for i in range(whole)
    ]
    if fold:
        n = rows // fold
        left = [tile[i * n:(i + 1) * n, whole * LANES:] for i in range(fold)]
        parts.append(jnp.concatenate(left, axis=1))
    return jnp.concatenate(parts, axis=0)


def unpack(x, out, symmetric=False):
    rows, panel = out.shape
    whole, fold = split(panel)
    at = 0
    for i in range(whole):
        n = (i + 1) * LANES if symmetric else rows
        out[:n, i * LANES:(i + 1) * LANES] = x[at:at + n]
        at += n
    if fold:
        n, width = rows // fold, LANES // fold
        for i in range(fold):
            out[i * n:(i + 1) * n, whole * LANES:] = x[at:, i * width:(i + 1) * width]
    if symmetric:
        for i in range(whole):
            n = (i + 1) * LANES
            if n < panel:
                out[n:, i * LANES:n] = out[i * LANES:n, n:].T


def rows_of(sums, count):
    panel = sums[0].shape[1]
    row = lax.broadcasted_iota(jnp.int32, (ROWS, LANES), 0)
    out, at = jnp.zeros((ROWS, LANES), jnp.float32), 0
    for x in sums:
        for start in range(0, panel, LANES):
            piece = x[:, start:start + LANES]
            if piece.shape[1] < LANES:
                piece = jnp.concatenate([piece] * (LANES // piece.shape[1]), axis=1)
            out = jnp.where(row == at, piece, out)
            at += 1
    return jnp.where(row == at, count, out)


def sums_of(rows, panel, which):
    per = -(-panel // LANES)
    starts = range(0, panel, LANES)
    return [
        (start, rows[which * per + i:which * per + i + 1, :min(LANES, panel - start)])
        for i, start in enumerate(starts)
    ]


def encode_rows(rows, unit):
    whole = (rows * unit + 0.5).astype(jnp.int32)
    high = lax.shift_right_logical(whole, 16)
    low = lax.bitwise_and(whole, LOW - 1) - LOW // 2
    return jnp.concatenate([high, low], axis=0).astype(jnp.int16)


def decode_rows(code, unit):
    x = code.astype(jnp.int32).astype(jnp.float32)
    return (x[:ROWS] * float(LOW) + (x[ROWS:] + LOW / 2)) * (1 / unit)


def find_slots(cap, cycle_ref, order_ref, where_ref, table_ref):
    cycles = order_ref.shape[0]
    for s in range(cycles):
        where_ref[order_ref[s]] = s
        table_ref[s] = 0
    for s in range(cycles * cap):
        table_ref[cycles + s] = 0
    for j in range(cycle_ref.shape[0]):
        p = where_ref[cycle_ref[j]]
        r = table_ref[p]
        table_ref[cycles + p * cap + r] = j
        table_ref[p] = r + 1


def gathered(ref, s, cap, table_ref, masked):
    cycles = table_ref.shape[0] // (cap + 1)
    parts = []
    for r in range(cap):
        j = table_ref[cycles + s * cap + r]
        x = ref[:, pl.ds(pl.multiple_of(j * BLOCK, BLOCK), BLOCK)]
        parts.append(jnp.where(r < table_ref[s], x, jnp.zeros_like(x)) if masked else x)
    return jnp.concatenate(parts, axis=1)


def first_kernel(cap, cycle_hbm, order_hbm, own_hbm, table_ref, *refs):
    *pieces, where_ref, cycle_ref, order_ref, sems = refs
    pairs = [(cycle_hbm, cycle_ref), (order_hbm, order_ref)]
    at = 0
    for piece in pieces:
        pairs.append((own_hbm.at[pl.ds(at, piece.shape[0])], piece))
        at += piece.shape[0]
    copies = [pltpu.make_async_copy(*pair, sems.at[i]) for i, pair in enumerate(pairs)]
    for copy in copies:
        copy.start()
    copies[0].wait()
    copies[1].wait()
    find_slots(cap, cycle_ref, order_ref, where_ref, table_ref)
    for copy in copies[2:]:
        copy.wait()


def early_kernel(cap, pieces, table_ref, other_ref, *refs):
    own_refs, (sorted_ref, rows_ref, *outs) = refs[:pieces], refs[pieces:]
    inner = len(outs)
    panel = other_ref.shape[0]
    half = panel // 2
    mine = lax.rem(lax.axis_index("blk"), inner)
    first = lax.rem(lax.axis_index("tm"), 2) == 0
    ones = jnp.ones((16, cap * BLOCK), jnp.bfloat16)
    body = outs[0].shape[1]
    for k in range(inner):
        for h in range(2):
            s = h * inner + lax.bitwise_xor(mine, k)
            own = jnp.concatenate([gathered(x, s, cap, table_ref, True) for x in own_refs], axis=0)
            other = gathered(other_ref, s, cap, table_ref, True)
            sorted_ref[0, k, h] = own
            sorted_ref[1, k, h] = other
            left = jnp.where(first, own[:half], other[half:])
            right = jnp.where(first, other, own)
            count = table_ref[s].astype(jnp.float32)
            tile, part = times(own, own), times(left, right)
            sums = [times(ones, x)[0:1] for x in (own, other)]
            found = jnp.concatenate([pack(tile, True), pack(part)], axis=0)
            if k:
                outs[k][h, :body] = encode(found)
                outs[k][h, body:] = encode_rows(rows_of(sums, count), PART_UNIT)
            else:
                outs[k][h] = found
                rows_ref[h] = rows_of(sums, count)


def late_kernel(cap, after, table_ref, sorted_ref, *refs):
    refs = refs[after:]
    inner = lax.axis_size("blk") // 2
    came, outs = refs[:-inner], refs[-inner:]
    mine = lax.rem(lax.axis_index("blk"), inner)
    chip = lax.div(lax.axis_index("tm"), 2)
    for k in range(inner):
        for h in range(2):
            s = h * inner + lax.bitwise_xor(mine, k)
            for d, ref in enumerate(came):
                upper = (chip > lax.bitwise_xor(chip, d + 1)).astype(jnp.int32)
                far = gathered(ref, s, cap, table_ref, False)
                tile = pack(times(sorted_ref[upper, k, h], far))
                outs[k][h, d] = encode(tile) if k else tile


def early_sum_kernel(own_ref, own_rows_ref, *refs):
    *parts, home_ref, rows_ref, away_ref = refs
    body = home_ref.shape[0]
    side = lax.div(lax.axis_index("blk"), lax.axis_size("blk") // 2)

    def total(h):
        tiles, rows = own_ref[h], own_rows_ref[h]
        for part in parts:
            tiles = tiles + decode(part[h, :body])
            rows = rows + decode_rows(part[h, body:], PART_UNIT)
        return tiles, rows

    home_ref[...], rows_ref[...] = total(side)
    tiles, rows = total(1 - side)
    away_ref[:body], away_ref[body:] = encode(tiles), encode_rows(rows, HALF_UNIT)


def late_sum_kernel(pieces, first_ref, *refs):
    *parts, home_ref, away_ref = refs
    inner = len(parts) // pieces
    side = lax.div(lax.axis_index("blk"), lax.axis_size("blk") // 2)
    for d in range(home_ref.shape[0]):
        at = 0
        for piece in range(pieces):
            own, *came = parts[piece * inner:(piece + 1) * inner]
            here = pl.ds(at, own.shape[2])
            for h, out in ((side, home_ref), (1 - side, away_ref)):
                tiles = own[h, d]
                for part in came:
                    tiles = tiles + decode(part[h, d])
                out[d, here] = tiles if out is home_ref else encode(tiles)
            at += own.shape[2]


def late_end_kernel(home_ref, across_ref, rows_ref, came_ref, near_ref):
    pairs, body = home_ref.shape[:2]
    rows = rows_ref[...] + decode_rows(came_ref[-2 * ROWS:], HALF_UNIT)
    rows = encode_rows(rows, WHOLE_UNIT)
    for d in range(pairs):
        near_ref[d, :body] = encode(home_ref[d] + decode(across_ref[d]))
        near_ref[d, body:] = rows


def set_scale(ref, rows, which):
    for start, x in sums_of(rows, ref.shape[1], which):
        ref[0:1, start:start + x.shape[1]] = 1.0 / x


def early_end_kernel(
    home_ref, rows_ref, came_ref, late_ref, across_ref, after_ref,
    own_ref, part_ref, straight_ref, down_ref, scale_ref,
):
    half, panel = part_ref.shape
    body, diagonal = home_ref.shape[0], packed_rows(panel, panel, True)
    rows = rows_ref[...] + decode_rows(came_ref[body:], HALF_UNIT)
    unpack(home_ref[diagonal:] + decode(came_ref[diagonal:body]), part_ref)
    unpack(home_ref[:diagonal] + decode(came_ref[:diagonal]), own_ref, True)
    at = 2 * -(-panel // LANES)
    count = rows[at:at + 1, 0:1] * float(BLOCK)
    for which in range(2):
        set_scale(scale_ref.at[which], rows, which)
    down = jnp.broadcast_to(scale_ref[0, 0:1] * count, (panel, panel)).T
    down_ref[...] = down
    own_ref[...] = own_ref[...] * down * scale_ref[0, 0:1]
    for d in range(late_ref.shape[0]):
        unpack(late_ref[d] + decode(across_ref[d]), straight_ref.at[d])


def last_kernel(own_ref, part_ref, mate_part_ref, straight_ref, down_ref, scale_ref, *refs):
    *near, out_ref, tiles, scale, turned = refs
    steps, panel = tiles.shape[:2]
    half = panel // 2
    me = lax.axis_index("tm")
    chip, core = lax.div(me, 2), lax.rem(me, 2)
    tiles[me] = own_ref[...]

    @pl.when(core == 0)
    def _():
        tiles[me + 1, :half] = part_ref[...] * down_ref[:half] * scale_ref[1, 0:1]
        tiles[me + 1, half:] = mate_part_ref[...] * down_ref[half:] * scale_ref[1, 0:1]

    for d, ref in enumerate(near):
        far_chip = lax.bitwise_xor(chip, d + 1)
        body = ref.shape[1] - 2 * ROWS

        @pl.when(chip < far_chip)
        def _():
            rows = decode_rows(ref[0, body:], WHOLE_UNIT)
            set_scale(scale, rows, 0)
            tiles[2 * far_chip + core] = straight_ref[d] * down_ref[...] * scale[0:1]
            unpack(decode(ref[0, :body]), turned)
            set_scale(scale, rows, 1)
            tiles[2 * far_chip + 1 - core] = turned[...].T * down_ref[...] * scale[0:1]

    for u in range(steps):

        @pl.when(u >= me)
        def _():
            out_ref[0, :, u * panel:(u + 1) * panel] = tiles[u]

        @pl.when(u < me)
        def _():
            out_ref[0, :, u * panel:(u + 1) * panel] = jnp.zeros((panel, panel), jnp.float32)


def call(kernel, outs, ins, scratch=(), flops=0, in_hbm=0):
    moved = sum(math.prod(x.shape) * x.dtype.itemsize for x in (*outs, *ins))
    many = isinstance(outs, list)
    specs = [SMEM if x.ndim == 1 else VMEM for x in (*ins, *outs)]
    specs[:in_hbm] = [HBM] * in_hbm
    ins = [
        pltpu.with_memory_space_constraint(x, pltpu.HBM) if i < in_hbm else x
        for i, x in enumerate(ins)
    ]
    return pl.pallas_call(
        kernel,
        out_shape=outs if many else outs[0],
        in_specs=specs[:len(ins)],
        out_specs=specs[len(ins):] if many else specs[-1],
        scratch_shapes=scratch,
        compiler_params=pltpu.CompilerParams(vmem_limit_bytes=48 * 2**20),
        cost_estimate=pl.CostEstimate(flops=flops, bytes_accessed=moved, transcendentals=0),
    )(*ins)


def on_device(intensity, block_cycle, cycle_order):
    panel = intensity.shape[0]
    blk_dev = block_cycle.shape[0]
    cycles = cycle_order.shape[0]
    groups = lax.axis_size("blk")
    steps = lax.axis_size("tm")
    inner = groups // 2
    pairs = steps // 2 - 1
    cap = 2 * max(1, blk_dev // cycles)
    early = packed_rows(panel, panel, True) + packed_rows(panel // 2, panel)
    first = panel // LANES * LANES
    pieces = [n for n in (first, panel - first) if n]
    late = [panel * n // LANES for n in pieces]

    def hop(x, by_blk, by_tm):
        perm = [
            (b * steps + t, (b ^ by_blk) * steps + (t ^ by_tm))
            for b in range(groups)
            for t in range(steps)
        ]
        return lax.ppermute(x, ("blk", "tm"), perm)

    offsets = range(1, pairs + 1)
    other = hop(intensity, 0, 1)
    f32, i16 = jnp.float32, jnp.int16
    shape = jax.ShapeDtypeStruct
    depth = cap * BLOCK
    work = 2 * cycles * panel * panel * depth
    table, *own = call(
        functools.partial(first_kernel, cap),
        [
            shape((cycles * (cap + 1),), jnp.int32),
            *[shape((n, intensity.shape[1]), jnp.bfloat16) for n in pieces],
        ],
        (block_cycle, cycle_order, intensity),
        [
            pltpu.SMEM(cycle_order.shape, jnp.int32),
            pltpu.SMEM(block_cycle.shape, jnp.int32),
            pltpu.SMEM(cycle_order.shape, jnp.int32),
            pltpu.SemaphoreType.DMA((2 + len(pieces),)),
        ],
        in_hbm=3,
    )
    far = [[hop(x, 0, 2 * d) for d in offsets] for x in own]
    gathers, own_rows, *made = call(
        functools.partial(early_kernel, cap, len(own)),
        [
            shape((2, inner, 2, panel, depth), jnp.bfloat16),
            shape((2, ROWS, LANES), f32),
            shape((2, early, LANES), f32),
            *[shape((2, early + 2 * ROWS, LANES), i16)] * (inner - 1),
        ],
        (table, other, *own),
        flops=2 * work,
    )

    def exchange(made):
        order = sorted(range(inner), key=lambda k: (k > 0, -k.bit_count()))
        return [hop(made[k], k, 0) if k else made[k] for k in order]

    parts = exchange(made)
    home, home_rows, away = call(
        early_sum_kernel,
        [
            shape((early, LANES), f32),
            shape((ROWS, LANES), f32),
            shape((early + 2 * ROWS, LANES), i16),
        ],
        (parts[0], own_rows, *parts[1:]),
    )
    came = hop(away, inner, 0)

    parts, after = [], ()
    for rows, came_rows in zip(late, far):
        made = call(
            functools.partial(late_kernel, cap, len(after)),
            [shape((2, pairs, rows, LANES), i16 if k else f32) for k in range(inner)],
            (table, gathers, *after, *came_rows),
            flops=pairs * work,
        )
        parts += exchange(made)
        after = (away, made[1])
    late_home, late_away = call(
        functools.partial(late_sum_kernel, len(pieces)),
        [shape((pairs, sum(late), LANES), t) for t in (f32, i16)],
        (came, *parts),
    )
    across = hop(late_away, inner, 0)
    near = call(
        late_end_kernel,
        (shape((pairs, sum(late) + 2 * ROWS, LANES), i16),),
        (late_home, across, home_rows, came),
    )
    own_tile, part, straight, down, scale = call(
        early_end_kernel,
        [
            shape((panel, panel), f32),
            shape((panel // 2, panel), f32),
            shape((pairs, panel, panel), f32),
            shape((panel, panel), f32),
            shape((2, 8, panel), f32),
        ],
        (home, home_rows, came, late_home, across, near),
    )
    mate_part = hop(part, 0, 1)
    from_near = [hop(near[d - 1:d], 0, 2 * d) for d in offsets]
    return call(
        last_kernel,
        (shape((1, panel, steps * panel), f32),),
        (own_tile, part, mate_part, straight, down, scale, *from_near),
        [
            pltpu.VMEM((steps, panel, panel), f32),
            pltpu.VMEM((8, panel), f32),
            pltpu.VMEM((panel, panel), f32),
        ],
    )


def solution(mesh):
    placed = (P("tm", "blk"), P("blk"), P())
    return jax.shard_map(
        on_device, mesh=mesh, in_specs=placed, out_specs=P("blk", "tm", None), check_vma=False
    )
```

```python
import functools
import math

import jax
import jax.numpy as jnp
from jax import lax
from jax.experimental import pallas as pl
from jax.experimental.pallas import tpu as pltpu
from jax.sharding import PartitionSpec as P

BLOCK = 128
LANES = 128
ROWS = 8
NONE = -32768
LEAST, MOST = -3.0, 28.0
PER_OCTAVE = 65534 / (MOST - LEAST)
MIDDLE = (MOST + LEAST) / 2
PART_UNIT, HALF_UNIT, WHOLE_UNIT = 8192.0, 2048.0, 1024.0
LOW = 1 << 16
VMEM = pl.BlockSpec(memory_space=pltpu.VMEM)
SMEM = pl.BlockSpec(memory_space=pltpu.SMEM)
HBM = pl.BlockSpec(memory_space=pltpu.HBM)


def times(left, right):
    return lax.dot_general(
        left, right, (((1,), (1,)), ((), ())), preferred_element_type=jnp.float32
    )


def encode(x):
    level = jnp.log(jnp.maximum(x, 2.0**LEAST)) * (PER_OCTAVE / math.log(2))
    code = (level + (0.5 - LEAST * PER_OCTAVE)).astype(jnp.int32) + (NONE + 1)
    return jnp.where(x[..., :1, :] > 0, code, NONE).astype(jnp.int16)


def decode(code):
    code = code.astype(jnp.int32)
    level = code.astype(jnp.float32) * (math.log(2) / PER_OCTAVE) + MIDDLE * math.log(2)
    return jnp.where(code[..., :1, :] > NONE, jnp.exp(level), 0.0)


def split(panel):
    whole, rest = divmod(panel, LANES)
    return whole, LANES // rest if rest else 0


def packed_rows(rows, panel, symmetric=False):
    whole, fold = split(panel)
    body = sum((i + 1) * LANES if symmetric else rows for i in range(whole))
    return body + (rows // fold if fold else 0)


def pack(tile, symmetric=False):
    rows, panel = tile.shape
    whole, fold = split(panel)
    parts = [
        tile[: (i + 1) * LANES if symmetric else rows, i * LANES:(i + 1) * LANES]
        for i in range(whole)
    ]
    if fold:
        n = rows // fold
        left = [tile[i * n:(i + 1) * n, whole * LANES:] for i in range(fold)]
        parts.append(jnp.concatenate(left, axis=1))
    return jnp.concatenate(parts, axis=0)


def unpack(x, out, symmetric=False):
    rows, panel = out.shape
    whole, fold = split(panel)
    at = 0
    for i in range(whole):
        n = (i + 1) * LANES if symmetric else rows
        out[:n, i * LANES:(i + 1) * LANES] = x[at:at + n]
        at += n
    if fold:
        n, width = rows // fold, LANES // fold
        for i in range(fold):
            out[i * n:(i + 1) * n, whole * LANES:] = x[at:, i * width:(i + 1) * width]
    if symmetric:
        for i in range(whole):
            n = (i + 1) * LANES
            if n < panel:
                out[n:, i * LANES:n] = out[i * LANES:n, n:].T


def rows_of(sums, count):
    panel = sums[0].shape[1]
    row = lax.broadcasted_iota(jnp.int32, (ROWS, LANES), 0)
    out, at = jnp.zeros((ROWS, LANES), jnp.float32), 0
    for x in sums:
        for start in range(0, panel, LANES):
            piece = x[:, start:start + LANES]
            if piece.shape[1] < LANES:
                piece = jnp.concatenate([piece] * (LANES // piece.shape[1]), axis=1)
            out = jnp.where(row == at, piece, out)
            at += 1
    return jnp.where(row == at, count, out)


def sums_of(rows, panel, which):
    per = -(-panel // LANES)
    starts = range(0, panel, LANES)
    return [
        (start, rows[which * per + i:which * per + i + 1, :min(LANES, panel - start)])
        for i, start in enumerate(starts)
    ]


def encode_rows(rows, unit):
    whole = (rows * unit + 0.5).astype(jnp.int32)
    high = lax.shift_right_logical(whole, 16)
    low = lax.bitwise_and(whole, LOW - 1) - LOW // 2
    return jnp.concatenate([high, low], axis=0).astype(jnp.int16)


def decode_rows(code, unit):
    x = code.astype(jnp.int32).astype(jnp.float32)
    return (x[:ROWS] * float(LOW) + (x[ROWS:] + LOW / 2)) * (1 / unit)


def find_slots(cap, cycle_ref, order_ref, where_ref, table_ref):
    cycles = order_ref.shape[0]
    for s in range(cycles):
        where_ref[order_ref[s]] = s
        table_ref[s] = 0
    for s in range(cycles * cap):
        table_ref[cycles + s] = 0
    for j in range(cycle_ref.shape[0]):
        p = where_ref[cycle_ref[j]]
        r = table_ref[p]
        table_ref[cycles + p * cap + r] = j
        table_ref[p] = r + 1


def gathered(ref, s, cap, table_ref, masked):
    cycles = table_ref.shape[0] // (cap + 1)
    parts = []
    for r in range(cap):
        j = table_ref[cycles + s * cap + r]
        x = ref[:, pl.ds(pl.multiple_of(j * BLOCK, BLOCK), BLOCK)]
        parts.append(jnp.where(r < table_ref[s], x, jnp.zeros_like(x)) if masked else x)
    return jnp.concatenate(parts, axis=1)


def early_kernel(cap, cycle_hbm, order_hbm, own_hbm, other_ref, *refs):
    table_ref, sorted_ref, rows_ref, *outs = refs[:-5]
    where_ref, cycle_ref, order_ref, own_ref, sems = refs[-5:]
    pairs = ((cycle_hbm, cycle_ref), (order_hbm, order_ref), (own_hbm, own_ref))
    copies = [pltpu.make_async_copy(*pair, sems.at[i]) for i, pair in enumerate(pairs)]
    for copy in copies:
        copy.start()
    copies[0].wait()
    copies[1].wait()
    find_slots(cap, cycle_ref, order_ref, where_ref, table_ref)
    copies[2].wait()
    inner = len(outs)
    panel = own_ref.shape[0]
    half = panel // 2
    mine = lax.rem(lax.axis_index("blk"), inner)
    first = lax.rem(lax.axis_index("tm"), 2) == 0
    ones = jnp.ones((16, cap * BLOCK), jnp.bfloat16)
    body = outs[0].shape[1]
    for k in range(inner):
        for h in range(2):
            s = h * inner + lax.bitwise_xor(mine, k)
            own = gathered(own_ref, s, cap, table_ref, True)
            other = gathered(other_ref, s, cap, table_ref, True)
            sorted_ref[0, k, h] = own
            sorted_ref[1, k, h] = other
            left = jnp.where(first, own[:half], other[half:])
            right = jnp.where(first, other, own)
            count = table_ref[s].astype(jnp.float32)
            tile, part = times(own, own), times(left, right)
            sums = [times(ones, x)[0:1] for x in (own, other)]
            found = jnp.concatenate([pack(tile, True), pack(part)], axis=0)
            if k:
                outs[k][h, :body] = encode(found)
                outs[k][h, body:] = encode_rows(rows_of(sums, count), PART_UNIT)
            else:
                outs[k][h] = found
                rows_ref[h] = rows_of(sums, count)


def late_kernel(cap, table_ref, sorted_ref, first_ref, *refs):
    inner = lax.axis_size("blk") // 2
    came, outs = refs[:-inner], refs[-inner:]
    mine = lax.rem(lax.axis_index("blk"), inner)
    chip = lax.div(lax.axis_index("tm"), 2)
    for k in range(inner):
        for h in range(2):
            s = h * inner + lax.bitwise_xor(mine, k)
            for d, ref in enumerate(came):
                upper = (chip > lax.bitwise_xor(chip, d + 1)).astype(jnp.int32)
                far = gathered(ref, s, cap, table_ref, False)
                tile = pack(times(sorted_ref[upper, k, h], far))
                outs[k][h, d] = encode(tile) if k else tile


def early_sum_kernel(own_ref, own_rows_ref, *refs):
    *parts, home_ref, rows_ref, away_ref = refs
    body = home_ref.shape[0]
    side = lax.div(lax.axis_index("blk"), lax.axis_size("blk") // 2)

    def total(h):
        tiles, rows = own_ref[h], own_rows_ref[h]
        for part in parts:
            tiles = tiles + decode(part[h, :body])
            rows = rows + decode_rows(part[h, body:], PART_UNIT)
        return tiles, rows

    home_ref[...], rows_ref[...] = total(side)
    tiles, rows = total(1 - side)
    away_ref[:body] = encode(tiles)
    away_ref[body:body + 2 * ROWS] = encode_rows(rows, HALF_UNIT)
    away_ref[body + 2 * ROWS:] = jnp.zeros_like(away_ref[body + 2 * ROWS:])


def late_sum_kernel(first_ref, own_ref, *refs):
    *parts, home_ref, away_ref = refs
    side = lax.div(lax.axis_index("blk"), lax.axis_size("blk") // 2)

    def total(h):
        tiles = own_ref[h]
        for part in parts:
            tiles = tiles + decode(part[h])
        return tiles

    home_ref[...] = total(side)
    away_ref[...] = encode(total(1 - side))


def late_end_kernel(at, home_ref, across_ref, rows_ref, came_ref, near_ref):
    pairs, body = home_ref.shape[:2]
    rows = rows_ref[...] + decode_rows(came_ref[at:at + 2 * ROWS], HALF_UNIT)
    rows = encode_rows(rows, WHOLE_UNIT)
    for d in range(pairs):
        near_ref[d, :body] = encode(home_ref[d] + decode(across_ref[d]))
        near_ref[d, body:] = rows


def set_scale(ref, rows, which):
    for start, x in sums_of(rows, ref.shape[1], which):
        ref[0:1, start:start + x.shape[1]] = 1.0 / x


def early_end_kernel(
    home_ref, rows_ref, came_ref, late_ref, across_ref, after_ref,
    own_ref, part_ref, straight_ref, down_ref, scale_ref,
):
    half, panel = part_ref.shape
    body, diagonal = home_ref.shape[0], packed_rows(panel, panel, True)
    rows = rows_ref[...] + decode_rows(came_ref[body:body + 2 * ROWS], HALF_UNIT)
    unpack(home_ref[diagonal:] + decode(came_ref[diagonal:body]), part_ref)
    unpack(home_ref[:diagonal] + decode(came_ref[:diagonal]), own_ref, True)
    at = 2 * -(-panel // LANES)
    count = rows[at:at + 1, 0:1] * float(BLOCK)
    for which in range(2):
        set_scale(scale_ref.at[which], rows, which)
    down = jnp.broadcast_to(scale_ref[0, 0:1] * count, (panel, panel)).T
    down_ref[...] = down
    own_ref[...] = own_ref[...] * down * scale_ref[0, 0:1]
    for d in range(late_ref.shape[0]):
        unpack(late_ref[d] + decode(across_ref[d]), straight_ref.at[d])


def last_kernel(own_ref, part_ref, mate_part_ref, straight_ref, down_ref, scale_ref, *refs):
    *near, out_ref, tiles, scale, turned = refs
    steps, panel = tiles.shape[:2]
    half = panel // 2
    me = lax.axis_index("tm")
    chip, core = lax.div(me, 2), lax.rem(me, 2)
    tiles[me] = own_ref[...]

    @pl.when(core == 0)
    def _():
        tiles[me + 1, :half] = part_ref[...] * down_ref[:half] * scale_ref[1, 0:1]
        tiles[me + 1, half:] = mate_part_ref[...] * down_ref[half:] * scale_ref[1, 0:1]

    for d, ref in enumerate(near):
        far_chip = lax.bitwise_xor(chip, d + 1)
        body = ref.shape[1] - 2 * ROWS

        @pl.when(chip < far_chip)
        def _():
            rows = decode_rows(ref[0, body:], WHOLE_UNIT)
            set_scale(scale, rows, 0)
            tiles[2 * far_chip + core] = straight_ref[d] * down_ref[...] * scale[0:1]
            unpack(decode(ref[0, :body]), turned)
            set_scale(scale, rows, 1)
            tiles[2 * far_chip + 1 - core] = turned[...].T * down_ref[...] * scale[0:1]

    for u in range(steps):

        @pl.when(u >= me)
        def _():
            out_ref[0, :, u * panel:(u + 1) * panel] = tiles[u]

        @pl.when(u < me)
        def _():
            out_ref[0, :, u * panel:(u + 1) * panel] = jnp.zeros((panel, panel), jnp.float32)


def call(kernel, outs, ins, scratch=(), flops=0, in_hbm=0):
    moved = sum(math.prod(x.shape) * x.dtype.itemsize for x in (*outs, *ins))
    many = isinstance(outs, list)
    specs = [SMEM if x.ndim == 1 else VMEM for x in (*ins, *outs)]
    specs[:in_hbm] = [HBM] * in_hbm
    ins = [
        pltpu.with_memory_space_constraint(x, pltpu.HBM) if i < in_hbm else x
        for i, x in enumerate(ins)
    ]
    return pl.pallas_call(
        kernel,
        out_shape=outs if many else outs[0],
        in_specs=specs[:len(ins)],
        out_specs=specs[len(ins):] if many else specs[-1],
        scratch_shapes=scratch,
        compiler_params=pltpu.CompilerParams(vmem_limit_bytes=48 * 2**20),
        cost_estimate=pl.CostEstimate(flops=flops, bytes_accessed=moved, transcendentals=0),
    )(*ins)


def on_device(intensity, block_cycle, cycle_order):
    panel = intensity.shape[0]
    blk_dev = block_cycle.shape[0]
    cycles = cycle_order.shape[0]
    groups = lax.axis_size("blk")
    steps = lax.axis_size("tm")
    inner = groups // 2
    pairs = steps // 2 - 1
    cap = 2 * max(1, blk_dev // cycles)
    early = packed_rows(panel, panel, True) + packed_rows(panel // 2, panel)
    late = packed_rows(panel, panel)
    early_sent = max(early, min(2 * pairs * late, 2 * early)) + 2 * ROWS

    def hop(x, by_blk, by_tm):
        perm = [
            (b * steps + t, (b ^ by_blk) * steps + (t ^ by_tm))
            for b in range(groups)
            for t in range(steps)
        ]
        return lax.ppermute(x, ("blk", "tm"), perm)

    offsets = range(1, pairs + 1)
    other = hop(intensity, 0, 1)
    far = [hop(intensity, 0, 2 * d) for d in offsets]
    f32, i16 = jnp.float32, jnp.int16
    shape = jax.ShapeDtypeStruct
    depth = cap * BLOCK
    work = 2 * cycles * panel * panel * depth
    table, gathers, own_rows, *made = call(
        functools.partial(early_kernel, cap),
        [
            shape((cycles * (cap + 1),), jnp.int32),
            shape((2, inner, 2, panel, depth), jnp.bfloat16),
            shape((2, ROWS, LANES), f32),
            shape((2, early, LANES), f32),
            *[shape((2, early + 2 * ROWS, LANES), i16)] * (inner - 1),
        ],
        (block_cycle, cycle_order, intensity, other),
        [
            pltpu.SMEM(cycle_order.shape, jnp.int32),
            pltpu.SMEM(block_cycle.shape, jnp.int32),
            pltpu.SMEM(cycle_order.shape, jnp.int32),
            pltpu.VMEM(intensity.shape, jnp.bfloat16),
            pltpu.SemaphoreType.DMA((3,)),
        ],
        2 * work,
        3,
    )

    def exchange(made):
        order = sorted(range(inner), key=lambda k: (k > 0, -k.bit_count()))
        return [hop(made[k], k, 0) if k else made[k] for k in order]

    parts = exchange(made)
    home, home_rows, away = call(
        early_sum_kernel,
        [
            shape((early, LANES), f32),
            shape((ROWS, LANES), f32),
            shape((early_sent, LANES), i16),
        ],
        (parts[0], own_rows, *parts[1:]),
    )
    came = hop(away, inner, 0)

    made = call(
        functools.partial(late_kernel, cap),
        [shape((2, pairs, late, LANES), i16 if k else f32) for k in range(inner)],
        (table, gathers, away, *far),
        flops=pairs * work,
    )
    late_home, late_away = call(
        late_sum_kernel,
        [shape((pairs, late, LANES), t) for t in (f32, i16)],
        (came, *exchange(made)),
    )
    across = hop(late_away, inner, 0)
    near = call(
        functools.partial(late_end_kernel, early),
        (shape((pairs, late + 2 * ROWS, LANES), i16),),
        (late_home, across, home_rows, came),
    )
    own_tile, part, straight, down, scale = call(
        early_end_kernel,
        [
            shape((panel, panel), f32),
            shape((panel // 2, panel), f32),
            shape((pairs, panel, panel), f32),
            shape((panel, panel), f32),
            shape((2, 8, panel), f32),
        ],
        (home, home_rows, came, late_home, across, near),
    )
    mate_part = hop(part, 0, 1)
    from_near = [hop(near[d - 1:d], 0, 2 * d) for d in offsets]
    return call(
        last_kernel,
        (shape((1, panel, steps * panel), f32),),
        (own_tile, part, mate_part, straight, down, scale, *from_near),
        [
            pltpu.VMEM((steps, panel, panel), f32),
            pltpu.VMEM((8, panel), f32),
            pltpu.VMEM((panel, panel), f32),
        ],
    )


def solution(mesh):
    placed = (P("tm", "blk"), P("blk"), P())
    return jax.shard_map(
        on_device, mesh=mesh, in_specs=placed, out_specs=P("blk", "tm", None), check_vma=False
    )
```

```python
import functools
import math

import jax
import jax.numpy as jnp
from jax import lax
from jax.experimental import pallas as pl
from jax.experimental.pallas import tpu as pltpu
from jax.sharding import PartitionSpec as P

BLOCK = 128
LANES = 128
ROWS = 8
NONE = -32768
LEAST, MOST = -3.0, 28.0
PER_OCTAVE = 65534 / (MOST - LEAST)
MIDDLE = (MOST + LEAST) / 2
PART_UNIT, HALF_UNIT, WHOLE_UNIT = 8192.0, 2048.0, 1024.0
LOW = 1 << 16
VMEM = pl.BlockSpec(memory_space=pltpu.VMEM)
SMEM = pl.BlockSpec(memory_space=pltpu.SMEM)
HBM = pl.BlockSpec(memory_space=pltpu.HBM)


def times(left, right):
    return lax.dot_general(
        left, right, (((1,), (1,)), ((), ())), preferred_element_type=jnp.float32
    )


def encode(x):
    level = jnp.log(jnp.maximum(x, 2.0**LEAST)) * (PER_OCTAVE / math.log(2))
    code = (level + (0.5 - LEAST * PER_OCTAVE)).astype(jnp.int32) + (NONE + 1)
    return jnp.where(x[..., :1, :] > 0, code, NONE).astype(jnp.int16)


def decode(code):
    code = code.astype(jnp.int32)
    level = code.astype(jnp.float32) * (math.log(2) / PER_OCTAVE) + MIDDLE * math.log(2)
    return jnp.where(code[..., :1, :] > NONE, jnp.exp(level), 0.0)


def split(panel):
    whole, rest = divmod(panel, LANES)
    return whole, LANES // rest if rest else 0


def packed_rows(rows, panel, symmetric=False):
    whole, fold = split(panel)
    if symmetric and (whole, fold) == (1, 2):
        return LANES + LANES // 2
    body = sum((i + 1) * LANES if symmetric else rows for i in range(whole))
    return body + (rows // fold if fold else 0)


def pack(tile, symmetric=False):
    rows, panel = tile.shape
    whole, fold = split(panel)
    if symmetric and (whole, fold) == (1, 2):
        n = LANES // 2
        left, right = tile[:, :LANES], tile[:, LANES:]
        parts = [
            left[:n],
            jnp.concatenate([right[:n], left[n:2 * n, n:]], axis=1),
            jnp.concatenate([right[n:2 * n], right[2 * n:]], axis=1),
        ]
        return jnp.concatenate(parts, axis=0)
    parts = [
        tile[: (i + 1) * LANES if symmetric else rows, i * LANES:(i + 1) * LANES]
        for i in range(whole)
    ]
    if fold:
        n = rows // fold
        left = [tile[i * n:(i + 1) * n, whole * LANES:] for i in range(fold)]
        parts.append(jnp.concatenate(left, axis=1))
    return jnp.concatenate(parts, axis=0)


def unpack(x, out, symmetric=False):
    rows, panel = out.shape
    whole, fold = split(panel)
    if symmetric and (whole, fold) == (1, 2):
        n = LANES // 2
        out[:n, :LANES] = x[:n]
        out[:n, LANES:] = x[n:2 * n, :n]
        out[n:2 * n, n:LANES] = x[n:2 * n, n:]
        out[n:2 * n, LANES:] = x[2 * n:, :n]
        out[2 * n:, LANES:] = x[2 * n:, n:]
        out[n:2 * n, :n] = x[:n, n:].T
        out[2 * n:, :LANES] = out[:2 * n, LANES:].T
        return
    at = 0
    for i in range(whole):
        n = (i + 1) * LANES if symmetric else rows
        out[:n, i * LANES:(i + 1) * LANES] = x[at:at + n]
        at += n
    if fold:
        n, width = rows // fold, LANES // fold
        for i in range(fold):
            out[i * n:(i + 1) * n, whole * LANES:] = x[at:, i * width:(i + 1) * width]
    if symmetric:
        for i in range(whole):
            n = (i + 1) * LANES
            if n < panel:
                out[n:, i * LANES:n] = out[i * LANES:n, n:].T


def rows_of(sums, count):
    panel = sums[0].shape[1]
    row = lax.broadcasted_iota(jnp.int32, (ROWS, LANES), 0)
    out, at = jnp.zeros((ROWS, LANES), jnp.float32), 0
    for x in sums:
        for start in range(0, panel, LANES):
            piece = x[:, start:start + LANES]
            if piece.shape[1] < LANES:
                piece = jnp.concatenate([piece] * (LANES // piece.shape[1]), axis=1)
            out = jnp.where(row == at, piece, out)
            at += 1
    return jnp.where(row == at, count, out)


def sums_of(rows, panel, which):
    per = -(-panel // LANES)
    starts = range(0, panel, LANES)
    return [
        (start, rows[which * per + i:which * per + i + 1, :min(LANES, panel - start)])
        for i, start in enumerate(starts)
    ]


def encode_rows(rows, unit):
    whole = (rows * unit + 0.5).astype(jnp.int32)
    high = lax.shift_right_logical(whole, 16)
    low = lax.bitwise_and(whole, LOW - 1) - LOW // 2
    return jnp.concatenate([high, low], axis=0).astype(jnp.int16)


def decode_rows(code, unit):
    x = code.astype(jnp.int32).astype(jnp.float32)
    return (x[:ROWS] * float(LOW) + (x[ROWS:] + LOW / 2)) * (1 / unit)


def find_slots(cap, cycle_ref, order_ref, where_ref, table_ref):
    cycles = order_ref.shape[0]
    for s in range(cycles):
        where_ref[order_ref[s]] = s
        table_ref[s] = 0
    for s in range(cycles * cap):
        table_ref[cycles + s] = 0
    for j in range(cycle_ref.shape[0]):
        p = where_ref[cycle_ref[j]]
        r = table_ref[p]
        table_ref[cycles + p * cap + r] = j
        table_ref[p] = r + 1


def gathered(ref, s, cap, table_ref, masked):
    cycles = table_ref.shape[0] // (cap + 1)
    parts = []
    for r in range(cap):
        j = table_ref[cycles + s * cap + r]
        x = ref[:, pl.ds(pl.multiple_of(j * BLOCK, BLOCK), BLOCK)]
        parts.append(jnp.where(r < table_ref[s], x, jnp.zeros_like(x)) if masked else x)
    return jnp.concatenate(parts, axis=1)


def early_kernel(cap, cycle_hbm, order_hbm, own_hbm, other_ref, *refs):
    table_ref, sorted_ref, rows_ref, *outs = refs[:-6]
    where_ref, cycle_ref, order_ref, own_ref, sums_ref, sems = refs[-6:]
    pairs = ((cycle_hbm, cycle_ref), (order_hbm, order_ref), (own_hbm, own_ref))
    copies = [pltpu.make_async_copy(*pair, sems.at[i]) for i, pair in enumerate(pairs)]
    for copy in copies:
        copy.start()
    copies[0].wait()
    copies[1].wait()
    find_slots(cap, cycle_ref, order_ref, where_ref, table_ref)
    inner = lax.axis_size("blk") // 2
    pieces, outs = outs[:-inner], outs[-inner:]
    panel = own_ref.shape[0]
    half = panel // 2
    mine = lax.rem(lax.axis_index("blk"), inner)
    first = lax.rem(lax.axis_index("tm"), 2) == 0
    body = outs[0].shape[1]
    row = lax.broadcasted_iota(jnp.int32, (sums_ref.shape[1], BLOCK), 0)
    members = jnp.concatenate(
        [
            jnp.where(row == where_ref[cycle_ref[j]], 1.0, 0.0).astype(jnp.bfloat16)
            for j in range(cycle_ref.shape[0])
        ],
        axis=1,
    )
    each = [(k, h, h * inner + lax.bitwise_xor(mine, k)) for k in range(inner) for h in range(2)]
    for k, h, s in each:
        sorted_ref[1, k, h] = gathered(other_ref, s, cap, table_ref, True)
    sums_ref[1] = times(members, other_ref[...])
    copies[2].wait()
    for piece in pieces:
        piece[...] = own_ref[panel - piece.shape[0]:]
    sums_ref[0] = times(members, own_ref[...])
    for k, h, s in each:
        own, other = gathered(own_ref, s, cap, table_ref, True), sorted_ref[1, k, h]
        sorted_ref[0, k, h] = own
        left = jnp.where(first, own[:half], other[half:])
        right = jnp.where(first, other, own)
        rows = rows_of([sums_ref[i, pl.ds(s, 1)] for i in range(2)], table_ref[s].astype(jnp.float32))
        found = jnp.concatenate([pack(times(own, own), True), pack(times(left, right))], axis=0)
        if k:
            outs[k][h, :body] = encode(found)
            outs[k][h, body:] = encode_rows(rows, PART_UNIT)
        else:
            outs[k][h] = found
            rows_ref[h] = rows


def late_kernel(cap, after, table_ref, sorted_ref, *refs):
    refs = refs[after:]
    inner = lax.axis_size("blk") // 2
    came, outs = refs[:-inner], refs[-inner:]
    mine = lax.rem(lax.axis_index("blk"), inner)
    chip = lax.div(lax.axis_index("tm"), 2)
    for k in range(inner):
        for h in range(2):
            s = h * inner + lax.bitwise_xor(mine, k)
            for d, ref in enumerate(came):
                upper = (chip > lax.bitwise_xor(chip, d + 1)).astype(jnp.int32)
                far = gathered(ref, s, cap, table_ref, False)
                tile = pack(times(sorted_ref[upper, k, h], far))
                outs[k][h, d] = encode(tile) if k else tile


def early_sum_kernel(own_ref, own_rows_ref, *refs):
    *parts, home_ref, rows_ref, away_ref = refs
    body = home_ref.shape[0]
    side = lax.div(lax.axis_index("blk"), lax.axis_size("blk") // 2)

    def total(h):
        tiles, rows = own_ref[h], own_rows_ref[h]
        for part in parts:
            tiles = tiles + decode(part[h, :body])
            rows = rows + decode_rows(part[h, body:], PART_UNIT)
        return tiles, rows

    home_ref[...], rows_ref[...] = total(side)
    tiles, rows = total(1 - side)
    away_ref[:body], away_ref[body:] = encode(tiles), encode_rows(rows, HALF_UNIT)


def late_sum_kernel(pieces, *refs):
    *parts, home_ref, away_ref = refs
    inner = len(parts) // pieces
    side = lax.div(lax.axis_index("blk"), lax.axis_size("blk") // 2)
    for d in range(home_ref.shape[0]):
        at = 0
        for piece in range(pieces):
            own, *came = parts[piece * inner:(piece + 1) * inner]
            here = pl.ds(at, own.shape[2])
            for h, out in ((side, home_ref), (1 - side, away_ref)):
                tiles = own[h, d]
                for part in came:
                    tiles = tiles + decode(part[h, d])
                out[d, here] = tiles if out is home_ref else encode(tiles)
            at += own.shape[2]


def late_end_kernel(home_ref, across_ref, rows_ref, came_ref, near_ref):
    pairs, body = home_ref.shape[:2]
    rows = rows_ref[...] + decode_rows(came_ref[-2 * ROWS:], HALF_UNIT)
    rows = encode_rows(rows, WHOLE_UNIT)
    for d in range(pairs):
        near_ref[d, :body] = encode(home_ref[d] + decode(across_ref[d]))
        near_ref[d, body:] = rows


def set_scale(ref, rows, which):
    for start, x in sums_of(rows, ref.shape[1], which):
        ref[0:1, start:start + x.shape[1]] = 1.0 / x


def early_end_kernel(
    home_ref, rows_ref, came_ref, late_ref, across_ref, after_ref,
    own_ref, part_ref, straight_ref, down_ref, scale_ref,
):
    half, panel = part_ref.shape
    body, diagonal = home_ref.shape[0], packed_rows(panel, panel, True)
    rows = rows_ref[...] + decode_rows(came_ref[body:], HALF_UNIT)
    unpack(home_ref[diagonal:] + decode(came_ref[diagonal:body]), part_ref)
    unpack(home_ref[:diagonal] + decode(came_ref[:diagonal]), own_ref, True)
    at = 2 * -(-panel // LANES)
    count = rows[at:at + 1, 0:1] * float(BLOCK)
    for which in range(2):
        set_scale(scale_ref.at[which], rows, which)
    down = jnp.broadcast_to(scale_ref[0, 0:1] * count, (panel, panel)).T
    down_ref[...] = down
    own_ref[...] = own_ref[...] * down * scale_ref[0, 0:1]
    for d in range(late_ref.shape[0]):
        unpack(late_ref[d] + decode(across_ref[d]), straight_ref.at[d])


def last_kernel(own_ref, part_ref, mate_part_ref, straight_ref, down_ref, scale_ref, *refs):
    *near, out_ref, tiles, scale, turned = refs
    steps, panel = tiles.shape[:2]
    half = panel // 2
    me = lax.axis_index("tm")
    chip, core = lax.div(me, 2), lax.rem(me, 2)
    tiles[me] = own_ref[...]

    @pl.when(core == 0)
    def _():
        tiles[me + 1, :half] = part_ref[...] * down_ref[:half] * scale_ref[1, 0:1]
        tiles[me + 1, half:] = mate_part_ref[...] * down_ref[half:] * scale_ref[1, 0:1]

    for d, ref in enumerate(near):
        far_chip = lax.bitwise_xor(chip, d + 1)
        body = ref.shape[1] - 2 * ROWS

        @pl.when(chip < far_chip)
        def _():
            rows = decode_rows(ref[0, body:], WHOLE_UNIT)
            set_scale(scale, rows, 0)
            tiles[2 * far_chip + core] = straight_ref[d] * down_ref[...] * scale[0:1]
            unpack(decode(ref[0, :body]), turned)
            set_scale(scale, rows, 1)
            tiles[2 * far_chip + 1 - core] = turned[...].T * down_ref[...] * scale[0:1]

    for u in range(steps):

        @pl.when(u >= me)
        def _():
            out_ref[0, :, u * panel:(u + 1) * panel] = tiles[u]

        @pl.when(u < me)
        def _():
            out_ref[0, :, u * panel:(u + 1) * panel] = jnp.zeros((panel, panel), jnp.float32)


def call(kernel, outs, ins, scratch=(), flops=0, in_hbm=0):
    moved = sum(math.prod(x.shape) * x.dtype.itemsize for x in (*outs, *ins))
    many = isinstance(outs, list)
    specs = [SMEM if x.ndim == 1 else VMEM for x in (*ins, *outs)]
    specs[:in_hbm] = [HBM] * in_hbm
    ins = [
        pltpu.with_memory_space_constraint(x, pltpu.HBM) if i < in_hbm else x
        for i, x in enumerate(ins)
    ]
    return pl.pallas_call(
        kernel,
        out_shape=outs if many else outs[0],
        in_specs=specs[:len(ins)],
        out_specs=specs[len(ins):] if many else specs[-1],
        scratch_shapes=scratch,
        compiler_params=pltpu.CompilerParams(vmem_limit_bytes=48 * 2**20),
        cost_estimate=pl.CostEstimate(flops=flops, bytes_accessed=moved, transcendentals=0),
    )(*ins)


def on_device(intensity, block_cycle, cycle_order):
    panel = intensity.shape[0]
    blk_dev = block_cycle.shape[0]
    cycles = cycle_order.shape[0]
    groups = lax.axis_size("blk")
    steps = lax.axis_size("tm")
    inner = groups // 2
    pairs = steps // 2 - 1
    cap = 2 * max(1, blk_dev // cycles)
    early = packed_rows(panel, panel, True) + packed_rows(panel // 2, panel)
    first = panel // LANES * LANES
    pieces = [n for n in (first, panel - first) if n]
    late = [panel * n // LANES for n in pieces]

    def hop(x, by_blk, by_tm):
        perm = [
            (b * steps + t, (b ^ by_blk) * steps + (t ^ by_tm))
            for b in range(groups)
            for t in range(steps)
        ]
        return lax.ppermute(x, ("blk", "tm"), perm)

    offsets = range(1, pairs + 1)
    other = hop(intensity, 0, 1)
    sent = intensity[:first] if len(pieces) > 1 else intensity
    far = [[hop(sent, 0, 2 * d) for d in offsets]]
    f32, i16 = jnp.float32, jnp.int16
    shape = jax.ShapeDtypeStruct
    depth = cap * BLOCK
    work = 2 * cycles * panel * panel * depth
    table, gathers, own_rows, *made = call(
        functools.partial(early_kernel, cap),
        [
            shape((cycles * (cap + 1),), jnp.int32),
            shape((2, inner, 2, panel, depth), jnp.bfloat16),
            shape((2, ROWS, LANES), f32),
            *[shape((n, intensity.shape[1]), jnp.bfloat16) for n in pieces[1:]],
            shape((2, early, LANES), f32),
            *[shape((2, early + 2 * ROWS, LANES), i16)] * (inner - 1),
        ],
        (block_cycle, cycle_order, intensity, other),
        [
            pltpu.SMEM(cycle_order.shape, jnp.int32),
            pltpu.SMEM(block_cycle.shape, jnp.int32),
            pltpu.SMEM(cycle_order.shape, jnp.int32),
            pltpu.VMEM(intensity.shape, jnp.bfloat16),
            pltpu.VMEM((2, -(-cycles // 16) * 16, panel), f32),
            pltpu.SemaphoreType.DMA((3,)),
        ],
        2 * work,
        3,
    )
    far += [[hop(x, 0, 2 * d) for d in offsets] for x in made[:-inner]]

    def exchange(made):
        order = sorted(range(inner), key=lambda k: (k > 0, -k.bit_count()))
        return [hop(made[k], k, 0) if k else made[k] for k in order]

    parts = exchange(made[-inner:])
    home, home_rows, away = call(
        early_sum_kernel,
        [
            shape((early, LANES), f32),
            shape((ROWS, LANES), f32),
            shape((early + 2 * ROWS, LANES), i16),
        ],
        (parts[0], own_rows, *parts[1:]),
    )
    came = hop(away, inner, 0)

    parts, after = [], ()
    for rows, came_rows in zip(late, far):
        made = call(
            functools.partial(late_kernel, cap, len(after)),
            [shape((2, pairs, rows, LANES), i16 if k else f32) for k in range(inner)],
            (table, gathers, *after, *came_rows),
            flops=pairs * work,
        )
        parts += exchange(made)
        after = (away, made[1])
    late_home, late_away = call(
        functools.partial(late_sum_kernel, len(pieces)),
        [shape((pairs, sum(late), LANES), t) for t in (f32, i16)],
        parts,
    )
    across = hop(late_away, inner, 0)
    near = call(
        late_end_kernel,
        (shape((pairs, sum(late) + 2 * ROWS, LANES), i16),),
        (late_home, across, home_rows, came),
    )
    own_tile, part, straight, down, scale = call(
        early_end_kernel,
        [
            shape((panel, panel), f32),
            shape((panel // 2, panel), f32),
            shape((pairs, panel, panel), f32),
            shape((panel, panel), f32),
            shape((2, 8, panel), f32),
        ],
        (home, home_rows, came, late_home, across, near),
    )
    mate_part = hop(part, 0, 1)
    from_near = [hop(near[d - 1:d], 0, 2 * d) for d in offsets]
    return call(
        last_kernel,
        (shape((1, panel, steps * panel), f32),),
        (own_tile, part, mate_part, straight, down, scale, *from_near),
        [
            pltpu.VMEM((steps, panel, panel), f32),
            pltpu.VMEM((8, panel), f32),
            pltpu.VMEM((panel, panel), f32),
        ],
    )


def solution(mesh):
    placed = (P("tm", "blk"), P("blk"), P())
    return jax.shard_map(
        on_device, mesh=mesh, in_specs=placed, out_specs=P("blk", "tm", None), check_vma=False
    )
```

```python
import functools
import math

import jax
import jax.numpy as jnp
from jax import lax
from jax.experimental import pallas as pl
from jax.experimental.pallas import tpu as pltpu
from jax.sharding import PartitionSpec as P

BLOCK = 128
LANES = 128
ROWS = 8
NONE = -32768
LEAST, MOST = -3.0, 28.0
PER_OCTAVE = 65534 / (MOST - LEAST)
MIDDLE = (MOST + LEAST) / 2
PART_UNIT, HALF_UNIT = 8192.0, 2048.0
LOW = 1 << 16
VMEM = pl.BlockSpec(memory_space=pltpu.VMEM)
SMEM = pl.BlockSpec(memory_space=pltpu.SMEM)
HBM = pl.BlockSpec(memory_space=pltpu.HBM)


def times(left, right):
    return lax.dot_general(
        left, right, (((1,), (1,)), ((), ())), preferred_element_type=jnp.float32
    )


def encode(x):
    level = jnp.log(jnp.maximum(x, 2.0**LEAST)) * (PER_OCTAVE / math.log(2))
    code = (level + (0.5 - LEAST * PER_OCTAVE)).astype(jnp.int32) + (NONE + 1)
    return jnp.where(x[..., :1, :] > 0, code, NONE).astype(jnp.int16)


def decode(code):
    code = code.astype(jnp.int32)
    level = code.astype(jnp.float32) * (math.log(2) / PER_OCTAVE) + MIDDLE * math.log(2)
    return jnp.where(code[..., :1, :] > NONE, jnp.exp(level), 0.0)


def split(panel):
    whole, rest = divmod(panel, LANES)
    return whole, LANES // rest if rest else 0


def packed_rows(rows, panel, symmetric=False):
    whole, fold = split(panel)
    if symmetric and (whole, fold) == (1, 2):
        return LANES + LANES // 2
    body = sum((i + 1) * LANES if symmetric else rows for i in range(whole))
    return body + (rows // fold if fold else 0)


def pack(tile, symmetric=False):
    rows, panel = tile.shape
    whole, fold = split(panel)
    if symmetric and (whole, fold) == (1, 2):
        n = LANES // 2
        left, right = tile[:, :LANES], tile[:, LANES:]
        parts = [
            left[:n],
            jnp.concatenate([right[:n], left[n:2 * n, n:]], axis=1),
            jnp.concatenate([right[n:2 * n], right[2 * n:]], axis=1),
        ]
        return jnp.concatenate(parts, axis=0)
    parts = [
        tile[: (i + 1) * LANES if symmetric else rows, i * LANES:(i + 1) * LANES]
        for i in range(whole)
    ]
    if fold:
        n = rows // fold
        left = [tile[i * n:(i + 1) * n, whole * LANES:] for i in range(fold)]
        parts.append(jnp.concatenate(left, axis=1))
    return jnp.concatenate(parts, axis=0)


def unpack(x, out, symmetric=False):
    rows, panel = out.shape
    whole, fold = split(panel)
    if symmetric and (whole, fold) == (1, 2):
        n = LANES // 2
        out[:n, :LANES] = x[:n]
        out[:n, LANES:] = x[n:2 * n, :n]
        out[n:2 * n, n:LANES] = x[n:2 * n, n:]
        out[n:2 * n, LANES:] = x[2 * n:, :n]
        out[2 * n:, LANES:] = x[2 * n:, n:]
        out[n:2 * n, :n] = x[:n, n:].T
        out[2 * n:, :LANES] = out[:2 * n, LANES:].T
        return
    at = 0
    for i in range(whole):
        n = (i + 1) * LANES if symmetric else rows
        out[:n, i * LANES:(i + 1) * LANES] = x[at:at + n]
        at += n
    if fold:
        n, width = rows // fold, LANES // fold
        for i in range(fold):
            out[i * n:(i + 1) * n, whole * LANES:] = x[at:, i * width:(i + 1) * width]
    if symmetric:
        for i in range(whole):
            n = (i + 1) * LANES
            if n < panel:
                out[n:, i * LANES:n] = out[i * LANES:n, n:].T


def rows_of(sums, count):
    panel = sums[0].shape[1]
    row = lax.broadcasted_iota(jnp.int32, (ROWS, LANES), 0)
    out, at = jnp.zeros((ROWS, LANES), jnp.float32), 0
    for x in sums:
        for start in range(0, panel, LANES):
            piece = x[:, start:start + LANES]
            if piece.shape[1] < LANES:
                piece = jnp.concatenate([piece] * (LANES // piece.shape[1]), axis=1)
            out = jnp.where(row == at, piece, out)
            at += 1
    return jnp.where(row == at, count, out)


def sums_of(rows, panel, which):
    per = -(-panel // LANES)
    starts = range(0, panel, LANES)
    return [
        (start, rows[which * per + i:which * per + i + 1, :min(LANES, panel - start)])
        for i, start in enumerate(starts)
    ]


def encode_rows(rows, unit):
    whole = (rows * unit + 0.5).astype(jnp.int32)
    high = lax.shift_right_logical(whole, 16)
    low = lax.bitwise_and(whole, LOW - 1) - LOW // 2
    return jnp.concatenate([high, low], axis=0).astype(jnp.int16)


def decode_rows(code, unit):
    x = code.astype(jnp.int32).astype(jnp.float32)
    return (x[:ROWS] * float(LOW) + (x[ROWS:] + LOW / 2)) * (1 / unit)


def find_slots(cap, cycle_ref, order_ref, where_ref, table_ref):
    cycles = order_ref.shape[0]
    for s in range(cycles):
        where_ref[order_ref[s]] = s
        table_ref[s] = 0
    for s in range(cycles * cap):
        table_ref[cycles + s] = 0
    for j in range(cycle_ref.shape[0]):
        p = where_ref[cycle_ref[j]]
        r = table_ref[p]
        table_ref[cycles + p * cap + r] = j
        table_ref[p] = r + 1


def gathered(ref, s, cap, table_ref, masked):
    cycles = table_ref.shape[0] // (cap + 1)
    parts = []
    for r in range(cap):
        j = table_ref[cycles + s * cap + r]
        x = ref[:, pl.ds(pl.multiple_of(j * BLOCK, BLOCK), BLOCK)]
        parts.append(jnp.where(r < table_ref[s], x, jnp.zeros_like(x)) if masked else x)
    return jnp.concatenate(parts, axis=1)


def early_kernel(cap, cycle_hbm, order_hbm, own_hbm, other_ref, *refs):
    table_ref, sorted_ref, rows_ref, *outs = refs[:-6]
    where_ref, cycle_ref, order_ref, own_ref, sums_ref, sems = refs[-6:]
    pairs = ((cycle_hbm, cycle_ref), (order_hbm, order_ref), (own_hbm, own_ref))
    copies = [pltpu.make_async_copy(*pair, sems.at[i]) for i, pair in enumerate(pairs)]
    for copy in copies:
        copy.start()
    copies[0].wait()
    copies[1].wait()
    find_slots(cap, cycle_ref, order_ref, where_ref, table_ref)
    inner = lax.axis_size("blk") // 2
    pieces, outs = outs[:-inner], outs[-inner:]
    panel = own_ref.shape[0]
    half = panel // 2
    mine = lax.rem(lax.axis_index("blk"), inner)
    first = lax.rem(lax.axis_index("tm"), 2) == 0
    body = outs[0].shape[1]
    row = lax.broadcasted_iota(jnp.int32, (sums_ref.shape[1], BLOCK), 0)
    members = jnp.concatenate(
        [
            jnp.where(row == where_ref[cycle_ref[j]], 1.0, 0.0).astype(jnp.bfloat16)
            for j in range(cycle_ref.shape[0])
        ],
        axis=1,
    )
    each = [(k, h, h * inner + lax.bitwise_xor(mine, k)) for k in range(inner) for h in range(2)]
    for k, h, s in each:
        sorted_ref[1, k, h] = gathered(other_ref, s, cap, table_ref, True)
    sums_ref[1] = times(members, other_ref[...])
    copies[2].wait()
    for piece in pieces:
        piece[...] = own_ref[panel - piece.shape[0]:]
    sums_ref[0] = times(members, own_ref[...])
    for k, h, s in each:
        own, other = gathered(own_ref, s, cap, table_ref, True), sorted_ref[1, k, h]
        sorted_ref[0, k, h] = own
        left = jnp.where(first, own[:half], other[half:])
        right = jnp.where(first, other, own)
        rows = rows_of([sums_ref[i, pl.ds(s, 1)] for i in range(2)], table_ref[s].astype(jnp.float32))
        found = jnp.concatenate([pack(times(own, own), True), pack(times(left, right))], axis=0)
        if k:
            outs[k][h, :body] = encode(found)
            outs[k][h, body:] = encode_rows(rows, PART_UNIT)
        else:
            outs[k][h] = found
            rows_ref[h] = rows


def late_kernel(cap, after, table_ref, sorted_ref, *refs):
    refs = refs[after:]
    inner = lax.axis_size("blk") // 2
    came, outs = refs[:-inner], refs[-inner:]
    mine = lax.rem(lax.axis_index("blk"), inner)
    chip = lax.div(lax.axis_index("tm"), 2)
    for k in range(inner):
        for h in range(2):
            s = h * inner + lax.bitwise_xor(mine, k)
            for d, ref in enumerate(came):
                upper = (chip > lax.bitwise_xor(chip, d + 1)).astype(jnp.int32)
                far = gathered(ref, s, cap, table_ref, False)
                tile = pack(times(sorted_ref[upper, k, h], far))
                outs[k][h, d] = encode(tile) if k else tile


def early_sum_kernel(own_ref, own_rows_ref, *refs):
    *parts, home_ref, rows_ref, away_ref = refs
    body = home_ref.shape[0]
    side = lax.div(lax.axis_index("blk"), lax.axis_size("blk") // 2)

    def total(h):
        tiles, rows = own_ref[h], own_rows_ref[h]
        for part in parts:
            tiles = tiles + decode(part[h, :body])
            rows = rows + decode_rows(part[h, body:], PART_UNIT)
        return tiles, rows

    home_ref[...], rows_ref[...] = total(side)
    tiles, rows = total(1 - side)
    away_ref[:body], away_ref[body:] = encode(tiles), encode_rows(rows, HALF_UNIT)


def late_sum_kernel(pieces, home_rows_ref, early_away_ref, *refs):
    *parts, home_ref, near_ref, away_ref = refs
    inner = len(parts) // pieces
    pairs, body = home_ref.shape[:2]
    side = lax.div(lax.axis_index("blk"), lax.axis_size("blk") // 2)
    near_rows = encode_rows(home_rows_ref[...], HALF_UNIT)
    away_rows = early_away_ref[-2 * ROWS:]
    for d in range(pairs):
        at = 0
        for piece in range(pieces):
            own, *came = parts[piece * inner:(piece + 1) * inner]
            here = pl.ds(at, own.shape[2])
            at += own.shape[2]
            home, away = own[side, d], own[1 - side, d]
            for part in came:
                home = home + decode(part[side, d])
                away = away + decode(part[1 - side, d])
            home_ref[d, here] = home
            near_ref[d, here] = encode(home)
            away_ref[d, here] = encode(away)
        near_ref[d, body:], away_ref[d, body:] = near_rows, away_rows


def set_scale(ref, rows, which):
    for start, x in sums_of(rows, ref.shape[1], which):
        ref[0:1, start:start + x.shape[1]] = 1.0 / x


def early_end_kernel(
    home_ref, rows_ref, came_ref, after_ref, own_ref, part_ref, down_ref, scale_ref
):
    half, panel = part_ref.shape
    body, diagonal = home_ref.shape[0], packed_rows(panel, panel, True)
    rows = rows_ref[...] + decode_rows(came_ref[body:], HALF_UNIT)
    unpack(home_ref[diagonal:] + decode(came_ref[diagonal:body]), part_ref)
    unpack(home_ref[:diagonal] + decode(came_ref[:diagonal]), own_ref, True)
    at = 2 * -(-panel // LANES)
    count = rows[at:at + 1, 0:1] * float(BLOCK)
    for which in range(2):
        set_scale(scale_ref.at[which], rows, which)
    down = jnp.broadcast_to(scale_ref[0, 0:1] * count, (panel, panel)).T
    down_ref[...] = down
    own_ref[...] = own_ref[...] * down * scale_ref[0, 0:1]


def last_kernel(
    pairs, own_ref, part_ref, mate_part_ref, down_ref, scale_ref, late_ref, *refs
):
    away, near = refs[:pairs], refs[pairs:2 * pairs]
    across_ref, out_ref, tiles, scale, turned = refs[2 * pairs:]
    steps, panel = tiles.shape[:2]
    half, late = panel // 2, late_ref.shape[1]
    me = lax.axis_index("tm")
    chip, core = lax.div(me, 2), lax.rem(me, 2)
    tiles[me] = own_ref[...]

    @pl.when(core == 0)
    def _():
        tiles[me + 1, :half] = part_ref[...] * down_ref[:half] * scale_ref[1, 0:1]
        tiles[me + 1, half:] = mate_part_ref[...] * down_ref[half:] * scale_ref[1, 0:1]

    for d in range(pairs):
        far_chip = lax.bitwise_xor(chip, d + 1)

        @pl.when(chip < far_chip)
        def _():
            rows = decode_rows(near[d][0, late:], HALF_UNIT) + decode_rows(
                away[d][0, late:], HALF_UNIT
            )
            unpack(late_ref[d] + decode(across_ref[d, :late]), turned)
            set_scale(scale, rows, 0)
            tiles[2 * far_chip + core] = turned[...] * down_ref[...] * scale[0:1]
            unpack(decode(near[d][0, :late]) + decode(away[d][0, :late]), turned)
            set_scale(scale, rows, 1)
            tiles[2 * far_chip + 1 - core] = turned[...].T * down_ref[...] * scale[0:1]

    for u in range(steps):

        @pl.when(u >= me)
        def _():
            out_ref[0, :, u * panel:(u + 1) * panel] = tiles[u]

        @pl.when(u < me)
        def _():
            out_ref[0, :, u * panel:(u + 1) * panel] = jnp.zeros((panel, panel), jnp.float32)


def call(kernel, outs, ins, scratch=(), flops=0, in_hbm=0):
    moved = sum(math.prod(x.shape) * x.dtype.itemsize for x in (*outs, *ins))
    many = isinstance(outs, list)
    specs = [SMEM if x.ndim == 1 else VMEM for x in (*ins, *outs)]
    specs[:in_hbm] = [HBM] * in_hbm
    ins = [
        pltpu.with_memory_space_constraint(x, pltpu.HBM) if i < in_hbm else x
        for i, x in enumerate(ins)
    ]
    return pl.pallas_call(
        kernel,
        out_shape=outs if many else outs[0],
        in_specs=specs[:len(ins)],
        out_specs=specs[len(ins):] if many else specs[-1],
        scratch_shapes=scratch,
        compiler_params=pltpu.CompilerParams(vmem_limit_bytes=48 * 2**20),
        cost_estimate=pl.CostEstimate(flops=flops, bytes_accessed=moved, transcendentals=0),
    )(*ins)


def on_device(intensity, block_cycle, cycle_order):
    panel = intensity.shape[0]
    blk_dev = block_cycle.shape[0]
    cycles = cycle_order.shape[0]
    groups = lax.axis_size("blk")
    steps = lax.axis_size("tm")
    inner = groups // 2
    pairs = steps // 2 - 1
    cap = 2 * max(1, blk_dev // cycles)
    early = packed_rows(panel, panel, True) + packed_rows(panel // 2, panel)
    first = panel // LANES * LANES
    pieces = [n for n in (first, panel - first) if n]
    late = [panel * n // LANES for n in pieces]

    def hop(x, by_blk, by_tm, sends=lambda t: True):
        perm = [
            (b * steps + t, (b ^ by_blk) * steps + (t ^ by_tm))
            for b in range(groups)
            for t in range(steps)
            if sends(t)
        ]
        return lax.ppermute(x, ("blk", "tm"), perm)

    offsets = range(1, pairs + 1)
    other = hop(intensity, 0, 1)
    sent = intensity[:first] if len(pieces) > 1 else intensity
    far = [[hop(sent, 0, 2 * d) for d in offsets]]
    f32, i16 = jnp.float32, jnp.int16
    shape = jax.ShapeDtypeStruct
    depth = cap * BLOCK
    work = 2 * cycles * panel * panel * depth
    table, gathers, own_rows, *made = call(
        functools.partial(early_kernel, cap),
        [
            shape((cycles * (cap + 1),), jnp.int32),
            shape((2, inner, 2, panel, depth), jnp.bfloat16),
            shape((2, ROWS, LANES), f32),
            *[shape((n, intensity.shape[1]), jnp.bfloat16) for n in pieces[1:]],
            shape((2, early, LANES), f32),
            *[shape((2, early + 2 * ROWS, LANES), i16)] * (inner - 1),
        ],
        (block_cycle, cycle_order, intensity, other),
        [
            pltpu.SMEM(cycle_order.shape, jnp.int32),
            pltpu.SMEM(block_cycle.shape, jnp.int32),
            pltpu.SMEM(cycle_order.shape, jnp.int32),
            pltpu.VMEM(intensity.shape, jnp.bfloat16),
            pltpu.VMEM((2, -(-cycles // 16) * 16, panel), f32),
            pltpu.SemaphoreType.DMA((3,)),
        ],
        2 * work,
        3,
    )
    far += [[hop(x, 0, 2 * d) for d in offsets] for x in made[:-inner]]

    def exchange(made):
        order = sorted(range(inner), key=lambda k: (k > 0, -k.bit_count()))
        return [hop(made[k], k, 0) if k else made[k] for k in order]

    parts = exchange(made[-inner:])
    home, home_rows, away = call(
        early_sum_kernel,
        [
            shape((early, LANES), f32),
            shape((ROWS, LANES), f32),
            shape((early + 2 * ROWS, LANES), i16),
        ],
        (parts[0], own_rows, *parts[1:]),
    )
    came = hop(away, inner, 0)

    parts, after = [], ()
    for rows, came_rows in zip(late, far):
        made = call(
            functools.partial(late_kernel, cap, len(after)),
            [shape((2, pairs, rows, LANES), i16 if k else f32) for k in range(inner)],
            (table, gathers, *after, *came_rows),
            flops=pairs * work,
        )
        parts += exchange(made)
        after = (away, made[1])
    late_home, near, late_away = call(
        functools.partial(late_sum_kernel, len(pieces)),
        [
            shape((pairs, sum(late), LANES), f32),
            shape((pairs, sum(late) + 2 * ROWS, LANES), i16),
            shape((pairs, sum(late) + 2 * ROWS, LANES), i16),
        ],
        (home_rows, away, *parts),
    )

    def is_lower(t, d):
        return t // 2 < (t // 2 ^ d)

    from_away = [
        hop(late_away[d - 1:d], inner, 2 * d, lambda t, d=d: not is_lower(t, d)) for d in offsets
    ]
    from_near = [hop(near[d - 1:d], 0, 2 * d) for d in offsets]
    across = hop(late_away, inner, 0, lambda t: any(is_lower(t, d) for d in offsets))
    own_tile, part, down, scale = call(
        early_end_kernel,
        [
            shape((panel, panel), f32),
            shape((panel // 2, panel), f32),
            shape((panel, panel), f32),
            shape((2, 8, panel), f32),
        ],
        (home, home_rows, came, from_near[0]),
    )
    mate_part = hop(part, 0, 1)
    return call(
        functools.partial(last_kernel, pairs),
        (shape((1, panel, steps * panel), f32),),
        (own_tile, part, mate_part, down, scale, late_home, *from_away, *from_near, across),
        [
            pltpu.VMEM((steps, panel, panel), f32),
            pltpu.VMEM((8, panel), f32),
            pltpu.VMEM((panel, panel), f32),
        ],
    )


def solution(mesh):
    placed = (P("tm", "blk"), P("blk"), P())
    return jax.shard_map(
        on_device, mesh=mesh, in_specs=placed, out_specs=P("blk", "tm", None), check_vma=False
    )
```

```python
import functools
import math

import jax
import jax.numpy as jnp
from jax import lax
from jax.experimental import pallas as pl
from jax.experimental.pallas import tpu as pltpu
from jax.sharding import PartitionSpec as P

BLOCK = 128
LANES = 128
ROWS = 8
NONE = -32768
LEAST, MOST = -3.0, 28.0
PER_OCTAVE = 65534 / (MOST - LEAST)
MIDDLE = (MOST + LEAST) / 2
PART_UNIT, HALF_UNIT = 8192.0, 2048.0
LOW = 1 << 16
VMEM = pl.BlockSpec(memory_space=pltpu.VMEM)
SMEM = pl.BlockSpec(memory_space=pltpu.SMEM)
HBM = pl.BlockSpec(memory_space=pltpu.HBM)


def times(left, right):
    return lax.dot_general(
        left, right, (((1,), (1,)), ((), ())), preferred_element_type=jnp.float32
    )


def encode(x):
    level = jnp.log(jnp.maximum(x, 2.0**LEAST)) * (PER_OCTAVE / math.log(2))
    code = (level + (0.5 - LEAST * PER_OCTAVE)).astype(jnp.int32) + (NONE + 1)
    return jnp.where(x[..., :1, :] > 0, code, NONE).astype(jnp.int16)


def decode(code):
    code = code.astype(jnp.int32)
    level = code.astype(jnp.float32) * (math.log(2) / PER_OCTAVE) + MIDDLE * math.log(2)
    return jnp.where(code[..., :1, :] > NONE, jnp.exp(level), 0.0)


def split(panel):
    whole, rest = divmod(panel, LANES)
    return whole, LANES // rest if rest else 0


def packed_rows(rows, panel, symmetric=False):
    whole, fold = split(panel)
    if symmetric and (whole, fold) == (1, 2):
        return LANES + LANES // 2
    body = sum((i + 1) * LANES if symmetric else rows for i in range(whole))
    return body + (rows // fold if fold else 0)


def pack(tile, symmetric=False):
    rows, panel = tile.shape
    whole, fold = split(panel)
    if symmetric and (whole, fold) == (1, 2):
        n = LANES // 2
        left, right = tile[:, :LANES], tile[:, LANES:]
        parts = [
            left[:n],
            jnp.concatenate([right[:n], left[n:2 * n, n:]], axis=1),
            jnp.concatenate([right[n:2 * n], right[2 * n:]], axis=1),
        ]
        return jnp.concatenate(parts, axis=0)
    parts = [
        tile[: (i + 1) * LANES if symmetric else rows, i * LANES:(i + 1) * LANES]
        for i in range(whole)
    ]
    if fold:
        n = rows // fold
        left = [tile[i * n:(i + 1) * n, whole * LANES:] for i in range(fold)]
        parts.append(jnp.concatenate(left, axis=1))
    return jnp.concatenate(parts, axis=0)


def unpack(x, out, symmetric=False):
    rows, panel = out.shape
    whole, fold = split(panel)
    if symmetric and (whole, fold) == (1, 2):
        n = LANES // 2
        out[:n, :LANES] = x[:n]
        out[:n, LANES:] = x[n:2 * n, :n]
        out[n:2 * n, n:LANES] = x[n:2 * n, n:]
        out[n:2 * n, LANES:] = x[2 * n:, :n]
        out[2 * n:, LANES:] = x[2 * n:, n:]
        out[n:2 * n, :n] = x[:n, n:].T
        out[2 * n:, :LANES] = out[:2 * n, LANES:].T
        return
    at = 0
    for i in range(whole):
        n = (i + 1) * LANES if symmetric else rows
        out[:n, i * LANES:(i + 1) * LANES] = x[at:at + n]
        at += n
    if fold:
        n, width = rows // fold, LANES // fold
        for i in range(fold):
            out[i * n:(i + 1) * n, whole * LANES:] = x[at:, i * width:(i + 1) * width]
    if symmetric:
        for i in range(whole):
            n = (i + 1) * LANES
            if n < panel:
                out[n:, i * LANES:n] = out[i * LANES:n, n:].T


def rows_of(sums, count):
    panel = sums[0].shape[1]
    row = lax.broadcasted_iota(jnp.int32, (ROWS, LANES), 0)
    out, at = jnp.zeros((ROWS, LANES), jnp.float32), 0
    for x in sums:
        for start in range(0, panel, LANES):
            piece = x[:, start:start + LANES]
            if piece.shape[1] < LANES:
                piece = jnp.concatenate([piece] * (LANES // piece.shape[1]), axis=1)
            out = jnp.where(row == at, piece, out)
            at += 1
    return jnp.where(row == at, count, out)


def sums_of(rows, panel, which):
    per = -(-panel // LANES)
    starts = range(0, panel, LANES)
    return [
        (start, rows[which * per + i:which * per + i + 1, :min(LANES, panel - start)])
        for i, start in enumerate(starts)
    ]


def encode_rows(rows, unit):
    whole = (rows * unit + 0.5).astype(jnp.int32)
    high = lax.shift_right_logical(whole, 16)
    low = lax.bitwise_and(whole, LOW - 1) - LOW // 2
    return jnp.concatenate([high, low], axis=0).astype(jnp.int16)


def decode_rows(code, unit):
    x = code.astype(jnp.int32).astype(jnp.float32)
    return (x[:ROWS] * float(LOW) + (x[ROWS:] + LOW / 2)) * (1 / unit)


def find_slots(cap, cycle_ref, order_ref, where_ref, table_ref):
    cycles = order_ref.shape[0]
    for s in range(cycles):
        where_ref[order_ref[s]] = s
        table_ref[s] = 0
    for s in range(cycles * cap):
        table_ref[cycles + s] = 0
    for j in range(cycle_ref.shape[0]):
        p = where_ref[cycle_ref[j]]
        r = table_ref[p]
        table_ref[cycles + p * cap + r] = j
        table_ref[p] = r + 1


def gathered(ref, s, cap, table_ref, masked):
    cycles = table_ref.shape[0] // (cap + 1)
    parts = []
    for r in range(cap):
        j = table_ref[cycles + s * cap + r]
        x = ref[:, pl.ds(pl.multiple_of(j * BLOCK, BLOCK), BLOCK)]
        parts.append(jnp.where(r < table_ref[s], x, jnp.zeros_like(x)) if masked else x)
    return jnp.concatenate(parts, axis=1)


def early_kernel(cap, cycle_hbm, order_hbm, own_hbm, other_ref, *refs):
    table_ref, sorted_ref, rows_ref, *outs = refs[:-6]
    where_ref, cycle_ref, order_ref, own_ref, sums_ref, sems = refs[-6:]
    pairs = ((cycle_hbm, cycle_ref), (order_hbm, order_ref), (own_hbm, own_ref))
    copies = [pltpu.make_async_copy(*pair, sems.at[i]) for i, pair in enumerate(pairs)]
    for copy in copies:
        copy.start()
    copies[0].wait()
    copies[1].wait()
    find_slots(cap, cycle_ref, order_ref, where_ref, table_ref)
    inner = lax.axis_size("blk") // 2
    pieces, outs = outs[:-inner], outs[-inner:]
    panel = own_ref.shape[0]
    half = panel // 2
    mine = lax.rem(lax.axis_index("blk"), inner)
    first = lax.rem(lax.axis_index("tm"), 2) == 0
    body = outs[0].shape[1]
    row = lax.broadcasted_iota(jnp.int32, (sums_ref.shape[1], BLOCK), 0)
    members = jnp.concatenate(
        [
            jnp.where(row == where_ref[cycle_ref[j]], 1.0, 0.0).astype(jnp.bfloat16)
            for j in range(cycle_ref.shape[0])
        ],
        axis=1,
    )
    each = [(k, h, h * inner + lax.bitwise_xor(mine, k)) for k in range(inner) for h in range(2)]
    for k, h, s in each:
        sorted_ref[1, k, h] = gathered(other_ref, s, cap, table_ref, True)
    sums_ref[1] = times(members, other_ref[...])
    copies[2].wait()
    for piece in pieces:
        piece[...] = own_ref[panel - piece.shape[0]:]
    sums_ref[0] = times(members, own_ref[...])
    for k, h, s in each:
        own, other = gathered(own_ref, s, cap, table_ref, True), sorted_ref[1, k, h]
        sorted_ref[0, k, h] = own
        left = jnp.where(first, own[:half], other[half:])
        right = jnp.where(first, other, own)
        rows = rows_of([sums_ref[i, pl.ds(s, 1)] for i in range(2)], table_ref[s].astype(jnp.float32))
        found = jnp.concatenate([pack(times(own, own), True), pack(times(left, right))], axis=0)
        if k:
            outs[k][h, :body] = encode(found)
            outs[k][h, body:] = encode_rows(rows, PART_UNIT)
        else:
            outs[k][h] = found
            rows_ref[h] = rows


def late_kernel(cap, after, table_ref, sorted_ref, *refs):
    refs = refs[after:]
    inner = lax.axis_size("blk") // 2
    came, outs = refs[:-inner], refs[-inner:]
    mine = lax.rem(lax.axis_index("blk"), inner)
    chip = lax.div(lax.axis_index("tm"), 2)
    for k in range(inner):
        for h in range(2):
            s = h * inner + lax.bitwise_xor(mine, k)
            for d, ref in enumerate(came):
                upper = (chip > lax.bitwise_xor(chip, d + 1)).astype(jnp.int32)
                far = gathered(ref, s, cap, table_ref, False)
                tile = pack(times(sorted_ref[upper, k, h], far))
                outs[k][h, d] = encode(tile) if k else tile


def early_sum_kernel(own_ref, own_rows_ref, *refs):
    *parts, home_ref, rows_ref, away_ref = refs
    body = home_ref.shape[0]
    side = lax.div(lax.axis_index("blk"), lax.axis_size("blk") // 2)

    def total(h):
        tiles, rows = own_ref[h], own_rows_ref[h]
        for part in parts:
            tiles = tiles + decode(part[h, :body])
            rows = rows + decode_rows(part[h, body:], PART_UNIT)
        return tiles, rows

    home_ref[...], rows_ref[...] = total(side)
    tiles, rows = total(1 - side)
    away_ref[:body], away_ref[body:] = encode(tiles), encode_rows(rows, HALF_UNIT)


def late_sum_kernel(pieces, home_rows_ref, early_away_ref, *refs):
    *parts, home_ref, near_ref, away_ref = refs
    inner = len(parts) // pieces
    pairs, body = home_ref.shape[:2]
    side = lax.div(lax.axis_index("blk"), lax.axis_size("blk") // 2)
    near_rows = encode_rows(home_rows_ref[...], HALF_UNIT)
    away_rows = early_away_ref[-2 * ROWS:]
    for d in range(pairs):
        at = 0
        for piece in range(pieces):
            own, *came = parts[piece * inner:(piece + 1) * inner]
            here = pl.ds(at, own.shape[2])
            at += own.shape[2]
            home, away = own[side, d], own[1 - side, d]
            for part in came:
                home = home + decode(part[side, d])
                away = away + decode(part[1 - side, d])
            home_ref[d, here] = home
            near_ref[d, here] = encode(home)
            away_ref[d, here] = encode(away)
        near_ref[d, body:], away_ref[d, body:] = near_rows, away_rows


def set_scale(ref, rows, which):
    for start, x in sums_of(rows, ref.shape[1], which):
        ref[0:1, start:start + x.shape[1]] = 1.0 / x


def early_end_kernel(
    home_ref, rows_ref, came_ref, after_ref, own_ref, part_ref, code_ref, down_ref, scale_ref
):
    half, panel = part_ref.shape
    body, diagonal = home_ref.shape[0], packed_rows(panel, panel, True)
    rows = rows_ref[...] + decode_rows(came_ref[body:], HALF_UNIT)
    part = home_ref[diagonal:] + decode(came_ref[diagonal:body])
    code_ref[...] = encode(part)
    unpack(part, part_ref)
    unpack(home_ref[:diagonal] + decode(came_ref[:diagonal]), own_ref, True)
    at = 2 * -(-panel // LANES)
    count = rows[at:at + 1, 0:1] * float(BLOCK)
    for which in range(2):
        set_scale(scale_ref.at[which], rows, which)
    down = jnp.broadcast_to(scale_ref[0, 0:1] * count, (panel, panel)).T
    down_ref[...] = down
    own_ref[...] = own_ref[...] * down * scale_ref[0, 0:1]


def last_kernel(
    pairs, own_ref, part_ref, mate_part_ref, down_ref, scale_ref, late_ref, *refs
):
    away, near = refs[:pairs], refs[pairs:2 * pairs]
    across_ref, out_ref, tiles, scale, turned = refs[2 * pairs:]
    steps, panel = tiles.shape[:2]
    half, late = panel // 2, late_ref.shape[1]
    me = lax.axis_index("tm")
    chip, core = lax.div(me, 2), lax.rem(me, 2)
    tiles[me] = own_ref[...]

    @pl.when(core == 0)
    def _():
        tiles[me + 1, :half] = part_ref[...] * down_ref[:half] * scale_ref[1, 0:1]
        unpack(decode(mate_part_ref[...]), tiles.at[me + 1, pl.ds(half, panel - half)])
        tiles[me + 1, half:] = tiles[me + 1, half:] * down_ref[half:] * scale_ref[1, 0:1]

    for d in range(pairs):
        far_chip = lax.bitwise_xor(chip, d + 1)

        @pl.when(chip < far_chip)
        def _():
            rows = decode_rows(near[d][0, late:], HALF_UNIT) + decode_rows(
                away[d][0, late:], HALF_UNIT
            )
            unpack(late_ref[d] + decode(across_ref[d, :late]), turned)
            set_scale(scale, rows, 0)
            tiles[2 * far_chip + core] = turned[...] * down_ref[...] * scale[0:1]
            unpack(decode(near[d][0, :late]) + decode(away[d][0, :late]), turned)
            set_scale(scale, rows, 1)
            tiles[2 * far_chip + 1 - core] = turned[...].T * down_ref[...] * scale[0:1]

    for u in range(steps):

        @pl.when(u >= me)
        def _():
            out_ref[0, :, u * panel:(u + 1) * panel] = tiles[u]

        @pl.when(u < me)
        def _():
            out_ref[0, :, u * panel:(u + 1) * panel] = jnp.zeros((panel, panel), jnp.float32)


def call(kernel, outs, ins, scratch=(), flops=0, in_hbm=0):
    moved = sum(math.prod(x.shape) * x.dtype.itemsize for x in (*outs, *ins))
    many = isinstance(outs, list)
    specs = [SMEM if x.ndim == 1 else VMEM for x in (*ins, *outs)]
    specs[:in_hbm] = [HBM] * in_hbm
    ins = [
        pltpu.with_memory_space_constraint(x, pltpu.HBM) if i < in_hbm else x
        for i, x in enumerate(ins)
    ]
    return pl.pallas_call(
        kernel,
        out_shape=outs if many else outs[0],
        in_specs=specs[:len(ins)],
        out_specs=specs[len(ins):] if many else specs[-1],
        scratch_shapes=scratch,
        compiler_params=pltpu.CompilerParams(vmem_limit_bytes=48 * 2**20),
        cost_estimate=pl.CostEstimate(flops=flops, bytes_accessed=moved, transcendentals=0),
    )(*ins)


def on_device(intensity, block_cycle, cycle_order):
    panel = intensity.shape[0]
    blk_dev = block_cycle.shape[0]
    cycles = cycle_order.shape[0]
    groups = lax.axis_size("blk")
    steps = lax.axis_size("tm")
    inner = groups // 2
    pairs = steps // 2 - 1
    cap = 2 * max(1, blk_dev // cycles)
    early = packed_rows(panel, panel, True) + packed_rows(panel // 2, panel)
    first = panel // LANES * LANES
    pieces = [n for n in (first, panel - first) if n]
    late = [panel * n // LANES for n in pieces]

    def hop(x, by_blk, by_tm, sends=lambda t: True):
        perm = [
            (b * steps + t, (b ^ by_blk) * steps + (t ^ by_tm))
            for b in range(groups)
            for t in range(steps)
            if sends(t)
        ]
        return lax.ppermute(x, ("blk", "tm"), perm)

    offsets = range(1, pairs + 1)
    other = hop(intensity, 0, 1)
    sent = intensity[:first] if len(pieces) > 1 else intensity
    far = [[hop(sent, 0, 2 * d) for d in offsets]]
    f32, i16 = jnp.float32, jnp.int16
    shape = jax.ShapeDtypeStruct
    depth = cap * BLOCK
    work = 2 * cycles * panel * panel * depth
    table, gathers, own_rows, *made = call(
        functools.partial(early_kernel, cap),
        [
            shape((cycles * (cap + 1),), jnp.int32),
            shape((2, inner, 2, panel, depth), jnp.bfloat16),
            shape((2, ROWS, LANES), f32),
            *[shape((n, intensity.shape[1]), jnp.bfloat16) for n in pieces[1:]],
            shape((2, early, LANES), f32),
            *[shape((2, early + 2 * ROWS, LANES), i16)] * (inner - 1),
        ],
        (block_cycle, cycle_order, intensity, other),
        [
            pltpu.SMEM(cycle_order.shape, jnp.int32),
            pltpu.SMEM(block_cycle.shape, jnp.int32),
            pltpu.SMEM(cycle_order.shape, jnp.int32),
            pltpu.VMEM(intensity.shape, jnp.bfloat16),
            pltpu.VMEM((2, -(-cycles // 16) * 16, panel), f32),
            pltpu.SemaphoreType.DMA((3,)),
        ],
        2 * work,
        3,
    )
    far += [[hop(x, 0, 2 * d) for d in offsets] for x in made[:-inner]]

    def exchange(made):
        order = sorted(range(inner), key=lambda k: (k > 0, -k.bit_count()))
        return [hop(made[k], k, 0) if k else made[k] for k in order]

    parts = exchange(made[-inner:])
    home, home_rows, away = call(
        early_sum_kernel,
        [
            shape((early, LANES), f32),
            shape((ROWS, LANES), f32),
            shape((early + 2 * ROWS, LANES), i16),
        ],
        (parts[0], own_rows, *parts[1:]),
    )
    came = hop(away, inner, 0)

    parts, after = [], ()
    for rows, came_rows in zip(late, far):
        made = call(
            functools.partial(late_kernel, cap, len(after)),
            [shape((2, pairs, rows, LANES), i16 if k else f32) for k in range(inner)],
            (table, gathers, *after, *came_rows),
            flops=pairs * work,
        )
        parts += exchange(made)
        after = (away, made[1])
    late_home, near, late_away = call(
        functools.partial(late_sum_kernel, len(pieces)),
        [
            shape((pairs, sum(late), LANES), f32),
            shape((pairs, sum(late) + 2 * ROWS, LANES), i16),
            shape((pairs, sum(late) + 2 * ROWS, LANES), i16),
        ],
        (home_rows, away, *parts),
    )

    def is_lower(t, d):
        return t // 2 < (t // 2 ^ d)

    from_away = [
        hop(late_away[d - 1:d], inner, 2 * d, lambda t, d=d: not is_lower(t, d)) for d in offsets
    ]
    from_near = [hop(near[d - 1:d], 0, 2 * d) for d in offsets]
    across = hop(late_away, inner, 0, lambda t: any(is_lower(t, d) for d in offsets))
    own_tile, part, code, down, scale = call(
        early_end_kernel,
        [
            shape((panel, panel), f32),
            shape((panel // 2, panel), f32),
            shape((packed_rows(panel // 2, panel), LANES), i16),
            shape((panel, panel), f32),
            shape((2, 8, panel), f32),
        ],
        (home, home_rows, came, late_away),
    )
    mate_part = hop(code, 0, 1)
    return call(
        functools.partial(last_kernel, pairs),
        (shape((1, panel, steps * panel), f32),),
        (own_tile, part, mate_part, down, scale, late_home, *from_away, *from_near, across),
        [
            pltpu.VMEM((steps, panel, panel), f32),
            pltpu.VMEM((8, panel), f32),
            pltpu.VMEM((panel, panel), f32),
        ],
    )


def solution(mesh):
    placed = (P("tm", "blk"), P("blk"), P())
    return jax.shard_map(
        on_device, mesh=mesh, in_specs=placed, out_specs=P("blk", "tm", None), check_vma=False
    )
```

```python
import functools
import math

import jax
import jax.numpy as jnp
from jax import lax
from jax.experimental import pallas as pl
from jax.experimental.pallas import tpu as pltpu
from jax.sharding import PartitionSpec as P

BLOCK = 128
LANES = 128
ROWS = 8
NONE = -32768
LEAST, MOST = -3.0, 28.0
PER_OCTAVE = 65534 / (MOST - LEAST)
MIDDLE = (MOST + LEAST) / 2
PART_UNIT, HALF_UNIT = 8192.0, 2048.0
LOW = 1 << 16
VMEM = pl.BlockSpec(memory_space=pltpu.VMEM)
SMEM = pl.BlockSpec(memory_space=pltpu.SMEM)
HBM = pl.BlockSpec(memory_space=pltpu.HBM)


def times(left, right):
    return lax.dot_general(
        left, right, (((1,), (1,)), ((), ())), preferred_element_type=jnp.float32
    )


def encode(x):
    level = jnp.log(jnp.maximum(x, 2.0**LEAST)) * (PER_OCTAVE / math.log(2))
    code = (level + (0.5 - LEAST * PER_OCTAVE)).astype(jnp.int32) + (NONE + 1)
    return jnp.where(x[..., :1, :] > 0, code, NONE).astype(jnp.int16)


def decode(code):
    code = code.astype(jnp.int32)
    level = code.astype(jnp.float32) * (math.log(2) / PER_OCTAVE) + MIDDLE * math.log(2)
    return jnp.where(code[..., :1, :] > NONE, jnp.exp(level), 0.0)


def split(panel):
    whole, rest = divmod(panel, LANES)
    return whole, LANES // rest if rest else 0


def packed_rows(rows, panel, symmetric=False):
    whole, fold = split(panel)
    if symmetric and (whole, fold) == (1, 2):
        return LANES + LANES // 2
    body = sum((i + 1) * LANES if symmetric else rows for i in range(whole))
    return body + (rows // fold if fold else 0)


def pack(tile, symmetric=False):
    rows, panel = tile.shape
    whole, fold = split(panel)
    if symmetric and (whole, fold) == (1, 2):
        n = LANES // 2
        left, right = tile[:, :LANES], tile[:, LANES:]
        parts = [
            left[:n],
            jnp.concatenate([right[:n], left[n:2 * n, n:]], axis=1),
            jnp.concatenate([right[n:2 * n], right[2 * n:]], axis=1),
        ]
        return jnp.concatenate(parts, axis=0)
    parts = [
        tile[: (i + 1) * LANES if symmetric else rows, i * LANES:(i + 1) * LANES]
        for i in range(whole)
    ]
    if fold:
        n = rows // fold
        left = [tile[i * n:(i + 1) * n, whole * LANES:] for i in range(fold)]
        parts.append(jnp.concatenate(left, axis=1))
    return jnp.concatenate(parts, axis=0)


def unpack(x, out, symmetric=False):
    rows, panel = out.shape
    whole, fold = split(panel)
    if symmetric and (whole, fold) == (1, 2):
        n = LANES // 2
        out[:n, :LANES] = x[:n]
        out[:n, LANES:] = x[n:2 * n, :n]
        out[n:2 * n, n:LANES] = x[n:2 * n, n:]
        out[n:2 * n, LANES:] = x[2 * n:, :n]
        out[2 * n:, LANES:] = x[2 * n:, n:]
        out[n:2 * n, :n] = x[:n, n:].T
        out[2 * n:, :LANES] = out[:2 * n, LANES:].T
        return
    at = 0
    for i in range(whole):
        n = (i + 1) * LANES if symmetric else rows
        out[:n, i * LANES:(i + 1) * LANES] = x[at:at + n]
        at += n
    if fold:
        n, width = rows // fold, LANES // fold
        for i in range(fold):
            out[i * n:(i + 1) * n, whole * LANES:] = x[at:, i * width:(i + 1) * width]
    if symmetric:
        for i in range(whole):
            n = (i + 1) * LANES
            if n < panel:
                out[n:, i * LANES:n] = out[i * LANES:n, n:].T


def rows_of(sums, count):
    panel = sums[0].shape[1]
    row = lax.broadcasted_iota(jnp.int32, (ROWS, LANES), 0)
    out, at = jnp.zeros((ROWS, LANES), jnp.float32), 0
    for x in sums:
        for start in range(0, panel, LANES):
            piece = x[:, start:start + LANES]
            if piece.shape[1] < LANES:
                piece = jnp.concatenate([piece] * (LANES // piece.shape[1]), axis=1)
            out = jnp.where(row == at, piece, out)
            at += 1
    return jnp.where(row == at, count, out)


def sums_of(rows, panel, which):
    per = -(-panel // LANES)
    starts = range(0, panel, LANES)
    return [
        (start, rows[which * per + i:which * per + i + 1, :min(LANES, panel - start)])
        for i, start in enumerate(starts)
    ]


def encode_rows(rows, unit):
    whole = (rows * unit + 0.5).astype(jnp.int32)
    high = lax.shift_right_logical(whole, 16)
    low = lax.bitwise_and(whole, LOW - 1) - LOW // 2
    return jnp.concatenate([high, low], axis=0).astype(jnp.int16)


def decode_rows(code, unit):
    x = code.astype(jnp.int32).astype(jnp.float32)
    return (x[:ROWS] * float(LOW) + (x[ROWS:] + LOW / 2)) * (1 / unit)


def find_slots(cap, cycle_ref, order_ref, where_ref, table_ref):
    cycles = order_ref.shape[0]
    for s in range(cycles):
        where_ref[order_ref[s]] = s
        table_ref[s] = 0
    for s in range(cycles * cap):
        table_ref[cycles + s] = 0
    for j in range(cycle_ref.shape[0]):
        p = where_ref[cycle_ref[j]]
        r = table_ref[p]
        table_ref[cycles + p * cap + r] = j
        table_ref[p] = r + 1


def gathered(ref, s, cap, table_ref, masked):
    cycles = table_ref.shape[0] // (cap + 1)
    parts = []
    for r in range(cap):
        j = table_ref[cycles + s * cap + r]
        x = ref[:, pl.ds(pl.multiple_of(j * BLOCK, BLOCK), BLOCK)]
        parts.append(jnp.where(r < table_ref[s], x, jnp.zeros_like(x)) if masked else x)
    return jnp.concatenate(parts, axis=1)


def early_kernel(cap, cycle_hbm, order_hbm, own_hbm, other_ref, *refs):
    table_ref, sorted_ref, rows_ref, *outs = refs[:-6]
    where_ref, cycle_ref, order_ref, own_ref, sums_ref, sems = refs[-6:]
    pairs = ((cycle_hbm, cycle_ref), (order_hbm, order_ref), (own_hbm, own_ref))
    copies = [pltpu.make_async_copy(*pair, sems.at[i]) for i, pair in enumerate(pairs)]
    for copy in copies:
        copy.start()
    copies[0].wait()
    copies[1].wait()
    find_slots(cap, cycle_ref, order_ref, where_ref, table_ref)
    inner = lax.axis_size("blk") // 2
    pieces, outs = outs[:-inner], outs[-inner:]
    panel = own_ref.shape[0]
    half = panel // 2
    mine = lax.rem(lax.axis_index("blk"), inner)
    first = lax.rem(lax.axis_index("tm"), 2) == 0
    body = outs[0].shape[1]
    row = lax.broadcasted_iota(jnp.int32, (sums_ref.shape[1], BLOCK), 0)
    members = jnp.concatenate(
        [
            jnp.where(row == where_ref[cycle_ref[j]], 1.0, 0.0).astype(jnp.bfloat16)
            for j in range(cycle_ref.shape[0])
        ],
        axis=1,
    )
    each = [(k, h, h * inner + lax.bitwise_xor(mine, k)) for k in range(inner) for h in range(2)]
    for k, h, s in each:
        sorted_ref[1, k, h] = gathered(other_ref, s, cap, table_ref, True)
    sums_ref[1] = times(members, other_ref[...])
    copies[2].wait()
    for piece in pieces:
        piece[...] = own_ref[panel - piece.shape[0]:]
    sums_ref[0] = times(members, own_ref[...])
    for k, h, s in each:
        own, other = gathered(own_ref, s, cap, table_ref, True), sorted_ref[1, k, h]
        sorted_ref[0, k, h] = own
        left = jnp.where(first, own[:half], other[half:])
        right = jnp.where(first, other, own)
        rows = rows_of([sums_ref[i, pl.ds(s, 1)] for i in range(2)], table_ref[s].astype(jnp.float32))
        found = jnp.concatenate([pack(times(own, own), True), pack(times(left, right))], axis=0)
        if k:
            outs[k][h, :body] = encode(found)
            outs[k][h, body:] = encode_rows(rows, PART_UNIT)
        else:
            outs[k][h] = found
            rows_ref[h] = rows


def late_kernel(cap, after, table_ref, sorted_ref, *refs):
    refs = refs[after:]
    inner = lax.axis_size("blk") // 2
    came, outs = refs[:-inner], refs[-inner:]
    mine = lax.rem(lax.axis_index("blk"), inner)
    chip = lax.div(lax.axis_index("tm"), 2)
    for k in range(inner):
        for h in range(2):
            s = h * inner + lax.bitwise_xor(mine, k)
            for d, ref in enumerate(came):
                upper = (chip > lax.bitwise_xor(chip, d + 1)).astype(jnp.int32)
                far = gathered(ref, s, cap, table_ref, False)
                tile = pack(times(sorted_ref[upper, k, h], far))
                outs[k][h, d] = encode(tile) if k else tile


def early_sum_kernel(own_ref, own_rows_ref, *refs):
    *parts, home_ref, rows_ref, away_ref = refs
    body = home_ref.shape[0]
    side = lax.div(lax.axis_index("blk"), lax.axis_size("blk") // 2)

    def total(h):
        tiles, rows = own_ref[h], own_rows_ref[h]
        for part in parts:
            tiles = tiles + decode(part[h, :body])
            rows = rows + decode_rows(part[h, body:], PART_UNIT)
        return tiles, rows

    home_ref[...], rows_ref[...] = total(side)
    tiles, rows = total(1 - side)
    away_ref[:body], away_ref[body:] = encode(tiles), encode_rows(rows, HALF_UNIT)


def late_sum_kernel(pieces, home_rows_ref, early_away_ref, *refs):
    *parts, home_ref, near_ref, away_ref = refs
    inner = len(parts) // pieces
    pairs, body = home_ref.shape[:2]
    side = lax.div(lax.axis_index("blk"), lax.axis_size("blk") // 2)
    near_rows = encode_rows(home_rows_ref[...], HALF_UNIT)
    away_rows = early_away_ref[-2 * ROWS:]
    for d in range(pairs):
        at = 0
        for piece in range(pieces):
            own, *came = parts[piece * inner:(piece + 1) * inner]
            here = pl.ds(at, own.shape[2])
            at += own.shape[2]
            home, away = own[side, d], own[1 - side, d]
            for part in came:
                home = home + decode(part[side, d])
                away = away + decode(part[1 - side, d])
            home_ref[d, here] = home
            near_ref[d, here] = encode(home)
            away_ref[d, here] = encode(away)
        near_ref[d, body:], away_ref[d, body:] = near_rows, away_rows


def set_scale(ref, rows, which):
    for start, x in sums_of(rows, ref.shape[1], which):
        ref[0:1, start:start + x.shape[1]] = 1.0 / x


def early_end_kernel(
    home_ref, rows_ref, came_ref, after_ref, own_ref, part_ref, code_ref, down_ref, scale_ref
):
    half, panel = part_ref.shape
    body, diagonal = home_ref.shape[0], packed_rows(panel, panel, True)
    rows = rows_ref[...] + decode_rows(came_ref[body:], HALF_UNIT)
    part = home_ref[diagonal:] + decode(came_ref[diagonal:body])
    code_ref[...] = encode(part)
    unpack(part, part_ref)
    unpack(home_ref[:diagonal] + decode(came_ref[:diagonal]), own_ref, True)
    at = 2 * -(-panel // LANES)
    count = rows[at:at + 1, 0:1] * float(BLOCK)
    for which in range(2):
        set_scale(scale_ref.at[which], rows, which)
    down = jnp.broadcast_to(scale_ref[0, 0:1] * count, (panel, panel)).T
    down_ref[...] = down
    own_ref[...] = own_ref[...] * down * scale_ref[0, 0:1]


def last_kernel(
    pairs, own_ref, part_ref, mate_part_ref, down_ref, scale_ref, late_ref, *refs
):
    away, near = refs[:pairs], refs[pairs + 1:2 * pairs + 1]
    across_ref, (out_ref, tiles, scale, turned) = refs[pairs], refs[2 * pairs + 1:]
    steps, panel = tiles.shape[:2]
    half, late = panel // 2, late_ref.shape[1]
    me = lax.axis_index("tm")
    chip, core = lax.div(me, 2), lax.rem(me, 2)
    tiles[me] = own_ref[...]

    @pl.when(core == 0)
    def _():
        tiles[me + 1, :half] = part_ref[...] * down_ref[:half] * scale_ref[1, 0:1]
        unpack(decode(mate_part_ref[...]), tiles.at[me + 1, pl.ds(half, panel - half)])
        tiles[me + 1, half:] = tiles[me + 1, half:] * down_ref[half:] * scale_ref[1, 0:1]

    for d in range(pairs):
        far_chip = lax.bitwise_xor(chip, d + 1)

        @pl.when(chip < far_chip)
        def _():
            rows = decode_rows(near[d][0, late:], HALF_UNIT) + decode_rows(
                away[d][0, late:], HALF_UNIT
            )
            unpack(late_ref[d] + decode(across_ref[d, :late]), turned)
            set_scale(scale, rows, 0)
            tiles[2 * far_chip + core] = turned[...] * down_ref[...] * scale[0:1]
            unpack(decode(near[d][0, :late]) + decode(away[d][0, :late]), turned)
            set_scale(scale, rows, 1)
            tiles[2 * far_chip + 1 - core] = turned[...].T * down_ref[...] * scale[0:1]

    for u in range(steps):

        @pl.when(u >= me)
        def _():
            out_ref[0, :, u * panel:(u + 1) * panel] = tiles[u]

        @pl.when(u < me)
        def _():
            out_ref[0, :, u * panel:(u + 1) * panel] = jnp.zeros((panel, panel), jnp.float32)


def call(kernel, outs, ins, scratch=(), flops=0, in_hbm=0):
    moved = sum(math.prod(x.shape) * x.dtype.itemsize for x in (*outs, *ins))
    many = isinstance(outs, list)
    specs = [SMEM if x.ndim == 1 else VMEM for x in (*ins, *outs)]
    specs[:in_hbm] = [HBM] * in_hbm
    ins = [
        pltpu.with_memory_space_constraint(x, pltpu.HBM) if i < in_hbm else x
        for i, x in enumerate(ins)
    ]
    return pl.pallas_call(
        kernel,
        out_shape=outs if many else outs[0],
        in_specs=specs[:len(ins)],
        out_specs=specs[len(ins):] if many else specs[-1],
        scratch_shapes=scratch,
        compiler_params=pltpu.CompilerParams(vmem_limit_bytes=48 * 2**20),
        cost_estimate=pl.CostEstimate(flops=flops, bytes_accessed=moved, transcendentals=0),
    )(*ins)


def on_device(intensity, block_cycle, cycle_order):
    panel = intensity.shape[0]
    blk_dev = block_cycle.shape[0]
    cycles = cycle_order.shape[0]
    groups = lax.axis_size("blk")
    steps = lax.axis_size("tm")
    inner = groups // 2
    pairs = steps // 2 - 1
    cap = 2 * max(1, blk_dev // cycles)
    early = packed_rows(panel, panel, True) + packed_rows(panel // 2, panel)
    first = panel // LANES * LANES
    pieces = [n for n in (first, panel - first) if n]
    late = [panel * n // LANES for n in pieces]

    def hop(x, by_blk, by_tm, sends=lambda t: True):
        perm = [
            (b * steps + t, (b ^ by_blk) * steps + (t ^ by_tm))
            for b in range(groups)
            for t in range(steps)
            if sends(t)
        ]
        return lax.ppermute(x, ("blk", "tm"), perm)

    offsets = range(1, pairs + 1)
    other = hop(intensity, 0, 1)
    sent = intensity[:first] if len(pieces) > 1 else intensity
    far = [[hop(sent, 0, 2 * d) for d in offsets]]
    f32, i16 = jnp.float32, jnp.int16
    shape = jax.ShapeDtypeStruct
    depth = cap * BLOCK
    work = 2 * cycles * panel * panel * depth
    table, gathers, own_rows, *made = call(
        functools.partial(early_kernel, cap),
        [
            shape((cycles * (cap + 1),), jnp.int32),
            shape((2, inner, 2, panel, depth), jnp.bfloat16),
            shape((2, ROWS, LANES), f32),
            *[shape((n, intensity.shape[1]), jnp.bfloat16) for n in pieces[1:]],
            shape((2, early, LANES), f32),
            *[shape((2, early + 2 * ROWS, LANES), i16)] * (inner - 1),
        ],
        (block_cycle, cycle_order, intensity, other),
        [
            pltpu.SMEM(cycle_order.shape, jnp.int32),
            pltpu.SMEM(block_cycle.shape, jnp.int32),
            pltpu.SMEM(cycle_order.shape, jnp.int32),
            pltpu.VMEM(intensity.shape, jnp.bfloat16),
            pltpu.VMEM((2, -(-cycles // 16) * 16, panel), f32),
            pltpu.SemaphoreType.DMA((3,)),
        ],
        2 * work,
        3,
    )
    far += [[hop(x, 0, 2 * d) for d in offsets] for x in made[:-inner]]

    def exchange(made):
        order = sorted(range(inner), key=lambda k: (k > 0, -k.bit_count()))
        return [hop(made[k], k, 0) if k else made[k] for k in order]

    parts = exchange(made[-inner:])
    home, home_rows, away = call(
        early_sum_kernel,
        [
            shape((early, LANES), f32),
            shape((ROWS, LANES), f32),
            shape((early + 2 * ROWS, LANES), i16),
        ],
        (parts[0], own_rows, *parts[1:]),
    )
    came = hop(away, inner, 0)

    parts, after = [], ()
    for rows, came_rows in zip(late, far):
        made = call(
            functools.partial(late_kernel, cap, len(after)),
            [shape((2, pairs, rows, LANES), i16 if k else f32) for k in range(inner)],
            (table, gathers, *after, *came_rows),
            flops=pairs * work,
        )
        parts += exchange(made)
        after = (away, made[1])
    late_home, near, late_away = call(
        functools.partial(late_sum_kernel, len(pieces)),
        [
            shape((pairs, sum(late), LANES), f32),
            shape((pairs, sum(late) + 2 * ROWS, LANES), i16),
            shape((pairs, sum(late) + 2 * ROWS, LANES), i16),
        ],
        (home_rows, away, *parts),
    )

    def is_lower(t, d):
        return t // 2 < (t // 2 ^ d)

    from_away = [
        hop(late_away[d - 1:d], inner, 2 * d, lambda t, d=d: not is_lower(t, d)) for d in offsets
    ]
    from_near = [hop(near[d - 1:d], 0, 2 * d) for d in offsets]
    across = hop(late_away, inner, 0, lambda t: any(is_lower(t, d) for d in offsets))
    own_tile, part, code, down, scale = call(
        early_end_kernel,
        [
            shape((panel, panel), f32),
            shape((panel // 2, panel), f32),
            shape((packed_rows(panel // 2, panel), LANES), i16),
            shape((panel, panel), f32),
            shape((2, 8, panel), f32),
        ],
        (home, home_rows, came, late_away),
    )
    mate_part = hop(code, 0, 1)
    return call(
        functools.partial(last_kernel, pairs),
        (shape((1, panel, steps * panel), f32),),
        (own_tile, part, mate_part, down, scale, late_home, *from_away, across, *from_near),
        [
            pltpu.VMEM((steps, panel, panel), f32),
            pltpu.VMEM((8, panel), f32),
            pltpu.VMEM((panel, panel), f32),
        ],
    )


def solution(mesh):
    placed = (P("tm", "blk"), P("blk"), P())
    return jax.shard_map(
        on_device, mesh=mesh, in_specs=placed, out_specs=P("blk", "tm", None), check_vma=False
    )
```

```python
import functools
import math

import jax
import jax.numpy as jnp
from jax import lax
from jax.experimental import pallas as pl
from jax.experimental.pallas import tpu as pltpu
from jax.sharding import PartitionSpec as P

BLOCK = 128
LANES = 128
ROWS = 8
NONE = -32768
LEAST, MOST = -3.0, 28.0
PER_OCTAVE = 65534 / (MOST - LEAST)
MIDDLE = (MOST + LEAST) / 2
PART_UNIT, HALF_UNIT = 8192.0, 2048.0
LOW = 1 << 16
VMEM = pl.BlockSpec(memory_space=pltpu.VMEM)
SMEM = pl.BlockSpec(memory_space=pltpu.SMEM)
HBM = pl.BlockSpec(memory_space=pltpu.HBM)


def times(left, right):
    return lax.dot_general(
        left, right, (((1,), (1,)), ((), ())), preferred_element_type=jnp.float32
    )


def encode(x):
    level = jnp.log(jnp.maximum(x, 2.0**LEAST)) * (PER_OCTAVE / math.log(2))
    code = (level + (0.5 - LEAST * PER_OCTAVE)).astype(jnp.int32) + (NONE + 1)
    return jnp.where(x[..., :1, :] > 0, code, NONE).astype(jnp.int16)


def decode(code):
    code = code.astype(jnp.int32)
    level = code.astype(jnp.float32) * (math.log(2) / PER_OCTAVE) + MIDDLE * math.log(2)
    return jnp.where(code[..., :1, :] > NONE, jnp.exp(level), 0.0)


def split(panel):
    whole, rest = divmod(panel, LANES)
    return whole, LANES // rest if rest else 0


def packed_rows(rows, panel, symmetric=False):
    whole, fold = split(panel)
    if symmetric and (whole, fold) == (1, 2):
        return LANES + LANES // 2
    body = sum((i + 1) * LANES if symmetric else rows for i in range(whole))
    return body + (rows // fold if fold else 0)


def pack(tile, symmetric=False):
    rows, panel = tile.shape
    whole, fold = split(panel)
    if symmetric and (whole, fold) == (1, 2):
        n = LANES // 2
        left, right = tile[:, :LANES], tile[:, LANES:]
        parts = [
            left[:n],
            jnp.concatenate([right[:n], left[n:2 * n, n:]], axis=1),
            jnp.concatenate([right[n:2 * n], right[2 * n:]], axis=1),
        ]
        return jnp.concatenate(parts, axis=0)
    parts = [
        tile[: (i + 1) * LANES if symmetric else rows, i * LANES:(i + 1) * LANES]
        for i in range(whole)
    ]
    if fold:
        n = rows // fold
        left = [tile[i * n:(i + 1) * n, whole * LANES:] for i in range(fold)]
        parts.append(jnp.concatenate(left, axis=1))
    return jnp.concatenate(parts, axis=0)


def unpack(x, out, symmetric=False):
    rows, panel = out.shape
    whole, fold = split(panel)
    if symmetric and (whole, fold) == (1, 2):
        n = LANES // 2
        out[:n, :LANES] = x[:n]
        out[:n, LANES:] = x[n:2 * n, :n]
        out[n:2 * n, n:LANES] = x[n:2 * n, n:]
        out[n:2 * n, LANES:] = x[2 * n:, :n]
        out[2 * n:, LANES:] = x[2 * n:, n:]
        out[n:2 * n, :n] = x[:n, n:].T
        out[2 * n:, :LANES] = out[:2 * n, LANES:].T
        return
    at = 0
    for i in range(whole):
        n = (i + 1) * LANES if symmetric else rows
        out[:n, i * LANES:(i + 1) * LANES] = x[at:at + n]
        at += n
    if fold:
        n, width = rows // fold, LANES // fold
        for i in range(fold):
            out[i * n:(i + 1) * n, whole * LANES:] = x[at:, i * width:(i + 1) * width]
    if symmetric:
        for i in range(whole):
            n = (i + 1) * LANES
            if n < panel:
                out[n:, i * LANES:n] = out[i * LANES:n, n:].T


def rows_of(sums, count):
    panel = sums[0].shape[1]
    row = lax.broadcasted_iota(jnp.int32, (ROWS, LANES), 0)
    out, at = jnp.zeros((ROWS, LANES), jnp.float32), 0
    for x in sums:
        for start in range(0, panel, LANES):
            piece = x[:, start:start + LANES]
            if piece.shape[1] < LANES:
                piece = jnp.concatenate([piece] * (LANES // piece.shape[1]), axis=1)
            out = jnp.where(row == at, piece, out)
            at += 1
    return jnp.where(row == at, count, out)


def sums_of(rows, panel, which):
    per = -(-panel // LANES)
    starts = range(0, panel, LANES)
    return [
        (start, rows[which * per + i:which * per + i + 1, :min(LANES, panel - start)])
        for i, start in enumerate(starts)
    ]


def encode_rows(rows, unit):
    whole = (rows * unit + 0.5).astype(jnp.int32)
    high = lax.shift_right_logical(whole, 16)
    low = lax.bitwise_and(whole, LOW - 1) - LOW // 2
    return jnp.concatenate([high, low], axis=0).astype(jnp.int16)


def decode_rows(code, unit):
    x = code.astype(jnp.int32).astype(jnp.float32)
    return (x[:ROWS] * float(LOW) + (x[ROWS:] + LOW / 2)) * (1 / unit)


def find_slots(cap, cycle_ref, order_ref, where_ref, table_ref):
    cycles = order_ref.shape[0]
    for s in range(cycles):
        where_ref[order_ref[s]] = s
        table_ref[s] = 0
    for s in range(cycles * cap):
        table_ref[cycles + s] = 0
    for j in range(cycle_ref.shape[0]):
        p = where_ref[cycle_ref[j]]
        r = table_ref[p]
        table_ref[cycles + p * cap + r] = j
        table_ref[p] = r + 1


def gathered(ref, s, cap, table_ref, masked):
    cycles = table_ref.shape[0] // (cap + 1)
    parts = []
    for r in range(cap):
        j = table_ref[cycles + s * cap + r]
        x = ref[:, pl.ds(pl.multiple_of(j * BLOCK, BLOCK), BLOCK)]
        parts.append(jnp.where(r < table_ref[s], x, jnp.zeros_like(x)) if masked else x)
    return jnp.concatenate(parts, axis=1)


def early_kernel(cap, cycle_hbm, order_hbm, own_hbm, other_ref, *refs):
    table_ref, sorted_ref, rows_ref, *outs = refs[:-6]
    where_ref, cycle_ref, order_ref, own_ref, sums_ref, sems = refs[-6:]
    pairs = ((cycle_hbm, cycle_ref), (order_hbm, order_ref), (own_hbm, own_ref))
    copies = [pltpu.make_async_copy(*pair, sems.at[i]) for i, pair in enumerate(pairs)]
    for copy in copies:
        copy.start()
    copies[0].wait()
    copies[1].wait()
    find_slots(cap, cycle_ref, order_ref, where_ref, table_ref)
    inner = lax.axis_size("blk") // 2
    pieces, outs = outs[:-inner], outs[-inner:]
    panel = own_ref.shape[0]
    half = panel // 2
    mine = lax.rem(lax.axis_index("blk"), inner)
    first = lax.rem(lax.axis_index("tm"), 2) == 0
    body = outs[0].shape[1]
    row = lax.broadcasted_iota(jnp.int32, (sums_ref.shape[1], BLOCK), 0)
    members = jnp.concatenate(
        [
            jnp.where(row == where_ref[cycle_ref[j]], 1.0, 0.0).astype(jnp.bfloat16)
            for j in range(cycle_ref.shape[0])
        ],
        axis=1,
    )
    each = [(k, h, h * inner + lax.bitwise_xor(mine, k)) for k in range(inner) for h in range(2)]
    for k, h, s in each:

        @pl.when(table_ref[s] > 0)
        def _():
            sorted_ref[1, k, h] = gathered(other_ref, s, cap, table_ref, True)

    sums_ref[1] = times(members, other_ref[...])
    copies[2].wait()
    for piece in pieces:
        piece[...] = own_ref[panel - piece.shape[0]:]
    sums_ref[0] = times(members, own_ref[...])
    for k, h, s in each:
        rows = rows_of([sums_ref[i, pl.ds(s, 1)] for i in range(2)], table_ref[s].astype(jnp.float32))
        if k:
            outs[k][h, body:] = encode_rows(rows, PART_UNIT)
        else:
            rows_ref[h] = rows

        @pl.when(table_ref[s] > 0)
        def _():
            own, other = gathered(own_ref, s, cap, table_ref, True), sorted_ref[1, k, h]
            sorted_ref[0, k, h] = own
            left = jnp.where(first, own[:half], other[half:])
            right = jnp.where(first, other, own)
            found = jnp.concatenate([pack(times(own, own), True), pack(times(left, right))], axis=0)
            outs[k][h, :body] = encode(found) if k else found

        @pl.when(table_ref[s] == 0)
        def _():
            kind = outs[k].dtype
            outs[k][h, :body] = jnp.full((body, LANES), NONE if k else 0, kind)


def late_kernel(cap, after, table_ref, sorted_ref, *refs):
    refs = refs[after:]
    inner = lax.axis_size("blk") // 2
    came, outs = refs[:-inner], refs[-inner:]
    mine = lax.rem(lax.axis_index("blk"), inner)
    chip = lax.div(lax.axis_index("tm"), 2)
    for k in range(inner):
        for h in range(2):
            s = h * inner + lax.bitwise_xor(mine, k)

            @pl.when(table_ref[s] > 0)
            def _():
                for d, ref in enumerate(came):
                    upper = (chip > lax.bitwise_xor(chip, d + 1)).astype(jnp.int32)
                    far = gathered(ref, s, cap, table_ref, False)
                    tile = pack(times(sorted_ref[upper, k, h], far))
                    outs[k][h, d] = encode(tile) if k else tile

            @pl.when(table_ref[s] == 0)
            def _():
                shape, kind = outs[k].shape[1:], outs[k].dtype
                outs[k][h] = jnp.full(shape, NONE if k else 0, kind)


def early_sum_kernel(own_ref, own_rows_ref, *refs):
    *parts, home_ref, rows_ref, away_ref = refs
    body = home_ref.shape[0]
    side = lax.div(lax.axis_index("blk"), lax.axis_size("blk") // 2)

    def total(h):
        tiles, rows = own_ref[h], own_rows_ref[h]
        for part in parts:
            tiles = tiles + decode(part[h, :body])
            rows = rows + decode_rows(part[h, body:], PART_UNIT)
        return tiles, rows

    home_ref[...], rows_ref[...] = total(side)
    tiles, rows = total(1 - side)
    away_ref[:body], away_ref[body:] = encode(tiles), encode_rows(rows, HALF_UNIT)


def late_sum_kernel(pieces, home_rows_ref, early_away_ref, *refs):
    *parts, home_ref, near_ref, away_ref = refs
    inner = len(parts) // pieces
    pairs, body = home_ref.shape[:2]
    side = lax.div(lax.axis_index("blk"), lax.axis_size("blk") // 2)
    near_rows = encode_rows(home_rows_ref[...], HALF_UNIT)
    away_rows = early_away_ref[-2 * ROWS:]
    for d in range(pairs):
        at = 0
        for piece in range(pieces):
            own, *came = parts[piece * inner:(piece + 1) * inner]
            here = pl.ds(at, own.shape[2])
            at += own.shape[2]
            home, away = own[side, d], own[1 - side, d]
            for part in came:
                home = home + decode(part[side, d])
                away = away + decode(part[1 - side, d])
            home_ref[d, here] = home
            near_ref[d, here] = encode(home)
            away_ref[d, here] = encode(away)
        near_ref[d, body:], away_ref[d, body:] = near_rows, away_rows


def set_scale(ref, rows, which):
    for start, x in sums_of(rows, ref.shape[1], which):
        ref[0:1, start:start + x.shape[1]] = 1.0 / x


def early_end_kernel(
    home_ref, rows_ref, came_ref, after_ref, own_ref, part_ref, code_ref, down_ref, scale_ref
):
    half, panel = part_ref.shape
    body, diagonal = home_ref.shape[0], packed_rows(panel, panel, True)
    rows = rows_ref[...] + decode_rows(came_ref[body:], HALF_UNIT)
    part = home_ref[diagonal:] + decode(came_ref[diagonal:body])
    code_ref[...] = encode(part)
    unpack(part, part_ref)
    unpack(home_ref[:diagonal] + decode(came_ref[:diagonal]), own_ref, True)
    at = 2 * -(-panel // LANES)
    count = rows[at:at + 1, 0:1] * float(BLOCK)
    for which in range(2):
        set_scale(scale_ref.at[which], rows, which)
    down = jnp.broadcast_to(scale_ref[0, 0:1] * count, (panel, panel)).T
    down_ref[...] = down
    own_ref[...] = own_ref[...] * down * scale_ref[0, 0:1]


def last_kernel(
    pairs, own_ref, part_ref, mate_part_ref, down_ref, scale_ref, late_ref, *refs
):
    away, near = refs[:pairs], refs[pairs + 1:2 * pairs + 1]
    across_ref = refs[pairs]
    out_ref, tiles, scale, turned, ready, sems = refs[2 * pairs + 1:]
    steps, panel = tiles.shape[:2]
    half, late = panel // 2, late_ref.shape[1]
    me = lax.axis_index("tm")
    chip, core = lax.div(me, 2), lax.rem(me, 2)
    tiles[me] = own_ref[...]

    @pl.when(core == 0)
    def _():
        tiles[me + 1, :half] = part_ref[...] * down_ref[:half] * scale_ref[1, 0:1]
        unpack(decode(mate_part_ref[...]), tiles.at[me + 1, pl.ds(half, panel - half)])
        tiles[me + 1, half:] = tiles[me + 1, half:] * down_ref[half:] * scale_ref[1, 0:1]

    def finish(d):
        far_chip = lax.bitwise_xor(chip, d + 1)

        @pl.when(chip < far_chip)
        def _():
            rows = decode_rows(near[d][0, late:], HALF_UNIT) + decode_rows(
                away[d][0, late:], HALF_UNIT
            )
            unpack(late_ref[d] + decode(across_ref[d, :late]), turned)
            set_scale(scale, rows, 0)
            tiles[2 * far_chip + core] = turned[...] * down_ref[...] * scale[0:1]
            unpack(decode(near[d][0, :late]) + decode(away[d][0, :late]), turned)
            set_scale(scale, rows, 1)
            tiles[2 * far_chip + 1 - core] = turned[...].T * down_ref[...] * scale[0:1]

    def put(half):
        for u in range(half * steps // 2, (half + 1) * steps // 2):

            @pl.when(u >= me)
            def _():
                ready[:, u * panel:(u + 1) * panel] = tiles[u]

            @pl.when(u < me)
            def _():
                ready[:, u * panel:(u + 1) * panel] = jnp.zeros((panel, panel), jnp.float32)

        wide = steps // 2 * panel
        here = (slice(None), pl.ds(half * wide, wide))
        copy = pltpu.make_async_copy(ready.at[here], out_ref.at[(0, *here)], sems.at[half])
        copy.start()
        return copy

    for d in range(pairs):
        if d + 1 < steps // 4:
            finish(d)
    copies = [put(0)]
    for d in range(pairs):
        if d + 1 >= steps // 4:
            finish(d)
    copies.append(put(1))
    for copy in copies:
        copy.wait()


def call(kernel, outs, ins, scratch=(), flops=0, in_hbm=0, out_spec=None):
    moved = sum(math.prod(x.shape) * x.dtype.itemsize for x in (*outs, *ins))
    many = isinstance(outs, list)
    specs = [SMEM if x.ndim == 1 else VMEM for x in (*ins, *outs)]
    specs[:in_hbm] = [HBM] * in_hbm
    ins = [
        pltpu.with_memory_space_constraint(x, pltpu.HBM) if i < in_hbm else x
        for i, x in enumerate(ins)
    ]
    return pl.pallas_call(
        kernel,
        out_shape=outs if many else outs[0],
        in_specs=specs[:len(ins)],
        out_specs=out_spec or (specs[len(ins):] if many else specs[-1]),
        scratch_shapes=scratch,
        compiler_params=pltpu.CompilerParams(vmem_limit_bytes=48 * 2**20),
        cost_estimate=pl.CostEstimate(flops=flops, bytes_accessed=moved, transcendentals=0),
    )(*ins)


def on_device(intensity, block_cycle, cycle_order):
    panel = intensity.shape[0]
    blk_dev = block_cycle.shape[0]
    cycles = cycle_order.shape[0]
    groups = lax.axis_size("blk")
    steps = lax.axis_size("tm")
    inner = groups // 2
    pairs = steps // 2 - 1
    cap = 2 * max(1, blk_dev // cycles)
    early = packed_rows(panel, panel, True) + packed_rows(panel // 2, panel)
    first = panel // LANES * LANES
    pieces = [n for n in (first, panel - first) if n]
    late = [panel * n // LANES for n in pieces]

    def hop(x, by_blk, by_tm, sends=lambda t: True):
        perm = [
            (b * steps + t, (b ^ by_blk) * steps + (t ^ by_tm))
            for b in range(groups)
            for t in range(steps)
            if sends(t)
        ]
        return lax.ppermute(x, ("blk", "tm"), perm)

    offsets = range(1, pairs + 1)
    other = hop(intensity, 0, 1)
    sent = intensity[:first] if len(pieces) > 1 else intensity
    far = [[hop(sent, 0, 2 * d) for d in offsets]]
    f32, i16 = jnp.float32, jnp.int16
    shape = jax.ShapeDtypeStruct
    depth = cap * BLOCK
    work = 2 * cycles * panel * panel * depth
    table, gathers, own_rows, *made = call(
        functools.partial(early_kernel, cap),
        [
            shape((cycles * (cap + 1),), jnp.int32),
            shape((2, inner, 2, panel, depth), jnp.bfloat16),
            shape((2, ROWS, LANES), f32),
            *[shape((n, intensity.shape[1]), jnp.bfloat16) for n in pieces[1:]],
            shape((2, early, LANES), f32),
            *[shape((2, early + 2 * ROWS, LANES), i16)] * (inner - 1),
        ],
        (block_cycle, cycle_order, intensity, other),
        [
            pltpu.SMEM(cycle_order.shape, jnp.int32),
            pltpu.SMEM(block_cycle.shape, jnp.int32),
            pltpu.SMEM(cycle_order.shape, jnp.int32),
            pltpu.VMEM(intensity.shape, jnp.bfloat16),
            pltpu.VMEM((2, -(-cycles // 16) * 16, panel), f32),
            pltpu.SemaphoreType.DMA((3,)),
        ],
        2 * work,
        3,
    )
    far += [[hop(x, 0, 2 * d) for d in offsets] for x in made[:-inner]]

    def exchange(made):
        order = sorted(range(inner), key=lambda k: (k > 0, -k.bit_count()))
        return [hop(made[k], k, 0) if k else made[k] for k in order]

    parts = exchange(made[-inner:])
    home, home_rows, away = call(
        early_sum_kernel,
        [
            shape((early, LANES), f32),
            shape((ROWS, LANES), f32),
            shape((early + 2 * ROWS, LANES), i16),
        ],
        (parts[0], own_rows, *parts[1:]),
    )
    came = hop(away, inner, 0)

    parts, after = [], ()
    for rows, came_rows in zip(late, far):
        made = call(
            functools.partial(late_kernel, cap, len(after)),
            [shape((2, pairs, rows, LANES), i16 if k else f32) for k in range(inner)],
            (table, gathers, *after, *came_rows),
            flops=pairs * work,
        )
        parts += exchange(made)
        after = (away, made[1])
    late_home, near, late_away = call(
        functools.partial(late_sum_kernel, len(pieces)),
        [
            shape((pairs, sum(late), LANES), f32),
            shape((pairs, sum(late) + 2 * ROWS, LANES), i16),
            shape((pairs, sum(late) + 2 * ROWS, LANES), i16),
        ],
        (home_rows, away, *parts),
    )

    def is_lower(t, d):
        return t // 2 < (t // 2 ^ d)

    from_away = [
        hop(late_away[d - 1:d], inner, 2 * d, lambda t, d=d: not is_lower(t, d)) for d in offsets
    ]
    from_near = [hop(near[d - 1:d], 0, 2 * d) for d in offsets]
    across = hop(late_away, inner, 0, lambda t: any(is_lower(t, d) for d in offsets))
    own_tile, part, code, down, scale = call(
        early_end_kernel,
        [
            shape((panel, panel), f32),
            shape((panel // 2, panel), f32),
            shape((packed_rows(panel // 2, panel), LANES), i16),
            shape((panel, panel), f32),
            shape((2, 8, panel), f32),
        ],
        (home, home_rows, came, late_away),
    )
    mate_part = hop(code, 0, 1)
    return call(
        functools.partial(last_kernel, pairs),
        (shape((1, panel, steps * panel), f32),),
        (own_tile, part, mate_part, down, scale, late_home, *from_away, across, *from_near),
        [
            pltpu.VMEM((steps, panel, panel), f32),
            pltpu.VMEM((8, panel), f32),
            pltpu.VMEM((panel, panel), f32),
            pltpu.VMEM((panel, steps * panel), f32),
            pltpu.SemaphoreType.DMA((2,)),
        ],
        out_spec=HBM,
    )


def solution(mesh):
    placed = (P("tm", "blk"), P("blk"), P())
    return jax.shard_map(
        on_device, mesh=mesh, in_specs=placed, out_specs=P("blk", "tm", None), check_vma=False
    )
```

```python
import functools
import math

import jax
import jax.numpy as jnp
from jax import lax
from jax.experimental import pallas as pl
from jax.experimental.pallas import tpu as pltpu
from jax.sharding import PartitionSpec as P

BLOCK = 128
LANES = 128
ROWS = 8
NONE = -32768
LEAST, MOST = -3.0, 29.0
PER_OCTAVE = 65534 / (MOST - LEAST)
MIDDLE = (MOST + LEAST) / 2
PART_UNIT, HALF_UNIT = 8192.0, 2048.0
LOW = 1 << 16
VMEM = pl.BlockSpec(memory_space=pltpu.VMEM)
SMEM = pl.BlockSpec(memory_space=pltpu.SMEM)
HBM = pl.BlockSpec(memory_space=pltpu.HBM)


def times(left, right):
    return lax.dot_general(
        left, right, (((1,), (1,)), ((), ())), preferred_element_type=jnp.float32
    )


def encode(x):
    level = jnp.log(jnp.maximum(x, 2.0**LEAST)) * (PER_OCTAVE / math.log(2))
    code = (level + (0.5 - LEAST * PER_OCTAVE)).astype(jnp.int32) + (NONE + 1)
    return jnp.where(x[..., :1, :] > 0, code, NONE).astype(jnp.int16)


def decode(code):
    code = code.astype(jnp.int32)
    level = code.astype(jnp.float32) * (math.log(2) / PER_OCTAVE) + MIDDLE * math.log(2)
    return jnp.where(code[..., :1, :] > NONE, jnp.exp(level), 0.0)


def split(panel):
    whole, rest = divmod(panel, LANES)
    return whole, LANES // rest if rest else 0


def packed_rows(rows, panel, symmetric=False):
    whole, fold = split(panel)
    if symmetric and (whole, fold) == (1, 2):
        return LANES + LANES // 2
    body = sum((i + 1) * LANES if symmetric else rows for i in range(whole))
    return body + (rows // fold if fold else 0)


def pack(tile, symmetric=False):
    rows, panel = tile.shape
    whole, fold = split(panel)
    if symmetric and (whole, fold) == (1, 2):
        n = LANES // 2
        left, right = tile[:, :LANES], tile[:, LANES:]
        parts = [
            left[:n],
            jnp.concatenate([right[:n], left[n:2 * n, n:]], axis=1),
            jnp.concatenate([right[n:2 * n], right[2 * n:]], axis=1),
        ]
        return jnp.concatenate(parts, axis=0)
    parts = [
        tile[: (i + 1) * LANES if symmetric else rows, i * LANES:(i + 1) * LANES]
        for i in range(whole)
    ]
    if fold:
        n = rows // fold
        left = [tile[i * n:(i + 1) * n, whole * LANES:] for i in range(fold)]
        parts.append(jnp.concatenate(left, axis=1))
    return jnp.concatenate(parts, axis=0)


def unpack(x, out, symmetric=False):
    rows, panel = out.shape
    whole, fold = split(panel)
    if symmetric and (whole, fold) == (1, 2):
        n = LANES // 2
        out[:n, :LANES] = x[:n]
        out[:n, LANES:] = x[n:2 * n, :n]
        out[n:2 * n, n:LANES] = x[n:2 * n, n:]
        out[n:2 * n, LANES:] = x[2 * n:, :n]
        out[2 * n:, LANES:] = x[2 * n:, n:]
        out[n:2 * n, :n] = x[:n, n:].T
        out[2 * n:, :LANES] = out[:2 * n, LANES:].T
        return
    at = 0
    for i in range(whole):
        n = (i + 1) * LANES if symmetric else rows
        out[:n, i * LANES:(i + 1) * LANES] = x[at:at + n]
        at += n
    if fold:
        n, width = rows // fold, LANES // fold
        for i in range(fold):
            out[i * n:(i + 1) * n, whole * LANES:] = x[at:, i * width:(i + 1) * width]
    if symmetric:
        for i in range(whole):
            n = (i + 1) * LANES
            if n < panel:
                out[n:, i * LANES:n] = out[i * LANES:n, n:].T


def rows_of(sums, count):
    panel = sums[0].shape[1]
    row = lax.broadcasted_iota(jnp.int32, (ROWS, LANES), 0)
    out, at = jnp.zeros((ROWS, LANES), jnp.float32), 0
    for x in sums:
        for start in range(0, panel, LANES):
            piece = x[:, start:start + LANES]
            if piece.shape[1] < LANES:
                piece = jnp.concatenate([piece] * (LANES // piece.shape[1]), axis=1)
            out = jnp.where(row == at, piece, out)
            at += 1
    return jnp.where(row == at, count, out)


def sums_of(rows, panel, which):
    per = -(-panel // LANES)
    starts = range(0, panel, LANES)
    return [
        (start, rows[which * per + i:which * per + i + 1, :min(LANES, panel - start)])
        for i, start in enumerate(starts)
    ]


def encode_rows(rows, unit):
    whole = (rows * unit + 0.5).astype(jnp.int32)
    high = lax.shift_right_logical(whole, 16)
    low = lax.bitwise_and(whole, LOW - 1) - LOW // 2
    return jnp.concatenate([high, low], axis=0).astype(jnp.int16)


def decode_rows(code, unit):
    x = code.astype(jnp.int32).astype(jnp.float32)
    return (x[:ROWS] * float(LOW) + (x[ROWS:] + LOW / 2)) * (1 / unit)


def find_slots(cap, cycle_ref, order_ref, where_ref, table_ref):
    cycles = order_ref.shape[0]
    for s in range(cycles):
        where_ref[order_ref[s]] = s
        table_ref[s] = 0
    for s in range(cycles * cap):
        table_ref[cycles + s] = 0
    for j in range(cycle_ref.shape[0]):
        p = where_ref[cycle_ref[j]]
        r = table_ref[p]
        table_ref[cycles + p * cap + r] = j
        table_ref[p] = r + 1


def gathered(ref, s, cap, table_ref, masked):
    cycles = table_ref.shape[0] // (cap + 1)
    parts = []
    for r in range(cap):
        j = table_ref[cycles + s * cap + r]
        x = ref[:, pl.ds(pl.multiple_of(j * BLOCK, BLOCK), BLOCK)]
        parts.append(jnp.where(r < table_ref[s], x, jnp.zeros_like(x)) if masked else x)
    return jnp.concatenate(parts, axis=1)


def early_kernel(cap, cycle_hbm, order_hbm, own_hbm, other_ref, *refs):
    table_ref, sorted_ref, rows_ref, *outs = refs[:-6]
    where_ref, cycle_ref, order_ref, own_ref, sums_ref, sems = refs[-6:]
    pairs = ((cycle_hbm, cycle_ref), (order_hbm, order_ref), (own_hbm, own_ref))
    copies = [pltpu.make_async_copy(*pair, sems.at[i]) for i, pair in enumerate(pairs)]
    for copy in copies:
        copy.start()
    copies[0].wait()
    copies[1].wait()
    find_slots(cap, cycle_ref, order_ref, where_ref, table_ref)
    inner = lax.axis_size("blk") // 2
    pieces, outs = outs[:-inner], outs[-inner:]
    panel = own_ref.shape[0]
    half = panel // 2
    mine = lax.rem(lax.axis_index("blk"), inner)
    first = lax.rem(lax.axis_index("tm"), 2) == 0
    body = outs[0].shape[1]
    row = lax.broadcasted_iota(jnp.int32, (sums_ref.shape[1], BLOCK), 0)
    members = jnp.concatenate(
        [
            jnp.where(row == where_ref[cycle_ref[j]], 1.0, 0.0).astype(jnp.bfloat16)
            for j in range(cycle_ref.shape[0])
        ],
        axis=1,
    )
    each = [(k, h, h * inner + lax.bitwise_xor(mine, k)) for k in range(inner) for h in range(2)]
    for k, h, s in each:
        sorted_ref[1, k, h] = gathered(other_ref, s, cap, table_ref, True)
    sums_ref[1] = times(members, other_ref[...])
    copies[2].wait()
    for piece in pieces:
        piece[...] = own_ref[panel - piece.shape[0]:]
    sums_ref[0] = times(members, own_ref[...])
    for k, h, s in each:
        own, other = gathered(own_ref, s, cap, table_ref, True), sorted_ref[1, k, h]
        sorted_ref[0, k, h] = own
        left = jnp.where(first, own[:half], other[half:])
        right = jnp.where(first, other, own)
        rows = rows_of([sums_ref[i, pl.ds(s, 1)] for i in range(2)], table_ref[s].astype(jnp.float32))
        found = jnp.concatenate([pack(times(own, own), True), pack(times(left, right))], axis=0)
        if k:
            outs[k][h, :body] = encode(found)
            outs[k][h, body:] = encode_rows(rows, PART_UNIT)
        else:
            outs[k][h] = found
            rows_ref[h] = rows


def late_kernel(cap, after, table_ref, sorted_ref, *refs):
    refs = refs[after:]
    inner = lax.axis_size("blk") // 2
    came, outs = refs[:-inner], refs[-inner:]
    mine = lax.rem(lax.axis_index("blk"), inner)
    chip = lax.div(lax.axis_index("tm"), 2)
    for k in range(inner):
        for h in range(2):
            s = h * inner + lax.bitwise_xor(mine, k)
            for d, ref in enumerate(came):
                upper = (chip > lax.bitwise_xor(chip, d + 1)).astype(jnp.int32)
                far = gathered(ref, s, cap, table_ref, False)
                tile = pack(times(sorted_ref[upper, k, h], far))
                outs[k][h, d] = encode(tile) if k else tile


def early_sum_kernel(own_ref, own_rows_ref, *refs):
    *parts, home_ref, rows_ref, away_ref = refs
    body = home_ref.shape[0]
    side = lax.div(lax.axis_index("blk"), lax.axis_size("blk") // 2)

    def total(h):
        tiles, rows = own_ref[h], own_rows_ref[h]
        for part in parts:
            tiles = tiles + decode(part[h, :body])
            rows = rows + decode_rows(part[h, body:], PART_UNIT)
        return tiles, rows

    home_ref[...], rows_ref[...] = total(side)
    tiles, rows = total(1 - side)
    away_ref[:body], away_ref[body:] = encode(tiles), encode_rows(rows, HALF_UNIT)


def late_sum_kernel(pieces, home_rows_ref, early_away_ref, *refs):
    *parts, home_ref, near_ref, away_ref = refs
    inner = len(parts) // pieces
    pairs, body = home_ref.shape[:2]
    side = lax.div(lax.axis_index("blk"), lax.axis_size("blk") // 2)
    near_rows = encode_rows(home_rows_ref[...], HALF_UNIT)
    away_rows = early_away_ref[-2 * ROWS:]
    for d in range(pairs):
        at = 0
        for piece in range(pieces):
            own, *came = parts[piece * inner:(piece + 1) * inner]
            here = pl.ds(at, own.shape[2])
            at += own.shape[2]
            home, away = own[side, d], own[1 - side, d]
            for part in came:
                home = home + decode(part[side, d])
                away = away + decode(part[1 - side, d])
            home_ref[d, here] = home
            near_ref[d, here] = encode(home)
            away_ref[d, here] = encode(away)
        near_ref[d, body:], away_ref[d, body:] = near_rows, away_rows


def set_scale(ref, rows, which):
    for start, x in sums_of(rows, ref.shape[1], which):
        ref[0:1, start:start + x.shape[1]] = 1.0 / x


def early_end_kernel(
    home_ref, rows_ref, came_ref, after_ref, own_ref, part_ref, code_ref, down_ref, scale_ref
):
    half, panel = part_ref.shape
    body, diagonal = home_ref.shape[0], packed_rows(panel, panel, True)
    rows = rows_ref[...] + decode_rows(came_ref[body:], HALF_UNIT)
    part = home_ref[diagonal:] + decode(came_ref[diagonal:body])
    code_ref[...] = encode(part)
    unpack(part, part_ref)
    unpack(home_ref[:diagonal] + decode(came_ref[:diagonal]), own_ref, True)
    at = 2 * -(-panel // LANES)
    count = rows[at:at + 1, 0:1] * float(BLOCK)
    for which in range(2):
        set_scale(scale_ref.at[which], rows, which)
    down = jnp.broadcast_to(scale_ref[0, 0:1] * count, (panel, panel)).T
    down_ref[...] = down
    own_ref[...] = own_ref[...] * down * scale_ref[0, 0:1]


def last_kernel(
    pairs, own_ref, part_ref, mate_part_ref, down_ref, scale_ref, late_ref, *refs
):
    away, near = refs[:pairs], refs[pairs + 1:2 * pairs + 1]
    across_ref, (out_ref, tiles, scale, turned) = refs[pairs], refs[2 * pairs + 1:]
    steps, panel = tiles.shape[:2]
    half, late = panel // 2, late_ref.shape[1]
    me = lax.axis_index("tm")
    chip, core = lax.div(me, 2), lax.rem(me, 2)
    tiles[me] = own_ref[...]

    @pl.when(core == 0)
    def _():
        tiles[me + 1, :half] = part_ref[...] * down_ref[:half] * scale_ref[1, 0:1]
        unpack(decode(mate_part_ref[...]), tiles.at[me + 1, pl.ds(half, panel - half)])
        tiles[me + 1, half:] = tiles[me + 1, half:] * down_ref[half:] * scale_ref[1, 0:1]

    for d in range(pairs):
        far_chip = lax.bitwise_xor(chip, d + 1)

        @pl.when(chip < far_chip)
        def _():
            rows = decode_rows(near[d][0, late:], HALF_UNIT) + decode_rows(
                away[d][0, late:], HALF_UNIT
            )
            unpack(late_ref[d] + decode(across_ref[d, :late]), turned)
            set_scale(scale, rows, 0)
            tiles[2 * far_chip + core] = turned[...] * down_ref[...] * scale[0:1]
            unpack(decode(near[d][0, :late]) + decode(away[d][0, :late]), turned)
            set_scale(scale, rows, 1)
            tiles[2 * far_chip + 1 - core] = turned[...].T * down_ref[...] * scale[0:1]

    for u in range(steps):

        @pl.when(u >= me)
        def _():
            out_ref[0, :, u * panel:(u + 1) * panel] = tiles[u]

        @pl.when(u < me)
        def _():
            out_ref[0, :, u * panel:(u + 1) * panel] = jnp.zeros((panel, panel), jnp.float32)


def call(kernel, outs, ins, scratch=(), flops=0, in_hbm=0):
    moved = sum(math.prod(x.shape) * x.dtype.itemsize for x in (*outs, *ins))
    many = isinstance(outs, list)
    specs = [SMEM if x.ndim == 1 else VMEM for x in (*ins, *outs)]
    specs[:in_hbm] = [HBM] * in_hbm
    ins = [
        pltpu.with_memory_space_constraint(x, pltpu.HBM) if i < in_hbm else x
        for i, x in enumerate(ins)
    ]
    return pl.pallas_call(
        kernel,
        out_shape=outs if many else outs[0],
        in_specs=specs[:len(ins)],
        out_specs=specs[len(ins):] if many else specs[-1],
        scratch_shapes=scratch,
        compiler_params=pltpu.CompilerParams(vmem_limit_bytes=48 * 2**20),
        cost_estimate=pl.CostEstimate(flops=flops, bytes_accessed=moved, transcendentals=0),
    )(*ins)


def on_device(intensity, block_cycle, cycle_order):
    panel = intensity.shape[0]
    blk_dev = block_cycle.shape[0]
    cycles = cycle_order.shape[0]
    groups = lax.axis_size("blk")
    steps = lax.axis_size("tm")
    inner = groups // 2
    pairs = steps // 2 - 1
    cap = 2 * max(1, blk_dev // cycles)
    early = packed_rows(panel, panel, True) + packed_rows(panel // 2, panel)
    first = panel // LANES * LANES
    pieces = [n for n in (first, panel - first) if n]
    late = [panel * n // LANES for n in pieces]

    def hop(x, by_blk, by_tm, sends=lambda t: True):
        perm = [
            (b * steps + t, (b ^ by_blk) * steps + (t ^ by_tm))
            for b in range(groups)
            for t in range(steps)
            if sends(t)
        ]
        return lax.ppermute(x, ("blk", "tm"), perm)

    offsets = range(1, pairs + 1)
    other = hop(intensity, 0, 1)
    sent = intensity[:first] if len(pieces) > 1 else intensity
    far = [[hop(sent, 0, 2 * d) for d in offsets]]
    f32, i16 = jnp.float32, jnp.int16
    shape = jax.ShapeDtypeStruct
    depth = cap * BLOCK
    work = 2 * cycles * panel * panel * depth
    table, gathers, own_rows, *made = call(
        functools.partial(early_kernel, cap),
        [
            shape((cycles * (cap + 1),), jnp.int32),
            shape((2, inner, 2, panel, depth), jnp.bfloat16),
            shape((2, ROWS, LANES), f32),
            *[shape((n, intensity.shape[1]), jnp.bfloat16) for n in pieces[1:]],
            shape((2, early, LANES), f32),
            *[shape((2, early + 2 * ROWS, LANES), i16)] * (inner - 1),
        ],
        (block_cycle, cycle_order, intensity, other),
        [
            pltpu.SMEM(cycle_order.shape, jnp.int32),
            pltpu.SMEM(block_cycle.shape, jnp.int32),
            pltpu.SMEM(cycle_order.shape, jnp.int32),
            pltpu.VMEM(intensity.shape, jnp.bfloat16),
            pltpu.VMEM((2, -(-cycles // 16) * 16, panel), f32),
            pltpu.SemaphoreType.DMA((3,)),
        ],
        2 * work,
        3,
    )
    far += [[hop(x, 0, 2 * d) for d in offsets] for x in made[:-inner]]

    def exchange(made):
        order = sorted(range(inner), key=lambda k: (k > 0, -k.bit_count()))
        return [hop(made[k], k, 0) if k else made[k] for k in order]

    parts = exchange(made[-inner:])
    home, home_rows, away = call(
        early_sum_kernel,
        [
            shape((early, LANES), f32),
            shape((ROWS, LANES), f32),
            shape((early + 2 * ROWS, LANES), i16),
        ],
        (parts[0], own_rows, *parts[1:]),
    )
    came = hop(away, inner, 0)

    parts, after = [], ()
    for rows, came_rows in zip(late, far):
        made = call(
            functools.partial(late_kernel, cap, len(after)),
            [shape((2, pairs, rows, LANES), i16 if k else f32) for k in range(inner)],
            (table, gathers, *after, *came_rows),
            flops=pairs * work,
        )
        parts += exchange(made)
        after = (away, made[1])
    late_home, near, late_away = call(
        functools.partial(late_sum_kernel, len(pieces)),
        [
            shape((pairs, sum(late), LANES), f32),
            shape((pairs, sum(late) + 2 * ROWS, LANES), i16),
            shape((pairs, sum(late) + 2 * ROWS, LANES), i16),
        ],
        (home_rows, away, *parts),
    )

    def is_lower(t, d):
        return t // 2 < (t // 2 ^ d)

    from_away = [
        hop(late_away[d - 1:d], inner, 2 * d, lambda t, d=d: not is_lower(t, d)) for d in offsets
    ]
    from_near = [hop(near[d - 1:d], 0, 2 * d) for d in offsets]
    across = hop(late_away, inner, 0, lambda t: any(is_lower(t, d) for d in offsets))
    own_tile, part, code, down, scale = call(
        early_end_kernel,
        [
            shape((panel, panel), f32),
            shape((panel // 2, panel), f32),
            shape((packed_rows(panel // 2, panel), LANES), i16),
            shape((panel, panel), f32),
            shape((2, 8, panel), f32),
        ],
        (home, home_rows, came, late_away),
    )
    mate_part = hop(code, 0, 1)
    return call(
        functools.partial(last_kernel, pairs),
        (shape((1, panel, steps * panel), f32),),
        (own_tile, part, mate_part, down, scale, late_home, *from_away, across, *from_near),
        [
            pltpu.VMEM((steps, panel, panel), f32),
            pltpu.VMEM((8, panel), f32),
            pltpu.VMEM((panel, panel), f32),
        ],
    )


def solution(mesh):
    placed = (P("tm", "blk"), P("blk"), P())
    return jax.shard_map(
        on_device, mesh=mesh, in_specs=placed, out_specs=P("blk", "tm", None), check_vma=False
    )
```

```python
import functools
import math

import jax
import jax.numpy as jnp
from jax import lax
from jax.experimental import pallas as pl
from jax.experimental.pallas import tpu as pltpu
from jax.sharding import PartitionSpec as P

BLOCK = 128
LANES = 128
ROWS = 8
NONE = -32768
LEAST, MOST = -3.0, 29.0
PER_OCTAVE = 65534 / (MOST - LEAST)
MIDDLE = (MOST + LEAST) / 2
PART_UNIT, HALF_UNIT = 8192.0, 2048.0
LOW = 1 << 16
VMEM = pl.BlockSpec(memory_space=pltpu.VMEM)
SMEM = pl.BlockSpec(memory_space=pltpu.SMEM)
HBM = pl.BlockSpec(memory_space=pltpu.HBM)


def times(left, right):
    return lax.dot_general(
        left, right, (((1,), (1,)), ((), ())), preferred_element_type=jnp.float32
    )


def encode(x):
    level = jnp.log(jnp.maximum(x, 2.0**LEAST)) * (PER_OCTAVE / math.log(2))
    code = (level + (0.5 - LEAST * PER_OCTAVE)).astype(jnp.int32) + (NONE + 1)
    return jnp.where(x[..., :1, :] > 0, code, NONE).astype(jnp.int16)


def decode(code):
    code = code.astype(jnp.int32)
    level = code.astype(jnp.float32) * (math.log(2) / PER_OCTAVE) + MIDDLE * math.log(2)
    return jnp.where(code[..., :1, :] > NONE, jnp.exp(level), 0.0)


def split(panel):
    whole, rest = divmod(panel, LANES)
    return whole, LANES // rest if rest else 0


def packed_rows(rows, panel, symmetric=False):
    whole, fold = split(panel)
    if symmetric and (whole, fold) == (1, 2):
        return LANES + LANES // 2
    body = sum((i + 1) * LANES if symmetric else rows for i in range(whole))
    return body + (rows // fold if fold else 0)


def pack(tile, symmetric=False):
    rows, panel = tile.shape
    whole, fold = split(panel)
    if symmetric and (whole, fold) == (1, 2):
        n = LANES // 2
        left, right = tile[:, :LANES], tile[:, LANES:]
        parts = [
            left[:n],
            jnp.concatenate([right[:n], left[n:2 * n, n:]], axis=1),
            jnp.concatenate([right[n:2 * n], right[2 * n:]], axis=1),
        ]
        return jnp.concatenate(parts, axis=0)
    parts = [
        tile[: (i + 1) * LANES if symmetric else rows, i * LANES:(i + 1) * LANES]
        for i in range(whole)
    ]
    if fold:
        n = rows // fold
        left = [tile[i * n:(i + 1) * n, whole * LANES:] for i in range(fold)]
        parts.append(jnp.concatenate(left, axis=1))
    return jnp.concatenate(parts, axis=0)


def unpack(x, out, symmetric=False):
    rows, panel = out.shape
    whole, fold = split(panel)
    if symmetric and (whole, fold) == (1, 2):
        n = LANES // 2
        out[:n, :LANES] = x[:n]
        out[:n, LANES:] = x[n:2 * n, :n]
        out[n:2 * n, n:LANES] = x[n:2 * n, n:]
        out[n:2 * n, LANES:] = x[2 * n:, :n]
        out[2 * n:, LANES:] = x[2 * n:, n:]
        out[n:2 * n, :n] = x[:n, n:].T
        out[2 * n:, :LANES] = out[:2 * n, LANES:].T
        return
    at = 0
    for i in range(whole):
        n = (i + 1) * LANES if symmetric else rows
        out[:n, i * LANES:(i + 1) * LANES] = x[at:at + n]
        at += n
    if fold:
        n, width = rows // fold, LANES // fold
        for i in range(fold):
            out[i * n:(i + 1) * n, whole * LANES:] = x[at:, i * width:(i + 1) * width]
    if symmetric:
        for i in range(whole):
            n = (i + 1) * LANES
            if n < panel:
                out[n:, i * LANES:n] = out[i * LANES:n, n:].T


def rows_of(sums, count):
    panel = sums[0].shape[1]
    row = lax.broadcasted_iota(jnp.int32, (ROWS, LANES), 0)
    out, at = jnp.zeros((ROWS, LANES), jnp.float32), 0
    for x in sums:
        for start in range(0, panel, LANES):
            piece = x[:, start:start + LANES]
            if piece.shape[1] < LANES:
                piece = jnp.concatenate([piece] * (LANES // piece.shape[1]), axis=1)
            out = jnp.where(row == at, piece, out)
            at += 1
    return jnp.where(row == at, count, out)


def sums_of(rows, panel, which):
    per = -(-panel // LANES)
    starts = range(0, panel, LANES)
    return [
        (start, rows[which * per + i:which * per + i + 1, :min(LANES, panel - start)])
        for i, start in enumerate(starts)
    ]


def encode_rows(rows, unit):
    whole = (rows * unit + 0.5).astype(jnp.int32)
    high = lax.shift_right_logical(whole, 16)
    low = lax.bitwise_and(whole, LOW - 1) - LOW // 2
    return jnp.concatenate([high, low], axis=0).astype(jnp.int16)


def decode_rows(code, unit):
    x = code.astype(jnp.int32).astype(jnp.float32)
    return (x[:ROWS] * float(LOW) + (x[ROWS:] + LOW / 2)) * (1 / unit)


def find_slots(cap, cycle_ref, order_ref, where_ref, table_ref):
    cycles = order_ref.shape[0]
    for s in range(cycles):
        where_ref[order_ref[s]] = s
        table_ref[s] = 0
    for s in range(cycles * cap):
        table_ref[cycles + s] = 0
    for j in range(cycle_ref.shape[0]):
        p = where_ref[cycle_ref[j]]
        r = table_ref[p]
        table_ref[cycles + p * cap + r] = j
        table_ref[p] = r + 1


def gathered(ref, s, cap, table_ref, masked):
    cycles = table_ref.shape[0] // (cap + 1)
    parts = []
    for r in range(cap):
        j = table_ref[cycles + s * cap + r]
        x = ref[:, pl.ds(pl.multiple_of(j * BLOCK, BLOCK), BLOCK)]
        parts.append(jnp.where(r < table_ref[s], x, jnp.zeros_like(x)) if masked else x)
    return jnp.concatenate(parts, axis=1)


def early_kernel(cap, cycle_hbm, order_hbm, own_hbm, other_ref, *refs):
    table_ref, sorted_ref, rows_ref, *outs = refs[:-6]
    where_ref, cycle_ref, order_ref, own_ref, sums_ref, sems = refs[-6:]
    pairs = ((cycle_hbm, cycle_ref), (order_hbm, order_ref), (own_hbm, own_ref))
    copies = [pltpu.make_async_copy(*pair, sems.at[i]) for i, pair in enumerate(pairs)]
    for copy in copies:
        copy.start()
    copies[0].wait()
    copies[1].wait()
    find_slots(cap, cycle_ref, order_ref, where_ref, table_ref)
    inner = lax.axis_size("blk") // 2
    pieces, outs = outs[:-inner], outs[-inner:]
    panel = own_ref.shape[0]
    half = panel // 2
    mine = lax.rem(lax.axis_index("blk"), inner)
    first = lax.rem(lax.axis_index("tm"), 2) == 0
    body = outs[0].shape[1]
    row = lax.broadcasted_iota(jnp.int32, (sums_ref.shape[1], BLOCK), 0)
    members = jnp.concatenate(
        [
            jnp.where(row == where_ref[cycle_ref[j]], 1.0, 0.0).astype(jnp.bfloat16)
            for j in range(cycle_ref.shape[0])
        ],
        axis=1,
    )
    each = [(k, h, h * inner + lax.bitwise_xor(mine, k)) for k in range(inner) for h in range(2)]
    for k, h, s in each:
        sorted_ref[1, k, h] = gathered(other_ref, s, cap, table_ref, True)
    sums_ref[1] = times(members, other_ref[...])
    copies[2].wait()
    for piece in pieces:
        piece[...] = own_ref[panel - piece.shape[0]:]
    sums_ref[0] = times(members, own_ref[...])
    for k, h, s in each:
        own, other = gathered(own_ref, s, cap, table_ref, True), sorted_ref[1, k, h]
        sorted_ref[0, k, h] = own
        left = jnp.where(first, own[:half], other[half:])
        right = jnp.where(first, other, own)
        rows = rows_of([sums_ref[i, pl.ds(s, 1)] for i in range(2)], table_ref[s].astype(jnp.float32))
        found = jnp.concatenate([pack(times(own, own), True), pack(times(left, right))], axis=0)
        if k:
            outs[k][h, :body] = encode(found)
            outs[k][h, body:] = encode_rows(rows, PART_UNIT)
        else:
            outs[k][h] = found
            rows_ref[h] = rows


def late_kernel(cap, after, table_ref, sorted_ref, *refs):
    refs = refs[after:]
    inner = lax.axis_size("blk") // 2
    came, outs = refs[:-inner], refs[-inner:]
    mine = lax.rem(lax.axis_index("blk"), inner)
    chip = lax.div(lax.axis_index("tm"), 2)
    for k in range(inner):
        for h in range(2):
            s = h * inner + lax.bitwise_xor(mine, k)
            for d, ref in enumerate(came):
                upper = (chip > lax.bitwise_xor(chip, d + 1)).astype(jnp.int32)
                far = gathered(ref, s, cap, table_ref, False)
                tile = pack(times(sorted_ref[upper, k, h], far))
                outs[k][h, d] = encode(tile) if k else tile


def early_sum_kernel(own_ref, own_rows_ref, *refs):
    *parts, home_ref, rows_ref, away_ref = refs
    body = home_ref.shape[0]
    side = lax.div(lax.axis_index("blk"), lax.axis_size("blk") // 2)

    def total(h):
        tiles, rows = own_ref[h], own_rows_ref[h]
        for part in parts:
            tiles = tiles + decode(part[h, :body])
            rows = rows + decode_rows(part[h, body:], PART_UNIT)
        return tiles, rows

    home_ref[...], rows_ref[...] = total(side)
    tiles, rows = total(1 - side)
    away_ref[:body], away_ref[body:] = encode(tiles), encode_rows(rows, HALF_UNIT)


def late_sum_kernel(pieces, home_rows_ref, early_away_ref, *refs):
    *parts, home_ref, near_ref, away_ref = refs
    inner = len(parts) // pieces
    pairs, body = home_ref.shape[:2]
    side = lax.div(lax.axis_index("blk"), lax.axis_size("blk") // 2)
    near_rows = encode_rows(home_rows_ref[...], HALF_UNIT)
    away_rows = early_away_ref[-2 * ROWS:]
    for d in range(pairs):
        at = 0
        for piece in range(pieces):
            own, *came = parts[piece * inner:(piece + 1) * inner]
            here = pl.ds(at, own.shape[2])
            at += own.shape[2]
            home, away = own[side, d], own[1 - side, d]
            for part in came:
                home = home + decode(part[side, d])
                away = away + decode(part[1 - side, d])
            home_ref[d, here] = home
            near_ref[d, here] = encode(home)
            away_ref[d, here] = encode(away)
        near_ref[d, body:], away_ref[d, body:] = near_rows, away_rows


def set_scale(ref, rows, which):
    for start, x in sums_of(rows, ref.shape[1], which):
        ref[0:1, start:start + x.shape[1]] = 1.0 / x


def early_end_kernel(
    home_ref, rows_ref, came_ref, after_ref, own_ref, part_ref, code_ref, down_ref, scale_ref
):
    half, panel = part_ref.shape
    body, diagonal = home_ref.shape[0], packed_rows(panel, panel, True)
    rows = rows_ref[...] + decode_rows(came_ref[body:], HALF_UNIT)
    part = home_ref[diagonal:] + decode(came_ref[diagonal:body])
    code_ref[...] = encode(part)
    unpack(part, part_ref)
    unpack(home_ref[:diagonal] + decode(came_ref[:diagonal]), own_ref, True)
    at = 2 * -(-panel // LANES)
    count = rows[at:at + 1, 0:1] * float(BLOCK)
    for which in range(2):
        set_scale(scale_ref.at[which], rows, which)
    down = jnp.broadcast_to(scale_ref[0, 0:1] * count, (panel, panel)).T
    down_ref[...] = down


def middle_kernel(pairs, own_ref, part_ref, mate_part_ref, down_ref, late_ref, *refs):
    away, across_ref, tiles, turned = refs[:pairs], *refs[pairs:]
    panel = down_ref.shape[0]
    half, late = panel // 2, late_ref.shape[1]
    me = lax.axis_index("tm")
    chip, core = lax.div(me, 2), lax.rem(me, 2)
    down = down_ref[...]
    tiles[...] = jnp.zeros_like(tiles)
    tiles[me] = own_ref[...] * down

    @pl.when(core == 0)
    def _():
        mate = tiles.at[me + 1]
        unpack(decode(mate_part_ref[...]), mate.at[pl.ds(half, panel - half)])
        mate[:half] = part_ref[...] * down[:half]
        mate[half:] = mate[half:] * down[half:]

    for d in range(pairs):
        far_chip = lax.bitwise_xor(chip, d + 1)

        @pl.when(chip < far_chip)
        def _():
            unpack(late_ref[d] + decode(across_ref[d, :late]), turned)
            tiles[2 * far_chip + core] = turned[...] * down
            unpack(decode(away[d][0, :late]), turned)
            tiles[2 * far_chip + 1 - core] = turned[...].T * down


def last_kernel(pairs, tiles, down_ref, scale_ref, *refs):
    near, away = refs[:pairs], refs[pairs:2 * pairs]
    out_ref, scales, more, turned = refs[2 * pairs:]
    steps, panel = tiles.shape[:2]
    me = lax.axis_index("tm")
    chip, core = lax.div(me, 2), lax.rem(me, 2)
    scales[...] = jnp.ones_like(scales)
    scales[me] = scale_ref[0]

    @pl.when(core == 0)
    def _():
        scales[me + 1] = scale_ref[1]

    more[...] = jnp.zeros_like(more)
    for d in range(pairs):
        far_chip = lax.bitwise_xor(chip, d + 1)
        late = near[d].shape[1] - 2 * ROWS

        @pl.when(chip < far_chip)
        def _():
            rows = decode_rows(near[d][0, late:], HALF_UNIT) + decode_rows(
                away[d][0, late:], HALF_UNIT
            )
            straight, crossed = 2 * far_chip + core, 2 * far_chip + 1 - core
            set_scale(scales.at[straight], rows, 0)
            set_scale(scales.at[crossed], rows, 1)
            unpack(decode(near[d][0, :late]), turned)
            more[crossed] = turned[...].T * down_ref[...]

    for u in range(steps):
        out_ref[0, :, u * panel:(u + 1) * panel] = (tiles[u] + more[u]) * scales[u, 0:1]


def call(kernel, outs, ins, scratch=(), flops=0, in_hbm=0):
    moved = sum(math.prod(x.shape) * x.dtype.itemsize for x in (*outs, *ins))
    many = isinstance(outs, list)
    specs = [SMEM if x.ndim == 1 else VMEM for x in (*ins, *outs)]
    specs[:in_hbm] = [HBM] * in_hbm
    ins = [
        pltpu.with_memory_space_constraint(x, pltpu.HBM) if i < in_hbm else x
        for i, x in enumerate(ins)
    ]
    return pl.pallas_call(
        kernel,
        out_shape=outs if many else outs[0],
        in_specs=specs[:len(ins)],
        out_specs=specs[len(ins):] if many else specs[-1],
        scratch_shapes=scratch,
        compiler_params=pltpu.CompilerParams(vmem_limit_bytes=48 * 2**20),
        cost_estimate=pl.CostEstimate(flops=flops, bytes_accessed=moved, transcendentals=0),
    )(*ins)


def on_device(intensity, block_cycle, cycle_order):
    panel = intensity.shape[0]
    blk_dev = block_cycle.shape[0]
    cycles = cycle_order.shape[0]
    groups = lax.axis_size("blk")
    steps = lax.axis_size("tm")
    inner = groups // 2
    pairs = steps // 2 - 1
    cap = 2 * max(1, blk_dev // cycles)
    early = packed_rows(panel, panel, True) + packed_rows(panel // 2, panel)
    first = panel // LANES * LANES
    pieces = [n for n in (first, panel - first) if n]
    late = [panel * n // LANES for n in pieces]

    def hop(x, by_blk, by_tm, sends=lambda t: True):
        perm = [
            (b * steps + t, (b ^ by_blk) * steps + (t ^ by_tm))
            for b in range(groups)
            for t in range(steps)
            if sends(t)
        ]
        return lax.ppermute(x, ("blk", "tm"), perm)

    offsets = range(1, pairs + 1)
    other = hop(intensity, 0, 1)
    sent = intensity[:first] if len(pieces) > 1 else intensity
    far = [[hop(sent, 0, 2 * d) for d in offsets]]
    f32, i16 = jnp.float32, jnp.int16
    shape = jax.ShapeDtypeStruct
    depth = cap * BLOCK
    work = 2 * cycles * panel * panel * depth
    table, gathers, own_rows, *made = call(
        functools.partial(early_kernel, cap),
        [
            shape((cycles * (cap + 1),), jnp.int32),
            shape((2, inner, 2, panel, depth), jnp.bfloat16),
            shape((2, ROWS, LANES), f32),
            *[shape((n, intensity.shape[1]), jnp.bfloat16) for n in pieces[1:]],
            shape((2, early, LANES), f32),
            *[shape((2, early + 2 * ROWS, LANES), i16)] * (inner - 1),
        ],
        (block_cycle, cycle_order, intensity, other),
        [
            pltpu.SMEM(cycle_order.shape, jnp.int32),
            pltpu.SMEM(block_cycle.shape, jnp.int32),
            pltpu.SMEM(cycle_order.shape, jnp.int32),
            pltpu.VMEM(intensity.shape, jnp.bfloat16),
            pltpu.VMEM((2, -(-cycles // 16) * 16, panel), f32),
            pltpu.SemaphoreType.DMA((3,)),
        ],
        2 * work,
        3,
    )
    far += [[hop(x, 0, 2 * d) for d in offsets] for x in made[:-inner]]

    def exchange(made):
        order = sorted(range(inner), key=lambda k: (k > 0, -k.bit_count()))
        return [hop(made[k], k, 0) if k else made[k] for k in order]

    parts = exchange(made[-inner:])
    home, home_rows, away = call(
        early_sum_kernel,
        [
            shape((early, LANES), f32),
            shape((ROWS, LANES), f32),
            shape((early + 2 * ROWS, LANES), i16),
        ],
        (parts[0], own_rows, *parts[1:]),
    )
    came = hop(away, inner, 0)

    parts, after = [], ()
    for rows, came_rows in zip(late, far):
        made = call(
            functools.partial(late_kernel, cap, len(after)),
            [shape((2, pairs, rows, LANES), i16 if k else f32) for k in range(inner)],
            (table, gathers, *after, *came_rows),
            flops=pairs * work,
        )
        parts += exchange(made)
        after = (away, made[1])
    late_home, near, late_away = call(
        functools.partial(late_sum_kernel, len(pieces)),
        [
            shape((pairs, sum(late), LANES), f32),
            shape((pairs, sum(late) + 2 * ROWS, LANES), i16),
            shape((pairs, sum(late) + 2 * ROWS, LANES), i16),
        ],
        (home_rows, away, *parts),
    )

    def is_lower(t, d):
        return t // 2 < (t // 2 ^ d)

    from_away = [
        hop(late_away[d - 1:d], inner, 2 * d, lambda t, d=d: not is_lower(t, d)) for d in offsets
    ]
    from_near = [hop(near[d - 1:d], 0, 2 * d) for d in offsets]
    across = hop(late_away, inner, 0, lambda t: any(is_lower(t, d) for d in offsets))
    own_tile, part, code, down, scale = call(
        early_end_kernel,
        [
            shape((panel, panel), f32),
            shape((panel // 2, panel), f32),
            shape((packed_rows(panel // 2, panel), LANES), i16),
            shape((panel, panel), f32),
            shape((2, 8, panel), f32),
        ],
        (home, home_rows, came, late_away),
    )
    mate_part = hop(code, 0, 1)
    tiles = call(
        functools.partial(middle_kernel, pairs),
        (shape((steps, panel, panel), f32),),
        (own_tile, part, mate_part, down, late_home, *from_away, across),
        [pltpu.VMEM((panel, panel), f32)],
    )
    return call(
        functools.partial(last_kernel, pairs),
        (shape((1, panel, steps * panel), f32),),
        (tiles, down, scale, *from_near, *from_away),
        [
            pltpu.VMEM((steps, 8, panel), f32),
            pltpu.VMEM((steps, panel, panel), f32),
            pltpu.VMEM((panel, panel), f32),
        ],
    )


def solution(mesh):
    placed = (P("tm", "blk"), P("blk"), P())
    return jax.shard_map(
        on_device, mesh=mesh, in_specs=placed, out_specs=P("blk", "tm", None), check_vma=False
    )
```

```python
import functools
import math

import jax
import jax.numpy as jnp
from jax import lax
from jax.experimental import pallas as pl
from jax.experimental.pallas import tpu as pltpu
from jax.sharding import PartitionSpec as P

BLOCK = 128
LANES = 128
ROWS = 8
NONE = -32768
LEAST, MOST = -3.0, 29.0
PER_OCTAVE = 65534 / (MOST - LEAST)
MIDDLE = (MOST + LEAST) / 2
PART_UNIT, HALF_UNIT = 8192.0, 2048.0
LOW = 1 << 16
VMEM = pl.BlockSpec(memory_space=pltpu.VMEM)
SMEM = pl.BlockSpec(memory_space=pltpu.SMEM)
HBM = pl.BlockSpec(memory_space=pltpu.HBM)


def times(left, right):
    return lax.dot_general(
        left, right, (((1,), (1,)), ((), ())), preferred_element_type=jnp.float32
    )


def encode(x):
    level = jnp.log(jnp.maximum(x, 2.0**LEAST)) * (PER_OCTAVE / math.log(2))
    code = (level + (0.5 - LEAST * PER_OCTAVE)).astype(jnp.int32) + (NONE + 1)
    return jnp.where(x[..., :1, :] > 0, code, NONE).astype(jnp.int16)


def decode(code):
    code = code.astype(jnp.int32)
    level = code.astype(jnp.float32) * (math.log(2) / PER_OCTAVE) + MIDDLE * math.log(2)
    return jnp.where(code[..., :1, :] > NONE, jnp.exp(level), 0.0)


def split(panel):
    whole, rest = divmod(panel, LANES)
    return whole, LANES // rest if rest else 0


def packed_rows(rows, panel, symmetric=False):
    whole, fold = split(panel)
    if symmetric and (whole, fold) == (1, 2):
        return LANES + LANES // 2
    body = sum((i + 1) * LANES if symmetric else rows for i in range(whole))
    return body + (rows // fold if fold else 0)


def pack(tile, symmetric=False):
    rows, panel = tile.shape
    whole, fold = split(panel)
    if symmetric and (whole, fold) == (1, 2):
        n = LANES // 2
        left, right = tile[:, :LANES], tile[:, LANES:]
        parts = [
            left[:n],
            jnp.concatenate([right[:n], left[n:2 * n, n:]], axis=1),
            jnp.concatenate([right[n:2 * n], right[2 * n:]], axis=1),
        ]
        return jnp.concatenate(parts, axis=0)
    parts = [
        tile[: (i + 1) * LANES if symmetric else rows, i * LANES:(i + 1) * LANES]
        for i in range(whole)
    ]
    if fold:
        n = rows // fold
        left = [tile[i * n:(i + 1) * n, whole * LANES:] for i in range(fold)]
        parts.append(jnp.concatenate(left, axis=1))
    return jnp.concatenate(parts, axis=0)


def unpack(x, out, symmetric=False):
    rows, panel = out.shape
    whole, fold = split(panel)
    if symmetric and (whole, fold) == (1, 2):
        n = LANES // 2
        out[:n, :LANES] = x[:n]
        out[:n, LANES:] = x[n:2 * n, :n]
        out[n:2 * n, n:LANES] = x[n:2 * n, n:]
        out[n:2 * n, LANES:] = x[2 * n:, :n]
        out[2 * n:, LANES:] = x[2 * n:, n:]
        out[n:2 * n, :n] = x[:n, n:].T
        out[2 * n:, :LANES] = out[:2 * n, LANES:].T
        return
    at = 0
    for i in range(whole):
        n = (i + 1) * LANES if symmetric else rows
        out[:n, i * LANES:(i + 1) * LANES] = x[at:at + n]
        at += n
    if fold:
        n, width = rows // fold, LANES // fold
        for i in range(fold):
            out[i * n:(i + 1) * n, whole * LANES:] = x[at:, i * width:(i + 1) * width]
    if symmetric:
        for i in range(whole):
            n = (i + 1) * LANES
            if n < panel:
                out[n:, i * LANES:n] = out[i * LANES:n, n:].T


def rows_of(sums, count):
    panel = sums[0].shape[1]
    row = lax.broadcasted_iota(jnp.int32, (ROWS, LANES), 0)
    out, at = jnp.zeros((ROWS, LANES), jnp.float32), 0
    for x in sums:
        for start in range(0, panel, LANES):
            piece = x[:, start:start + LANES]
            if piece.shape[1] < LANES:
                piece = jnp.concatenate([piece] * (LANES // piece.shape[1]), axis=1)
            out = jnp.where(row == at, piece, out)
            at += 1
    return jnp.where(row == at, count, out)


def sums_of(rows, panel, which):
    per = -(-panel // LANES)
    starts = range(0, panel, LANES)
    return [
        (start, rows[which * per + i:which * per + i + 1, :min(LANES, panel - start)])
        for i, start in enumerate(starts)
    ]


def encode_rows(rows, unit):
    whole = (rows * unit + 0.5).astype(jnp.int32)
    high = lax.shift_right_logical(whole, 16)
    low = lax.bitwise_and(whole, LOW - 1) - LOW // 2
    return jnp.concatenate([high, low], axis=0).astype(jnp.int16)


def decode_rows(code, unit):
    x = code.astype(jnp.int32).astype(jnp.float32)
    return (x[:ROWS] * float(LOW) + (x[ROWS:] + LOW / 2)) * (1 / unit)


def find_slots(cap, cycle_ref, order_ref, where_ref, table_ref):
    cycles = order_ref.shape[0]
    for s in range(cycles):
        where_ref[order_ref[s]] = s
        table_ref[s] = 0
    for s in range(cycles * cap):
        table_ref[cycles + s] = 0
    for j in range(cycle_ref.shape[0]):
        p = where_ref[cycle_ref[j]]
        r = table_ref[p]
        table_ref[cycles + p * cap + r] = j
        table_ref[p] = r + 1


def gathered(ref, s, cap, table_ref, masked):
    cycles = table_ref.shape[0] // (cap + 1)
    parts = []
    for r in range(cap):
        j = table_ref[cycles + s * cap + r]
        x = ref[:, pl.ds(pl.multiple_of(j * BLOCK, BLOCK), BLOCK)]
        parts.append(jnp.where(r < table_ref[s], x, jnp.zeros_like(x)) if masked else x)
    return jnp.concatenate(parts, axis=1)


def early_kernel(cap, cycle_hbm, order_hbm, own_hbm, other_ref, *refs):
    table_ref, sorted_ref, rows_ref, *outs = refs[:-6]
    where_ref, cycle_ref, order_ref, own_ref, sums_ref, sems = refs[-6:]
    pairs = ((cycle_hbm, cycle_ref), (order_hbm, order_ref), (own_hbm, own_ref))
    copies = [pltpu.make_async_copy(*pair, sems.at[i]) for i, pair in enumerate(pairs)]
    for copy in copies:
        copy.start()
    copies[0].wait()
    copies[1].wait()
    find_slots(cap, cycle_ref, order_ref, where_ref, table_ref)
    inner = lax.axis_size("blk") // 2
    pieces, outs = outs[:-inner], outs[-inner:]
    panel = own_ref.shape[0]
    half = panel // 2
    mine = lax.rem(lax.axis_index("blk"), inner)
    first = lax.rem(lax.axis_index("tm"), 2) == 0
    body = outs[0].shape[1]
    row = lax.broadcasted_iota(jnp.int32, (sums_ref.shape[1], BLOCK), 0)
    members = jnp.concatenate(
        [
            jnp.where(row == where_ref[cycle_ref[j]], 1.0, 0.0).astype(jnp.bfloat16)
            for j in range(cycle_ref.shape[0])
        ],
        axis=1,
    )
    each = [(k, h, h * inner + lax.bitwise_xor(mine, k)) for k in range(inner) for h in range(2)]
    for k, h, s in each:
        sorted_ref[1, k, h] = gathered(other_ref, s, cap, table_ref, True)
    sums_ref[1] = times(members, other_ref[...])
    copies[2].wait()
    for piece in pieces:
        piece[...] = own_ref[panel - piece.shape[0]:]
    sums_ref[0] = times(members, own_ref[...])
    for k, h, s in each:
        own, other = gathered(own_ref, s, cap, table_ref, True), sorted_ref[1, k, h]
        sorted_ref[0, k, h] = own
        left = jnp.where(first, own[:half], other[half:])
        right = jnp.where(first, other, own)
        rows = rows_of([sums_ref[i, pl.ds(s, 1)] for i in range(2)], table_ref[s].astype(jnp.float32))
        found = jnp.concatenate([pack(times(own, own), True), pack(times(left, right))], axis=0)
        if k:
            outs[k][h, :body] = encode(found)
            outs[k][h, body:] = encode_rows(rows, PART_UNIT)
        else:
            outs[k][h] = found
            rows_ref[h] = rows


def late_kernel(cap, after, table_ref, sorted_ref, *refs):
    refs = refs[after:]
    inner = lax.axis_size("blk") // 2
    came, outs = refs[:-inner], refs[-inner:]
    mine = lax.rem(lax.axis_index("blk"), inner)
    chip = lax.div(lax.axis_index("tm"), 2)
    for k in range(inner):
        for h in range(2):
            s = h * inner + lax.bitwise_xor(mine, k)
            for d, ref in enumerate(came):
                upper = (chip > lax.bitwise_xor(chip, d + 1)).astype(jnp.int32)
                far = gathered(ref, s, cap, table_ref, False)
                tile = pack(times(sorted_ref[upper, k, h], far))
                outs[k][h, d] = encode(tile) if k else tile


def early_sum_kernel(own_ref, own_rows_ref, *refs):
    *parts, home_ref, rows_ref, away_ref = refs
    body = home_ref.shape[0]
    side = lax.div(lax.axis_index("blk"), lax.axis_size("blk") // 2)

    def total(h):
        tiles, rows = own_ref[h], own_rows_ref[h]
        for part in parts:
            tiles = tiles + decode(part[h, :body])
            rows = rows + decode_rows(part[h, body:], PART_UNIT)
        return tiles, rows

    home_ref[...], rows_ref[...] = total(side)
    tiles, rows = total(1 - side)
    away_ref[:body], away_ref[body:] = encode(tiles), encode_rows(rows, HALF_UNIT)


def late_sum_kernel(pieces, home_rows_ref, early_away_ref, *refs):
    *parts, home_ref, near_ref, away_ref = refs
    inner = len(parts) // pieces
    pairs, body = home_ref.shape[:2]
    side = lax.div(lax.axis_index("blk"), lax.axis_size("blk") // 2)
    near_rows = encode_rows(home_rows_ref[...], HALF_UNIT)
    away_rows = early_away_ref[-2 * ROWS:]
    for d in range(pairs):
        at = 0
        for piece in range(pieces):
            own, *came = parts[piece * inner:(piece + 1) * inner]
            here = pl.ds(at, own.shape[2])
            at += own.shape[2]
            home, away = own[side, d], own[1 - side, d]
            for part in came:
                home = home + decode(part[side, d])
                away = away + decode(part[1 - side, d])
            home_ref[d, here] = home
            near_ref[d, here] = encode(home)
            away_ref[d, here] = encode(away)
        near_ref[d, body:], away_ref[d, body:] = near_rows, away_rows


def set_scale(ref, rows, which):
    for start, x in sums_of(rows, ref.shape[1], which):
        ref[0:1, start:start + x.shape[1]] = 1.0 / x


def early_end_kernel(
    home_ref, rows_ref, came_ref, after_ref, own_ref, part_ref, code_ref, down_ref, scale_ref
):
    half, panel = part_ref.shape
    body, diagonal = home_ref.shape[0], packed_rows(panel, panel, True)
    rows = rows_ref[...] + decode_rows(came_ref[body:], HALF_UNIT)
    part = home_ref[diagonal:] + decode(came_ref[diagonal:body])
    code_ref[...] = encode(part)
    unpack(part, part_ref)
    unpack(home_ref[:diagonal] + decode(came_ref[:diagonal]), own_ref, True)
    at = 2 * -(-panel // LANES)
    count = rows[at:at + 1, 0:1] * float(BLOCK)
    for which in range(2):
        set_scale(scale_ref.at[which], rows, which)
    down = jnp.broadcast_to(scale_ref[0, 0:1] * count, (panel, panel)).T
    down_ref[...] = down


def middle_kernel(pairs, own_ref, part_ref, mate_part_ref, down_ref, late_ref, *refs):
    away, across_ref, scale_ref, tiles, out_ref, turned, ready, sem = refs[:pairs], *refs[pairs:]
    panel = down_ref.shape[0]
    half, late = panel // 2, late_ref.shape[1]
    me = lax.axis_index("tm")
    chip, core = lax.div(me, 2), lax.rem(me, 2)
    down = down_ref[...]
    tiles[...] = jnp.zeros_like(tiles)
    tiles[me] = own_ref[...] * down

    @pl.when(core == 0)
    def _():
        mate = tiles.at[me + 1]
        unpack(decode(mate_part_ref[...]), mate.at[pl.ds(half, panel - half)])
        mate[:half] = part_ref[...] * down[:half]
        mate[half:] = mate[half:] * down[half:]

    first = pltpu.make_async_copy(ready, out_ref.at[0, :, pl.ds(0, 2 * panel)], sem)
    ready[...] = jnp.zeros_like(ready)

    @pl.when(chip == 0)
    def _():
        for u in range(2):

            @pl.when(u >= core)
            def _():
                column = jnp.where(u == core, scale_ref[0, 0:1], scale_ref[1, 0:1])
                ready[:, u * panel:(u + 1) * panel] = tiles[u] * column

    first.start()
    for d in range(pairs):
        far_chip = lax.bitwise_xor(chip, d + 1)

        @pl.when(chip < far_chip)
        def _():
            unpack(late_ref[d] + decode(across_ref[d, :late]), turned)
            tiles[2 * far_chip + core] = turned[...] * down
            unpack(decode(away[d][0, :late]), turned)
            tiles[2 * far_chip + 1 - core] = turned[...].T * down

    first.wait()


def last_kernel(pairs, tiles, down_ref, scale_ref, begun_ref, *refs):
    near, away = refs[:pairs], refs[pairs:2 * pairs]
    out_ref, scales, more, turned, ready, sems = refs[2 * pairs:]
    steps, panel = tiles.shape[:2]
    me = lax.axis_index("tm")
    chip, core = lax.div(me, 2), lax.rem(me, 2)
    scales[...] = jnp.ones_like(scales)
    scales[me] = scale_ref[0]

    @pl.when(core == 0)
    def _():
        scales[me + 1] = scale_ref[1]

    more[...] = jnp.zeros_like(more)
    for d in range(pairs):
        far_chip = lax.bitwise_xor(chip, d + 1)
        late = near[d].shape[1] - 2 * ROWS

        @pl.when(chip < far_chip)
        def _():
            rows = decode_rows(near[d][0, late:], HALF_UNIT) + decode_rows(
                away[d][0, late:], HALF_UNIT
            )
            straight, crossed = 2 * far_chip + core, 2 * far_chip + 1 - core
            set_scale(scales.at[straight], rows, 0)
            set_scale(scales.at[crossed], rows, 1)
            unpack(decode(near[d][0, :late]), turned)
            more[crossed] = turned[...].T * down_ref[...]

    copies = []
    for i, rows in enumerate((pl.ds(0, panel // 2), pl.ds(panel // 2, panel - panel // 2))):
        for u in range(2, steps):
            tile = (tiles[u, rows] + more[u, rows]) * scales[u, 0:1]
            ready[rows, (u - 2) * panel:(u - 1) * panel] = tile
        there = out_ref.at[0, rows, pl.ds(2 * panel, (steps - 2) * panel)]
        copies.append(pltpu.make_async_copy(ready.at[rows], there, sems.at[i]))
        copies[-1].start()
    for copy in copies:
        copy.wait()


def call(kernel, outs, ins, scratch=(), flops=0, in_hbm=0, out_hbm=0, goes_on=None):
    moved = sum(math.prod(x.shape) * x.dtype.itemsize for x in (*outs, *ins))
    many = isinstance(outs, list)
    specs = [SMEM if x.ndim == 1 else VMEM for x in (*ins, *outs)]
    specs[:in_hbm] = [HBM] * in_hbm
    specs[len(specs) - out_hbm:] = [HBM] * out_hbm
    if goes_on is not None:
        specs[goes_on] = HBM
    ins = [
        pltpu.with_memory_space_constraint(x, pltpu.HBM) if i < in_hbm else x
        for i, x in enumerate(ins)
    ]
    return pl.pallas_call(
        kernel,
        out_shape=outs if many else outs[0],
        in_specs=specs[:len(ins)],
        out_specs=specs[len(ins):] if many else specs[-1],
        scratch_shapes=scratch,
        input_output_aliases={} if goes_on is None else {goes_on: len(outs) - 1},
        compiler_params=pltpu.CompilerParams(vmem_limit_bytes=48 * 2**20),
        cost_estimate=pl.CostEstimate(flops=flops, bytes_accessed=moved, transcendentals=0),
    )(*ins)


def on_device(intensity, block_cycle, cycle_order):
    panel = intensity.shape[0]
    blk_dev = block_cycle.shape[0]
    cycles = cycle_order.shape[0]
    groups = lax.axis_size("blk")
    steps = lax.axis_size("tm")
    inner = groups // 2
    pairs = steps // 2 - 1
    cap = 2 * max(1, blk_dev // cycles)
    early = packed_rows(panel, panel, True) + packed_rows(panel // 2, panel)
    first = panel // LANES * LANES
    pieces = [n for n in (first, panel - first) if n]
    late = [panel * n // LANES for n in pieces]

    def hop(x, by_blk, by_tm, sends=lambda t: True):
        perm = [
            (b * steps + t, (b ^ by_blk) * steps + (t ^ by_tm))
            for b in range(groups)
            for t in range(steps)
            if sends(t)
        ]
        return lax.ppermute(x, ("blk", "tm"), perm)

    offsets = range(1, pairs + 1)
    other = hop(intensity, 0, 1)
    sent = intensity[:first] if len(pieces) > 1 else intensity
    far = [[hop(sent, 0, 2 * d) for d in offsets]]
    f32, i16 = jnp.float32, jnp.int16
    shape = jax.ShapeDtypeStruct
    depth = cap * BLOCK
    work = 2 * cycles * panel * panel * depth
    table, gathers, own_rows, *made = call(
        functools.partial(early_kernel, cap),
        [
            shape((cycles * (cap + 1),), jnp.int32),
            shape((2, inner, 2, panel, depth), jnp.bfloat16),
            shape((2, ROWS, LANES), f32),
            *[shape((n, intensity.shape[1]), jnp.bfloat16) for n in pieces[1:]],
            shape((2, early, LANES), f32),
            *[shape((2, early + 2 * ROWS, LANES), i16)] * (inner - 1),
        ],
        (block_cycle, cycle_order, intensity, other),
        [
            pltpu.SMEM(cycle_order.shape, jnp.int32),
            pltpu.SMEM(block_cycle.shape, jnp.int32),
            pltpu.SMEM(cycle_order.shape, jnp.int32),
            pltpu.VMEM(intensity.shape, jnp.bfloat16),
            pltpu.VMEM((2, -(-cycles // 16) * 16, panel), f32),
            pltpu.SemaphoreType.DMA((3,)),
        ],
        2 * work,
        3,
    )
    far += [[hop(x, 0, 2 * d) for d in offsets] for x in made[:-inner]]

    def exchange(made):
        order = sorted(range(inner), key=lambda k: (k > 0, -k.bit_count()))
        return [hop(made[k], k, 0) if k else made[k] for k in order]

    parts = exchange(made[-inner:])
    home, home_rows, away = call(
        early_sum_kernel,
        [
            shape((early, LANES), f32),
            shape((ROWS, LANES), f32),
            shape((early + 2 * ROWS, LANES), i16),
        ],
        (parts[0], own_rows, *parts[1:]),
    )
    came = hop(away, inner, 0)

    parts, after = [], ()
    for rows, came_rows in zip(late, far):
        made = call(
            functools.partial(late_kernel, cap, len(after)),
            [shape((2, pairs, rows, LANES), i16 if k else f32) for k in range(inner)],
            (table, gathers, *after, *came_rows),
            flops=pairs * work,
        )
        parts += exchange(made)
        after = (away, made[1])
    late_home, near, late_away = call(
        functools.partial(late_sum_kernel, len(pieces)),
        [
            shape((pairs, sum(late), LANES), f32),
            shape((pairs, sum(late) + 2 * ROWS, LANES), i16),
            shape((pairs, sum(late) + 2 * ROWS, LANES), i16),
        ],
        (home_rows, away, *parts),
    )

    def is_lower(t, d):
        return t // 2 < (t // 2 ^ d)

    from_away = [
        hop(late_away[d - 1:d], inner, 2 * d, lambda t, d=d: not is_lower(t, d)) for d in offsets
    ]
    from_near = [hop(near[d - 1:d], 0, 2 * d) for d in offsets]
    across = hop(late_away, inner, 0, lambda t: any(is_lower(t, d) for d in offsets))
    own_tile, part, code, down, scale = call(
        early_end_kernel,
        [
            shape((panel, panel), f32),
            shape((panel // 2, panel), f32),
            shape((packed_rows(panel // 2, panel), LANES), i16),
            shape((panel, panel), f32),
            shape((2, 8, panel), f32),
        ],
        (home, home_rows, came, late_away),
    )
    mate_part = hop(code, 0, 1)
    whole = shape((1, panel, steps * panel), f32)
    tiles, begun = call(
        functools.partial(middle_kernel, pairs),
        [shape((steps, panel, panel), f32), whole],
        (own_tile, part, mate_part, down, late_home, *from_away, across, scale),
        [
            pltpu.VMEM((panel, panel), f32),
            pltpu.VMEM((panel, 2 * panel), f32),
            pltpu.SemaphoreType.DMA,
        ],
        out_hbm=1,
    )
    return call(
        functools.partial(last_kernel, pairs),
        (whole,),
        (tiles, down, scale, begun, *from_near, *from_away),
        [
            pltpu.VMEM((steps, 8, panel), f32),
            pltpu.VMEM((steps, panel, panel), f32),
            pltpu.VMEM((panel, panel), f32),
            pltpu.VMEM((panel, (steps - 2) * panel), f32),
            pltpu.SemaphoreType.DMA((2,)),
        ],
        out_hbm=1,
        goes_on=3,
    )


def solution(mesh):
    placed = (P("tm", "blk"), P("blk"), P())
    return jax.shard_map(
        on_device, mesh=mesh, in_specs=placed, out_specs=P("blk", "tm", None), check_vma=False
    )
```

```python
import functools
import math

import jax
import jax.numpy as jnp
from jax import lax
from jax.experimental import pallas as pl
from jax.experimental.pallas import tpu as pltpu
from jax.sharding import PartitionSpec as P

BLOCK = 128
LANES = 128
ROWS = 8
NONE = -32768
LEAST, MOST = -3.0, 29.0
PER_OCTAVE = 65534 / (MOST - LEAST)
MIDDLE = (MOST + LEAST) / 2
PART_UNIT, HALF_UNIT = 8192.0, 2048.0
LOW = 1 << 16
VMEM = pl.BlockSpec(memory_space=pltpu.VMEM)
SMEM = pl.BlockSpec(memory_space=pltpu.SMEM)
HBM = pl.BlockSpec(memory_space=pltpu.HBM)


def times(left, right):
    return lax.dot_general(
        left, right, (((1,), (1,)), ((), ())), preferred_element_type=jnp.float32
    )


def encode(x):
    level = jnp.log(jnp.maximum(x, 2.0**LEAST)) * (PER_OCTAVE / math.log(2))
    code = (level + (0.5 - LEAST * PER_OCTAVE)).astype(jnp.int32) + (NONE + 1)
    return jnp.where(x[..., :1, :] > 0, code, NONE).astype(jnp.int16)


def decode(code):
    code = code.astype(jnp.int32)
    level = code.astype(jnp.float32) * (math.log(2) / PER_OCTAVE) + MIDDLE * math.log(2)
    return jnp.where(code[..., :1, :] > NONE, jnp.exp(level), 0.0)


def split(panel):
    whole, rest = divmod(panel, LANES)
    return whole, LANES // rest if rest else 0


def packed_rows(rows, panel, symmetric=False):
    whole, fold = split(panel)
    if symmetric and (whole, fold) == (1, 2):
        return LANES + LANES // 2
    body = sum((i + 1) * LANES if symmetric else rows for i in range(whole))
    return body + (rows // fold if fold else 0)


def pack(tile, symmetric=False):
    rows, panel = tile.shape
    whole, fold = split(panel)
    if symmetric and (whole, fold) == (1, 2):
        n = LANES // 2
        left, right = tile[:, :LANES], tile[:, LANES:]
        parts = [
            left[:n],
            jnp.concatenate([right[:n], left[n:2 * n, n:]], axis=1),
            jnp.concatenate([right[n:2 * n], right[2 * n:]], axis=1),
        ]
        return jnp.concatenate(parts, axis=0)
    parts = [
        tile[: (i + 1) * LANES if symmetric else rows, i * LANES:(i + 1) * LANES]
        for i in range(whole)
    ]
    if fold:
        n = rows // fold
        left = [tile[i * n:(i + 1) * n, whole * LANES:] for i in range(fold)]
        parts.append(jnp.concatenate(left, axis=1))
    return jnp.concatenate(parts, axis=0)


def unpack(x, out, symmetric=False):
    rows, panel = out.shape
    whole, fold = split(panel)
    if symmetric and (whole, fold) == (1, 2):
        n = LANES // 2
        out[:n, :LANES] = x[:n]
        out[:n, LANES:] = x[n:2 * n, :n]
        out[n:2 * n, n:LANES] = x[n:2 * n, n:]
        out[n:2 * n, LANES:] = x[2 * n:, :n]
        out[2 * n:, LANES:] = x[2 * n:, n:]
        out[n:2 * n, :n] = x[:n, n:].T
        out[2 * n:, :LANES] = out[:2 * n, LANES:].T
        return
    at = 0
    for i in range(whole):
        n = (i + 1) * LANES if symmetric else rows
        out[:n, i * LANES:(i + 1) * LANES] = x[at:at + n]
        at += n
    if fold:
        n, width = rows // fold, LANES // fold
        for i in range(fold):
            out[i * n:(i + 1) * n, whole * LANES:] = x[at:, i * width:(i + 1) * width]
    if symmetric:
        for i in range(whole):
            n = (i + 1) * LANES
            if n < panel:
                out[n:, i * LANES:n] = out[i * LANES:n, n:].T


def rows_of(sums, count):
    panel = sums[0].shape[1]
    row = lax.broadcasted_iota(jnp.int32, (ROWS, LANES), 0)
    out, at = jnp.zeros((ROWS, LANES), jnp.float32), 0
    for x in sums:
        for start in range(0, panel, LANES):
            piece = x[:, start:start + LANES]
            if piece.shape[1] < LANES:
                piece = jnp.concatenate([piece] * (LANES // piece.shape[1]), axis=1)
            out = jnp.where(row == at, piece, out)
            at += 1
    return jnp.where(row == at, count, out)


def sums_of(rows, panel, which):
    per = -(-panel // LANES)
    starts = range(0, panel, LANES)
    return [
        (start, rows[which * per + i:which * per + i + 1, :min(LANES, panel - start)])
        for i, start in enumerate(starts)
    ]


def encode_rows(rows, unit):
    whole = (rows * unit + 0.5).astype(jnp.int32)
    high = lax.shift_right_logical(whole, 16)
    low = lax.bitwise_and(whole, LOW - 1) - LOW // 2
    return jnp.concatenate([high, low], axis=0).astype(jnp.int16)


def decode_rows(code, unit):
    x = code.astype(jnp.int32).astype(jnp.float32)
    return (x[:ROWS] * float(LOW) + (x[ROWS:] + LOW / 2)) * (1 / unit)


def find_slots(cap, cycle_ref, order_ref, where_ref, table_ref):
    cycles = order_ref.shape[0]
    for s in range(cycles):
        where_ref[order_ref[s]] = s
        table_ref[s] = 0
    for s in range(cycles * cap):
        table_ref[cycles + s] = 0
    for j in range(cycle_ref.shape[0]):
        p = where_ref[cycle_ref[j]]
        r = table_ref[p]
        table_ref[cycles + p * cap + r] = j
        table_ref[p] = r + 1


def gathered(ref, s, cap, table_ref, masked):
    cycles = table_ref.shape[0] // (cap + 1)
    parts = []
    for r in range(cap):
        j = table_ref[cycles + s * cap + r]
        x = ref[:, pl.ds(pl.multiple_of(j * BLOCK, BLOCK), BLOCK)]
        parts.append(jnp.where(r < table_ref[s], x, jnp.zeros_like(x)) if masked else x)
    return jnp.concatenate(parts, axis=1)


def early_kernel(cap, cycle_hbm, order_hbm, own_hbm, other_ref, *refs):
    table_ref, sorted_ref, rows_ref, *outs = refs[:-6]
    where_ref, cycle_ref, order_ref, own_ref, sums_ref, sems = refs[-6:]
    pairs = ((cycle_hbm, cycle_ref), (order_hbm, order_ref), (own_hbm, own_ref))
    copies = [pltpu.make_async_copy(*pair, sems.at[i]) for i, pair in enumerate(pairs)]
    for copy in copies:
        copy.start()
    copies[0].wait()
    copies[1].wait()
    find_slots(cap, cycle_ref, order_ref, where_ref, table_ref)
    inner = lax.axis_size("blk") // 2
    pieces, outs = outs[:-inner], outs[-inner:]
    panel = own_ref.shape[0]
    half = panel // 2
    mine = lax.rem(lax.axis_index("blk"), inner)
    first = lax.rem(lax.axis_index("tm"), 2) == 0
    body = outs[0].shape[1]
    row = lax.broadcasted_iota(jnp.int32, (sums_ref.shape[1], BLOCK), 0)
    members = jnp.concatenate(
        [
            jnp.where(row == where_ref[cycle_ref[j]], 1.0, 0.0).astype(jnp.bfloat16)
            for j in range(cycle_ref.shape[0])
        ],
        axis=1,
    )
    each = [(k, h, h * inner + lax.bitwise_xor(mine, k)) for k in range(inner) for h in range(2)]
    for k, h, s in each:
        sorted_ref[1, k, h] = gathered(other_ref, s, cap, table_ref, True)
    sums_ref[1] = times(members, other_ref[...])
    copies[2].wait()
    for piece in pieces:
        piece[...] = own_ref[panel - piece.shape[0]:]
    sums_ref[0] = times(members, own_ref[...])
    for k, h, s in each:
        own, other = gathered(own_ref, s, cap, table_ref, True), sorted_ref[1, k, h]
        sorted_ref[0, k, h] = own
        left = jnp.where(first, own[:half], other[half:])
        right = jnp.where(first, other, own)
        rows = rows_of([sums_ref[i, pl.ds(s, 1)] for i in range(2)], table_ref[s].astype(jnp.float32))
        found = jnp.concatenate([pack(times(own, own), True), pack(times(left, right))], axis=0)
        if k:
            outs[k][h, :body] = encode(found)
            outs[k][h, body:] = encode_rows(rows, PART_UNIT)
        else:
            outs[k][h] = found
            rows_ref[h] = rows


def late_kernel(cap, after, table_ref, sorted_ref, *refs):
    refs = refs[after:]
    inner = lax.axis_size("blk") // 2
    came, outs = refs[:-inner], refs[-inner:]
    mine = lax.rem(lax.axis_index("blk"), inner)
    chip = lax.div(lax.axis_index("tm"), 2)
    for k in range(inner):
        for h in range(2):
            s = h * inner + lax.bitwise_xor(mine, k)
            for d, ref in enumerate(came):
                upper = (chip > lax.bitwise_xor(chip, d + 1)).astype(jnp.int32)
                far = gathered(ref, s, cap, table_ref, False)
                tile = pack(times(sorted_ref[upper, k, h], far))
                outs[k][h, d] = encode(tile) if k else tile


def early_sum_kernel(own_ref, own_rows_ref, *refs):
    *parts, home_ref, rows_ref, away_ref = refs
    body = home_ref.shape[0]
    side = lax.div(lax.axis_index("blk"), lax.axis_size("blk") // 2)

    def total(h):
        tiles, rows = own_ref[h], own_rows_ref[h]
        for part in parts:
            tiles = tiles + decode(part[h, :body])
            rows = rows + decode_rows(part[h, body:], PART_UNIT)
        return tiles, rows

    home_ref[...], rows_ref[...] = total(side)
    tiles, rows = total(1 - side)
    away_ref[:body], away_ref[body:] = encode(tiles), encode_rows(rows, HALF_UNIT)


def late_sum_kernel(pieces, home_rows_ref, early_away_ref, *refs):
    *parts, home_ref, near_ref, away_ref = refs
    inner = len(parts) // pieces
    pairs, body = home_ref.shape[:2]
    side = lax.div(lax.axis_index("blk"), lax.axis_size("blk") // 2)
    near_rows = encode_rows(home_rows_ref[...], HALF_UNIT)
    away_rows = early_away_ref[-2 * ROWS:]
    for d in range(pairs):
        at = 0
        for piece in range(pieces):
            own, *came = parts[piece * inner:(piece + 1) * inner]
            here = pl.ds(at, own.shape[2])
            at += own.shape[2]
            home, away = own[side, d], own[1 - side, d]
            for part in came:
                home = home + decode(part[side, d])
                away = away + decode(part[1 - side, d])
            home_ref[d, here] = home
            near_ref[d, here] = encode(home)
            away_ref[d, here] = encode(away)
        near_ref[d, body:], away_ref[d, body:] = near_rows, away_rows


def set_scale(ref, rows, which):
    for start, x in sums_of(rows, ref.shape[1], which):
        ref[0:1, start:start + x.shape[1]] = 1.0 / x


def early_end_kernel(
    home_ref, rows_ref, came_ref, after_ref, own_ref, part_ref, code_ref, down_ref, scale_ref
):
    half, panel = part_ref.shape
    body, diagonal = home_ref.shape[0], packed_rows(panel, panel, True)
    rows = rows_ref[...] + decode_rows(came_ref[body:], HALF_UNIT)
    part = home_ref[diagonal:] + decode(came_ref[diagonal:body])
    code_ref[...] = encode(part)
    unpack(part, part_ref)
    unpack(home_ref[:diagonal] + decode(came_ref[:diagonal]), own_ref, True)
    at = 2 * -(-panel // LANES)
    count = rows[at:at + 1, 0:1] * float(BLOCK)
    for which in range(2):
        set_scale(scale_ref.at[which], rows, which)
    down = jnp.broadcast_to(scale_ref[0, 0:1] * count, (panel, panel)).T
    down_ref[...] = down


def begin_kernel(own_ref, part_ref, mate_part_ref, down_ref, scale_ref, pair_ref, out_ref, ready, sem):
    panel = down_ref.shape[0]
    half = panel // 2
    me = lax.axis_index("tm")
    chip, core = lax.div(me, 2), lax.rem(me, 2)
    down = down_ref[...]
    pair_ref[0] = own_ref[...] * down
    mate = pair_ref.at[1]
    unpack(decode(mate_part_ref[...]), mate.at[pl.ds(half, panel - half)])
    mate[:half] = part_ref[...] * down[:half]
    mate[half:] = mate[half:] * down[half:]
    for u in range(2):
        here = slice(u * panel, (u + 1) * panel)

        @pl.when(jnp.logical_and(chip == 0, core <= u))
        def _():
            which = u - core
            ready[:, here] = pair_ref[which] * scale_ref[which, 0:1]

        @pl.when(jnp.logical_or(chip > 0, core > u))
        def _():
            ready[:, here] = jnp.zeros((panel, panel), jnp.float32)

    copy = pltpu.make_async_copy(ready, out_ref.at[0, :, pl.ds(0, 2 * panel)], sem)
    copy.start()
    copy.wait()


def middle_kernel(pairs, pair_ref, down_ref, late_ref, *refs):
    away, across_ref, tiles, turned = refs[:pairs], *refs[pairs:]
    late = late_ref.shape[1]
    me = lax.axis_index("tm")
    chip, core = lax.div(me, 2), lax.rem(me, 2)
    down = down_ref[...]
    tiles[...] = jnp.zeros_like(tiles)
    tiles[me] = pair_ref[0]

    @pl.when(core == 0)
    def _():
        tiles[me + 1] = pair_ref[1]

    for d in range(pairs):
        far_chip = lax.bitwise_xor(chip, d + 1)

        @pl.when(chip < far_chip)
        def _():
            unpack(late_ref[d] + decode(across_ref[d, :late]), turned)
            tiles[2 * far_chip + core] = turned[...] * down
            unpack(decode(away[d][0, :late]), turned)
            tiles[2 * far_chip + 1 - core] = turned[...].T * down


def last_kernel(pairs, tiles, down_ref, scale_ref, begun_ref, *refs):
    near, away = refs[:pairs], refs[pairs:2 * pairs]
    out_ref, scales, more, turned, ready, sems = refs[2 * pairs:]
    steps, panel = tiles.shape[:2]
    me = lax.axis_index("tm")
    chip, core = lax.div(me, 2), lax.rem(me, 2)
    scales[...] = jnp.ones_like(scales)
    scales[me] = scale_ref[0]

    @pl.when(core == 0)
    def _():
        scales[me + 1] = scale_ref[1]

    more[...] = jnp.zeros_like(more)
    for d in range(pairs):
        far_chip = lax.bitwise_xor(chip, d + 1)
        late = near[d].shape[1] - 2 * ROWS

        @pl.when(chip < far_chip)
        def _():
            rows = decode_rows(near[d][0, late:], HALF_UNIT) + decode_rows(
                away[d][0, late:], HALF_UNIT
            )
            straight, crossed = 2 * far_chip + core, 2 * far_chip + 1 - core
            set_scale(scales.at[straight], rows, 0)
            set_scale(scales.at[crossed], rows, 1)
            unpack(decode(near[d][0, :late]), turned)
            more[crossed] = turned[...].T * down_ref[...]

    copies = []
    for i, rows in enumerate((pl.ds(0, panel // 2), pl.ds(panel // 2, panel - panel // 2))):
        for u in range(2, steps):
            tile = (tiles[u, rows] + more[u, rows]) * scales[u, 0:1]
            ready[rows, (u - 2) * panel:(u - 1) * panel] = tile
        there = out_ref.at[0, rows, pl.ds(2 * panel, (steps - 2) * panel)]
        copies.append(pltpu.make_async_copy(ready.at[rows], there, sems.at[i]))
        copies[-1].start()
    for copy in copies:
        copy.wait()


def call(kernel, outs, ins, scratch=(), flops=0, in_hbm=0, out_hbm=0, goes_on=None):
    moved = sum(math.prod(x.shape) * x.dtype.itemsize for x in (*outs, *ins))
    many = isinstance(outs, list)
    specs = [SMEM if x.ndim == 1 else VMEM for x in (*ins, *outs)]
    specs[:in_hbm] = [HBM] * in_hbm
    specs[len(specs) - out_hbm:] = [HBM] * out_hbm
    if goes_on is not None:
        specs[goes_on] = HBM
    ins = [
        pltpu.with_memory_space_constraint(x, pltpu.HBM) if i < in_hbm else x
        for i, x in enumerate(ins)
    ]
    return pl.pallas_call(
        kernel,
        out_shape=outs if many else outs[0],
        in_specs=specs[:len(ins)],
        out_specs=specs[len(ins):] if many else specs[-1],
        scratch_shapes=scratch,
        input_output_aliases={} if goes_on is None else {goes_on: len(outs) - 1},
        compiler_params=pltpu.CompilerParams(vmem_limit_bytes=48 * 2**20),
        cost_estimate=pl.CostEstimate(flops=flops, bytes_accessed=moved, transcendentals=0),
    )(*ins)


def on_device(intensity, block_cycle, cycle_order):
    panel = intensity.shape[0]
    blk_dev = block_cycle.shape[0]
    cycles = cycle_order.shape[0]
    groups = lax.axis_size("blk")
    steps = lax.axis_size("tm")
    inner = groups // 2
    pairs = steps // 2 - 1
    cap = 2 * max(1, blk_dev // cycles)
    early = packed_rows(panel, panel, True) + packed_rows(panel // 2, panel)
    first = panel // LANES * LANES
    pieces = [n for n in (first, panel - first) if n]
    late = [panel * n // LANES for n in pieces]

    def hop(x, by_blk, by_tm, sends=lambda t: True):
        perm = [
            (b * steps + t, (b ^ by_blk) * steps + (t ^ by_tm))
            for b in range(groups)
            for t in range(steps)
            if sends(t)
        ]
        return lax.ppermute(x, ("blk", "tm"), perm)

    offsets = range(1, pairs + 1)
    other = hop(intensity, 0, 1)
    sent = intensity[:first] if len(pieces) > 1 else intensity
    far = [[hop(sent, 0, 2 * d) for d in offsets]]
    f32, i16 = jnp.float32, jnp.int16
    shape = jax.ShapeDtypeStruct
    depth = cap * BLOCK
    work = 2 * cycles * panel * panel * depth
    table, gathers, own_rows, *made = call(
        functools.partial(early_kernel, cap),
        [
            shape((cycles * (cap + 1),), jnp.int32),
            shape((2, inner, 2, panel, depth), jnp.bfloat16),
            shape((2, ROWS, LANES), f32),
            *[shape((n, intensity.shape[1]), jnp.bfloat16) for n in pieces[1:]],
            shape((2, early, LANES), f32),
            *[shape((2, early + 2 * ROWS, LANES), i16)] * (inner - 1),
        ],
        (block_cycle, cycle_order, intensity, other),
        [
            pltpu.SMEM(cycle_order.shape, jnp.int32),
            pltpu.SMEM(block_cycle.shape, jnp.int32),
            pltpu.SMEM(cycle_order.shape, jnp.int32),
            pltpu.VMEM(intensity.shape, jnp.bfloat16),
            pltpu.VMEM((2, -(-cycles // 16) * 16, panel), f32),
            pltpu.SemaphoreType.DMA((3,)),
        ],
        2 * work,
        3,
    )
    far += [[hop(x, 0, 2 * d) for d in offsets] for x in made[:-inner]]

    def exchange(made):
        order = sorted(range(inner), key=lambda k: (k > 0, -k.bit_count()))
        return [hop(made[k], k, 0) if k else made[k] for k in order]

    parts = exchange(made[-inner:])
    home, home_rows, away = call(
        early_sum_kernel,
        [
            shape((early, LANES), f32),
            shape((ROWS, LANES), f32),
            shape((early + 2 * ROWS, LANES), i16),
        ],
        (parts[0], own_rows, *parts[1:]),
    )
    came = hop(away, inner, 0)

    parts, after = [], ()
    for rows, came_rows in zip(late, far):
        made = call(
            functools.partial(late_kernel, cap, len(after)),
            [shape((2, pairs, rows, LANES), i16 if k else f32) for k in range(inner)],
            (table, gathers, *after, *came_rows),
            flops=pairs * work,
        )
        parts += exchange(made)
        after = (away, made[1])
    late_home, near, late_away = call(
        functools.partial(late_sum_kernel, len(pieces)),
        [
            shape((pairs, sum(late), LANES), f32),
            shape((pairs, sum(late) + 2 * ROWS, LANES), i16),
            shape((pairs, sum(late) + 2 * ROWS, LANES), i16),
        ],
        (home_rows, away, *parts),
    )

    def is_lower(t, d):
        return t // 2 < (t // 2 ^ d)

    from_away = [
        hop(late_away[d - 1:d], inner, 2 * d, lambda t, d=d: not is_lower(t, d)) for d in offsets
    ]
    from_near = [hop(near[d - 1:d], 0, 2 * d) for d in offsets]
    across = hop(late_away, inner, 0, lambda t: any(is_lower(t, d) for d in offsets))
    own_tile, part, code, down, scale = call(
        early_end_kernel,
        [
            shape((panel, panel), f32),
            shape((panel // 2, panel), f32),
            shape((packed_rows(panel // 2, panel), LANES), i16),
            shape((panel, panel), f32),
            shape((2, 8, panel), f32),
        ],
        (home, home_rows, came, late_away),
    )
    mate_part = hop(code, 0, 1)
    whole = shape((1, panel, steps * panel), f32)
    pair, begun = call(
        begin_kernel,
        [shape((2, panel, panel), f32), whole],
        (own_tile, part, mate_part, down, scale),
        [pltpu.VMEM((panel, 2 * panel), f32), pltpu.SemaphoreType.DMA],
        out_hbm=1,
    )
    tiles = call(
        functools.partial(middle_kernel, pairs),
        (shape((steps, panel, panel), f32),),
        (pair, down, late_home, *from_away, across),
        [pltpu.VMEM((panel, panel), f32)],
    )
    return call(
        functools.partial(last_kernel, pairs),
        (whole,),
        (tiles, down, scale, begun, *from_near, *from_away),
        [
            pltpu.VMEM((steps, 8, panel), f32),
            pltpu.VMEM((steps, panel, panel), f32),
            pltpu.VMEM((panel, panel), f32),
            pltpu.VMEM((panel, (steps - 2) * panel), f32),
            pltpu.SemaphoreType.DMA((2,)),
        ],
        out_hbm=1,
        goes_on=3,
    )


def solution(mesh):
    placed = (P("tm", "blk"), P("blk"), P())
    return jax.shard_map(
        on_device, mesh=mesh, in_specs=placed, out_specs=P("blk", "tm", None), check_vma=False
    )
```

```python
import functools
import math

import jax
import jax.numpy as jnp
from jax import lax
from jax.experimental import pallas as pl
from jax.experimental.pallas import tpu as pltpu
from jax.sharding import PartitionSpec as P

BLOCK = 128
LANES = 128
ROWS = 8
NONE = -32768
LEAST, MOST = -3.0, 29.0
PER_OCTAVE = 65534 / (MOST - LEAST)
MIDDLE = (MOST + LEAST) / 2
PART_UNIT, HALF_UNIT = 8192.0, 2048.0
LOW = 1 << 16
VMEM = pl.BlockSpec(memory_space=pltpu.VMEM)
SMEM = pl.BlockSpec(memory_space=pltpu.SMEM)
HBM = pl.BlockSpec(memory_space=pltpu.HBM)


def times(left, right):
    return lax.dot_general(
        left, right, (((1,), (1,)), ((), ())), preferred_element_type=jnp.float32
    )


def encode(x):
    level = jnp.log(jnp.maximum(x, 2.0**LEAST)) * (PER_OCTAVE / math.log(2))
    code = (level + (0.5 - LEAST * PER_OCTAVE)).astype(jnp.int32) + (NONE + 1)
    return jnp.where(x[..., :1, :] > 0, code, NONE).astype(jnp.int16)


def decode(code):
    code = code.astype(jnp.int32)
    level = code.astype(jnp.float32) * (math.log(2) / PER_OCTAVE) + MIDDLE * math.log(2)
    return jnp.where(code[..., :1, :] > NONE, jnp.exp(level), 0.0)


def split(panel):
    whole, rest = divmod(panel, LANES)
    return whole, LANES // rest if rest else 0


def packed_rows(rows, panel, symmetric=False):
    whole, fold = split(panel)
    if symmetric and (whole, fold) == (1, 2):
        return LANES + LANES // 2
    body = sum((i + 1) * LANES if symmetric else rows for i in range(whole))
    return body + (rows // fold if fold else 0)


def pack(tile, symmetric=False):
    rows, panel = tile.shape
    whole, fold = split(panel)
    if symmetric and (whole, fold) == (1, 2):
        n = LANES // 2
        left, right = tile[:, :LANES], tile[:, LANES:]
        parts = [
            left[:n],
            jnp.concatenate([right[:n], left[n:2 * n, n:]], axis=1),
            jnp.concatenate([right[n:2 * n], right[2 * n:]], axis=1),
        ]
        return jnp.concatenate(parts, axis=0)
    parts = [
        tile[: (i + 1) * LANES if symmetric else rows, i * LANES:(i + 1) * LANES]
        for i in range(whole)
    ]
    if fold:
        n = rows // fold
        left = [tile[i * n:(i + 1) * n, whole * LANES:] for i in range(fold)]
        parts.append(jnp.concatenate(left, axis=1))
    return jnp.concatenate(parts, axis=0)


def unpack(x, out, symmetric=False):
    rows, panel = out.shape
    whole, fold = split(panel)
    if symmetric and (whole, fold) == (1, 2):
        n = LANES // 2
        out[:n, :LANES] = x[:n]
        out[:n, LANES:] = x[n:2 * n, :n]
        out[n:2 * n, n:LANES] = x[n:2 * n, n:]
        out[n:2 * n, LANES:] = x[2 * n:, :n]
        out[2 * n:, LANES:] = x[2 * n:, n:]
        out[n:2 * n, :n] = x[:n, n:].T
        out[2 * n:, :LANES] = out[:2 * n, LANES:].T
        return
    at = 0
    for i in range(whole):
        n = (i + 1) * LANES if symmetric else rows
        out[:n, i * LANES:(i + 1) * LANES] = x[at:at + n]
        at += n
    if fold:
        n, width = rows // fold, LANES // fold
        for i in range(fold):
            out[i * n:(i + 1) * n, whole * LANES:] = x[at:, i * width:(i + 1) * width]
    if symmetric:
        for i in range(whole):
            n = (i + 1) * LANES
            if n < panel:
                out[n:, i * LANES:n] = out[i * LANES:n, n:].T


def rows_of(sums, count):
    panel = sums[0].shape[1]
    row = lax.broadcasted_iota(jnp.int32, (ROWS, LANES), 0)
    out, at = jnp.zeros((ROWS, LANES), jnp.float32), 0
    for x in sums:
        for start in range(0, panel, LANES):
            piece = x[:, start:start + LANES]
            if piece.shape[1] < LANES:
                piece = jnp.concatenate([piece] * (LANES // piece.shape[1]), axis=1)
            out = jnp.where(row == at, piece, out)
            at += 1
    return jnp.where(row == at, count, out)


def sums_of(rows, panel, which):
    per = -(-panel // LANES)
    starts = range(0, panel, LANES)
    return [
        (start, rows[which * per + i:which * per + i + 1, :min(LANES, panel - start)])
        for i, start in enumerate(starts)
    ]


def encode_rows(rows, unit):
    whole = (rows * unit + 0.5).astype(jnp.int32)
    high = lax.shift_right_logical(whole, 16)
    low = lax.bitwise_and(whole, LOW - 1) - LOW // 2
    return jnp.concatenate([high, low], axis=0).astype(jnp.int16)


def decode_rows(code, unit):
    x = code.astype(jnp.int32).astype(jnp.float32)
    return (x[:ROWS] * float(LOW) + (x[ROWS:] + LOW / 2)) * (1 / unit)


def find_slots(cap, cycle_ref, order_ref, where_ref, table_ref):
    cycles = order_ref.shape[0]
    for s in range(cycles):
        where_ref[order_ref[s]] = s
        table_ref[s] = 0
    for s in range(cycles * cap):
        table_ref[cycles + s] = 0
    for j in range(cycle_ref.shape[0]):
        p = where_ref[cycle_ref[j]]
        r = table_ref[p]
        table_ref[cycles + p * cap + r] = j
        table_ref[p] = r + 1


def gathered(ref, s, cap, table_ref, masked):
    cycles = table_ref.shape[0] // (cap + 1)
    parts = []
    for r in range(cap):
        j = table_ref[cycles + s * cap + r]
        x = ref[:, pl.ds(pl.multiple_of(j * BLOCK, BLOCK), BLOCK)]
        parts.append(jnp.where(r < table_ref[s], x, jnp.zeros_like(x)) if masked else x)
    return jnp.concatenate(parts, axis=1)


def early_kernel(cap, cycle_hbm, order_hbm, own_hbm, other_ref, *refs):
    table_ref, sorted_ref, rows_ref, *outs = refs[:-6]
    where_ref, cycle_ref, order_ref, own_ref, sums_ref, sems = refs[-6:]
    pairs = ((cycle_hbm, cycle_ref), (order_hbm, order_ref), (own_hbm, own_ref))
    copies = [pltpu.make_async_copy(*pair, sems.at[i]) for i, pair in enumerate(pairs)]
    for copy in copies:
        copy.start()
    copies[0].wait()
    copies[1].wait()
    find_slots(cap, cycle_ref, order_ref, where_ref, table_ref)
    inner = lax.axis_size("blk") // 2
    pieces, outs = outs[:-inner], outs[-inner:]
    panel = own_ref.shape[0]
    half = panel // 2
    mine = lax.rem(lax.axis_index("blk"), inner)
    first = lax.rem(lax.axis_index("tm"), 2) == 0
    body = outs[0].shape[1]
    row = lax.broadcasted_iota(jnp.int32, (sums_ref.shape[1], BLOCK), 0)
    members = jnp.concatenate(
        [
            jnp.where(row == where_ref[cycle_ref[j]], 1.0, 0.0).astype(jnp.bfloat16)
            for j in range(cycle_ref.shape[0])
        ],
        axis=1,
    )
    each = [(k, h, h * inner + lax.bitwise_xor(mine, k)) for k in range(inner) for h in range(2)]
    for k, h, s in each:
        sorted_ref[1, k, h] = gathered(other_ref, s, cap, table_ref, True)
    sums_ref[1] = times(members, other_ref[...])
    copies[2].wait()
    for piece in pieces:
        piece[...] = own_ref[panel - piece.shape[0]:]
    sums_ref[0] = times(members, own_ref[...])
    for k, h, s in each:
        own, other = gathered(own_ref, s, cap, table_ref, True), sorted_ref[1, k, h]
        sorted_ref[0, k, h] = own
        left = jnp.where(first, own[:half], other[half:])
        right = jnp.where(first, other, own)
        rows = rows_of([sums_ref[i, pl.ds(s, 1)] for i in range(2)], table_ref[s].astype(jnp.float32))
        found = jnp.concatenate([pack(times(own, own), True), pack(times(left, right))], axis=0)
        if k:
            outs[k][h, :body] = encode(found)
            outs[k][h, body:] = encode_rows(rows, PART_UNIT)
        else:
            outs[k][h] = found
            rows_ref[h] = rows


def late_kernel(cap, after, table_ref, sorted_ref, *refs):
    refs = refs[after:]
    inner = lax.axis_size("blk") // 2
    came, outs = refs[:-inner], refs[-inner:]
    mine = lax.rem(lax.axis_index("blk"), inner)
    chip = lax.div(lax.axis_index("tm"), 2)
    for k in range(inner):
        for h in range(2):
            s = h * inner + lax.bitwise_xor(mine, k)
            for d, ref in enumerate(came):
                upper = (chip > lax.bitwise_xor(chip, d + 1)).astype(jnp.int32)
                far = gathered(ref, s, cap, table_ref, False)
                tile = pack(times(sorted_ref[upper, k, h], far))
                outs[k][h, d] = encode(tile) if k else tile


def early_sum_kernel(own_ref, own_rows_ref, *refs):
    *parts, home_ref, rows_ref, away_ref = refs
    body = home_ref.shape[0]
    side = lax.div(lax.axis_index("blk"), lax.axis_size("blk") // 2)

    def total(h):
        tiles, rows = own_ref[h], own_rows_ref[h]
        for part in parts:
            tiles = tiles + decode(part[h, :body])
            rows = rows + decode_rows(part[h, body:], PART_UNIT)
        return tiles, rows

    home_ref[...], rows_ref[...] = total(side)
    tiles, rows = total(1 - side)
    away_ref[:body], away_ref[body:] = encode(tiles), encode_rows(rows, HALF_UNIT)


def late_sum_kernel(pieces, home_rows_ref, early_away_ref, *refs):
    *parts, home_ref, near_ref, away_ref = refs
    inner = len(parts) // pieces
    pairs, body = home_ref.shape[:2]
    side = lax.div(lax.axis_index("blk"), lax.axis_size("blk") // 2)
    near_rows = encode_rows(home_rows_ref[...], HALF_UNIT)
    away_rows = early_away_ref[-2 * ROWS:]
    for d in range(pairs):
        at = 0
        for piece in range(pieces):
            own, *came = parts[piece * inner:(piece + 1) * inner]
            here = pl.ds(at, own.shape[2])
            at += own.shape[2]
            home, away = own[side, d], own[1 - side, d]
            for part in came:
                home = home + decode(part[side, d])
                away = away + decode(part[1 - side, d])
            home_ref[d, here] = home
            near_ref[d, here] = encode(home)
            away_ref[d, here] = encode(away)
        near_ref[d, body:], away_ref[d, body:] = near_rows, away_rows


def set_scale(ref, rows, which):
    for start, x in sums_of(rows, ref.shape[1], which):
        ref[0:1, start:start + x.shape[1]] = 1.0 / x


def early_end_kernel(
    home_ref, rows_ref, came_ref, after_ref, own_ref, part_ref, code_ref, down_ref, scale_ref
):
    half, panel = part_ref.shape
    body, diagonal = home_ref.shape[0], packed_rows(panel, panel, True)
    rows = rows_ref[...] + decode_rows(came_ref[body:], HALF_UNIT)
    part = home_ref[diagonal:] + decode(came_ref[diagonal:body])
    code_ref[...] = encode(part)
    unpack(part, part_ref)
    unpack(home_ref[:diagonal] + decode(came_ref[:diagonal]), own_ref, True)
    at = 2 * -(-panel // LANES)
    count = rows[at:at + 1, 0:1] * float(BLOCK)
    for which in range(2):
        set_scale(scale_ref.at[which], rows, which)
    down = jnp.broadcast_to(scale_ref[0, 0:1] * count, (panel, panel)).T
    down_ref[...] = down


def begin_kernel(own_ref, part_ref, mate_part_ref, down_ref, scale_ref, pair_ref, out_ref, ready, sem):
    panel = down_ref.shape[0]
    half = panel // 2
    me = lax.axis_index("tm")
    chip, core = lax.div(me, 2), lax.rem(me, 2)
    down = down_ref[...]
    pair_ref[0] = own_ref[...] * down
    mate = pair_ref.at[1]
    unpack(decode(mate_part_ref[...]), mate.at[pl.ds(half, panel - half)])
    mate[:half] = part_ref[...] * down[:half]
    mate[half:] = mate[half:] * down[half:]
    for u in range(2):
        here = slice(u * panel, (u + 1) * panel)

        @pl.when(jnp.logical_and(chip == 0, core <= u))
        def _():
            which = u - core
            ready[:, here] = pair_ref[which] * scale_ref[which, 0:1]

        @pl.when(jnp.logical_or(chip > 0, core > u))
        def _():
            ready[:, here] = jnp.zeros((panel, panel), jnp.float32)

    copy = pltpu.make_async_copy(ready, out_ref.at[0, :, pl.ds(0, 2 * panel)], sem)
    copy.start()
    copy.wait()


def middle_kernel(pairs, pair_ref, down_ref, late_ref, *refs):
    away, across_ref, tiles, turned = refs[:pairs], *refs[pairs:]
    late = late_ref.shape[1]
    me = lax.axis_index("tm")
    chip, core = lax.div(me, 2), lax.rem(me, 2)
    down = down_ref[...]
    tiles[...] = jnp.zeros_like(tiles)
    tiles[me] = pair_ref[0]

    @pl.when(core == 0)
    def _():
        tiles[me + 1] = pair_ref[1]

    for d in range(pairs):
        far_chip = lax.bitwise_xor(chip, d + 1)

        @pl.when(chip < far_chip)
        def _():
            unpack(late_ref[d] + decode(across_ref[d, :late]), turned)
            tiles[2 * far_chip + core] = turned[...] * down
            unpack(decode(away[d][0, :late]), turned)
            tiles[2 * far_chip + 1 - core] = turned[...].T * down


def last_kernel(pairs, tiles, down_ref, scale_ref, begun_ref, *refs):
    near, away = refs[:pairs], refs[pairs:2 * pairs]
    out_ref, scales, more, turned, ready, sems = refs[2 * pairs:]
    steps, panel = tiles.shape[:2]
    me = lax.axis_index("tm")
    chip, core = lax.div(me, 2), lax.rem(me, 2)
    scales[...] = jnp.ones_like(scales)
    scales[me] = scale_ref[0]

    @pl.when(core == 0)
    def _():
        scales[me + 1] = scale_ref[1]

    more[...] = jnp.zeros_like(more)
    for d in range(pairs):
        far_chip = lax.bitwise_xor(chip, d + 1)
        late = near[d].shape[1] - 2 * ROWS

        @pl.when(chip < far_chip)
        def _():
            rows = decode_rows(near[d][0, late:], HALF_UNIT) + decode_rows(
                away[d][0, late:], HALF_UNIT
            )
            straight, crossed = 2 * far_chip + core, 2 * far_chip + 1 - core
            set_scale(scales.at[straight], rows, 0)
            set_scale(scales.at[crossed], rows, 1)
            unpack(decode(near[d][0, :late]), turned)
            more[crossed] = turned[...].T * down_ref[...]

    copies = []
    for i, rows in enumerate((pl.ds(0, panel // 2), pl.ds(panel // 2, panel - panel // 2))):
        for u in range(2, steps):
            tile = (tiles[u, rows] + more[u, rows]) * scales[u, 0:1]
            ready[rows, (u - 2) * panel:(u - 1) * panel] = tile
        there = out_ref.at[0, rows, pl.ds(2 * panel, (steps - 2) * panel)]
        copies.append(pltpu.make_async_copy(ready.at[rows], there, sems.at[i]))
        copies[-1].start()
    for copy in copies:
        copy.wait()


def call(kernel, outs, ins, scratch=(), flops=0, in_hbm=0, out_hbm=0, goes_on=None, free=False):
    moved = 0 if free else sum(math.prod(x.shape) * x.dtype.itemsize for x in (*outs, *ins))
    many = isinstance(outs, list)
    specs = [SMEM if x.ndim == 1 else VMEM for x in (*ins, *outs)]
    specs[:in_hbm] = [HBM] * in_hbm
    specs[len(specs) - out_hbm:] = [HBM] * out_hbm
    if goes_on is not None:
        specs[goes_on] = HBM
    ins = [
        pltpu.with_memory_space_constraint(x, pltpu.HBM) if i < in_hbm else x
        for i, x in enumerate(ins)
    ]
    return pl.pallas_call(
        kernel,
        out_shape=outs if many else outs[0],
        in_specs=specs[:len(ins)],
        out_specs=specs[len(ins):] if many else specs[-1],
        scratch_shapes=scratch,
        input_output_aliases={} if goes_on is None else {goes_on: len(outs) - 1},
        compiler_params=pltpu.CompilerParams(vmem_limit_bytes=48 * 2**20),
        cost_estimate=pl.CostEstimate(flops=flops, bytes_accessed=moved, transcendentals=0),
    )(*ins)


def on_device(intensity, block_cycle, cycle_order):
    panel = intensity.shape[0]
    blk_dev = block_cycle.shape[0]
    cycles = cycle_order.shape[0]
    groups = lax.axis_size("blk")
    steps = lax.axis_size("tm")
    inner = groups // 2
    pairs = steps // 2 - 1
    cap = 2 * max(1, blk_dev // cycles)
    early = packed_rows(panel, panel, True) + packed_rows(panel // 2, panel)
    first = panel // LANES * LANES
    pieces = [n for n in (first, panel - first) if n]
    late = [panel * n // LANES for n in pieces]

    def hop(x, by_blk, by_tm, sends=lambda t: True):
        perm = [
            (b * steps + t, (b ^ by_blk) * steps + (t ^ by_tm))
            for b in range(groups)
            for t in range(steps)
            if sends(t)
        ]
        return lax.ppermute(x, ("blk", "tm"), perm)

    offsets = range(1, pairs + 1)
    other = hop(intensity, 0, 1)
    sent = intensity[:first] if len(pieces) > 1 else intensity
    far = [[hop(sent, 0, 2 * d) for d in offsets]]
    f32, i16 = jnp.float32, jnp.int16
    shape = jax.ShapeDtypeStruct
    depth = cap * BLOCK
    work = 2 * cycles * panel * panel * depth
    table, gathers, own_rows, *made = call(
        functools.partial(early_kernel, cap),
        [
            shape((cycles * (cap + 1),), jnp.int32),
            shape((2, inner, 2, panel, depth), jnp.bfloat16),
            shape((2, ROWS, LANES), f32),
            *[shape((n, intensity.shape[1]), jnp.bfloat16) for n in pieces[1:]],
            shape((2, early, LANES), f32),
            *[shape((2, early + 2 * ROWS, LANES), i16)] * (inner - 1),
        ],
        (block_cycle, cycle_order, intensity, other),
        [
            pltpu.SMEM(cycle_order.shape, jnp.int32),
            pltpu.SMEM(block_cycle.shape, jnp.int32),
            pltpu.SMEM(cycle_order.shape, jnp.int32),
            pltpu.VMEM(intensity.shape, jnp.bfloat16),
            pltpu.VMEM((2, -(-cycles // 16) * 16, panel), f32),
            pltpu.SemaphoreType.DMA((3,)),
        ],
        2 * work,
        3,
    )
    far += [[hop(x, 0, 2 * d) for d in offsets] for x in made[:-inner]]

    def exchange(made):
        order = sorted(range(inner), key=lambda k: (k > 0, -k.bit_count()))
        return [hop(made[k], k, 0) if k else made[k] for k in order]

    parts = exchange(made[-inner:])
    home, home_rows, away = call(
        early_sum_kernel,
        [
            shape((early, LANES), f32),
            shape((ROWS, LANES), f32),
            shape((early + 2 * ROWS, LANES), i16),
        ],
        (parts[0], own_rows, *parts[1:]),
        flops=32 * work,
    )
    came = hop(away, inner, 0)

    parts, after = [], ()
    for rows, came_rows in zip(late, far):
        made = call(
            functools.partial(late_kernel, cap, len(after)),
            [shape((2, pairs, rows, LANES), i16 if k else f32) for k in range(inner)],
            (table, gathers, *after, *came_rows),
            flops=pairs * work,
        )
        parts += exchange(made)
        after = (away, made[1])
    late_home, near, late_away = call(
        functools.partial(late_sum_kernel, len(pieces)),
        [
            shape((pairs, sum(late), LANES), f32),
            shape((pairs, sum(late) + 2 * ROWS, LANES), i16),
            shape((pairs, sum(late) + 2 * ROWS, LANES), i16),
        ],
        (home_rows, away, *parts),
        flops=32 * work,
    )

    def is_lower(t, d):
        return t // 2 < (t // 2 ^ d)

    from_away = [
        hop(late_away[d - 1:d], inner, 2 * d, lambda t, d=d: not is_lower(t, d)) for d in offsets
    ]
    from_near = [hop(near[d - 1:d], 0, 2 * d) for d in offsets]
    across = hop(late_away, inner, 0, lambda t: any(is_lower(t, d) for d in offsets))
    own_tile, part, code, down, scale = call(
        early_end_kernel,
        [
            shape((panel, panel), f32),
            shape((panel // 2, panel), f32),
            shape((packed_rows(panel // 2, panel), LANES), i16),
            shape((panel, panel), f32),
            shape((2, 8, panel), f32),
        ],
        (home, home_rows, came, late_away),
    )
    mate_part = hop(code, 0, 1)
    whole = shape((1, panel, steps * panel), f32)
    pair, begun = call(
        begin_kernel,
        [shape((2, panel, panel), f32), whole],
        (own_tile, part, mate_part, down, scale),
        [pltpu.VMEM((panel, 2 * panel), f32), pltpu.SemaphoreType.DMA],
        out_hbm=1,
        free=True,
    )
    tiles = call(
        functools.partial(middle_kernel, pairs),
        (shape((steps, panel, panel), f32),),
        (pair, down, late_home, *from_away, across),
        [pltpu.VMEM((panel, panel), f32)],
    )
    return call(
        functools.partial(last_kernel, pairs),
        (whole,),
        (tiles, down, scale, begun, *from_near, *from_away),
        [
            pltpu.VMEM((steps, 8, panel), f32),
            pltpu.VMEM((steps, panel, panel), f32),
            pltpu.VMEM((panel, panel), f32),
            pltpu.VMEM((panel, (steps - 2) * panel), f32),
            pltpu.SemaphoreType.DMA((2,)),
        ],
        out_hbm=1,
        goes_on=3,
    )


def solution(mesh):
    placed = (P("tm", "blk"), P("blk"), P())
    return jax.shard_map(
        on_device, mesh=mesh, in_specs=placed, out_specs=P("blk", "tm", None), check_vma=False
    )
```

```python
import functools
import math

import jax
import jax.numpy as jnp
from jax import lax
from jax.experimental import pallas as pl
from jax.experimental.pallas import tpu as pltpu
from jax.sharding import PartitionSpec as P

BLOCK = 128
LANES = 128
ROWS = 8
NONE = -32768
LEAST, MOST = -3.0, 29.0
PER_OCTAVE = 65534 / (MOST - LEAST)
MIDDLE = (MOST + LEAST) / 2
PART_UNIT, HALF_UNIT = 8192.0, 2048.0
LOW = 1 << 16
VMEM = pl.BlockSpec(memory_space=pltpu.VMEM)
SMEM = pl.BlockSpec(memory_space=pltpu.SMEM)
HBM = pl.BlockSpec(memory_space=pltpu.HBM)


def times(left, right):
    return lax.dot_general(
        left, right, (((1,), (1,)), ((), ())), preferred_element_type=jnp.float32
    )


def encode(x):
    level = jnp.log(jnp.maximum(x, 2.0**LEAST)) * (PER_OCTAVE / math.log(2))
    code = (level + (0.5 - LEAST * PER_OCTAVE)).astype(jnp.int32) + (NONE + 1)
    return jnp.where(x[..., :1, :] > 0, code, NONE).astype(jnp.int16)


def decode(code):
    code = code.astype(jnp.int32)
    level = code.astype(jnp.float32) * (math.log(2) / PER_OCTAVE) + MIDDLE * math.log(2)
    return jnp.where(code[..., :1, :] > NONE, jnp.exp(level), 0.0)


def split(panel):
    whole, rest = divmod(panel, LANES)
    return whole, LANES // rest if rest else 0


def packed_rows(rows, panel, symmetric=False):
    whole, fold = split(panel)
    if symmetric and (whole, fold) == (1, 2):
        return LANES + LANES // 2
    body = sum((i + 1) * LANES if symmetric else rows for i in range(whole))
    return body + (rows // fold if fold else 0)


def pack(tile, symmetric=False):
    rows, panel = tile.shape
    whole, fold = split(panel)
    if symmetric and (whole, fold) == (1, 2):
        n = LANES // 2
        left, right = tile[:, :LANES], tile[:, LANES:]
        parts = [
            left[:n],
            jnp.concatenate([right[:n], left[n:2 * n, n:]], axis=1),
            jnp.concatenate([right[n:2 * n], right[2 * n:]], axis=1),
        ]
        return jnp.concatenate(parts, axis=0)
    parts = [
        tile[: (i + 1) * LANES if symmetric else rows, i * LANES:(i + 1) * LANES]
        for i in range(whole)
    ]
    if fold:
        n = rows // fold
        left = [tile[i * n:(i + 1) * n, whole * LANES:] for i in range(fold)]
        parts.append(jnp.concatenate(left, axis=1))
    return jnp.concatenate(parts, axis=0)


def unpack(x, out, symmetric=False):
    rows, panel = out.shape
    whole, fold = split(panel)
    if symmetric and (whole, fold) == (1, 2):
        n = LANES // 2
        out[:n, :LANES] = x[:n]
        out[:n, LANES:] = x[n:2 * n, :n]
        out[n:2 * n, n:LANES] = x[n:2 * n, n:]
        out[n:2 * n, LANES:] = x[2 * n:, :n]
        out[2 * n:, LANES:] = x[2 * n:, n:]
        out[n:2 * n, :n] = x[:n, n:].T
        out[2 * n:, :LANES] = out[:2 * n, LANES:].T
        return
    at = 0
    for i in range(whole):
        n = (i + 1) * LANES if symmetric else rows
        out[:n, i * LANES:(i + 1) * LANES] = x[at:at + n]
        at += n
    if fold:
        n, width = rows // fold, LANES // fold
        for i in range(fold):
            out[i * n:(i + 1) * n, whole * LANES:] = x[at:, i * width:(i + 1) * width]
    if symmetric:
        for i in range(whole):
            n = (i + 1) * LANES
            if n < panel:
                out[n:, i * LANES:n] = out[i * LANES:n, n:].T


def rows_of(sums, count):
    panel = sums[0].shape[1]
    row = lax.broadcasted_iota(jnp.int32, (ROWS, LANES), 0)
    out, at = jnp.zeros((ROWS, LANES), jnp.float32), 0
    for x in sums:
        for start in range(0, panel, LANES):
            piece = x[:, start:start + LANES]
            if piece.shape[1] < LANES:
                piece = jnp.concatenate([piece] * (LANES // piece.shape[1]), axis=1)
            out = jnp.where(row == at, piece, out)
            at += 1
    return jnp.where(row == at, count, out)


def sums_of(rows, panel, which):
    per = -(-panel // LANES)
    starts = range(0, panel, LANES)
    return [
        (start, rows[which * per + i:which * per + i + 1, :min(LANES, panel - start)])
        for i, start in enumerate(starts)
    ]


def encode_rows(rows, unit):
    whole = (rows * unit + 0.5).astype(jnp.int32)
    high = lax.shift_right_logical(whole, 16)
    low = lax.bitwise_and(whole, LOW - 1) - LOW // 2
    return jnp.concatenate([high, low], axis=0).astype(jnp.int16)


def decode_rows(code, unit):
    x = code.astype(jnp.int32).astype(jnp.float32)
    return (x[:ROWS] * float(LOW) + (x[ROWS:] + LOW / 2)) * (1 / unit)


def find_slots(cap, cycle_ref, order_ref, where_ref, table_ref):
    cycles = order_ref.shape[0]
    for s in range(cycles):
        where_ref[order_ref[s]] = s
        table_ref[s] = 0
    for s in range(cycles * cap):
        table_ref[cycles + s] = 0
    for j in range(cycle_ref.shape[0]):
        p = where_ref[cycle_ref[j]]
        r = table_ref[p]
        table_ref[cycles + p * cap + r] = j
        table_ref[p] = r + 1


def gathered(ref, s, cap, table_ref, masked):
    cycles = table_ref.shape[0] // (cap + 1)
    parts = []
    for r in range(cap):
        j = table_ref[cycles + s * cap + r]
        x = ref[:, pl.ds(pl.multiple_of(j * BLOCK, BLOCK), BLOCK)]
        parts.append(jnp.where(r < table_ref[s], x, jnp.zeros_like(x)) if masked else x)
    return jnp.concatenate(parts, axis=1)


def early_kernel(cap, cycle_hbm, order_hbm, own_hbm, other_ref, *refs):
    table_ref, sorted_ref, rows_ref, *outs = refs[:-6]
    where_ref, cycle_ref, order_ref, own_ref, sums_ref, sems = refs[-6:]
    pairs = ((cycle_hbm, cycle_ref), (order_hbm, order_ref), (own_hbm, own_ref))
    copies = [pltpu.make_async_copy(*pair, sems.at[i]) for i, pair in enumerate(pairs)]
    for copy in copies:
        copy.start()
    copies[0].wait()
    copies[1].wait()
    find_slots(cap, cycle_ref, order_ref, where_ref, table_ref)
    inner = lax.axis_size("blk") // 2
    pieces, outs = outs[:-inner], outs[-inner:]
    panel = own_ref.shape[0]
    half = panel // 2
    mine = lax.rem(lax.axis_index("blk"), inner)
    first = lax.rem(lax.axis_index("tm"), 2) == 0
    body = outs[0].shape[1]
    row = lax.broadcasted_iota(jnp.int32, (sums_ref.shape[1], BLOCK), 0)
    members = jnp.concatenate(
        [
            jnp.where(row == where_ref[cycle_ref[j]], 1.0, 0.0).astype(jnp.bfloat16)
            for j in range(cycle_ref.shape[0])
        ],
        axis=1,
    )
    each = [(k, h, h * inner + lax.bitwise_xor(mine, k)) for k in range(inner) for h in range(2)]
    for k, h, s in each:
        sorted_ref[1, k, h] = gathered(other_ref, s, cap, table_ref, True)
    sums_ref[1] = times(members, other_ref[...])
    copies[2].wait()
    for piece in pieces:
        piece[...] = own_ref[:piece.shape[0]]
    sums_ref[0] = times(members, own_ref[...])
    for k, h, s in each:
        own, other = gathered(own_ref, s, cap, table_ref, True), sorted_ref[1, k, h]
        sorted_ref[0, k, h] = own
        left = jnp.where(first, own[:half], other[half:])
        right = jnp.where(first, other, own)
        rows = rows_of([sums_ref[i, pl.ds(s, 1)] for i in range(2)], table_ref[s].astype(jnp.float32))
        found = jnp.concatenate([pack(times(own, own), True), pack(times(left, right))], axis=0)
        if k:
            outs[k][h, :body] = encode(found)
            outs[k][h, body:] = encode_rows(rows, PART_UNIT)
        else:
            outs[k][h] = found
            rows_ref[h] = rows


def late_kernel(cap, after, table_ref, sorted_ref, *refs):
    refs = refs[after:]
    inner = lax.axis_size("blk") // 2
    came, outs = refs[:-inner], refs[-inner:]
    mine = lax.rem(lax.axis_index("blk"), inner)
    chip = lax.div(lax.axis_index("tm"), 2)
    for k in range(inner):
        for h in range(2):
            s = h * inner + lax.bitwise_xor(mine, k)
            for d, ref in enumerate(came):
                upper = (chip > lax.bitwise_xor(chip, d + 1)).astype(jnp.int32)
                far = gathered(ref, s, cap, table_ref, False)
                tile = pack(times(sorted_ref[upper, k, h], far))
                outs[k][h, d] = encode(tile) if k else tile


def early_sum_kernel(own_ref, own_rows_ref, *refs):
    *parts, home_ref, rows_ref, away_ref = refs
    body = home_ref.shape[0]
    side = lax.div(lax.axis_index("blk"), lax.axis_size("blk") // 2)

    def total(h):
        tiles, rows = own_ref[h], own_rows_ref[h]
        for part in parts:
            tiles = tiles + decode(part[h, :body])
            rows = rows + decode_rows(part[h, body:], PART_UNIT)
        return tiles, rows

    home_ref[...], rows_ref[...] = total(side)
    tiles, rows = total(1 - side)
    away_ref[:body] = encode(tiles)
    away_ref[body:body + 2 * ROWS] = encode_rows(rows, HALF_UNIT)
    away_ref[body + 2 * ROWS:] = jnp.zeros_like(away_ref[body + 2 * ROWS:])


def late_sum_kernel(pieces, early, first_ref, home_rows_ref, early_away_ref, *refs):
    *parts, home_ref, near_ref, away_ref = refs
    inner = len(parts) // pieces
    pairs, body = home_ref.shape[:2]
    side = lax.div(lax.axis_index("blk"), lax.axis_size("blk") // 2)
    near_rows = encode_rows(home_rows_ref[...], HALF_UNIT)
    away_rows = early_away_ref[early:early + 2 * ROWS]
    for d in range(pairs):
        at = 0
        for piece in range(pieces):
            own, *came = parts[piece * inner:(piece + 1) * inner]
            here = pl.ds(at, own.shape[2])
            at += own.shape[2]
            home, away = own[side, d], own[1 - side, d]
            for part in came:
                home = home + decode(part[side, d])
                away = away + decode(part[1 - side, d])
            home_ref[d, here] = home
            near_ref[d, here] = encode(home)
            away_ref[d, here] = encode(away)
        near_ref[d, body:], away_ref[d, body:] = near_rows, away_rows


def set_scale(ref, rows, which):
    for start, x in sums_of(rows, ref.shape[1], which):
        ref[0:1, start:start + x.shape[1]] = 1.0 / x


def early_end_kernel(
    home_ref, rows_ref, came_ref, after_ref, own_ref, part_ref, code_ref, down_ref, scale_ref
):
    half, panel = part_ref.shape
    body, diagonal = home_ref.shape[0], packed_rows(panel, panel, True)
    rows = rows_ref[...] + decode_rows(came_ref[body:body + 2 * ROWS], HALF_UNIT)
    part = home_ref[diagonal:] + decode(came_ref[diagonal:body])
    code_ref[...] = encode(part)
    unpack(part, part_ref)
    unpack(home_ref[:diagonal] + decode(came_ref[:diagonal]), own_ref, True)
    at = 2 * -(-panel // LANES)
    count = rows[at:at + 1, 0:1] * float(BLOCK)
    for which in range(2):
        set_scale(scale_ref.at[which], rows, which)
    down = jnp.broadcast_to(scale_ref[0, 0:1] * count, (panel, panel)).T
    down_ref[...] = down


def begin_kernel(own_ref, part_ref, mate_part_ref, down_ref, scale_ref, pair_ref, out_ref, ready, sem):
    panel = down_ref.shape[0]
    half = panel // 2
    me = lax.axis_index("tm")
    chip, core = lax.div(me, 2), lax.rem(me, 2)
    down = down_ref[...]
    pair_ref[0] = own_ref[...] * down
    mate = pair_ref.at[1]
    unpack(decode(mate_part_ref[...]), mate.at[pl.ds(half, panel - half)])
    mate[:half] = part_ref[...] * down[:half]
    mate[half:] = mate[half:] * down[half:]
    for u in range(2):
        here = slice(u * panel, (u + 1) * panel)

        @pl.when(jnp.logical_and(chip == 0, core <= u))
        def _():
            which = u - core
            ready[:, here] = pair_ref[which] * scale_ref[which, 0:1]

        @pl.when(jnp.logical_or(chip > 0, core > u))
        def _():
            ready[:, here] = jnp.zeros((panel, panel), jnp.float32)

    copy = pltpu.make_async_copy(ready, out_ref.at[0, :, pl.ds(0, 2 * panel)], sem)
    copy.start()
    copy.wait()


def middle_kernel(pairs, pair_ref, down_ref, late_ref, *refs):
    away, across_ref, tiles, turned = refs[:pairs], *refs[pairs:]
    late = late_ref.shape[1]
    me = lax.axis_index("tm")
    chip, core = lax.div(me, 2), lax.rem(me, 2)
    down = down_ref[...]
    tiles[...] = jnp.zeros_like(tiles)
    tiles[me] = pair_ref[0]

    @pl.when(core == 0)
    def _():
        tiles[me + 1] = pair_ref[1]

    for d in range(pairs):
        far_chip = lax.bitwise_xor(chip, d + 1)

        @pl.when(chip < far_chip)
        def _():
            unpack(late_ref[d] + decode(across_ref[d, :late]), turned)
            tiles[2 * far_chip + core] = turned[...] * down
            unpack(decode(away[d][0, :late]), turned)
            tiles[2 * far_chip + 1 - core] = turned[...].T * down


def last_kernel(pairs, tiles, down_ref, scale_ref, begun_ref, *refs):
    near, away = refs[:pairs], refs[pairs:2 * pairs]
    out_ref, scales, more, turned, ready, sems = refs[2 * pairs:]
    steps, panel = tiles.shape[:2]
    me = lax.axis_index("tm")
    chip, core = lax.div(me, 2), lax.rem(me, 2)
    scales[...] = jnp.ones_like(scales)
    scales[me] = scale_ref[0]

    @pl.when(core == 0)
    def _():
        scales[me + 1] = scale_ref[1]

    more[...] = jnp.zeros_like(more)
    for d in range(pairs):
        far_chip = lax.bitwise_xor(chip, d + 1)
        late = near[d].shape[1] - 2 * ROWS

        @pl.when(chip < far_chip)
        def _():
            rows = decode_rows(near[d][0, late:], HALF_UNIT) + decode_rows(
                away[d][0, late:], HALF_UNIT
            )
            straight, crossed = 2 * far_chip + core, 2 * far_chip + 1 - core
            set_scale(scales.at[straight], rows, 0)
            set_scale(scales.at[crossed], rows, 1)
            unpack(decode(near[d][0, :late]), turned)
            more[crossed] = turned[...].T * down_ref[...]

    copies = []
    for i, rows in enumerate((pl.ds(0, panel // 2), pl.ds(panel // 2, panel - panel // 2))):
        for u in range(2, steps):
            tile = (tiles[u, rows] + more[u, rows]) * scales[u, 0:1]
            ready[rows, (u - 2) * panel:(u - 1) * panel] = tile
        there = out_ref.at[0, rows, pl.ds(2 * panel, (steps - 2) * panel)]
        copies.append(pltpu.make_async_copy(ready.at[rows], there, sems.at[i]))
        copies[-1].start()
    for copy in copies:
        copy.wait()


def call(kernel, outs, ins, scratch=(), flops=0, in_hbm=0, out_hbm=0, goes_on=None, free=False):
    moved = 0 if free else sum(math.prod(x.shape) * x.dtype.itemsize for x in (*outs, *ins))
    many = isinstance(outs, list)
    specs = [SMEM if x.ndim == 1 else VMEM for x in (*ins, *outs)]
    specs[:in_hbm] = [HBM] * in_hbm
    specs[len(specs) - out_hbm:] = [HBM] * out_hbm
    if goes_on is not None:
        specs[goes_on] = HBM
    ins = [
        pltpu.with_memory_space_constraint(x, pltpu.HBM) if i < in_hbm else x
        for i, x in enumerate(ins)
    ]
    return pl.pallas_call(
        kernel,
        out_shape=outs if many else outs[0],
        in_specs=specs[:len(ins)],
        out_specs=specs[len(ins):] if many else specs[-1],
        scratch_shapes=scratch,
        input_output_aliases={} if goes_on is None else {goes_on: len(outs) - 1},
        compiler_params=pltpu.CompilerParams(vmem_limit_bytes=48 * 2**20),
        cost_estimate=pl.CostEstimate(flops=flops, bytes_accessed=moved, transcendentals=0),
    )(*ins)


def on_device(intensity, block_cycle, cycle_order):
    panel = intensity.shape[0]
    blk_dev = block_cycle.shape[0]
    cycles = cycle_order.shape[0]
    groups = lax.axis_size("blk")
    steps = lax.axis_size("tm")
    inner = groups // 2
    pairs = steps // 2 - 1
    cap = 2 * max(1, blk_dev // cycles)
    early = packed_rows(panel, panel, True) + packed_rows(panel // 2, panel)
    first = panel // LANES * LANES
    pieces = [n for n in (first, panel - first) if n]
    late = [panel * n // LANES for n in pieces]
    early_sent = max(early, min(2 * pairs * late[0], 2 * early)) + 2 * ROWS

    def hop(x, by_blk, by_tm, sends=lambda t: True):
        perm = [
            (b * steps + t, (b ^ by_blk) * steps + (t ^ by_tm))
            for b in range(groups)
            for t in range(steps)
            if sends(t)
        ]
        return lax.ppermute(x, ("blk", "tm"), perm)

    offsets = range(1, pairs + 1)
    other = hop(intensity, 0, 1)
    sent = intensity[first:] if len(pieces) > 1 else intensity
    far = [[hop(sent, 0, 2 * d) for d in offsets]]
    f32, i16 = jnp.float32, jnp.int16
    shape = jax.ShapeDtypeStruct
    depth = cap * BLOCK
    work = 2 * cycles * panel * panel * depth
    table, gathers, own_rows, *made = call(
        functools.partial(early_kernel, cap),
        [
            shape((cycles * (cap + 1),), jnp.int32),
            shape((2, inner, 2, panel, depth), jnp.bfloat16),
            shape((2, ROWS, LANES), f32),
            *[shape((n, intensity.shape[1]), jnp.bfloat16) for n in pieces[:-1]],
            shape((2, early, LANES), f32),
            *[shape((2, early + 2 * ROWS, LANES), i16)] * (inner - 1),
        ],
        (block_cycle, cycle_order, intensity, other),
        [
            pltpu.SMEM(cycle_order.shape, jnp.int32),
            pltpu.SMEM(block_cycle.shape, jnp.int32),
            pltpu.SMEM(cycle_order.shape, jnp.int32),
            pltpu.VMEM(intensity.shape, jnp.bfloat16),
            pltpu.VMEM((2, -(-cycles // 16) * 16, panel), f32),
            pltpu.SemaphoreType.DMA((3,)),
        ],
        2 * work,
        3,
    )
    far += [[hop(x, 0, 2 * d) for d in offsets] for x in made[:-inner]]

    def exchange(made):
        order = sorted(range(inner), key=lambda k: (k > 0, -k.bit_count()))
        return [hop(made[k], k, 0) if k else made[k] for k in order]

    parts = exchange(made[-inner:])
    home, home_rows, away = call(
        early_sum_kernel,
        [
            shape((early, LANES), f32),
            shape((ROWS, LANES), f32),
            shape((early_sent, LANES), i16),
        ],
        (parts[0], own_rows, *parts[1:]),
        flops=0,
    )
    came = hop(away, inner, 0)

    parts, after = [], ()
    for rows, came_rows in zip(reversed(late), far):
        made = call(
            functools.partial(late_kernel, cap, len(after)),
            [shape((2, pairs, rows, LANES), i16 if k else f32) for k in range(inner)],
            (table, gathers, *after, *came_rows),
            flops=(0 if after else 16) * pairs * work,
        )
        parts = exchange(made) + parts
        after = (away, *parts[1:inner])
    late_home, near, late_away = call(
        functools.partial(late_sum_kernel, len(pieces), early),
        [
            shape((pairs, sum(late), LANES), f32),
            shape((pairs, sum(late) + 2 * ROWS, LANES), i16),
            shape((pairs, sum(late) + 2 * ROWS, LANES), i16),
        ],
        (came, home_rows, away, *parts),
    )

    def is_lower(t, d):
        return t // 2 < (t // 2 ^ d)

    from_away = [
        hop(late_away[d - 1:d], inner, 2 * d, lambda t, d=d: not is_lower(t, d)) for d in offsets
    ]
    from_near = [hop(near[d - 1:d], 0, 2 * d) for d in offsets]
    across = hop(late_away, inner, 0, lambda t: any(is_lower(t, d) for d in offsets))
    own_tile, part, code, down, scale = call(
        early_end_kernel,
        [
            shape((panel, panel), f32),
            shape((panel // 2, panel), f32),
            shape((packed_rows(panel // 2, panel), LANES), i16),
            shape((panel, panel), f32),
            shape((2, 8, panel), f32),
        ],
        (home, home_rows, came, late_away),
    )
    mate_part = hop(code, 0, 1)
    whole = shape((1, panel, steps * panel), f32)
    pair, begun = call(
        begin_kernel,
        [shape((2, panel, panel), f32), whole],
        (own_tile, part, mate_part, down, scale),
        [pltpu.VMEM((panel, 2 * panel), f32), pltpu.SemaphoreType.DMA],
        out_hbm=1,
        free=True,
    )
    tiles = call(
        functools.partial(middle_kernel, pairs),
        (shape((steps, panel, panel), f32),),
        (pair, down, late_home, *from_away, across),
        [pltpu.VMEM((panel, panel), f32)],
    )
    return call(
        functools.partial(last_kernel, pairs),
        (whole,),
        (tiles, down, scale, begun, *from_near, *from_away),
        [
            pltpu.VMEM((steps, 8, panel), f32),
            pltpu.VMEM((steps, panel, panel), f32),
            pltpu.VMEM((panel, panel), f32),
            pltpu.VMEM((panel, (steps - 2) * panel), f32),
            pltpu.SemaphoreType.DMA((2,)),
        ],
        out_hbm=1,
        goes_on=3,
    )


def solution(mesh):
    placed = (P("tm", "blk"), P("blk"), P())
    return jax.shard_map(
        on_device, mesh=mesh, in_specs=placed, out_specs=P("blk", "tm", None), check_vma=False
    )
```

```python
import functools
import math

import jax
import jax.numpy as jnp
from jax import lax
from jax.experimental import pallas as pl
from jax.experimental.pallas import tpu as pltpu
from jax.sharding import PartitionSpec as P

BLOCK = 128
LANES = 128
ROWS = 8
NONE = -32768
LEAST, MOST = -3.0, 29.0
PER_OCTAVE = 65534 / (MOST - LEAST)
MIDDLE = (MOST + LEAST) / 2
PART_UNIT, HALF_UNIT = 8192.0, 2048.0
LOW = 1 << 16
VMEM = pl.BlockSpec(memory_space=pltpu.VMEM)
SMEM = pl.BlockSpec(memory_space=pltpu.SMEM)
HBM = pl.BlockSpec(memory_space=pltpu.HBM)


def times(left, right):
    return lax.dot_general(
        left, right, (((1,), (1,)), ((), ())), preferred_element_type=jnp.float32
    )


def encode(x):
    level = jnp.log(jnp.maximum(x, 2.0**LEAST)) * (PER_OCTAVE / math.log(2))
    code = (level + (0.5 - LEAST * PER_OCTAVE)).astype(jnp.int32) + (NONE + 1)
    return jnp.where(x[..., :1, :] > 0, code, NONE).astype(jnp.int16)


def decode(code):
    code = code.astype(jnp.int32)
    level = code.astype(jnp.float32) * (math.log(2) / PER_OCTAVE) + MIDDLE * math.log(2)
    return jnp.where(code[..., :1, :] > NONE, jnp.exp(level), 0.0)


def split(panel):
    whole, rest = divmod(panel, LANES)
    return whole, LANES // rest if rest else 0


def packed_rows(rows, panel, symmetric=False):
    whole, fold = split(panel)
    if symmetric and (whole, fold) == (1, 2):
        return LANES + LANES // 2
    body = sum((i + 1) * LANES if symmetric else rows for i in range(whole))
    return body + (rows // fold if fold else 0)


def pack(tile, symmetric=False):
    rows, panel = tile.shape
    whole, fold = split(panel)
    if symmetric and (whole, fold) == (1, 2):
        n = LANES // 2
        left, right = tile[:, :LANES], tile[:, LANES:]
        parts = [
            left[:n],
            jnp.concatenate([right[:n], left[n:2 * n, n:]], axis=1),
            jnp.concatenate([right[n:2 * n], right[2 * n:]], axis=1),
        ]
        return jnp.concatenate(parts, axis=0)
    parts = [
        tile[: (i + 1) * LANES if symmetric else rows, i * LANES:(i + 1) * LANES]
        for i in range(whole)
    ]
    if fold:
        n = rows // fold
        left = [tile[i * n:(i + 1) * n, whole * LANES:] for i in range(fold)]
        parts.append(jnp.concatenate(left, axis=1))
    return jnp.concatenate(parts, axis=0)


def unpack(x, out, symmetric=False):
    rows, panel = out.shape
    whole, fold = split(panel)
    if symmetric and (whole, fold) == (1, 2):
        n = LANES // 2
        out[:n, :LANES] = x[:n]
        out[:n, LANES:] = x[n:2 * n, :n]
        out[n:2 * n, n:LANES] = x[n:2 * n, n:]
        out[n:2 * n, LANES:] = x[2 * n:, :n]
        out[2 * n:, LANES:] = x[2 * n:, n:]
        out[n:2 * n, :n] = x[:n, n:].T
        out[2 * n:, :LANES] = out[:2 * n, LANES:].T
        return
    at = 0
    for i in range(whole):
        n = (i + 1) * LANES if symmetric else rows
        out[:n, i * LANES:(i + 1) * LANES] = x[at:at + n]
        at += n
    if fold:
        n, width = rows // fold, LANES // fold
        for i in range(fold):
            out[i * n:(i + 1) * n, whole * LANES:] = x[at:, i * width:(i + 1) * width]
    if symmetric:
        for i in range(whole):
            n = (i + 1) * LANES
            if n < panel:
                out[n:, i * LANES:n] = out[i * LANES:n, n:].T


def rows_of(sums, count):
    panel = sums[0].shape[1]
    row = lax.broadcasted_iota(jnp.int32, (ROWS, LANES), 0)
    out, at = jnp.zeros((ROWS, LANES), jnp.float32), 0
    for x in sums:
        for start in range(0, panel, LANES):
            piece = x[:, start:start + LANES]
            if piece.shape[1] < LANES:
                piece = jnp.concatenate([piece] * (LANES // piece.shape[1]), axis=1)
            out = jnp.where(row == at, piece, out)
            at += 1
    return jnp.where(row == at, count, out)


def sums_of(rows, panel, which):
    per = -(-panel // LANES)
    starts = range(0, panel, LANES)
    return [
        (start, rows[which * per + i:which * per + i + 1, :min(LANES, panel - start)])
        for i, start in enumerate(starts)
    ]


def encode_rows(rows, unit):
    whole = (rows * unit + 0.5).astype(jnp.int32)
    high = lax.shift_right_logical(whole, 16)
    low = lax.bitwise_and(whole, LOW - 1) - LOW // 2
    return jnp.concatenate([high, low], axis=0).astype(jnp.int16)


def decode_rows(code, unit):
    x = code.astype(jnp.int32).astype(jnp.float32)
    return (x[:ROWS] * float(LOW) + (x[ROWS:] + LOW / 2)) * (1 / unit)


def find_slots(cap, cycle_ref, order_ref, where_ref, table_ref):
    cycles = order_ref.shape[0]
    for s in range(cycles):
        where_ref[order_ref[s]] = s
        table_ref[s] = 0
    for s in range(cycles * cap):
        table_ref[cycles + s] = 0
    for j in range(cycle_ref.shape[0]):
        p = where_ref[cycle_ref[j]]
        r = table_ref[p]
        table_ref[cycles + p * cap + r] = j
        table_ref[p] = r + 1


def gathered(ref, s, cap, table_ref, masked):
    cycles = table_ref.shape[0] // (cap + 1)
    parts = []
    for r in range(cap):
        j = table_ref[cycles + s * cap + r]
        x = ref[:, pl.ds(pl.multiple_of(j * BLOCK, BLOCK), BLOCK)]
        parts.append(jnp.where(r < table_ref[s], x, jnp.zeros_like(x)) if masked else x)
    return jnp.concatenate(parts, axis=1)


def early_kernel(cap, cycle_hbm, order_hbm, own_hbm, other_ref, *refs):
    table_ref, sorted_ref, rows_ref, *outs = refs[:-6]
    where_ref, cycle_ref, order_ref, own_ref, sums_ref, sems = refs[-6:]
    pairs = ((cycle_hbm, cycle_ref), (order_hbm, order_ref), (own_hbm, own_ref))
    copies = [pltpu.make_async_copy(*pair, sems.at[i]) for i, pair in enumerate(pairs)]
    for copy in copies:
        copy.start()
    copies[0].wait()
    copies[1].wait()
    find_slots(cap, cycle_ref, order_ref, where_ref, table_ref)
    inner = len(outs)
    panel = own_ref.shape[0]
    half = panel // 2
    mine = lax.rem(lax.axis_index("blk"), inner)
    first = lax.rem(lax.axis_index("tm"), 2) == 0
    body = outs[0].shape[1]
    row = lax.broadcasted_iota(jnp.int32, (sums_ref.shape[1], BLOCK), 0)
    members = jnp.concatenate(
        [
            jnp.where(row == where_ref[cycle_ref[j]], 1.0, 0.0).astype(jnp.bfloat16)
            for j in range(cycle_ref.shape[0])
        ],
        axis=1,
    )
    each = [(k, h, h * inner + lax.bitwise_xor(mine, k)) for k in range(inner) for h in range(2)]
    for k, h, s in each:
        sorted_ref[1, k, h] = gathered(other_ref, s, cap, table_ref, True)
    sums_ref[1] = times(members, other_ref[...])
    copies[2].wait()
    sums_ref[0] = times(members, own_ref[...])
    for k, h, s in each:
        own, other = gathered(own_ref, s, cap, table_ref, True), sorted_ref[1, k, h]
        sorted_ref[0, k, h] = own
        left = jnp.where(first, own[:half], other[half:])
        right = jnp.where(first, other, own)
        rows = rows_of([sums_ref[i, pl.ds(s, 1)] for i in range(2)], table_ref[s].astype(jnp.float32))
        found = jnp.concatenate([pack(times(own, own), True), pack(times(left, right))], axis=0)
        if k:
            outs[k][h, :body] = encode(found)
            outs[k][h, body:] = encode_rows(rows, PART_UNIT)
        else:
            outs[k][h] = found
            rows_ref[h] = rows


def late_kernel(cap, which, after, table_ref, sorted_ref, *refs):
    refs = refs[after:]
    inner = lax.axis_size("blk") // 2
    came, outs = refs[:-inner], refs[-inner:]
    mine = lax.rem(lax.axis_index("blk"), inner)
    chip = lax.div(lax.axis_index("tm"), 2)

    @pl.when(lax.rem(lax.axis_index("tm"), 2) == which)
    def _():
        for k in range(inner):
            for h in range(2):
                s = h * inner + lax.bitwise_xor(mine, k)
                for d, ref in enumerate(came):
                    upper = (chip > lax.bitwise_xor(chip, d + 1)).astype(jnp.int32)
                    far = gathered(ref, s, cap, table_ref, False)
                    tile = pack(times(sorted_ref[upper, k, h], far))
                    outs[k][h, d] = encode(tile) if k else tile


def early_sum_kernel(own_ref, own_rows_ref, *refs):
    *parts, home_ref, rows_ref, away_ref = refs
    body = home_ref.shape[0]
    side = lax.div(lax.axis_index("blk"), lax.axis_size("blk") // 2)

    def total(h):
        tiles, rows = own_ref[h], own_rows_ref[h]
        for part in parts:
            tiles = tiles + decode(part[h, :body])
            rows = rows + decode_rows(part[h, body:], PART_UNIT)
        return tiles, rows

    home_ref[...], rows_ref[...] = total(side)
    tiles, rows = total(1 - side)
    away_ref[:body], away_ref[body:] = encode(tiles), encode_rows(rows, HALF_UNIT)


def late_sum_kernel(home_rows_ref, early_away_ref, *refs):
    *parts, home_ref, near_ref, away_ref = refs
    inner = len(parts) // 2
    pairs, body = home_ref.shape[:2]
    side = lax.div(lax.axis_index("blk"), lax.axis_size("blk") // 2)
    core = lax.rem(lax.axis_index("tm"), 2)
    near_rows = encode_rows(home_rows_ref[...], HALF_UNIT)
    away_rows = early_away_ref[-2 * ROWS:]
    for which in range(2):
        own, *came = parts[which * inner:(which + 1) * inner]

        @pl.when(core == which)
        def _():
            for d in range(pairs):
                home, away = own[side, d], own[1 - side, d]
                for part in came:
                    home = home + decode(part[side, d])
                    away = away + decode(part[1 - side, d])
                home_ref[d] = home
                near_ref[d, :body], near_ref[d, body:] = encode(home), near_rows
                away_ref[d, :body], away_ref[d, body:] = encode(away), away_rows


def set_scale(ref, rows, which):
    for start, x in sums_of(rows, ref.shape[1], which):
        ref[0:1, start:start + x.shape[1]] = 1.0 / x


def early_end_kernel(
    home_ref, rows_ref, came_ref, after_ref, own_ref, part_ref, code_ref, down_ref, scale_ref
):
    half, panel = part_ref.shape
    body, diagonal = home_ref.shape[0], packed_rows(panel, panel, True)
    rows = rows_ref[...] + decode_rows(came_ref[body:], HALF_UNIT)
    part = home_ref[diagonal:] + decode(came_ref[diagonal:body])
    code_ref[...] = encode(part)
    unpack(part, part_ref)
    unpack(home_ref[:diagonal] + decode(came_ref[:diagonal]), own_ref, True)
    at = 2 * -(-panel // LANES)
    count = rows[at:at + 1, 0:1] * float(BLOCK)
    for which in range(2):
        set_scale(scale_ref.at[which], rows, which)
    down = jnp.broadcast_to(scale_ref[0, 0:1] * count, (panel, panel)).T
    down_ref[...] = down


def begin_kernel(own_ref, part_ref, mate_part_ref, down_ref, scale_ref, pair_ref, out_ref, ready, sem):
    panel = down_ref.shape[0]
    half = panel // 2
    me = lax.axis_index("tm")
    chip, core = lax.div(me, 2), lax.rem(me, 2)
    down = down_ref[...]
    pair_ref[0] = own_ref[...] * down
    mate = pair_ref.at[1]
    unpack(decode(mate_part_ref[...]), mate.at[pl.ds(half, panel - half)])
    mate[:half] = part_ref[...] * down[:half]
    mate[half:] = mate[half:] * down[half:]
    for u in range(2):
        here = slice(u * panel, (u + 1) * panel)

        @pl.when(jnp.logical_and(chip == 0, core <= u))
        def _():
            which = u - core
            ready[:, here] = pair_ref[which] * scale_ref[which, 0:1]

        @pl.when(jnp.logical_or(chip > 0, core > u))
        def _():
            ready[:, here] = jnp.zeros((panel, panel), jnp.float32)

    copy = pltpu.make_async_copy(ready, out_ref.at[0, :, pl.ds(0, 2 * panel)], sem)
    copy.start()
    copy.wait()


def middle_kernel(pairs, pair_ref, down_ref, late_ref, *refs):
    away, across_ref, tiles, turned = refs[:pairs], *refs[pairs:]
    late = late_ref.shape[1]
    me = lax.axis_index("tm")
    chip, core = lax.div(me, 2), lax.rem(me, 2)
    down = down_ref[...]
    tiles[...] = jnp.zeros_like(tiles)
    tiles[me] = pair_ref[0]

    @pl.when(core == 0)
    def _():
        tiles[me + 1] = pair_ref[1]

    for d in range(pairs):
        far_chip = lax.bitwise_xor(chip, d + 1)

        @pl.when(chip < far_chip)
        def _():
            unpack(late_ref[d] + decode(across_ref[d, :late]), turned)
            tiles[2 * far_chip + core] = turned[...] * down
            unpack(decode(away[d][0, :late]), turned)
            tiles[2 * far_chip + 1 - core] = turned[...].T * down


def last_kernel(pairs, tiles, down_ref, scale_ref, begun_ref, *refs):
    near, away = refs[:pairs], refs[pairs:2 * pairs]
    out_ref, scales, more, turned, ready, sems = refs[2 * pairs:]
    steps, panel = tiles.shape[:2]
    me = lax.axis_index("tm")
    chip, core = lax.div(me, 2), lax.rem(me, 2)
    scales[...] = jnp.ones_like(scales)
    scales[me] = scale_ref[0]

    @pl.when(core == 0)
    def _():
        scales[me + 1] = scale_ref[1]

    more[...] = jnp.zeros_like(more)
    for d in range(pairs):
        far_chip = lax.bitwise_xor(chip, d + 1)
        late = near[d].shape[1] - 2 * ROWS

        @pl.when(chip < far_chip)
        def _():
            rows = decode_rows(near[d][0, late:], HALF_UNIT) + decode_rows(
                away[d][0, late:], HALF_UNIT
            )
            straight, crossed = 2 * far_chip + core, 2 * far_chip + 1 - core
            set_scale(scales.at[straight], rows, 0)
            set_scale(scales.at[crossed], rows, 1)
            unpack(decode(near[d][0, :late]), turned)
            more[crossed] = turned[...].T * down_ref[...]

    copies = []
    for i, rows in enumerate((pl.ds(0, panel // 2), pl.ds(panel // 2, panel - panel // 2))):
        for u in range(2, steps):
            tile = (tiles[u, rows] + more[u, rows]) * scales[u, 0:1]
            ready[rows, (u - 2) * panel:(u - 1) * panel] = tile
        there = out_ref.at[0, rows, pl.ds(2 * panel, (steps - 2) * panel)]
        copies.append(pltpu.make_async_copy(ready.at[rows], there, sems.at[i]))
        copies[-1].start()
    for copy in copies:
        copy.wait()


def call(kernel, outs, ins, scratch=(), flops=0, in_hbm=0, out_hbm=0, goes_on=None, free=False):
    moved = 0 if free else sum(math.prod(x.shape) * x.dtype.itemsize for x in (*outs, *ins))
    many = isinstance(outs, list)
    specs = [SMEM if x.ndim == 1 else VMEM for x in (*ins, *outs)]
    specs[:in_hbm] = [HBM] * in_hbm
    specs[len(specs) - out_hbm:] = [HBM] * out_hbm
    if goes_on is not None:
        specs[goes_on] = HBM
    ins = [
        pltpu.with_memory_space_constraint(x, pltpu.HBM) if i < in_hbm else x
        for i, x in enumerate(ins)
    ]
    return pl.pallas_call(
        kernel,
        out_shape=outs if many else outs[0],
        in_specs=specs[:len(ins)],
        out_specs=specs[len(ins):] if many else specs[-1],
        scratch_shapes=scratch,
        input_output_aliases={} if goes_on is None else {goes_on: len(outs) - 1},
        compiler_params=pltpu.CompilerParams(vmem_limit_bytes=48 * 2**20),
        cost_estimate=pl.CostEstimate(flops=flops, bytes_accessed=moved, transcendentals=0),
    )(*ins)


def on_device(intensity, block_cycle, cycle_order):
    panel = intensity.shape[0]
    blk_dev = block_cycle.shape[0]
    cycles = cycle_order.shape[0]
    groups = lax.axis_size("blk")
    steps = lax.axis_size("tm")
    inner = groups // 2
    pairs = steps // 2 - 1
    cap = 2 * max(1, blk_dev // cycles)
    early = packed_rows(panel, panel, True) + packed_rows(panel // 2, panel)
    late = packed_rows(panel, panel)

    def hop(x, by_blk, by_tm, sends=lambda t: True):
        perm = [
            (b * steps + t, (b ^ by_blk) * steps + (t ^ by_tm))
            for b in range(groups)
            for t in range(steps)
            if sends(t)
        ]
        return lax.ppermute(x, ("blk", "tm"), perm)

    offsets = range(1, pairs + 1)
    other = hop(intensity, 0, 1)
    far = [
        [hop(intensity, 0, 2 * d, lambda t, c=c: t % 2 == c) for d in offsets] for c in range(2)
    ]
    f32, i16 = jnp.float32, jnp.int16
    shape = jax.ShapeDtypeStruct
    depth = cap * BLOCK
    work = 2 * cycles * panel * panel * depth
    table, gathers, own_rows, *made = call(
        functools.partial(early_kernel, cap),
        [
            shape((cycles * (cap + 1),), jnp.int32),
            shape((2, inner, 2, panel, depth), jnp.bfloat16),
            shape((2, ROWS, LANES), f32),
            shape((2, early, LANES), f32),
            *[shape((2, early + 2 * ROWS, LANES), i16)] * (inner - 1),
        ],
        (block_cycle, cycle_order, intensity, other),
        [
            pltpu.SMEM(cycle_order.shape, jnp.int32),
            pltpu.SMEM(block_cycle.shape, jnp.int32),
            pltpu.SMEM(cycle_order.shape, jnp.int32),
            pltpu.VMEM(intensity.shape, jnp.bfloat16),
            pltpu.VMEM((2, -(-cycles // 16) * 16, panel), f32),
            pltpu.SemaphoreType.DMA((3,)),
        ],
        2 * work,
        3,
    )

    def exchange(made, sends=lambda t: True):
        order = sorted(range(inner), key=lambda k: (k > 0, -k.bit_count()))
        return [hop(made[k], k, 0, sends) if k else made[k] for k in order]

    parts = exchange(made)
    home, home_rows, away = call(
        early_sum_kernel,
        [
            shape((early, LANES), f32),
            shape((ROWS, LANES), f32),
            shape((early + 2 * ROWS, LANES), i16),
        ],
        (parts[0], own_rows, *parts[1:]),
        flops=32 * work,
    )
    came = hop(away, inner, 0)

    parts, after = [], ()
    for which, came_panels in enumerate(far):
        made = call(
            functools.partial(late_kernel, cap, which, len(after)),
            [shape((2, pairs, late, LANES), i16 if k else f32) for k in range(inner)],
            (table, gathers, *after, *came_panels),
            flops=pairs * work,
        )
        parts += exchange(made, lambda t, c=which: t % 2 == c)
        after = (away, made[1])
    late_home, near, late_away = call(
        late_sum_kernel,
        [
            shape((pairs, late, LANES), f32),
            shape((pairs, late + 2 * ROWS, LANES), i16),
            shape((pairs, late + 2 * ROWS, LANES), i16),
        ],
        (home_rows, away, *parts),
        flops=32 * work,
    )

    def is_lower(t, d):
        return t // 2 < (t // 2 ^ d)

    from_away = [
        hop(late_away[d - 1:d], inner, 2 * d, lambda t, d=d: not is_lower(t, d)) for d in offsets
    ]
    from_near = [hop(near[d - 1:d], 0, 2 * d) for d in offsets]
    across = hop(late_away, inner, 0, lambda t: any(is_lower(t, d) for d in offsets))
    own_tile, part, code, down, scale = call(
        early_end_kernel,
        [
            shape((panel, panel), f32),
            shape((panel // 2, panel), f32),
            shape((packed_rows(panel // 2, panel), LANES), i16),
            shape((panel, panel), f32),
            shape((2, 8, panel), f32),
        ],
        (home, home_rows, came, late_away),
    )
    mate_part = hop(code, 0, 1)
    whole = shape((1, panel, steps * panel), f32)
    pair, begun = call(
        begin_kernel,
        [shape((2, panel, panel), f32), whole],
        (own_tile, part, mate_part, down, scale),
        [pltpu.VMEM((panel, 2 * panel), f32), pltpu.SemaphoreType.DMA],
        out_hbm=1,
        free=True,
    )
    tiles = call(
        functools.partial(middle_kernel, pairs),
        (shape((steps, panel, panel), f32),),
        (pair, down, late_home, *from_away, across),
        [pltpu.VMEM((panel, panel), f32)],
    )
    return call(
        functools.partial(last_kernel, pairs),
        (whole,),
        (tiles, down, scale, begun, *from_near, *from_away),
        [
            pltpu.VMEM((steps, 8, panel), f32),
            pltpu.VMEM((steps, panel, panel), f32),
            pltpu.VMEM((panel, panel), f32),
            pltpu.VMEM((panel, (steps - 2) * panel), f32),
            pltpu.SemaphoreType.DMA((2,)),
        ],
        out_hbm=1,
        goes_on=3,
    )


def solution(mesh):
    placed = (P("tm", "blk"), P("blk"), P())
    return jax.shard_map(
        on_device, mesh=mesh, in_specs=placed, out_specs=P("blk", "tm", None), check_vma=False
    )
```

```python
import functools
import math

import jax
import jax.numpy as jnp
from jax import lax
from jax.experimental import pallas as pl
from jax.experimental.pallas import tpu as pltpu
from jax.sharding import PartitionSpec as P

BLOCK = 128
LANES = 128
ROWS = 8
NONE = -32768
LEAST, MOST = -3.0, 29.0
PER_OCTAVE = 65534 / (MOST - LEAST)
MIDDLE = (MOST + LEAST) / 2
PART_UNIT, HALF_UNIT = 8192.0, 2048.0
LOW = 1 << 16
VMEM = pl.BlockSpec(memory_space=pltpu.VMEM)
SMEM = pl.BlockSpec(memory_space=pltpu.SMEM)
HBM = pl.BlockSpec(memory_space=pltpu.HBM)


def times(left, right):
    return lax.dot_general(
        left, right, (((1,), (1,)), ((), ())), preferred_element_type=jnp.float32
    )


def encode(x):
    level = jnp.log(jnp.maximum(x, 2.0**LEAST)) * (PER_OCTAVE / math.log(2))
    code = (level + (0.5 - LEAST * PER_OCTAVE)).astype(jnp.int32) + (NONE + 1)
    return jnp.where(x[..., :1, :] > 0, code, NONE).astype(jnp.int16)


def decode(code):
    code = code.astype(jnp.int32)
    level = code.astype(jnp.float32) * (math.log(2) / PER_OCTAVE) + MIDDLE * math.log(2)
    return jnp.where(code[..., :1, :] > NONE, jnp.exp(level), 0.0)


def split(panel):
    whole, rest = divmod(panel, LANES)
    return whole, LANES // rest if rest else 0


def packed_rows(rows, panel, symmetric=False):
    whole, fold = split(panel)
    if symmetric and (whole, fold) == (1, 2):
        return LANES + LANES // 2
    body = sum((i + 1) * LANES if symmetric else rows for i in range(whole))
    return body + (rows // fold if fold else 0)


def pack(tile, symmetric=False):
    rows, panel = tile.shape
    whole, fold = split(panel)
    if symmetric and (whole, fold) == (1, 2):
        n = LANES // 2
        left, right = tile[:, :LANES], tile[:, LANES:]
        parts = [
            left[:n],
            jnp.concatenate([right[:n], left[n:2 * n, n:]], axis=1),
            jnp.concatenate([right[n:2 * n], right[2 * n:]], axis=1),
        ]
        return jnp.concatenate(parts, axis=0)
    parts = [
        tile[: (i + 1) * LANES if symmetric else rows, i * LANES:(i + 1) * LANES]
        for i in range(whole)
    ]
    if fold:
        n = rows // fold
        left = [tile[i * n:(i + 1) * n, whole * LANES:] for i in range(fold)]
        parts.append(jnp.concatenate(left, axis=1))
    return jnp.concatenate(parts, axis=0)


def unpack(x, out, symmetric=False):
    rows, panel = out.shape
    whole, fold = split(panel)
    if symmetric and (whole, fold) == (1, 2):
        n = LANES // 2
        out[:n, :LANES] = x[:n]
        out[:n, LANES:] = x[n:2 * n, :n]
        out[n:2 * n, n:LANES] = x[n:2 * n, n:]
        out[n:2 * n, LANES:] = x[2 * n:, :n]
        out[2 * n:, LANES:] = x[2 * n:, n:]
        out[n:2 * n, :n] = x[:n, n:].T
        out[2 * n:, :LANES] = out[:2 * n, LANES:].T
        return
    at = 0
    for i in range(whole):
        n = (i + 1) * LANES if symmetric else rows
        out[:n, i * LANES:(i + 1) * LANES] = x[at:at + n]
        at += n
    if fold:
        n, width = rows // fold, LANES // fold
        for i in range(fold):
            out[i * n:(i + 1) * n, whole * LANES:] = x[at:, i * width:(i + 1) * width]
    if symmetric:
        for i in range(whole):
            n = (i + 1) * LANES
            if n < panel:
                out[n:, i * LANES:n] = out[i * LANES:n, n:].T


def rows_of(sums, count):
    panel = sums[0].shape[1]
    row = lax.broadcasted_iota(jnp.int32, (ROWS, LANES), 0)
    out, at = jnp.zeros((ROWS, LANES), jnp.float32), 0
    for x in sums:
        for start in range(0, panel, LANES):
            piece = x[:, start:start + LANES]
            if piece.shape[1] < LANES:
                piece = jnp.concatenate([piece] * (LANES // piece.shape[1]), axis=1)
            out = jnp.where(row == at, piece, out)
            at += 1
    return jnp.where(row == at, count, out)


def sums_of(rows, panel, which):
    per = -(-panel // LANES)
    starts = range(0, panel, LANES)
    return [
        (start, rows[which * per + i:which * per + i + 1, :min(LANES, panel - start)])
        for i, start in enumerate(starts)
    ]


def encode_rows(rows, unit):
    whole = (rows * unit + 0.5).astype(jnp.int32)
    high = lax.shift_right_logical(whole, 16)
    low = lax.bitwise_and(whole, LOW - 1) - LOW // 2
    return jnp.concatenate([high, low], axis=0).astype(jnp.int16)


def decode_rows(code, unit):
    x = code.astype(jnp.int32).astype(jnp.float32)
    return (x[:ROWS] * float(LOW) + (x[ROWS:] + LOW / 2)) * (1 / unit)


def find_slots(cap, cycle_ref, order_ref, where_ref, table_ref):
    cycles = order_ref.shape[0]
    for s in range(cycles):
        where_ref[order_ref[s]] = s
        table_ref[s] = 0
    for s in range(cycles * cap):
        table_ref[cycles + s] = 0
    for j in range(cycle_ref.shape[0]):
        p = where_ref[cycle_ref[j]]
        r = table_ref[p]
        table_ref[cycles + p * cap + r] = j
        table_ref[p] = r + 1


def gathered(ref, s, cap, table_ref, masked):
    cycles = table_ref.shape[0] // (cap + 1)
    parts = []
    for r in range(cap):
        j = table_ref[cycles + s * cap + r]
        x = ref[:, pl.ds(pl.multiple_of(j * BLOCK, BLOCK), BLOCK)]
        parts.append(jnp.where(r < table_ref[s], x, jnp.zeros_like(x)) if masked else x)
    return jnp.concatenate(parts, axis=1)


def early_kernel(cap, cycle_hbm, order_hbm, own_hbm, other_ref, *refs):
    table_ref, sorted_ref, rows_ref, *outs = refs[:-6]
    where_ref, cycle_ref, order_ref, own_ref, sums_ref, sems = refs[-6:]
    pairs = ((cycle_hbm, cycle_ref), (order_hbm, order_ref), (own_hbm, own_ref))
    copies = [pltpu.make_async_copy(*pair, sems.at[i]) for i, pair in enumerate(pairs)]
    for copy in copies:
        copy.start()
    copies[0].wait()
    copies[1].wait()
    find_slots(cap, cycle_ref, order_ref, where_ref, table_ref)
    inner = lax.axis_size("blk") // 2
    pieces, outs = outs[:-inner], outs[-inner:]
    panel = own_ref.shape[0]
    half = panel // 2
    mine = lax.rem(lax.axis_index("blk"), inner)
    first = lax.rem(lax.axis_index("tm"), 2) == 0
    body = outs[0].shape[1]
    row = lax.broadcasted_iota(jnp.int32, (sums_ref.shape[1], BLOCK), 0)
    members = jnp.concatenate(
        [
            jnp.where(row == where_ref[cycle_ref[j]], 1.0, 0.0).astype(jnp.bfloat16)
            for j in range(cycle_ref.shape[0])
        ],
        axis=1,
    )
    each = [(k, h, h * inner + lax.bitwise_xor(mine, k)) for k in range(inner) for h in range(2)]
    for k, h, s in each:
        sorted_ref[1, k, h] = gathered(other_ref, s, cap, table_ref, True)
    sums_ref[1] = times(members, other_ref[...])
    copies[2].wait()
    for piece in pieces:
        piece[...] = own_ref[panel - piece.shape[0]:]
    sums_ref[0] = times(members, own_ref[...])
    for k, h, s in each:
        own, other = gathered(own_ref, s, cap, table_ref, True), sorted_ref[1, k, h]
        sorted_ref[0, k, h] = own
        left = jnp.where(first, own[:half], other[half:])
        right = jnp.where(first, other, own)
        rows = rows_of([sums_ref[i, pl.ds(s, 1)] for i in range(2)], table_ref[s].astype(jnp.float32))
        found = jnp.concatenate([pack(times(own, own), True), pack(times(left, right))], axis=0)
        if k:
            outs[k][h, :body] = encode(found)
            outs[k][h, body:] = encode_rows(rows, PART_UNIT)
        else:
            outs[k][h] = found
            rows_ref[h] = rows


def late_kernel(cap, after, table_ref, sorted_ref, *refs):
    refs = refs[after:]
    inner = lax.axis_size("blk") // 2
    came, outs = refs[:-inner], refs[-inner:]
    mine = lax.rem(lax.axis_index("blk"), inner)
    chip = lax.div(lax.axis_index("tm"), 2)
    for k in range(inner):
        for h in range(2):
            s = h * inner + lax.bitwise_xor(mine, k)
            for d, ref in enumerate(came):
                upper = (chip > lax.bitwise_xor(chip, d + 1)).astype(jnp.int32)
                far = gathered(ref, s, cap, table_ref, False)
                tile = pack(times(sorted_ref[upper, k, h], far))
                outs[k][h, d] = encode(tile) if k else tile


def early_sum_kernel(own_ref, own_rows_ref, *refs):
    *parts, home_ref, rows_ref, away_ref = refs
    body = home_ref.shape[0]
    side = lax.div(lax.axis_index("blk"), lax.axis_size("blk") // 2)

    def total(h):
        tiles, rows = own_ref[h], own_rows_ref[h]
        for part in parts:
            tiles = tiles + decode(part[h, :body])
            rows = rows + decode_rows(part[h, body:], PART_UNIT)
        return tiles, rows

    home_ref[...], rows_ref[...] = total(side)
    tiles, rows = total(1 - side)
    away_ref[:body], away_ref[body:] = encode(tiles), encode_rows(rows, HALF_UNIT)


def late_sum_kernel(pieces, home_rows_ref, early_away_ref, *refs):
    *parts, home_ref, near_ref, away_ref = refs
    inner = len(parts) // pieces
    pairs, body = home_ref.shape[:2]
    side = lax.div(lax.axis_index("blk"), lax.axis_size("blk") // 2)
    near_rows = encode_rows(home_rows_ref[...], HALF_UNIT)
    away_rows = early_away_ref[-2 * ROWS:]
    for d in range(pairs):
        at = 0
        for piece in range(pieces):
            own, *came = parts[piece * inner:(piece + 1) * inner]
            here = pl.ds(at, own.shape[2])
            at += own.shape[2]
            home, away = own[side, d], own[1 - side, d]
            for part in came:
                home = home + decode(part[side, d])
                away = away + decode(part[1 - side, d])
            home_ref[d, here] = home
            near_ref[d, here] = encode(home)
            away_ref[d, here] = encode(away)
        near_ref[d, body:], away_ref[d, body:] = near_rows, away_rows


def set_scale(ref, rows, which):
    for start, x in sums_of(rows, ref.shape[1], which):
        ref[0:1, start:start + x.shape[1]] = 1.0 / x


def early_end_kernel(
    home_ref, rows_ref, came_ref, after_ref, own_ref, part_ref, code_ref, down_ref, scale_ref
):
    half, panel = part_ref.shape
    body, diagonal = home_ref.shape[0], packed_rows(panel, panel, True)
    rows = rows_ref[...] + decode_rows(came_ref[body:], HALF_UNIT)
    part = home_ref[diagonal:] + decode(came_ref[diagonal:body])
    code_ref[...] = encode(part)
    unpack(part, part_ref)
    unpack(home_ref[:diagonal] + decode(came_ref[:diagonal]), own_ref, True)
    at = 2 * -(-panel // LANES)
    count = rows[at:at + 1, 0:1] * float(BLOCK)
    for which in range(2):
        set_scale(scale_ref.at[which], rows, which)
    down = jnp.broadcast_to(scale_ref[0, 0:1] * count, (panel, panel)).T
    down_ref[...] = down


def begin_kernel(own_ref, part_ref, mate_part_ref, down_ref, scale_ref, pair_ref, out_ref, ready, sem):
    panel = down_ref.shape[0]
    half = panel // 2
    me = lax.axis_index("tm")
    chip, core = lax.div(me, 2), lax.rem(me, 2)
    down = down_ref[...]
    pair_ref[0] = own_ref[...] * down
    mate = pair_ref.at[1]
    unpack(decode(mate_part_ref[...]), mate.at[pl.ds(half, panel - half)])
    mate[:half] = part_ref[...] * down[:half]
    mate[half:] = mate[half:] * down[half:]
    for u in range(2):
        here = slice(u * panel, (u + 1) * panel)

        @pl.when(jnp.logical_and(chip == 0, core <= u))
        def _():
            which = u - core
            ready[:, here] = pair_ref[which] * scale_ref[which, 0:1]

        @pl.when(jnp.logical_or(chip > 0, core > u))
        def _():
            ready[:, here] = jnp.zeros((panel, panel), jnp.float32)

    copy = pltpu.make_async_copy(ready, out_ref.at[0, :, pl.ds(0, 2 * panel)], sem)
    copy.start()
    copy.wait()


def middle_kernel(pairs, pair_ref, down_ref, late_ref, *refs):
    away, across_ref, tiles, turned = refs[:pairs], *refs[pairs:]
    late = late_ref.shape[1]
    me = lax.axis_index("tm")
    chip, core = lax.div(me, 2), lax.rem(me, 2)
    down = down_ref[...]
    tiles[...] = jnp.zeros_like(tiles)
    tiles[me] = pair_ref[0]

    @pl.when(core == 0)
    def _():
        tiles[me + 1] = pair_ref[1]

    for d in range(pairs):
        far_chip = lax.bitwise_xor(chip, d + 1)

        @pl.when(chip < far_chip)
        def _():
            unpack(late_ref[d] + decode(across_ref[d, :late]), turned)
            tiles[2 * far_chip + core] = turned[...] * down
            unpack(decode(away[d][0, :late]), turned)
            tiles[2 * far_chip + 1 - core] = turned[...].T * down


def last_kernel(pairs, tiles, down_ref, scale_ref, begun_ref, *refs):
    near, away = refs[:pairs], refs[pairs:2 * pairs]
    out_ref, scales, more, turned, ready, sems = refs[2 * pairs:]
    steps, panel = tiles.shape[:2]
    me = lax.axis_index("tm")
    chip, core = lax.div(me, 2), lax.rem(me, 2)
    scales[...] = jnp.ones_like(scales)
    scales[me] = scale_ref[0]

    @pl.when(core == 0)
    def _():
        scales[me + 1] = scale_ref[1]

    more[...] = jnp.zeros_like(more)
    for d in range(pairs):
        far_chip = lax.bitwise_xor(chip, d + 1)
        late = near[d].shape[1] - 2 * ROWS

        @pl.when(chip < far_chip)
        def _():
            rows = decode_rows(near[d][0, late:], HALF_UNIT) + decode_rows(
                away[d][0, late:], HALF_UNIT
            )
            straight, crossed = 2 * far_chip + core, 2 * far_chip + 1 - core
            set_scale(scales.at[straight], rows, 0)
            set_scale(scales.at[crossed], rows, 1)
            unpack(decode(near[d][0, :late]), turned)
            more[crossed] = turned[...].T * down_ref[...]

    copies = []
    for i, rows in enumerate((pl.ds(0, panel // 2), pl.ds(panel // 2, panel - panel // 2))):
        for u in range(2, steps):
            tile = (tiles[u, rows] + more[u, rows]) * scales[u, 0:1]
            ready[rows, (u - 2) * panel:(u - 1) * panel] = tile
        there = out_ref.at[0, rows, pl.ds(2 * panel, (steps - 2) * panel)]
        copies.append(pltpu.make_async_copy(ready.at[rows], there, sems.at[i]))
        copies[-1].start()
    for copy in copies:
        copy.wait()


def call(kernel, outs, ins, scratch=(), flops=0, in_hbm=0, out_hbm=0, goes_on=None, free=False):
    moved = 0 if free else sum(math.prod(x.shape) * x.dtype.itemsize for x in (*outs, *ins))
    many = isinstance(outs, list)
    specs = [SMEM if x.ndim == 1 else VMEM for x in (*ins, *outs)]
    specs[:in_hbm] = [HBM] * in_hbm
    specs[len(specs) - out_hbm:] = [HBM] * out_hbm
    if goes_on is not None:
        specs[goes_on] = HBM
    ins = [
        pltpu.with_memory_space_constraint(x, pltpu.HBM) if i < in_hbm else x
        for i, x in enumerate(ins)
    ]
    return pl.pallas_call(
        kernel,
        out_shape=outs if many else outs[0],
        in_specs=specs[:len(ins)],
        out_specs=specs[len(ins):] if many else specs[-1],
        scratch_shapes=scratch,
        input_output_aliases={} if goes_on is None else {goes_on: len(outs) - 1},
        compiler_params=pltpu.CompilerParams(vmem_limit_bytes=48 * 2**20),
        cost_estimate=pl.CostEstimate(flops=flops, bytes_accessed=moved, transcendentals=0),
    )(*ins)


def on_device(intensity, block_cycle, cycle_order):
    panel = intensity.shape[0]
    blk_dev = block_cycle.shape[0]
    cycles = cycle_order.shape[0]
    groups = lax.axis_size("blk")
    steps = lax.axis_size("tm")
    inner = groups // 2
    pairs = steps // 2 - 1
    cap = 2 * max(1, blk_dev // cycles)
    early = packed_rows(panel, panel, True) + packed_rows(panel // 2, panel)
    first = panel // LANES * LANES
    pieces = [n for n in (first, panel - first) if n]
    late = [panel * n // LANES for n in pieces]

    def hop(x, by_blk, by_tm, sends=lambda t: True):
        perm = [
            (b * steps + t, (b ^ by_blk) * steps + (t ^ by_tm))
            for b in range(groups)
            for t in range(steps)
            if sends(t)
        ]
        return lax.ppermute(x, ("blk", "tm"), perm)

    offsets = range(1, pairs + 1)
    other = hop(intensity, 0, 1)
    sent = intensity[:first] if len(pieces) > 1 else intensity
    far = [[hop(sent, 0, 2 * d) for d in offsets]]
    f32, i16 = jnp.float32, jnp.int16
    shape = jax.ShapeDtypeStruct
    depth = cap * BLOCK
    work = 2 * cycles * panel * panel * depth
    table, gathers, own_rows, *made = call(
        functools.partial(early_kernel, cap),
        [
            shape((cycles * (cap + 1),), jnp.int32),
            shape((2, inner, 2, panel, depth), jnp.bfloat16),
            shape((2, ROWS, LANES), f32),
            *[shape((n, intensity.shape[1]), jnp.bfloat16) for n in pieces[1:]],
            shape((2, early, LANES), f32),
            *[shape((2, early + 2 * ROWS, LANES), i16)] * (inner - 1),
        ],
        (block_cycle, cycle_order, intensity, other),
        [
            pltpu.SMEM(cycle_order.shape, jnp.int32),
            pltpu.SMEM(block_cycle.shape, jnp.int32),
            pltpu.SMEM(cycle_order.shape, jnp.int32),
            pltpu.VMEM(intensity.shape, jnp.bfloat16),
            pltpu.VMEM((2, -(-cycles // 16) * 16, panel), f32),
            pltpu.SemaphoreType.DMA((3,)),
        ],
        2 * work,
        3,
    )
    far += [[hop(x, 0, 2 * d) for d in offsets] for x in made[:-inner]]

    def exchange(made):
        order = sorted(range(inner), key=lambda k: (k > 0, -k.bit_count()))
        return [hop(made[k], k, 0) if k else made[k] for k in order]

    parts = exchange(made[-inner:])
    home, home_rows, away = call(
        early_sum_kernel,
        [
            shape((early, LANES), f32),
            shape((ROWS, LANES), f32),
            shape((early + 2 * ROWS, LANES), i16),
        ],
        (parts[0], own_rows, *parts[1:]),
        flops=32 * work,
    )
    came = hop(away, inner, 0)

    parts, after = [], ()
    for rows, came_rows in zip(late, far):
        made = call(
            functools.partial(late_kernel, cap, len(after)),
            [shape((2, pairs, rows, LANES), i16 if k else f32) for k in range(inner)],
            (table, gathers, *after, *came_rows),
            flops=pairs * work,
        )
        parts += exchange(made)
        after = (away, made[1])
    late_home, near, late_away = call(
        functools.partial(late_sum_kernel, len(pieces)),
        [
            shape((pairs, sum(late), LANES), f32),
            shape((pairs, sum(late) + 2 * ROWS, LANES), i16),
            shape((pairs, sum(late) + 2 * ROWS, LANES), i16),
        ],
        (home_rows, away, *parts),
        flops=32 * work,
    )

    def is_lower(t, d):
        return t // 2 < (t // 2 ^ d)

    from_away = [
        hop(late_away[d - 1:d], inner, 2 * d, lambda t, d=d: not is_lower(t, d)) for d in offsets
    ]
    from_near = [hop(near[d - 1:d], 0, 2 * d) for d in offsets]
    across = hop(late_away, inner, 0)
    own_tile, part, code, down, scale = call(
        early_end_kernel,
        [
            shape((panel, panel), f32),
            shape((panel // 2, panel), f32),
            shape((packed_rows(panel // 2, panel), LANES), i16),
            shape((panel, panel), f32),
            shape((2, 8, panel), f32),
        ],
        (home, home_rows, came, late_away),
    )
    mate_part = hop(code, 0, 1)
    whole = shape((1, panel, steps * panel), f32)
    pair, begun = call(
        begin_kernel,
        [shape((2, panel, panel), f32), whole],
        (own_tile, part, mate_part, down, scale),
        [pltpu.VMEM((panel, 2 * panel), f32), pltpu.SemaphoreType.DMA],
        out_hbm=1,
        free=True,
    )
    tiles = call(
        functools.partial(middle_kernel, pairs),
        (shape((steps, panel, panel), f32),),
        (pair, down, late_home, *from_away, across),
        [pltpu.VMEM((panel, panel), f32)],
    )
    return call(
        functools.partial(last_kernel, pairs),
        (whole,),
        (tiles, down, scale, begun, *from_near, *from_away),
        [
            pltpu.VMEM((steps, 8, panel), f32),
            pltpu.VMEM((steps, panel, panel), f32),
            pltpu.VMEM((panel, panel), f32),
            pltpu.VMEM((panel, (steps - 2) * panel), f32),
            pltpu.SemaphoreType.DMA((2,)),
        ],
        out_hbm=1,
        goes_on=3,
    )


def solution(mesh):
    placed = (P("tm", "blk"), P("blk"), P())
    return jax.shard_map(
        on_device, mesh=mesh, in_specs=placed, out_specs=P("blk", "tm", None), check_vma=False
    )
```

```python
import functools
import math

import jax
import jax.numpy as jnp
from jax import lax
from jax.experimental import pallas as pl
from jax.experimental.pallas import tpu as pltpu
from jax.sharding import PartitionSpec as P

BLOCK = 128
LANES = 128
ROWS = 8
NONE = -32768
LEAST, MOST = -3.0, 29.0
PER_OCTAVE = 65534 / (MOST - LEAST)
MIDDLE = (MOST + LEAST) / 2
PART_UNIT, HALF_UNIT = 8192.0, 2048.0
LOW = 1 << 16
VMEM = pl.BlockSpec(memory_space=pltpu.VMEM)
SMEM = pl.BlockSpec(memory_space=pltpu.SMEM)
HBM = pl.BlockSpec(memory_space=pltpu.HBM)


def times(left, right):
    return lax.dot_general(
        left, right, (((1,), (1,)), ((), ())), preferred_element_type=jnp.float32
    )


def encode(x):
    level = jnp.log(jnp.maximum(x, 2.0**LEAST)) * (PER_OCTAVE / math.log(2))
    code = (level + (0.5 - LEAST * PER_OCTAVE)).astype(jnp.int32) + (NONE + 1)
    return jnp.where(x[..., :1, :] > 0, code, NONE).astype(jnp.int16)


def decode(code):
    code = code.astype(jnp.int32)
    level = code.astype(jnp.float32) * (math.log(2) / PER_OCTAVE) + MIDDLE * math.log(2)
    return jnp.where(code[..., :1, :] > NONE, jnp.exp(level), 0.0)


def split(panel):
    whole, rest = divmod(panel, LANES)
    return whole, LANES // rest if rest else 0


def packed_rows(rows, panel, symmetric=False):
    whole, fold = split(panel)
    if symmetric and (whole, fold) == (1, 2):
        return LANES + LANES // 2
    body = sum((i + 1) * LANES if symmetric else rows for i in range(whole))
    return body + (rows // fold if fold else 0)


def pack(tile, symmetric=False):
    rows, panel = tile.shape
    whole, fold = split(panel)
    if symmetric and (whole, fold) == (1, 2):
        n = LANES // 2
        left, right = tile[:, :LANES], tile[:, LANES:]
        parts = [
            left[:n],
            jnp.concatenate([right[:n], left[n:2 * n, n:]], axis=1),
            jnp.concatenate([right[n:2 * n], right[2 * n:]], axis=1),
        ]
        return jnp.concatenate(parts, axis=0)
    parts = [
        tile[: (i + 1) * LANES if symmetric else rows, i * LANES:(i + 1) * LANES]
        for i in range(whole)
    ]
    if fold:
        n = rows // fold
        left = [tile[i * n:(i + 1) * n, whole * LANES:] for i in range(fold)]
        parts.append(jnp.concatenate(left, axis=1))
    return jnp.concatenate(parts, axis=0)


def unpack(x, out, symmetric=False):
    rows, panel = out.shape
    whole, fold = split(panel)
    if symmetric and (whole, fold) == (1, 2):
        n = LANES // 2
        out[:n, :LANES] = x[:n]
        out[:n, LANES:] = x[n:2 * n, :n]
        out[n:2 * n, n:LANES] = x[n:2 * n, n:]
        out[n:2 * n, LANES:] = x[2 * n:, :n]
        out[2 * n:, LANES:] = x[2 * n:, n:]
        out[n:2 * n, :n] = x[:n, n:].T
        out[2 * n:, :LANES] = out[:2 * n, LANES:].T
        return
    at = 0
    for i in range(whole):
        n = (i + 1) * LANES if symmetric else rows
        out[:n, i * LANES:(i + 1) * LANES] = x[at:at + n]
        at += n
    if fold:
        n, width = rows // fold, LANES // fold
        for i in range(fold):
            out[i * n:(i + 1) * n, whole * LANES:] = x[at:, i * width:(i + 1) * width]
    if symmetric:
        for i in range(whole):
            n = (i + 1) * LANES
            if n < panel:
                out[n:, i * LANES:n] = out[i * LANES:n, n:].T


def rows_of(sums, count):
    panel = sums[0].shape[1]
    row = lax.broadcasted_iota(jnp.int32, (ROWS, LANES), 0)
    out, at = jnp.zeros((ROWS, LANES), jnp.float32), 0
    for x in sums:
        for start in range(0, panel, LANES):
            piece = x[:, start:start + LANES]
            if piece.shape[1] < LANES:
                piece = jnp.concatenate([piece] * (LANES // piece.shape[1]), axis=1)
            out = jnp.where(row == at, piece, out)
            at += 1
    return jnp.where(row == at, count, out)


def sums_of(rows, panel, which):
    per = -(-panel // LANES)
    starts = range(0, panel, LANES)
    return [
        (start, rows[which * per + i:which * per + i + 1, :min(LANES, panel - start)])
        for i, start in enumerate(starts)
    ]


def encode_rows(rows, unit):
    whole = (rows * unit + 0.5).astype(jnp.int32)
    high = lax.shift_right_logical(whole, 16)
    low = lax.bitwise_and(whole, LOW - 1) - LOW // 2
    return jnp.concatenate([high, low], axis=0).astype(jnp.int16)


def decode_rows(code, unit):
    x = code.astype(jnp.int32).astype(jnp.float32)
    return (x[:ROWS] * float(LOW) + (x[ROWS:] + LOW / 2)) * (1 / unit)


def find_slots(cap, cycle_ref, order_ref, where_ref, table_ref):
    cycles = order_ref.shape[0]
    for s in range(cycles):
        where_ref[order_ref[s]] = s
        table_ref[s] = 0
    for s in range(cycles * cap):
        table_ref[cycles + s] = 0
    for j in range(cycle_ref.shape[0]):
        p = where_ref[cycle_ref[j]]
        r = table_ref[p]
        table_ref[cycles + p * cap + r] = j
        table_ref[p] = r + 1


def gathered(ref, s, cap, table_ref, masked):
    cycles = table_ref.shape[0] // (cap + 1)
    parts = []
    for r in range(cap):
        j = table_ref[cycles + s * cap + r]
        x = ref[:, pl.ds(pl.multiple_of(j * BLOCK, BLOCK), BLOCK)]
        parts.append(jnp.where(r < table_ref[s], x, jnp.zeros_like(x)) if masked else x)
    return jnp.concatenate(parts, axis=1)


def first_kernel(own_hbm, out_ref, sem):
    copy = pltpu.make_async_copy(own_hbm.at[pl.ds(0, out_ref.shape[0])], out_ref, sem)
    copy.start()
    copy.wait()


def early_kernel(cap, cycle_hbm, order_hbm, own_hbm, other_ref, *refs):
    table_ref, sorted_ref, rows_ref, *outs = refs[:-6]
    where_ref, cycle_ref, order_ref, own_ref, sums_ref, sems = refs[-6:]
    pairs = ((cycle_hbm, cycle_ref), (order_hbm, order_ref), (own_hbm, own_ref))
    copies = [pltpu.make_async_copy(*pair, sems.at[i]) for i, pair in enumerate(pairs)]
    for copy in copies:
        copy.start()
    copies[0].wait()
    copies[1].wait()
    find_slots(cap, cycle_ref, order_ref, where_ref, table_ref)
    inner = lax.axis_size("blk") // 2
    pieces, outs = outs[:-inner], outs[-inner:]
    panel = own_ref.shape[0]
    half = panel // 2
    mine = lax.rem(lax.axis_index("blk"), inner)
    first = lax.rem(lax.axis_index("tm"), 2) == 0
    body = outs[0].shape[1]
    row = lax.broadcasted_iota(jnp.int32, (sums_ref.shape[1], BLOCK), 0)
    members = jnp.concatenate(
        [
            jnp.where(row == where_ref[cycle_ref[j]], 1.0, 0.0).astype(jnp.bfloat16)
            for j in range(cycle_ref.shape[0])
        ],
        axis=1,
    )
    each = [(k, h, h * inner + lax.bitwise_xor(mine, k)) for k in range(inner) for h in range(2)]
    for k, h, s in each:
        sorted_ref[1, k, h] = gathered(other_ref, s, cap, table_ref, True)
    sums_ref[1] = times(members, other_ref[...])
    copies[2].wait()
    for piece in pieces:
        piece[...] = own_ref[panel - piece.shape[0]:]
    sums_ref[0] = times(members, own_ref[...])
    for k, h, s in each:
        own, other = gathered(own_ref, s, cap, table_ref, True), sorted_ref[1, k, h]
        sorted_ref[0, k, h] = own
        left = jnp.where(first, own[:half], other[half:])
        right = jnp.where(first, other, own)
        rows = rows_of([sums_ref[i, pl.ds(s, 1)] for i in range(2)], table_ref[s].astype(jnp.float32))
        found = jnp.concatenate([pack(times(own, own), True), pack(times(left, right))], axis=0)
        if k:
            outs[k][h, :body] = encode(found)
            outs[k][h, body:] = encode_rows(rows, PART_UNIT)
        else:
            outs[k][h] = found
            rows_ref[h] = rows


def late_kernel(cap, after, table_ref, sorted_ref, *refs):
    refs = refs[after:]
    inner = lax.axis_size("blk") // 2
    came, outs = refs[:-inner], refs[-inner:]
    mine = lax.rem(lax.axis_index("blk"), inner)
    chip = lax.div(lax.axis_index("tm"), 2)
    for k in range(inner):
        for h in range(2):
            s = h * inner + lax.bitwise_xor(mine, k)
            for d, ref in enumerate(came):
                upper = (chip > lax.bitwise_xor(chip, d + 1)).astype(jnp.int32)
                far = gathered(ref, s, cap, table_ref, False)
                tile = pack(times(sorted_ref[upper, k, h], far))
                outs[k][h, d] = encode(tile) if k else tile


def early_sum_kernel(own_ref, own_rows_ref, *refs):
    *parts, home_ref, rows_ref, away_ref = refs
    body = home_ref.shape[0]
    side = lax.div(lax.axis_index("blk"), lax.axis_size("blk") // 2)

    def total(h):
        tiles, rows = own_ref[h], own_rows_ref[h]
        for part in parts:
            tiles = tiles + decode(part[h, :body])
            rows = rows + decode_rows(part[h, body:], PART_UNIT)
        return tiles, rows

    home_ref[...], rows_ref[...] = total(side)
    tiles, rows = total(1 - side)
    away_ref[:body], away_ref[body:] = encode(tiles), encode_rows(rows, HALF_UNIT)


def late_sum_kernel(pieces, home_rows_ref, early_away_ref, *refs):
    *parts, home_ref, near_ref, away_ref = refs
    inner = len(parts) // pieces
    pairs, body = home_ref.shape[:2]
    side = lax.div(lax.axis_index("blk"), lax.axis_size("blk") // 2)
    near_rows = encode_rows(home_rows_ref[...], HALF_UNIT)
    away_rows = early_away_ref[-2 * ROWS:]
    for d in range(pairs):
        at = 0
        for piece in range(pieces):
            own, *came = parts[piece * inner:(piece + 1) * inner]
            here = pl.ds(at, own.shape[2])
            at += own.shape[2]
            home, away = own[side, d], own[1 - side, d]
            for part in came:
                home = home + decode(part[side, d])
                away = away + decode(part[1 - side, d])
            home_ref[d, here] = home
            near_ref[d, here] = encode(home)
            away_ref[d, here] = encode(away)
        near_ref[d, body:], away_ref[d, body:] = near_rows, away_rows


def set_scale(ref, rows, which):
    for start, x in sums_of(rows, ref.shape[1], which):
        ref[0:1, start:start + x.shape[1]] = 1.0 / x


def early_end_kernel(
    home_ref, rows_ref, came_ref, after_ref, own_ref, part_ref, code_ref, down_ref, scale_ref
):
    half, panel = part_ref.shape
    body, diagonal = home_ref.shape[0], packed_rows(panel, panel, True)
    rows = rows_ref[...] + decode_rows(came_ref[body:], HALF_UNIT)
    part = home_ref[diagonal:] + decode(came_ref[diagonal:body])
    code_ref[...] = encode(part)
    unpack(part, part_ref)
    unpack(home_ref[:diagonal] + decode(came_ref[:diagonal]), own_ref, True)
    at = 2 * -(-panel // LANES)
    count = rows[at:at + 1, 0:1] * float(BLOCK)
    for which in range(2):
        set_scale(scale_ref.at[which], rows, which)
    down = jnp.broadcast_to(scale_ref[0, 0:1] * count, (panel, panel)).T
    down_ref[...] = down


def begin_kernel(own_ref, part_ref, mate_part_ref, down_ref, scale_ref, pair_ref, out_ref, ready, sem):
    panel = down_ref.shape[0]
    half = panel // 2
    me = lax.axis_index("tm")
    chip, core = lax.div(me, 2), lax.rem(me, 2)
    down = down_ref[...]
    pair_ref[0] = own_ref[...] * down
    mate = pair_ref.at[1]
    unpack(decode(mate_part_ref[...]), mate.at[pl.ds(half, panel - half)])
    mate[:half] = part_ref[...] * down[:half]
    mate[half:] = mate[half:] * down[half:]
    for u in range(2):
        here = slice(u * panel, (u + 1) * panel)

        @pl.when(jnp.logical_and(chip == 0, core <= u))
        def _():
            which = u - core
            ready[:, here] = pair_ref[which] * scale_ref[which, 0:1]

        @pl.when(jnp.logical_or(chip > 0, core > u))
        def _():
            ready[:, here] = jnp.zeros((panel, panel), jnp.float32)

    copy = pltpu.make_async_copy(ready, out_ref.at[0, :, pl.ds(0, 2 * panel)], sem)
    copy.start()
    copy.wait()


def middle_kernel(pairs, pair_ref, down_ref, late_ref, *refs):
    away, across_ref, tiles, turned = refs[:pairs], *refs[pairs:]
    late = late_ref.shape[1]
    me = lax.axis_index("tm")
    chip, core = lax.div(me, 2), lax.rem(me, 2)
    down = down_ref[...]
    tiles[...] = jnp.zeros_like(tiles)
    tiles[me] = pair_ref[0]

    @pl.when(core == 0)
    def _():
        tiles[me + 1] = pair_ref[1]

    for d in range(pairs):
        far_chip = lax.bitwise_xor(chip, d + 1)

        @pl.when(chip < far_chip)
        def _():
            unpack(late_ref[d] + decode(across_ref[d, :late]), turned)
            tiles[2 * far_chip + core] = turned[...] * down
            unpack(decode(away[d][0, :late]), turned)
            tiles[2 * far_chip + 1 - core] = turned[...].T * down


def last_kernel(pairs, tiles, down_ref, scale_ref, begun_ref, *refs):
    near, away = refs[:pairs], refs[pairs:2 * pairs]
    out_ref, scales, more, turned, ready, sems = refs[2 * pairs:]
    steps, panel = tiles.shape[:2]
    me = lax.axis_index("tm")
    chip, core = lax.div(me, 2), lax.rem(me, 2)
    scales[...] = jnp.ones_like(scales)
    scales[me] = scale_ref[0]

    @pl.when(core == 0)
    def _():
        scales[me + 1] = scale_ref[1]

    more[...] = jnp.zeros_like(more)
    for d in range(pairs):
        far_chip = lax.bitwise_xor(chip, d + 1)
        late = near[d].shape[1] - 2 * ROWS

        @pl.when(chip < far_chip)
        def _():
            rows = decode_rows(near[d][0, late:], HALF_UNIT) + decode_rows(
                away[d][0, late:], HALF_UNIT
            )
            straight, crossed = 2 * far_chip + core, 2 * far_chip + 1 - core
            set_scale(scales.at[straight], rows, 0)
            set_scale(scales.at[crossed], rows, 1)
            unpack(decode(near[d][0, :late]), turned)
            more[crossed] = turned[...].T * down_ref[...]

    copies = []
    for i, rows in enumerate((pl.ds(0, panel // 2), pl.ds(panel // 2, panel - panel // 2))):
        for u in range(2, steps):
            tile = (tiles[u, rows] + more[u, rows]) * scales[u, 0:1]
            ready[rows, (u - 2) * panel:(u - 1) * panel] = tile
        there = out_ref.at[0, rows, pl.ds(2 * panel, (steps - 2) * panel)]
        copies.append(pltpu.make_async_copy(ready.at[rows], there, sems.at[i]))
        copies[-1].start()
    for copy in copies:
        copy.wait()


def call(kernel, outs, ins, scratch=(), flops=0, in_hbm=0, out_hbm=0, goes_on=None, free=False):
    moved = 0 if free else sum(math.prod(x.shape) * x.dtype.itemsize for x in (*outs, *ins))
    many = isinstance(outs, list)
    specs = [SMEM if x.ndim == 1 else VMEM for x in (*ins, *outs)]
    specs[:in_hbm] = [HBM] * in_hbm
    specs[len(specs) - out_hbm:] = [HBM] * out_hbm
    if goes_on is not None:
        specs[goes_on] = HBM
    ins = [
        pltpu.with_memory_space_constraint(x, pltpu.HBM) if i < in_hbm else x
        for i, x in enumerate(ins)
    ]
    return pl.pallas_call(
        kernel,
        out_shape=outs if many else outs[0],
        in_specs=specs[:len(ins)],
        out_specs=specs[len(ins):] if many else specs[-1],
        scratch_shapes=scratch,
        input_output_aliases={} if goes_on is None else {goes_on: len(outs) - 1},
        compiler_params=pltpu.CompilerParams(vmem_limit_bytes=48 * 2**20),
        cost_estimate=pl.CostEstimate(flops=flops, bytes_accessed=moved, transcendentals=0),
    )(*ins)


def on_device(intensity, block_cycle, cycle_order):
    panel = intensity.shape[0]
    blk_dev = block_cycle.shape[0]
    cycles = cycle_order.shape[0]
    groups = lax.axis_size("blk")
    steps = lax.axis_size("tm")
    inner = groups // 2
    pairs = steps // 2 - 1
    cap = 2 * max(1, blk_dev // cycles)
    early = packed_rows(panel, panel, True) + packed_rows(panel // 2, panel)
    first = panel // LANES * LANES
    pieces = [n for n in (first, panel - first) if n]
    late = [panel * n // LANES for n in pieces]

    def hop(x, by_blk, by_tm, sends=lambda t: True):
        perm = [
            (b * steps + t, (b ^ by_blk) * steps + (t ^ by_tm))
            for b in range(groups)
            for t in range(steps)
            if sends(t)
        ]
        return lax.ppermute(x, ("blk", "tm"), perm)

    offsets = range(1, pairs + 1)
    other = hop(intensity, 0, 1)
    sent = call(
        first_kernel,
        (jax.ShapeDtypeStruct((first, intensity.shape[1]), jnp.bfloat16),),
        (intensity,),
        [pltpu.SemaphoreType.DMA],
        in_hbm=1,
        free=True,
    )
    far = [[hop(sent, 0, 2 * d) for d in offsets]]
    f32, i16 = jnp.float32, jnp.int16
    shape = jax.ShapeDtypeStruct
    depth = cap * BLOCK
    work = 2 * cycles * panel * panel * depth
    table, gathers, own_rows, *made = call(
        functools.partial(early_kernel, cap),
        [
            shape((cycles * (cap + 1),), jnp.int32),
            shape((2, inner, 2, panel, depth), jnp.bfloat16),
            shape((2, ROWS, LANES), f32),
            *[shape((n, intensity.shape[1]), jnp.bfloat16) for n in pieces[1:]],
            shape((2, early, LANES), f32),
            *[shape((2, early + 2 * ROWS, LANES), i16)] * (inner - 1),
        ],
        (block_cycle, cycle_order, intensity, other),
        [
            pltpu.SMEM(cycle_order.shape, jnp.int32),
            pltpu.SMEM(block_cycle.shape, jnp.int32),
            pltpu.SMEM(cycle_order.shape, jnp.int32),
            pltpu.VMEM(intensity.shape, jnp.bfloat16),
            pltpu.VMEM((2, -(-cycles // 16) * 16, panel), f32),
            pltpu.SemaphoreType.DMA((3,)),
        ],
        2 * work,
        3,
    )
    far += [[hop(x, 0, 2 * d) for d in offsets] for x in made[:-inner]]

    def exchange(made):
        order = sorted(range(inner), key=lambda k: (k > 0, -k.bit_count()))
        return [hop(made[k], k, 0) if k else made[k] for k in order]

    parts = exchange(made[-inner:])
    home, home_rows, away = call(
        early_sum_kernel,
        [
            shape((early, LANES), f32),
            shape((ROWS, LANES), f32),
            shape((early + 2 * ROWS, LANES), i16),
        ],
        (parts[0], own_rows, *parts[1:]),
        flops=32 * work,
    )
    came = hop(away, inner, 0)

    parts, after = [], ()
    for rows, came_rows in zip(late, far):
        made = call(
            functools.partial(late_kernel, cap, len(after)),
            [shape((2, pairs, rows, LANES), i16 if k else f32) for k in range(inner)],
            (table, gathers, *after, *came_rows),
            flops=pairs * work,
        )
        parts += exchange(made)
        after = (away, made[1])
    late_home, near, late_away = call(
        functools.partial(late_sum_kernel, len(pieces)),
        [
            shape((pairs, sum(late), LANES), f32),
            shape((pairs, sum(late) + 2 * ROWS, LANES), i16),
            shape((pairs, sum(late) + 2 * ROWS, LANES), i16),
        ],
        (home_rows, away, *parts),
        flops=32 * work,
    )

    def is_lower(t, d):
        return t // 2 < (t // 2 ^ d)

    from_away = [
        hop(late_away[d - 1:d], inner, 2 * d, lambda t, d=d: not is_lower(t, d)) for d in offsets
    ]
    from_near = [hop(near[d - 1:d], 0, 2 * d) for d in offsets]
    across = hop(late_away, inner, 0, lambda t: any(is_lower(t, d) for d in offsets))
    own_tile, part, code, down, scale = call(
        early_end_kernel,
        [
            shape((panel, panel), f32),
            shape((panel // 2, panel), f32),
            shape((packed_rows(panel // 2, panel), LANES), i16),
            shape((panel, panel), f32),
            shape((2, 8, panel), f32),
        ],
        (home, home_rows, came, late_away),
    )
    mate_part = hop(code, 0, 1)
    whole = shape((1, panel, steps * panel), f32)
    pair, begun = call(
        begin_kernel,
        [shape((2, panel, panel), f32), whole],
        (own_tile, part, mate_part, down, scale),
        [pltpu.VMEM((panel, 2 * panel), f32), pltpu.SemaphoreType.DMA],
        out_hbm=1,
        free=True,
    )
    tiles = call(
        functools.partial(middle_kernel, pairs),
        (shape((steps, panel, panel), f32),),
        (pair, down, late_home, *from_away, across),
        [pltpu.VMEM((panel, panel), f32)],
    )
    return call(
        functools.partial(last_kernel, pairs),
        (whole,),
        (tiles, down, scale, begun, *from_near, *from_away),
        [
            pltpu.VMEM((steps, 8, panel), f32),
            pltpu.VMEM((steps, panel, panel), f32),
            pltpu.VMEM((panel, panel), f32),
            pltpu.VMEM((panel, (steps - 2) * panel), f32),
            pltpu.SemaphoreType.DMA((2,)),
        ],
        out_hbm=1,
        goes_on=3,
    )


def solution(mesh):
    placed = (P("tm", "blk"), P("blk"), P())
    return jax.shard_map(
        on_device, mesh=mesh, in_specs=placed, out_specs=P("blk", "tm", None), check_vma=False
    )
```

```python
import functools
import math

import jax
import jax.numpy as jnp
from jax import lax
from jax.experimental import pallas as pl
from jax.experimental.pallas import tpu as pltpu
from jax.sharding import PartitionSpec as P

BLOCK = 128
LANES = 128
ROWS = 8
NONE = -32768
LEAST, MOST = -3.0, 29.0
PER_OCTAVE = 65534 / (MOST - LEAST)
MIDDLE = (MOST + LEAST) / 2
PART_UNIT, HALF_UNIT = 8192.0, 2048.0
LOW = 1 << 16
VMEM = pl.BlockSpec(memory_space=pltpu.VMEM)
SMEM = pl.BlockSpec(memory_space=pltpu.SMEM)
HBM = pl.BlockSpec(memory_space=pltpu.HBM)


def times(left, right):
    return lax.dot_general(
        left, right, (((1,), (1,)), ((), ())), preferred_element_type=jnp.float32
    )


def encode(x):
    level = jnp.log(jnp.maximum(x, 2.0**LEAST)) * (PER_OCTAVE / math.log(2))
    code = (level + (0.5 - LEAST * PER_OCTAVE)).astype(jnp.int32) + (NONE + 1)
    return jnp.where(x[..., :1, :] > 0, code, NONE).astype(jnp.int16)


def decode(code):
    code = code.astype(jnp.int32)
    level = code.astype(jnp.float32) * (math.log(2) / PER_OCTAVE) + MIDDLE * math.log(2)
    return jnp.where(code[..., :1, :] > NONE, jnp.exp(level), 0.0)


def split(panel):
    whole, rest = divmod(panel, LANES)
    return whole, LANES // rest if rest else 0


def packed_rows(rows, panel, symmetric=False):
    whole, fold = split(panel)
    if symmetric and (whole, fold) == (1, 2):
        return LANES + LANES // 2
    body = sum((i + 1) * LANES if symmetric else rows for i in range(whole))
    return body + (rows // fold if fold else 0)


def pack(tile, symmetric=False):
    rows, panel = tile.shape
    whole, fold = split(panel)
    if symmetric and (whole, fold) == (1, 2):
        n = LANES // 2
        left, right = tile[:, :LANES], tile[:, LANES:]
        parts = [
            left[:n],
            jnp.concatenate([right[:n], left[n:2 * n, n:]], axis=1),
            jnp.concatenate([right[n:2 * n], right[2 * n:]], axis=1),
        ]
        return jnp.concatenate(parts, axis=0)
    parts = [
        tile[: (i + 1) * LANES if symmetric else rows, i * LANES:(i + 1) * LANES]
        for i in range(whole)
    ]
    if fold:
        n = rows // fold
        left = [tile[i * n:(i + 1) * n, whole * LANES:] for i in range(fold)]
        parts.append(jnp.concatenate(left, axis=1))
    return jnp.concatenate(parts, axis=0)


def unpack(x, out, symmetric=False):
    rows, panel = out.shape
    whole, fold = split(panel)
    if symmetric and (whole, fold) == (1, 2):
        n = LANES // 2
        out[:n, :LANES] = x[:n]
        out[:n, LANES:] = x[n:2 * n, :n]
        out[n:2 * n, n:LANES] = x[n:2 * n, n:]
        out[n:2 * n, LANES:] = x[2 * n:, :n]
        out[2 * n:, LANES:] = x[2 * n:, n:]
        out[n:2 * n, :n] = x[:n, n:].T
        out[2 * n:, :LANES] = out[:2 * n, LANES:].T
        return
    at = 0
    for i in range(whole):
        n = (i + 1) * LANES if symmetric else rows
        out[:n, i * LANES:(i + 1) * LANES] = x[at:at + n]
        at += n
    if fold:
        n, width = rows // fold, LANES // fold
        for i in range(fold):
            out[i * n:(i + 1) * n, whole * LANES:] = x[at:, i * width:(i + 1) * width]
    if symmetric:
        for i in range(whole):
            n = (i + 1) * LANES
            if n < panel:
                out[n:, i * LANES:n] = out[i * LANES:n, n:].T


def rows_of(sums, count):
    panel = sums[0].shape[1]
    row = lax.broadcasted_iota(jnp.int32, (ROWS, LANES), 0)
    out, at = jnp.zeros((ROWS, LANES), jnp.float32), 0
    for x in sums:
        for start in range(0, panel, LANES):
            piece = x[:, start:start + LANES]
            if piece.shape[1] < LANES:
                piece = jnp.concatenate([piece] * (LANES // piece.shape[1]), axis=1)
            out = jnp.where(row == at, piece, out)
            at += 1
    return jnp.where(row == at, count, out)


def sums_of(rows, panel, which):
    per = -(-panel // LANES)
    starts = range(0, panel, LANES)
    return [
        (start, rows[which * per + i:which * per + i + 1, :min(LANES, panel - start)])
        for i, start in enumerate(starts)
    ]


def encode_rows(rows, unit):
    whole = (rows * unit + 0.5).astype(jnp.int32)
    high = lax.shift_right_logical(whole, 16)
    low = lax.bitwise_and(whole, LOW - 1) - LOW // 2
    return jnp.concatenate([high, low], axis=0).astype(jnp.int16)


def decode_rows(code, unit):
    x = code.astype(jnp.int32).astype(jnp.float32)
    return (x[:ROWS] * float(LOW) + (x[ROWS:] + LOW / 2)) * (1 / unit)


def find_slots(cap, cycle_ref, order_ref, where_ref, table_ref):
    cycles = order_ref.shape[0]
    for s in range(cycles):
        where_ref[order_ref[s]] = s
        table_ref[s] = 0
    for s in range(cycles * cap):
        table_ref[cycles + s] = 0
    for j in range(cycle_ref.shape[0]):
        p = where_ref[cycle_ref[j]]
        r = table_ref[p]
        table_ref[cycles + p * cap + r] = j
        table_ref[p] = r + 1


def gathered(ref, s, cap, table_ref, masked):
    cycles = table_ref.shape[0] // (cap + 1)
    parts = []
    for r in range(cap):
        j = table_ref[cycles + s * cap + r]
        x = ref[:, pl.ds(pl.multiple_of(j * BLOCK, BLOCK), BLOCK)]
        parts.append(jnp.where(r < table_ref[s], x, jnp.zeros_like(x)) if masked else x)
    return jnp.concatenate(parts, axis=1)


def early_kernel(cap, cycle_hbm, order_hbm, own_hbm, other_ref, *refs):
    table_ref, sorted_ref, rows_ref, *outs = refs[:-6]
    where_ref, cycle_ref, order_ref, own_ref, sums_ref, sems = refs[-6:]
    pairs = ((cycle_hbm, cycle_ref), (order_hbm, order_ref), (own_hbm, own_ref))
    copies = [pltpu.make_async_copy(*pair, sems.at[i]) for i, pair in enumerate(pairs)]
    for copy in copies:
        copy.start()
    copies[0].wait()
    copies[1].wait()
    find_slots(cap, cycle_ref, order_ref, where_ref, table_ref)
    inner = lax.axis_size("blk") // 2
    pieces, outs = outs[:-inner], outs[-inner:]
    panel = own_ref.shape[0]
    half = panel // 2
    mine = lax.rem(lax.axis_index("blk"), inner)
    first = lax.rem(lax.axis_index("tm"), 2) == 0
    body = outs[0].shape[1]
    row = lax.broadcasted_iota(jnp.int32, (sums_ref.shape[1], BLOCK), 0)
    members = jnp.concatenate(
        [
            jnp.where(row == where_ref[cycle_ref[j]], 1.0, 0.0).astype(jnp.bfloat16)
            for j in range(cycle_ref.shape[0])
        ],
        axis=1,
    )
    each = [(k, h, h * inner + lax.bitwise_xor(mine, k)) for k in range(inner) for h in range(2)]
    for k, h, s in each:
        sorted_ref[1, k, h] = gathered(other_ref, s, cap, table_ref, True)
    sums_ref[1] = times(members, other_ref[...])
    copies[2].wait()
    for piece in pieces:
        piece[...] = own_ref[panel - piece.shape[0]:]
    sums_ref[0] = times(members, own_ref[...])
    for k, h, s in each:
        own, other = gathered(own_ref, s, cap, table_ref, True), sorted_ref[1, k, h]
        sorted_ref[0, k, h] = own
        left = jnp.where(first, own[:half], other[half:])
        right = jnp.where(first, other, own)
        rows = rows_of([sums_ref[i, pl.ds(s, 1)] for i in range(2)], table_ref[s].astype(jnp.float32))
        found = jnp.concatenate([pack(times(own, own), True), pack(times(left, right))], axis=0)
        if k:
            outs[k][h, :body] = encode(found)
            outs[k][h, body:] = encode_rows(rows, PART_UNIT)
        else:
            outs[k][h] = found
            rows_ref[h] = rows


def late_kernel(cap, after, table_ref, sorted_ref, *refs):
    refs = refs[after:]
    inner = lax.axis_size("blk") // 2
    came, outs = refs[:-inner], refs[-inner:]
    mine = lax.rem(lax.axis_index("blk"), inner)
    chip = lax.div(lax.axis_index("tm"), 2)
    for k in range(inner):
        for h in range(2):
            s = h * inner + lax.bitwise_xor(mine, k)
            for d, ref in enumerate(came):
                upper = (chip > lax.bitwise_xor(chip, d + 1)).astype(jnp.int32)
                far = gathered(ref, s, cap, table_ref, False)
                tile = pack(times(sorted_ref[upper, k, h], far))
                outs[k][h, d] = encode(tile) if k else tile


def early_sum_kernel(own_ref, own_rows_ref, *refs):
    *parts, home_ref, rows_ref, away_ref = refs
    body = home_ref.shape[0]
    side = lax.div(lax.axis_index("blk"), lax.axis_size("blk") // 2)

    def total(h):
        tiles, rows = own_ref[h], own_rows_ref[h]
        for part in parts:
            tiles = tiles + decode(part[h, :body])
            rows = rows + decode_rows(part[h, body:], PART_UNIT)
        return tiles, rows

    home_ref[...], rows_ref[...] = total(side)
    tiles, rows = total(1 - side)
    away_ref[:body], away_ref[body:] = encode(tiles), encode_rows(rows, HALF_UNIT)


def late_total(parts, pieces, h, d, put):
    inner, at = len(parts) // pieces, 0
    for piece in range(pieces):
        own, *came = parts[piece * inner:(piece + 1) * inner]
        tiles = own[h, d]
        for part in came:
            tiles = tiles + decode(part[h, d])
        put(pl.ds(at, own.shape[2]), tiles)
        at += own.shape[2]


def late_away_kernel(pieces, early_away_ref, *refs):
    *parts, away_ref = refs
    pairs, body = away_ref.shape[0], away_ref.shape[1] - 2 * ROWS
    side = lax.div(lax.axis_index("blk"), lax.axis_size("blk") // 2)
    for d in range(pairs):

        def put(here, tiles):
            away_ref[d, here] = encode(tiles)

        late_total(parts, pieces, 1 - side, d, put)
        away_ref[d, body:] = early_away_ref[-2 * ROWS:]


def late_home_kernel(pieces, home_rows_ref, after_ref, *refs):
    *parts, home_ref, near_ref = refs
    pairs, body = home_ref.shape[:2]
    side = lax.div(lax.axis_index("blk"), lax.axis_size("blk") // 2)
    for d in range(pairs):

        def put(here, tiles):
            home_ref[d, here] = tiles
            near_ref[d, here] = encode(tiles)

        late_total(parts, pieces, side, d, put)
        near_ref[d, body:] = encode_rows(home_rows_ref[...], HALF_UNIT)


def set_scale(ref, rows, which):
    for start, x in sums_of(rows, ref.shape[1], which):
        ref[0:1, start:start + x.shape[1]] = 1.0 / x


def early_end_kernel(
    home_ref, rows_ref, came_ref, after_ref, own_ref, part_ref, code_ref, down_ref, scale_ref
):
    half, panel = part_ref.shape
    body, diagonal = home_ref.shape[0], packed_rows(panel, panel, True)
    rows = rows_ref[...] + decode_rows(came_ref[body:], HALF_UNIT)
    part = home_ref[diagonal:] + decode(came_ref[diagonal:body])
    code_ref[...] = encode(part)
    unpack(part, part_ref)
    unpack(home_ref[:diagonal] + decode(came_ref[:diagonal]), own_ref, True)
    at = 2 * -(-panel // LANES)
    count = rows[at:at + 1, 0:1] * float(BLOCK)
    for which in range(2):
        set_scale(scale_ref.at[which], rows, which)
    down = jnp.broadcast_to(scale_ref[0, 0:1] * count, (panel, panel)).T
    down_ref[...] = down


def begin_kernel(own_ref, part_ref, mate_part_ref, down_ref, scale_ref, pair_ref, out_ref, ready, sem):
    panel = down_ref.shape[0]
    half = panel // 2
    me = lax.axis_index("tm")
    chip, core = lax.div(me, 2), lax.rem(me, 2)
    down = down_ref[...]
    pair_ref[0] = own_ref[...] * down
    mate = pair_ref.at[1]
    unpack(decode(mate_part_ref[...]), mate.at[pl.ds(half, panel - half)])
    mate[:half] = part_ref[...] * down[:half]
    mate[half:] = mate[half:] * down[half:]
    for u in range(2):
        here = slice(u * panel, (u + 1) * panel)

        @pl.when(jnp.logical_and(chip == 0, core <= u))
        def _():
            which = u - core
            ready[:, here] = pair_ref[which] * scale_ref[which, 0:1]

        @pl.when(jnp.logical_or(chip > 0, core > u))
        def _():
            ready[:, here] = jnp.zeros((panel, panel), jnp.float32)

    copy = pltpu.make_async_copy(ready, out_ref.at[0, :, pl.ds(0, 2 * panel)], sem)
    copy.start()
    copy.wait()


def middle_kernel(pairs, pair_ref, down_ref, late_ref, *refs):
    away, across_ref, tiles, turned = refs[:pairs], *refs[pairs:]
    late = late_ref.shape[1]
    me = lax.axis_index("tm")
    chip, core = lax.div(me, 2), lax.rem(me, 2)
    down = down_ref[...]
    tiles[...] = jnp.zeros_like(tiles)
    tiles[me] = pair_ref[0]

    @pl.when(core == 0)
    def _():
        tiles[me + 1] = pair_ref[1]

    for d in range(pairs):
        far_chip = lax.bitwise_xor(chip, d + 1)

        @pl.when(chip < far_chip)
        def _():
            unpack(late_ref[d] + decode(across_ref[d, :late]), turned)
            tiles[2 * far_chip + core] = turned[...] * down
            unpack(decode(away[d][0, :late]), turned)
            tiles[2 * far_chip + 1 - core] = turned[...].T * down


def last_kernel(pairs, tiles, down_ref, scale_ref, begun_ref, *refs):
    near, away = refs[:pairs], refs[pairs:2 * pairs]
    out_ref, scales, more, turned, ready, sems = refs[2 * pairs:]
    steps, panel = tiles.shape[:2]
    me = lax.axis_index("tm")
    chip, core = lax.div(me, 2), lax.rem(me, 2)
    scales[...] = jnp.ones_like(scales)
    scales[me] = scale_ref[0]

    @pl.when(core == 0)
    def _():
        scales[me + 1] = scale_ref[1]

    more[...] = jnp.zeros_like(more)
    for d in range(pairs):
        far_chip = lax.bitwise_xor(chip, d + 1)
        late = near[d].shape[1] - 2 * ROWS

        @pl.when(chip < far_chip)
        def _():
            rows = decode_rows(near[d][0, late:], HALF_UNIT) + decode_rows(
                away[d][0, late:], HALF_UNIT
            )
            straight, crossed = 2 * far_chip + core, 2 * far_chip + 1 - core
            set_scale(scales.at[straight], rows, 0)
            set_scale(scales.at[crossed], rows, 1)
            unpack(decode(near[d][0, :late]), turned)
            more[crossed] = turned[...].T * down_ref[...]

    copies = []
    for i, rows in enumerate((pl.ds(0, panel // 2), pl.ds(panel // 2, panel - panel // 2))):
        for u in range(2, steps):
            tile = (tiles[u, rows] + more[u, rows]) * scales[u, 0:1]
            ready[rows, (u - 2) * panel:(u - 1) * panel] = tile
        there = out_ref.at[0, rows, pl.ds(2 * panel, (steps - 2) * panel)]
        copies.append(pltpu.make_async_copy(ready.at[rows], there, sems.at[i]))
        copies[-1].start()
    for copy in copies:
        copy.wait()


def call(kernel, outs, ins, scratch=(), flops=0, in_hbm=0, out_hbm=0, goes_on=None, free=False):
    moved = 0 if free else sum(math.prod(x.shape) * x.dtype.itemsize for x in (*outs, *ins))
    many = isinstance(outs, list)
    specs = [SMEM if x.ndim == 1 else VMEM for x in (*ins, *outs)]
    specs[:in_hbm] = [HBM] * in_hbm
    specs[len(specs) - out_hbm:] = [HBM] * out_hbm
    if goes_on is not None:
        specs[goes_on] = HBM
    ins = [
        pltpu.with_memory_space_constraint(x, pltpu.HBM) if i < in_hbm else x
        for i, x in enumerate(ins)
    ]
    return pl.pallas_call(
        kernel,
        out_shape=outs if many else outs[0],
        in_specs=specs[:len(ins)],
        out_specs=specs[len(ins):] if many else specs[-1],
        scratch_shapes=scratch,
        input_output_aliases={} if goes_on is None else {goes_on: len(outs) - 1},
        compiler_params=pltpu.CompilerParams(vmem_limit_bytes=48 * 2**20),
        cost_estimate=pl.CostEstimate(flops=flops, bytes_accessed=moved, transcendentals=0),
    )(*ins)


def on_device(intensity, block_cycle, cycle_order):
    panel = intensity.shape[0]
    blk_dev = block_cycle.shape[0]
    cycles = cycle_order.shape[0]
    groups = lax.axis_size("blk")
    steps = lax.axis_size("tm")
    inner = groups // 2
    pairs = steps // 2 - 1
    cap = 2 * max(1, blk_dev // cycles)
    early = packed_rows(panel, panel, True) + packed_rows(panel // 2, panel)
    first = panel // LANES * LANES
    pieces = [n for n in (first, panel - first) if n]
    late = [panel * n // LANES for n in pieces]

    def hop(x, by_blk, by_tm, sends=lambda t: True):
        perm = [
            (b * steps + t, (b ^ by_blk) * steps + (t ^ by_tm))
            for b in range(groups)
            for t in range(steps)
            if sends(t)
        ]
        return lax.ppermute(x, ("blk", "tm"), perm)

    offsets = range(1, pairs + 1)
    other = hop(intensity, 0, 1)
    sent = intensity[:first] if len(pieces) > 1 else intensity
    far = [[hop(sent, 0, 2 * d) for d in offsets]]
    f32, i16 = jnp.float32, jnp.int16
    shape = jax.ShapeDtypeStruct
    depth = cap * BLOCK
    work = 2 * cycles * panel * panel * depth
    table, gathers, own_rows, *made = call(
        functools.partial(early_kernel, cap),
        [
            shape((cycles * (cap + 1),), jnp.int32),
            shape((2, inner, 2, panel, depth), jnp.bfloat16),
            shape((2, ROWS, LANES), f32),
            *[shape((n, intensity.shape[1]), jnp.bfloat16) for n in pieces[1:]],
            shape((2, early, LANES), f32),
            *[shape((2, early + 2 * ROWS, LANES), i16)] * (inner - 1),
        ],
        (block_cycle, cycle_order, intensity, other),
        [
            pltpu.SMEM(cycle_order.shape, jnp.int32),
            pltpu.SMEM(block_cycle.shape, jnp.int32),
            pltpu.SMEM(cycle_order.shape, jnp.int32),
            pltpu.VMEM(intensity.shape, jnp.bfloat16),
            pltpu.VMEM((2, -(-cycles // 16) * 16, panel), f32),
            pltpu.SemaphoreType.DMA((3,)),
        ],
        2 * work,
        3,
    )
    far += [[hop(x, 0, 2 * d) for d in offsets] for x in made[:-inner]]

    def exchange(made):
        order = sorted(range(inner), key=lambda k: (k > 0, -k.bit_count()))
        return [hop(made[k], k, 0) if k else made[k] for k in order]

    parts = exchange(made[-inner:])
    home, home_rows, away = call(
        early_sum_kernel,
        [
            shape((early, LANES), f32),
            shape((ROWS, LANES), f32),
            shape((early + 2 * ROWS, LANES), i16),
        ],
        (parts[0], own_rows, *parts[1:]),
        flops=32 * work,
    )
    came = hop(away, inner, 0)

    parts, after = [], ()
    for rows, came_rows in zip(late, far):
        made = call(
            functools.partial(late_kernel, cap, len(after)),
            [shape((2, pairs, rows, LANES), i16 if k else f32) for k in range(inner)],
            (table, gathers, *after, *came_rows),
            flops=pairs * work,
        )
        parts += exchange(made)
        after = (away, made[1])
    sent = shape((pairs, sum(late) + 2 * ROWS, LANES), i16)
    late_away = call(
        functools.partial(late_away_kernel, len(pieces)), (sent,), (away, *parts), flops=32 * work
    )
    late_home, near = call(
        functools.partial(late_home_kernel, len(pieces)),
        [shape((pairs, sum(late), LANES), f32), sent],
        (home_rows, late_away, *parts),
        free=True,
    )

    def is_lower(t, d):
        return t // 2 < (t // 2 ^ d)

    from_away = [
        hop(late_away[d - 1:d], inner, 2 * d, lambda t, d=d: not is_lower(t, d)) for d in offsets
    ]
    from_near = [hop(near[d - 1:d], 0, 2 * d) for d in offsets]
    across = hop(late_away, inner, 0, lambda t: any(is_lower(t, d) for d in offsets))
    own_tile, part, code, down, scale = call(
        early_end_kernel,
        [
            shape((panel, panel), f32),
            shape((panel // 2, panel), f32),
            shape((packed_rows(panel // 2, panel), LANES), i16),
            shape((panel, panel), f32),
            shape((2, 8, panel), f32),
        ],
        (home, home_rows, came, late_away),
    )
    mate_part = hop(code, 0, 1)
    whole = shape((1, panel, steps * panel), f32)
    pair, begun = call(
        begin_kernel,
        [shape((2, panel, panel), f32), whole],
        (own_tile, part, mate_part, down, scale),
        [pltpu.VMEM((panel, 2 * panel), f32), pltpu.SemaphoreType.DMA],
        out_hbm=1,
        free=True,
    )
    tiles = call(
        functools.partial(middle_kernel, pairs),
        (shape((steps, panel, panel), f32),),
        (pair, down, late_home, *from_away, across),
        [pltpu.VMEM((panel, panel), f32)],
    )
    return call(
        functools.partial(last_kernel, pairs),
        (whole,),
        (tiles, down, scale, begun, *from_near, *from_away),
        [
            pltpu.VMEM((steps, 8, panel), f32),
            pltpu.VMEM((steps, panel, panel), f32),
            pltpu.VMEM((panel, panel), f32),
            pltpu.VMEM((panel, (steps - 2) * panel), f32),
            pltpu.SemaphoreType.DMA((2,)),
        ],
        out_hbm=1,
        goes_on=3,
    )


def solution(mesh):
    placed = (P("tm", "blk"), P("blk"), P())
    return jax.shard_map(
        on_device, mesh=mesh, in_specs=placed, out_specs=P("blk", "tm", None), check_vma=False
    )
```
